32 devices in a mesh: wide: 8 (over z, x), narrow: 4 (over y, core).
Axes of the slice: x: 2, y: 2, z: 4, core: 2. Of those that a mesh axis runs over, the one named last changes fastest.
Arguments:
- tokens: bfloat16 [8192, 1024], P(('wide', 'narrow')), may hold values from -10 to 10
- doc_ids: int32 [8192], P(('wide', 'narrow')), may hold values from 0 to 1023, as said below
- valid_mask: int32 [8192], P(('wide', 'narrow')), may hold values 0 or 1
- routes: int32 [8192, 1], P(('wide', 'narrow')), may hold values from 0 to 15; in each aligned block of 256 rows (0 to 255, 256 to 511, ...) at most 24 rows name the same one
- cotangent: bfloat16 [8192, 1024], P(('wide', 'narrow')), may hold values from -6 to 6
- attend_gain: bfloat16 [1024], P('wide'), may hold values from 0.5 to 1.5
- attend_weight: bfloat16 [1024, 3072], P('wide'), may hold values from -0.1875 to 0.1875
- output_weight: bfloat16 [1024, 1024], P('wide'), may hold values from -1.5 to 1.5
- mixer_gain: bfloat16 [1024], P('wide'), may hold values from 0.5 to 1.5
- router_weight: bfloat16 [1024, 16], P('wide'), may hold values from -0.125 to 0.125
- blend_weight: bfloat16 [1024, 2], P('wide'), may hold values from -0.1875 to 0.1875
- up_weight: bfloat16 [1024, 4096], P('wide'), may hold values from -0.1875 to 0.1875
- down_weight: bfloat16 [4096, 1024], P('wide'), may hold values from -0.09375 to 0.09375
- expert_up: bfloat16 [16, 1024, 4096], P('wide', None, 'narrow'), may hold values from -0.1875 to 0.1875
- expert_down: bfloat16 [16, 4096, 1024], P('wide', 'narrow'), may hold values from -1.5 to 1.5
Outputs:
- layer_out: bfloat16 [8192, 1024], P(('wide', 'narrow'))
- grad_tokens: bfloat16 [8192, 1024], P(('wide', 'narrow'))
- grad_attend_gain: float32 [1024], P('wide')
- grad_attend_weight: float32 [1024, 3072], P('wide')
- grad_output_weight: float32 [1024, 1024], P('wide')
- grad_mixer_gain: float32 [1024], P('wide')
- grad_router_weight: float32 [1024, 16], P('wide')
- grad_blend_weight: float32 [1024, 2], P('wide')
- grad_up_weight: float32 [1024, 4096], P('wide')
- grad_down_weight: float32 [4096, 1024], P('wide')
- grad_expert_up: float32 [16, 1024, 4096], P('wide', None, 'narrow')
- grad_expert_down: float32 [16, 4096, 1024], P('wide', 'narrow')
- root_means: float32 [4], replicated
The draws below stay inside these ranges and needn't reach their ends.
Inputs may be any that keep to these rules, and one draw needn't show every extreme that they name: `routes`: in each aligned block of 256 rows (the rows of one device) no expert is named by more than 24 rows, a bound that some block reaches. `doc_ids`: along each sequence of 1024 rows the ids never fall; rows of one sequence with equal ids form one document, and each id is the position of its document's last row within the sequence.
All inputs are finite; a program needn't handle non-finite values. No bound on the sum of `valid_mask` on one device may be relied on, other than what follows from the above.
Results may differ from the reference program's by a relative error of at most 0.013.
Values may be sent and summed in bfloat16 or wider, within the bound.
A program may use at most 256 MiB of HBM per device.

```python
import math
import jax
import jax.numpy as jnp
import numpy as np
from jax import lax

D = 1024
HEADS = 16
HEAD_DIM = 64
FF = 4096
TOK_DEV = 256
EXPERTS = 16
CAP = 24
SEQ = 1024
SEQS = 8
TOKENS = 8192


def draw_tokens(key, part):
    key = jax.random.fold_in(key, 5)
    entry_key, column_key = jax.random.split(key)
    row_place = jnp.arange(TOKENS, dtype=jnp.float32)[:, None] / TOKENS
    entries = jnp.clip(jax.random.normal(entry_key, (TOKENS, D), jnp.float32), -4.0, 4.0)
    row_scale = 0.5 + row_place
    column_scale = jnp.exp(jax.random.uniform(column_key, (1, D), jnp.float32, -0.9, 0.47))
    return (entries * row_scale * column_scale).astype(jnp.bfloat16)


def draw_doc_ids(key, part):
    key = jax.random.fold_in(key, 7)
    start_key, stop_key, flag_key = jax.random.split(key, 3)
    positions = jnp.arange(SEQ, dtype=jnp.int32)[None, :]
    long_start = jax.random.randint(start_key, (SEQS, 1), 1, TOK_DEV)
    long_stop = jax.random.randint(stop_key, (SEQS, 1), SEQ - TOK_DEV + 1, SEQ)
    breaks = jax.random.randint(flag_key, (SEQS, SEQ), 0, 24) == 0
    inside = (positions > long_start) & (positions < long_stop)
    starts = breaks & ~inside | (positions == long_start) | (positions == long_stop) | (positions == 0) | (positions == 1)
    marks = jnp.where(starts, positions, SEQ).astype(jnp.int32)
    later = jnp.concatenate([marks[:, 1:], jnp.full((SEQS, 1), SEQ, jnp.int32)], axis=1)
    ends = lax.cummin(later, axis=1, reverse=True)
    return (ends - 1).reshape(TOKENS).astype(jnp.int32)


def plant(values, own_key, smallest, top_value):
    place = [jax.random.randint(jax.random.fold_in(own_key, axis), (), 0, length) for axis, length in enumerate(values.shape)]
    longest = values.shape.index(max(values.shape))
    next_to = place[:longest] + [(place[longest] + 1) % values.shape[longest]] + place[longest + 1:]
    return values.at[tuple(place)].set(smallest).at[tuple(next_to)].set(top_value)


def steps_of(stream_key, extent, cuts, smallest, top_value):
    loudness = 1.0
    for dim, shards_of in cuts:
        heights = jax.random.uniform(jax.random.fold_in(jax.random.fold_in(stream_key, 6), dim), (shards_of,), jnp.float32, smallest / len(cuts), top_value / len(cuts))
        loudness = loudness * jnp.repeat(jnp.exp(heights), extent[dim] // shards_of).reshape((-1,) + (1,) * (len(extent) - 1 - dim))
    return loudness


def routed_block(own_key, own, number, rows, amount, top, most, lean):
    ranking = jax.random.permutation(own_key, amount)
    crowded, usual = load_shares(amount, rows * top, most, lean, True), load_shares(amount, rows * top, most, lean, False)
    places = jnp.arange(amount)

    def named(lengths, turn):
        used = int((lengths > 0).sum())
        fixed = max(1, used // 4)
        shifted = fixed + (places - fixed + turn * (used - fixed)) % max(1, amount - fixed)
        return jnp.zeros((amount,), jnp.int32).at[ranking[jnp.where(places < fixed, places, shifted)]].set(jnp.asarray(lengths, jnp.int32))

    lengths = jnp.where(number % 4 == 0, named(crowded, number // 4), named(usual, number - number // 4 - 1))
    mixed = jax.random.permutation(jax.random.fold_in(own, 3), amount)
    source_of, sink = mixed[0:amount // 2 * 2:2], mixed[1:amount // 2 * 2:2]
    margin = jnp.minimum(lengths[source_of] - 1, most - lengths[sink]) // 2
    margin = jnp.where((source_of == ranking[0]) | (sink == ranking[0]) | (lengths[sink] == 0), 0, jnp.maximum(margin, 0))
    shifted = jax.random.randint(jax.random.fold_in(own, 4), (amount // 2,), 0, 1 << 20) % (margin + 1)
    lengths = lengths.at[source_of].add(-shifted).at[sink].add(shifted)
    labels = jnp.searchsorted(jnp.cumsum(lengths), jnp.arange(rows * top), side="right").astype(jnp.int32)
    table = labels.reshape(top, rows).T
    table = table[jax.random.permutation(jax.random.fold_in(own, 1), rows)]
    turn = jax.random.randint(jax.random.fold_in(own, 2), (rows, 1), 0, top)
    return jnp.take_along_axis(table, (jnp.arange(top)[None, :] + turn) % top, axis=1)


def load_shares(count, total, most, lean, full):
    loads = [(1 << 20) // math.isqrt(standing ** lean) + 1 for standing in range(1, count + 1)]
    largest = most if full else min(most, max(-(-total // count), total * loads[0] // sum(loads)))
    least = 1 if total - largest >= count - 1 else 0
    given, surplus = [largest] + [least] * (count - 1), total - largest - least * (count - 1)
    while surplus > 0:
        movable = [i for i in range(1, count) if given[i] < largest] or [i for i in range(1, count) if given[i] < most]
        whole, remaining = sum([loads[i] for i in movable]), surplus
        for i in movable:
            more = min(most - given[i], max(1, remaining * loads[i] // whole), surplus)
            given[i] = given[i] + more
            surplus = surplus - more
    return np.array(given)


def centred(stream_key, shape, scale, limit, shards=(), held_as=jnp.bfloat16):
    drawn = jax.random.normal(stream_key, shape, jnp.float32) * scale
    if len(shards) > 0:
        drawn = steps_of(stream_key, shape, shards, -0.22, 0.18) * drawn
    return jnp.clip(drawn, min=-limit, max=limit).astype(held_as)


def setup_inputs(seed: int = 0) -> dict:
    arg_keys = jax.random.split(jax.random.key(seed), 16)
    tokens = draw_tokens(jax.random.fold_in(arg_keys[15], 71), 0)
    doc_ids = draw_doc_ids(jax.random.fold_in(arg_keys[15], 71), 0)
    valid_mask = plant((jax.random.randint(arg_keys[2], (TOKENS,), 0, 4) < 3).astype(jnp.int32), jax.random.fold_in(arg_keys[2], 1), 0, 1)
    routes_keys = jax.random.split(jax.random.fold_in(arg_keys[3], 1), TOKENS // TOK_DEV)
    routes_turns = jax.random.permutation(jax.random.fold_in(arg_keys[3], 3), TOKENS // TOK_DEV)
    routes = jax.vmap(lambda own, number: routed_block(jax.random.fold_in(arg_keys[3], 2), own, number, TOK_DEV, EXPERTS, 1, CAP, 2))(routes_keys, routes_turns).reshape((TOKENS, 1))
    cotangent = centred(arg_keys[4], (TOKENS, D), 1.0, 6.0, ((0, 32),))
    attend_gain = jnp.clip(1.0 + 0.1 * jax.random.normal(arg_keys[5], (D,), jnp.float32), 0.5, 1.5).astype(jnp.bfloat16)
    attend_weight = centred(arg_keys[6], (D, 3 * D), D ** -0.5, 0.1875, ((0, 8),))
    output_weight = centred(arg_keys[7], (D, D), (max(D // 64, 1)) ** -0.5, 1.5, ((0, 8),))
    mixer_gain = jnp.clip(1.0 + 0.1 * jax.random.normal(arg_keys[8], (D,), jnp.float32), 0.5, 1.5).astype(jnp.bfloat16)
    router_weight = centred(arg_keys[9], (D, EXPERTS), (2 * D) ** -0.5, 0.125, ((0, 8),))
    blend_weight = centred(arg_keys[10], (D, 2), D ** -0.5, 0.1875, ((0, 8),))
    up_weight = centred(arg_keys[11], (D, FF), D ** -0.5, 0.1875, ((0, 8),))
    down_weight = centred(arg_keys[12], (FF, D), FF ** -0.5, 0.09375, ((0, 8),))
    expert_up = centred(arg_keys[13], (EXPERTS, D, FF), D ** -0.5, 0.1875, ((0, 8), (2, 4)))
    expert_down = centred(arg_keys[14], (EXPERTS, FF, D), (max(FF // (EXPERTS * EXPERTS), 1)) ** -0.5, 1.5, ((0, 8), (1, 4)))
    return {"tokens": tokens, "doc_ids": doc_ids, "valid_mask": valid_mask, "routes": routes, "cotangent": cotangent, "attend_gain": attend_gain, "attend_weight": attend_weight, "output_weight": output_weight, "mixer_gain": mixer_gain, "router_weight": router_weight, "blend_weight": blend_weight, "up_weight": up_weight, "down_weight": down_weight, "expert_up": expert_up, "expert_down": expert_down}


eps_norm = 1e-05
masked_score = -1e+30
highest = lax.Precision.HIGHEST

@jax.custom_vjp
def low(v):
    return lax.optimization_barrier(v.astype(jnp.bfloat16)).astype(jnp.float32)

@jax.custom_vjp
def low_back(v):
    return v

def low_keep(v):
    return (low(v), None)

def low_pass(kept, grad):
    return (grad,)

def back_keep(v):
    return (v, None)

def back_low(kept, grad):
    return (low(grad),)
low.defvjp(low_keep, low_pass)
low_back.defvjp(back_keep, back_low)

def layer_norm(values, gain_vec):
    center = values - lax.optimization_barrier(jnp.mean(values, axis=-1, keepdims=True))
    spread = lax.optimization_barrier(jnp.mean(center * center, axis=-1, keepdims=True))
    return center * lax.rsqrt(spread + eps_norm) * gain_vec

def smooth_gelu(values):
    tanh_input = 0.7978845608028654 * (values + 0.044715 * values * values * values)
    return 0.5 * values * (1.0 + jnp.tanh(tanh_input))

def soft_max(logits):
    row_max = lax.optimization_barrier(jnp.max(logits, axis=-1, keepdims=True))
    exp_shift = jnp.exp(logits - row_max)
    return exp_shift / lax.optimization_barrier(jnp.sum(exp_shift, axis=-1, keepdims=True))

def matmul(left, right):
    return jnp.dot(left, right, precision=highest, preferred_element_type=jnp.float32)

def attend_sequence(pieces):
    queries, key_rows, value_rows, doc_row = pieces
    positions = jnp.arange(SEQ, dtype=jnp.int32)
    allowed = (positions[None, :] <= positions[:, None]) & (doc_row[None, :] == doc_row[:, None])
    query_heads = queries.reshape(SEQ, HEADS, HEAD_DIM)
    key_heads = key_rows.reshape(SEQ, HEADS, HEAD_DIM)
    value_heads = value_rows.reshape(SEQ, HEADS, HEAD_DIM)
    scores = jnp.einsum('thd,shd->hts', query_heads, key_heads, precision=highest) * HEAD_DIM ** (-0.5)
    scores = low_back(jnp.where(allowed[None], scores, masked_score))
    prob_rows = low(soft_max(scores))
    mixed_heads = jnp.einsum('hts,shd->thd', prob_rows, value_heads, precision=highest)
    return mixed_heads.reshape(SEQ, D)

def expert_rows(pieces):
    rows_in, weight_in, weight_out = pieces
    hidden = low_back(matmul(rows_in, weight_in))
    return matmul(low(smooth_gelu(hidden)), weight_out)

def experts_apply(normed_mix, routes, expert_up, expert_down):
    block_count = TOKENS // TOK_DEV
    route_rows = routes[:, 0].reshape(block_count, TOK_DEV)
    route_hits = (route_rows[:, :, None] == jnp.arange(EXPERTS, dtype=jnp.int32)[None, None, :]).astype(jnp.int32)
    slot_rank = lax.optimization_barrier(jnp.sum((jnp.cumsum(route_hits, axis=1) - 1) * route_hits, axis=2))
    slot_of = route_rows * CAP + slot_rank
    place_map = (slot_of[:, None, :] == jnp.arange(EXPERTS * CAP, dtype=jnp.int32)[None, :, None]).astype(jnp.float32)
    packed = jnp.einsum('bst,btd->bsd', place_map, normed_mix.reshape(block_count, TOK_DEV, D), precision=highest)
    by_expert = packed.reshape(block_count, EXPERTS, CAP, D).transpose(1, 0, 2, 3).reshape(EXPERTS, block_count * CAP, D)
    results = lax.map(jax.checkpoint(expert_rows), (by_expert, expert_up, expert_down))
    returned = results.reshape(EXPERTS, block_count, CAP, D).transpose(1, 0, 2, 3).reshape(block_count, EXPERTS * CAP, D)
    spread_back = jnp.einsum('bst,bsd->btd', place_map, returned, precision=highest)
    return spread_back.reshape(TOKENS, D)

def forward(tokens, attend_gain, attend_weight, output_weight, mixer_gain, router_weight, blend_weight, up_weight, down_weight, expert_up, expert_down, doc_ids, routes):
    normed_attend = low(layer_norm(tokens, attend_gain))
    projected = low_back(low(matmul(normed_attend, attend_weight)))
    pieces = (projected[:, :D].reshape(SEQS, SEQ, D), projected[:, D:2 * D].reshape(SEQS, SEQ, D), projected[:, 2 * D:].reshape(SEQS, SEQ, D), doc_ids.reshape(SEQS, SEQ))
    attn_mixed = low_back(low(lax.map(jax.checkpoint(attend_sequence), pieces).reshape(TOKENS, D)))
    attention_out = low_back(matmul(attn_mixed, output_weight))
    residual_mid = tokens + attention_out
    normed_mix = low(layer_norm(residual_mid, mixer_gain))
    router_probs = soft_max(matmul(normed_mix, router_weight))
    onehot = (routes[:, 0:1] == jnp.arange(EXPERTS, dtype=jnp.int32)[None, :]).astype(jnp.float32)
    chosen = lax.optimization_barrier(jnp.sum(router_probs * onehot, axis=1, keepdims=True))
    blend_probs = soft_max(matmul(normed_mix, blend_weight))
    up_pre = low_back(matmul(normed_mix, up_weight))
    dense_out = low_back(matmul(low(smooth_gelu(up_pre)), down_weight))
    expert_tok = low_back(experts_apply(normed_mix, routes, expert_up, expert_down))
    ffn_out = blend_probs[:, 0:1] * chosen * expert_tok + blend_probs[:, 1:2] * dense_out
    return (residual_mid + ffn_out, (residual_mid, attention_out, ffn_out))

def reference(tokens, doc_ids, valid_mask, routes, cotangent, attend_gain, attend_weight, output_weight, mixer_gain, router_weight, blend_weight, up_weight, down_weight, expert_up, expert_down):
    primals = tuple((argument.astype(jnp.float32) for argument in (tokens, attend_gain, attend_weight, output_weight, mixer_gain, router_weight, blend_weight, up_weight, down_weight, expert_up, expert_down)))

    def run_layer(*floats):
        return forward(*floats, doc_ids, routes)
    layer_full, pullback, streams_kept = jax.vjp(run_layer, *primals, has_aux=True)
    valid_rows = valid_mask.astype(jnp.float32)[:, None]
    gradients = pullback(cotangent.astype(jnp.float32) * valid_rows)
    residual_mid, attention_out, ffn_out = streams_kept
    square_sums = jnp.stack([jnp.sum(valid_rows * branch_value * branch_value) for branch_value in (residual_mid, layer_full, attention_out, ffn_out)])
    root_means = jnp.sqrt(square_sums / (jnp.maximum(jnp.sum(valid_rows), 1.0) * D))
    return (layer_full.astype(jnp.bfloat16), gradients[0].astype(jnp.bfloat16), gradients[1], gradients[2], gradients[3], gradients[4], gradients[5], gradients[6], gradients[7], gradients[8], gradients[9], gradients[10], root_means)
```

```python
import functools

import jax
import jax.numpy as jnp
from jax import lax
from jax.experimental import pallas as pl
from jax.experimental.pallas import tpu as pltpu
from jax.sharding import PartitionSpec as P

HEAD_DIM = 64
PAIR = 2 * HEAD_DIM
Q_TILE = 256
SMALL = 128
eps_norm = 1e-05
masked_score = -1e30
f32 = jnp.float32
bf16 = jnp.bfloat16


def mm(a, b, ca=1, cb=0):
    return lax.dot_general(a, b, (((ca,), (cb,)), ((), ())), preferred_element_type=f32)


def norm_stats(values):
    center = values - jnp.mean(values, axis=-1, keepdims=True)
    scale = lax.rsqrt(jnp.mean(center * center, axis=-1, keepdims=True) + eps_norm)
    return center * scale, scale


def norm_back(normed, scale, gain, grad):
    u = grad * gain
    return scale * (
        u
        - jnp.mean(u, axis=-1, keepdims=True)
        - normed * jnp.mean(u * normed, axis=-1, keepdims=True)
    )


GELU_A = 0.7978845608028654
GELU_B = 0.044715


def gelu(v):
    return 0.5 * v * (1.0 + jnp.tanh(GELU_A * (v + GELU_B * v * v * v)))


def gelu_both(v):
    t = jnp.tanh(GELU_A * (v + GELU_B * v * v * v))
    value = 0.5 * v * (1.0 + t)
    slope = 0.5 * (1.0 + t) + 0.5 * v * (1.0 - t * t) * (GELU_A * (1.0 + 3.0 * GELU_B * v * v))
    return value, slope


def soft_max(logits):
    shifted = jnp.exp(logits - jnp.max(logits, axis=-1, keepdims=True))
    return shifted / jnp.sum(shifted, axis=-1, keepdims=True)


def head_mask(half):
    lanes = lax.broadcasted_iota(jnp.int32, (1, PAIR), 1)
    return (lanes // HEAD_DIM) == half


def attend_tile(tile, qkv_ref, doc_cols, out_ref, lse_ref, mask_ref, vt_ref):
    cols = out_ref.shape[1]
    extent = (tile + 1) * Q_TILE
    here, seen = pl.ds(tile * Q_TILE, Q_TILE), pl.ds(0, extent)
    mask_tile(tile, doc_cols, mask_ref)

    def pair_step(pair, carry):
        q_cols = pl.ds(pl.multiple_of(pair * PAIR, PAIR), PAIR)
        k_cols = pl.ds(pl.multiple_of(cols + pair * PAIR, PAIR), PAIR)
        v_cols = pl.ds(pl.multiple_of(2 * cols + pair * PAIR, PAIR), PAIR)
        if tile == 0:
            vt_ref[pair] = qkv_ref[:, v_cols].T
        queries = qkv_ref[here, q_cols] * jnp.asarray(HEAD_DIM**-0.5, bf16)
        mixed = jnp.zeros((PAIR, Q_TILE), f32)
        for half in range(2):
            one = jnp.where(head_mask(half), queries, jnp.zeros_like(queries))
            scores = mm(qkv_ref[seen, k_cols], one, 1, 1) + mask_ref[seen, :]
            top = jnp.max(scores, axis=0, keepdims=True)
            shifted = jnp.exp(scores - top)
            total = jnp.sum(shifted, axis=0, keepdims=True)
            low = (shifted * (1.0 / total)).astype(bf16)
            lse_ref[pair, pl.ds(half, 1), here] = top + jnp.log(total)
            got = mm(vt_ref[pair, :, seen], low)
            sublanes = lax.broadcasted_iota(jnp.int32, (PAIR, 1), 0)
            mixed = jnp.where((sublanes // HEAD_DIM) == half, got, mixed)
        out_ref[here, q_cols] = mixed.T.astype(bf16)
        return carry

    lax.fori_loop(0, cols // PAIR, pair_step, 0)


def mask_tile(tile, doc_cols, mask_ref):
    row = (tile * Q_TILE + lax.broadcasted_iota(jnp.int32, (Q_TILE, Q_TILE), 1)).astype(f32)
    for block in range(tile + 1):
        allowed = doc_cols[block] >= row
        if block == tile:
            key = (tile * Q_TILE + lax.broadcasted_iota(jnp.int32, (Q_TILE, Q_TILE), 0)).astype(f32)
            allowed = allowed & (key <= row)
        mask_ref[pl.ds(block * Q_TILE, Q_TILE), :] = jnp.where(allowed, 0.0, masked_score)


def attend_back_kernel(qkv_ref, doc_ref, lse_ref, grad_ref, out_ref, mask_ref, dk_ref, dv_ref):
    rows, cols = grad_ref.shape
    pairs = cols // PAIR
    dk_ref[...] = jnp.zeros_like(dk_ref)
    dv_ref[...] = jnp.zeros_like(dv_ref)
    for tile in range(rows // Q_TILE):
        extent = (tile + 1) * Q_TILE
        here = pl.ds(tile * Q_TILE, Q_TILE)
        seen = pl.ds(0, extent)
        mask_tile(tile, [doc_ref[pl.ds(b * Q_TILE, Q_TILE), :] for b in range(tile + 1)], mask_ref)

        def pair_step(pair, carry):
            q_cols = pl.ds(pl.multiple_of(pair * PAIR, PAIR), PAIR)
            k_cols = pl.ds(pl.multiple_of(cols + pair * PAIR, PAIR), PAIR)
            v_cols = pl.ds(pl.multiple_of(2 * cols + pair * PAIR, PAIR), PAIR)
            queries = qkv_ref[here, q_cols] * jnp.asarray(HEAD_DIM**-0.5, bf16)
            keys, values = qkv_ref[seen, k_cols], qkv_ref[seen, v_cols]
            grads = grad_ref[here, q_cols]
            dq = jnp.zeros((PAIR, Q_TILE), f32)
            for half in range(2):
                on = head_mask(half)
                q_one = jnp.where(on, queries, jnp.zeros_like(queries))
                g_one = jnp.where(on, grads, jnp.zeros_like(grads))
                probs = jnp.exp(mm(keys, q_one, 1, 1) + mask_ref[seen, :] - lse_ref[pair, pl.ds(half, 1), here])
                dv_ref[pair, seen, :] += mm(probs.astype(bf16), g_one)
                back = mm(values, g_one, 1, 1)
                low = (probs * (back - jnp.sum(probs * back, axis=0, keepdims=True))).astype(bf16)
                dk_ref[pair, seen, :] += mm(low, q_one)
                got = mm(keys, low, 0, 0)
                sublanes = lax.broadcasted_iota(jnp.int32, (PAIR, 1), 0)
                dq = jnp.where((sublanes // HEAD_DIM) == half, got, dq)
            out_ref[here, q_cols] = (dq.T * HEAD_DIM**-0.5).astype(bf16)
            return carry

        lax.fori_loop(0, pairs, pair_step, 0)
    for pair in range(pairs):
        out_ref[:, cols + pair * PAIR : cols + (pair + 1) * PAIR] = dk_ref[pair].astype(bf16)
        out_ref[:, 2 * cols + pair * PAIR : 2 * cols + (pair + 1) * PAIR] = dv_ref[pair].astype(bf16)


def attend_back(qkv, doc_col, lse, grad):
    rows, cols = grad.shape
    vmem = pl.BlockSpec(memory_space=pltpu.VMEM)
    return pl.pallas_call(
        attend_back_kernel,
        out_shape=jax.ShapeDtypeStruct((rows, 3 * cols), bf16),
        in_specs=[vmem] * 4,
        out_specs=vmem,
        scratch_shapes=[
            pltpu.VMEM((rows, Q_TILE), f32),
            pltpu.VMEM((cols // PAIR, rows, PAIR), f32),
            pltpu.VMEM((cols // PAIR, rows, PAIR), f32),
        ],
        compiler_params=pltpu.CompilerParams(vmem_limit_bytes=56 * 2**20),
        cost_estimate=pl.CostEstimate(flops=20 * rows * rows * cols, bytes_accessed=16 * rows * cols, transcendentals=0),
        name="attend_back",
    )(qkv, doc_col, lse, grad)


MESH = pl.DeviceIdType.MESH


class Spot:
    def __init__(self, groups, lanes):
        self.W, self.L = groups, lanes
        self.X = 1 << ((groups.bit_length() - 1) // 2)
        self.Z, self.Y = groups // self.X, lanes // 2
        self.g, self.l = lax.axis_index("wide"), lax.axis_index("narrow")
        self.z, self.x = self.g // self.X, self.g % self.X
        self.y, self.c = self.l // 2, self.l % 2

    def zx_peer(self, dz, dx):
        return lax.rem(self.z + dz, self.Z) * self.X + lax.rem(self.x + dx, self.X)

    def z_peer(self, d):
        return self.zx_peer(d, 0)

    def x_peer(self, d):
        return self.zx_peer(0, d)

    def y_peer(self, d):
        return lax.rem(self.y + d, self.Y) * 2 + self.c

    def core_peer(self):
        return self.y * 2 + 1 - self.c

    def w_peer(self, d):
        return lax.rem(self.g + d, self.W)

    def l_peer(self, d):
        return lax.rem(self.l + d, self.L)

    def greet(self, lane_peers=True):
        barrier = pltpu.get_barrier_semaphore()
        met = self.L - 1
        for d in range(1, self.L):
            pl.semaphore_signal(barrier, 1, device_id=(self.g, self.l_peer(d)), device_id_type=MESH)
        if lane_peers:
            met += self.W - 1
            for d in range(1, self.W):
                pl.semaphore_signal(barrier, 1, device_id=(self.w_peer(d), self.l), device_id_type=MESH)
        pl.semaphore_wait(barrier, met)


def remote(src, dst, send_sem, recv_sem, group, lane):
    return pltpu.make_async_remote_copy(src, dst, send_sem, recv_sem, device_id=(group, lane), device_id_type=MESH)


class LaneGather:
    def __init__(self, spot, src, place, sems):
        self.s, self.src, self.place = spot, src, place
        self.z_sem, self.x_sem, self.r_sem, self.own_sem = sems

    @staticmethod
    def sems(W, X):
        dma = pltpu.SemaphoreType.DMA
        return [dma((W // X,)), dma((W // X, X)), dma((W,)), dma((1,))]

    def z_copy(self, d):
        s = self.s
        return remote(self.src, self.place(s.g), self.z_sem.at[d], self.r_sem.at[s.g], s.z_peer(d), s.l)

    def x_copy(self, d, e):
        s = self.s
        w = s.z_peer(d)
        src = self.src if d == 0 else self.place(w)
        return remote(src, self.place(w), self.x_sem.at[d, e], self.r_sem.at[w], s.x_peer(e), s.l)

    def got(self, w):
        s = self.s
        remote(self.src, self.place(w), self.z_sem.at[0], self.r_sem.at[w], s.x_peer(1), s.l).wait_recv()

    def own(self):
        return pltpu.make_async_copy(self.src, self.place(self.s.g), self.own_sem.at[0])

    def start(self):
        for d in range(1, self.s.Z):
            self.z_copy(d).start()
        for e in range(1, self.s.X):
            self.x_copy(0, e).start()
        self.own().start()

    def forward(self):
        for d in range(1, self.s.Z):
            self.got(self.s.z_peer(d))
            for e in range(1, self.s.X):
                self.x_copy(d, e).start()

    def arrive(self):
        s = self.s
        for d in range(s.Z):
            for e in range(1, s.X):
                self.got(s.zx_peer(d, e))
        self.own().wait()

    def sent(self):
        for d in range(1, self.s.Z):
            self.z_copy(d).wait_send()
        for d in range(self.s.Z):
            for e in range(1, self.s.X):
                self.x_copy(d, e).wait_send()


class GroupGather:
    def __init__(self, spot, src, place, sems, own=True):
        self.s, self.src, self.place, self.has_own = spot, src, place, own
        self.y_sem, self.c_sem, self.r_sem, self.own_sem = sems

    @staticmethod
    def sems(L):
        dma = pltpu.SemaphoreType.DMA
        return [dma((L // 2,)), dma((L // 2,)), dma((L,)), dma((1,))]

    def y_copy(self, d):
        s = self.s
        return remote(self.src, self.place(s.l), self.y_sem.at[d], self.r_sem.at[s.l], s.g, s.y_peer(d))

    def c_copy(self, d):
        s = self.s
        l = s.y_peer(d)
        src = self.src if d == 0 else self.place(l)
        return remote(src, self.place(l), self.c_sem.at[d], self.r_sem.at[l], s.g, s.core_peer())

    def got(self, l):
        s = self.s
        remote(self.src, self.place(l), self.y_sem.at[0], self.r_sem.at[l], s.g, s.core_peer()).wait_recv()

    def own(self):
        return pltpu.make_async_copy(self.src, self.place(self.s.l), self.own_sem.at[0])

    def start(self):
        for d in range(1, self.s.Y):
            self.y_copy(d).start()
        self.c_copy(0).start()
        if self.has_own:
            self.own().start()

    def forward(self):
        for d in range(1, self.s.Y):
            self.got(self.s.y_peer(d))
            self.c_copy(d).start()

    def arrive(self):
        s = self.s
        for d in range(s.Y):
            self.got(lax.rem(s.y + d, s.Y) * 2 + 1 - s.c)
        if self.has_own:
            self.own().wait()

    def sent(self):
        for d in range(1, self.s.Y):
            self.y_copy(d).wait_send()
        for d in range(self.s.Y):
            self.c_copy(d).wait_send()


class LaneSwap:
    def __init__(self, spot, src, dst, sems):
        self.s, self.src, self.dst = spot, src, dst
        self.s_sem, self.r_sem = sems

    @staticmethod
    def sems(W):
        return [pltpu.SemaphoreType.DMA((W,)), pltpu.SemaphoreType.DMA((W,))]

    def copy(self, d):
        s = self.s
        w = s.w_peer(d)
        return remote(self.src(w), self.dst(s.g), self.s_sem.at[d], self.r_sem.at[s.g], w, s.l)

    def own(self):
        return pltpu.make_async_copy(self.src(self.s.g), self.dst(self.s.g), self.s_sem.at[0])

    def start(self):
        for d in range(1, self.s.W):
            self.copy(d).start()
        self.own().start()

    def got(self, w):
        s = self.s
        remote(self.src(w), self.dst(w), self.s_sem.at[0], self.r_sem.at[w], s.w_peer(1), s.l).wait_recv()

    def arrive(self):
        for d in range(1, self.s.W):
            self.got(self.s.w_peer(self.s.W - d))
        self.own().wait()

    def sent(self):
        for d in range(1, self.s.W):
            self.copy(d).wait_send()


class GroupSwap:
    def __init__(self, spot, src, dst, sems):
        self.s, self.src, self.dst = spot, src, dst
        self.s_sem, self.r_sem = sems

    @staticmethod
    def sems(L):
        return [pltpu.SemaphoreType.DMA((L,)), pltpu.SemaphoreType.DMA((L,))]

    def copy(self, l):
        s = self.s
        return remote(self.src(l), self.dst(s.l), self.s_sem.at[l], self.r_sem.at[s.l], s.g, l)

    def own(self):
        s = self.s
        return pltpu.make_async_copy(self.src(s.l), self.dst(s.l), self.s_sem.at[s.l])

    def send(self, l):
        @pl.when(self.s.l == l)
        def _():
            self.own().start()

        @pl.when(self.s.l != l)
        def _():
            self.copy(l).start()

    def arrive(self):
        s = self.s
        for d in range(1, s.L):
            l = s.l_peer(d)
            remote(self.src(l), self.dst(l), self.s_sem.at[l], self.r_sem.at[l], s.g, l).wait_recv()
        self.own().wait()

    def sent(self):
        for d in range(1, self.s.L):
            self.copy(self.s.l_peer(d)).wait_send()


def rows_norm(src, gain, dst, count, step=64):
    def body(i, carry):
        at = pl.ds(pl.multiple_of(i * step, step), step)
        normed, _ = norm_stats(src[at, :].astype(f32))
        dst[at, :] = (normed * gain).astype(bf16)
        return carry

    lax.fori_loop(0, count // step, body, 0)


def front_kernel(
    groups, lanes, local, cap, slots,
    tokens, cot, meta, small, attend_w, output_w, up_w, down_w,
    normed_out, qkv, lse, attn_mixed, attention_out, mix_all, small_all, meta_all, place,
    attend_all, output_all, got_mix, got_cot, cot_all, up_all, down_all,
    tok_all, attend_mine, up_mine, mixed, mask, vt, packed_mix, packed_cot, stage_sem, spread_y, spread_c, spread_r, *sems,
):
    s = Spot(groups, lanes)
    rows, width = tokens.shape
    head_cols = width // lanes
    shard = attend_w.shape[0]
    depth = down_all.shape[0] // groups
    sems = list(sems)

    def take(n):
        out = sems[:n]
        del sems[:n]
        return out

    def blocks(ref, n):
        return lambda i: ref.at[pl.ds(pl.multiple_of(i * n, n), n)]

    def cols(i):
        return pl.ds(pl.multiple_of(i * head_cols, head_cols), head_cols)

    staged = [
        pltpu.make_async_copy(
            attend_w.at[:, pl.ds(pl.multiple_of(p * width + s.l * head_cols, head_cols), head_cols)],
            attend_mine.at[:, pl.ds(p * head_cols, head_cols)], stage_sem.at[p])
        for p in range(3)
    ]
    if up_w.shape[1] != up_mine.shape[1]:
        fine = up_mine.shape[1] // groups
        staged += [
            pltpu.make_async_copy(
                up_w.at[:, pl.ds(pl.multiple_of((w * lanes + s.l) * fine, fine), fine)],
                up_mine.at[:, pl.ds(w * fine, fine)], stage_sem.at[3 + w])
            for w in range(groups)
        ]
    else:
        staged += [pltpu.make_async_copy(up_w, up_mine, stage_sem.at[3])]
    for c in staged:
        c.start()

    tok = GroupGather(s, tokens, blocks(tok_all, rows), take(4))
    met = GroupGather(s, meta, lambda l: meta_all.at[l], take(4))
    cots = GroupGather(s, cot, blocks(cot_all, rows), take(4))
    mix = GroupGather(s, blocks(mix_all, rows)(s.l), blocks(mix_all, rows), take(4), own=False)
    outs = GroupGather(s, output_all.at[:, cols(s.l)], lambda l: output_all.at[:, cols(l)], take(4), own=False)
    cot_spread = GroupGather(s, got_cot.at[s.l], lambda l: got_cot.at[l], take(4), own=False)
    att = LaneGather(s, attend_mine, blocks(attend_all, shard), take(4))
    sml = LaneGather(s, small, blocks(small_all, shard), take(4))
    out = LaneGather(s, output_w.at[:, cols(s.l)],
                     lambda w: output_all.at[pl.ds(pl.multiple_of(w * shard, shard), shard), cols(s.l)], take(4))
    up = LaneGather(s, up_mine, blocks(up_all, shard), take(4))
    down = LaneGather(s, down_w.at[pl.ds(pl.multiple_of(s.l * depth, depth), depth)], blocks(down_all, depth), take(4))
    swap = GroupSwap(s, blocks(mixed, rows), lambda l: attn_mixed.at[:, cols(l)], take(2))
    mix_swap = LaneSwap(s, blocks(packed_mix, slots), lambda w: got_mix.at[s.l, w], take(2))
    cot_swap = LaneSwap(s, blocks(packed_cot, slots), lambda w: got_cot.at[s.l, w], take(2))

    def spread(d):
        w = s.w_peer(groups - d)
        return GroupGather(s, got_mix.at[s.l, w], lambda l: got_mix.at[l, w],
                           [spread_y.at[w], spread_c.at[w], spread_r.at[w], None], own=False)

    mix_spread = [spread(d) for d in range(groups)]

    s.greet()
    for c in staged[:3]:
        c.wait()
    sml.start()
    met.start()
    tok.start()
    att.start()
    for c in staged[3:]:
        c.wait()
    mine = meta[...].T
    valid, route = mine[:, 1:2], mine[:, 2:3].astype(jnp.int32)
    column = lax.broadcasted_iota(jnp.int32, (rows, SMALL), 1)
    hits = (column == route).astype(f32)
    earlier = lax.broadcasted_iota(jnp.int32, (rows, rows), 1) < lax.broadcasted_iota(jnp.int32, (rows, rows), 0)
    rank = jnp.sum(hits * mm(earlier.astype(f32).astype(bf16), hits.astype(bf16)), axis=1, keepdims=True).astype(jnp.int32)
    slot = (route // local) * slots + (route % local) * cap + rank
    spots = (slot == lax.broadcasted_iota(jnp.int32, (rows, groups * slots), 1)).astype(f32)
    place[...] = spots.astype(bf16)
    packed_cot[...] = mm((spots * valid).astype(bf16), cot[...], 0, 0).astype(bf16)
    sml.forward()
    met.forward()
    sml.arrive()
    met.arrive()
    tok.forward()
    att.forward()
    cots.start()
    tok.arrive()
    gains = small_all[...].astype(f32).T
    rows_norm(tok_all, gains[0:1, :], normed_out, rows * lanes)
    att.arrive()
    out.start()
    up.start()

    def project(i, carry):
        at = pl.ds(pl.multiple_of(i * Q_TILE, Q_TILE), Q_TILE)
        qkv[at, :] = mm(normed_out[at, :], attend_all[...]).astype(bf16)
        return carry

    lax.fori_loop(0, rows * lanes // Q_TILE, project, 0)
    out.forward()
    doc_cols = [meta_all[l].T[:, 0:1] for l in range(lanes)]
    for tile in range(lanes):
        attend_tile(tile, qkv, doc_cols, mixed, lse, mask, vt)
        swap.send(tile)
        if tile == 0:
            out.arrive()
            outs.start()
        if tile == 1:
            cots.forward()
    outs.forward()
    up.forward()
    down.start()
    outs.arrive()
    swap.arrive()
    attention_out[...] = mm(attn_mixed[...], output_all[...])
    gain = small_all[...].astype(f32).T[1:2, :]
    base = pl.multiple_of(s.l * rows, rows)

    def mid(i, carry):
        at = pl.ds(pl.multiple_of(i * 64, 64), 64)
        normed, _ = norm_stats(tokens[at, :].astype(f32) + attention_out[at, :])
        mix_all[pl.ds(pl.multiple_of(base + i * 64, 64), 64), :] = (normed * gain).astype(bf16)
        return carry

    lax.fori_loop(0, rows // 64, mid, 0)
    mix.start()
    packed_mix[...] = mm(place[...], mix_all[pl.ds(base, rows), :], 0, 0).astype(bf16)
    mix_swap.start()
    cot_swap.start()
    down.forward()
    mix.forward()
    for d in range(groups):
        if d:
            mix_swap.got(s.w_peer(groups - d))
        else:
            mix_swap.own().wait()
        mix_spread[d].start()
    cot_swap.arrive()
    cot_spread.start()
    for task in mix_spread:
        task.forward()
    cot_spread.forward()
    mix.arrive()
    for task in mix_spread:
        task.arrive()
    cot_spread.arrive()
    cots.arrive()
    up.arrive()
    down.arrive()
    for task in [tok, met, cots, mix, outs, cot_spread, att, sml, out, up, down, swap, mix_swap, cot_swap] + mix_spread:
        task.sent()


def front(groups, lanes, local, cap, slots, tokens, cot, meta, small, attend_w, output_w, up_w, down_w):
    rows, width = tokens.shape
    X = 1 << ((groups.bit_length() - 1) // 2)
    Y = lanes // 2
    everyone = rows * lanes
    head_cols = width // lanes
    hidden = down_w.shape[0] // lanes * groups
    shard = attend_w.shape[0]
    vmem, anywhere = pl.BlockSpec(memory_space=pltpu.VMEM), pl.BlockSpec(memory_space=pl.ANY)
    dma = pltpu.SemaphoreType.DMA
    of = jax.ShapeDtypeStruct
    sems = []
    for _ in range(6):
        sems += GroupGather.sems(lanes)
    for _ in range(5):
        sems += LaneGather.sems(groups, X)
    sems += GroupSwap.sems(lanes) + LaneSwap.sems(groups) + LaneSwap.sems(groups)
    outs = [
        (of((everyone, width), bf16), vmem),
        (of((everyone, 3 * head_cols), bf16), vmem),
        (of((head_cols // PAIR, 2, everyone), f32), vmem),
        (of((rows, width), bf16), vmem),
        (of((rows, width), f32), vmem),
        (of((everyone, width), bf16), vmem),
        (of((width, SMALL), bf16), vmem),
        (of((lanes, 8, rows), f32), vmem),
        (of((rows, groups * slots), bf16), vmem),
        (of((width, 3 * head_cols), bf16), vmem),
        (of((width, width), bf16), vmem),
        (of((lanes, groups, slots, width), bf16), anywhere),
        (of((lanes, groups, slots, width), bf16), anywhere),
        (of((everyone, width), bf16), anywhere),
        (of((width, hidden), bf16), anywhere),
        (of((hidden, width), bf16), anywhere),
    ]
    return pl.pallas_call(
        functools.partial(front_kernel, groups, lanes, local, cap, slots),
        out_shape=[o for o, _ in outs],
        in_specs=[vmem] * 4 + [anywhere] * 4,
        out_specs=[p for _, p in outs],
        scratch_shapes=[
            pltpu.VMEM((everyone, width), bf16),
            pltpu.VMEM((shard, 3 * head_cols), bf16),
            pltpu.VMEM((shard, hidden), bf16),
            pltpu.VMEM((everyone, head_cols), bf16),
            pltpu.VMEM((everyone, Q_TILE), f32),
            pltpu.VMEM((head_cols // PAIR, PAIR, everyone), bf16),
            pltpu.VMEM((groups * slots, width), bf16),
            pltpu.VMEM((groups * slots, width), bf16),
            dma((3 + groups,)),
            dma((groups, Y)),
            dma((groups, Y)),
            dma((groups, lanes)),
        ] + sems,
        compiler_params=pltpu.CompilerParams(collective_id=0, has_side_effects=True, vmem_limit_bytes=56 * 2**20),
        cost_estimate=pl.CostEstimate(flops=8 * 10**9, bytes_accessed=10**8, transcendentals=0),
        name="front",
    )(tokens, cot, meta, small, attend_w, output_w, up_w, down_w)


def lane_gather(part):
    return lax.all_gather(part, "wide", axis=0, tiled=True)


def lane_scatter(part):
    return lax.psum_scatter(part.astype(bf16), "wide", scatter_dimension=0, tiled=True)


def group_gather(part, axis=0):
    return lax.all_gather(part, "narrow", axis=axis, tiled=True)


def group_scatter(part, axis=0):
    return lax.psum_scatter(part.astype(bf16), "narrow", scatter_dimension=axis, tiled=True)


def lane_swap(part):
    return lax.all_to_all(part, "wide", split_axis=0, concat_axis=0, tiled=True)


def per_device(
    tokens, doc_ids, valid_mask, routes, cotangent, attend_gain, attend_weight, output_weight, mixer_gain,
    router_weight, blend_weight, up_weight, down_weight, expert_up, expert_down,
):
    rows, width = tokens.shape
    groups, lanes = lax.axis_size("wide"), lax.axis_size("narrow")
    group, lane = lax.axis_index("wide"), lax.axis_index("narrow")
    shard = attend_gain.shape[0]
    local = expert_up.shape[0]
    experts = local * groups
    hidden = up_weight.shape[1]
    fine = hidden // groups // lanes
    cap = max(2, (3 * rows + 2 * experts - 1) // (2 * experts))
    slots = -(-local * cap // 16) * 16
    all_rows = rows * lanes

    small = jnp.concatenate(
        [attend_gain[:, None], mixer_gain[:, None], blend_weight, router_weight,
         jnp.zeros((shard, SMALL - 4 - experts), bf16)], axis=1)
    meta = jnp.stack([doc_ids, valid_mask, routes[:, 0]]).astype(f32)
    meta = jnp.pad(meta, ((0, 5), (0, 0)))
    up_mine = up_weight
    if fine % 128:
        up_mine = lax.dynamic_index_in_dim(up_weight.reshape(shard, groups, lanes, fine), lane, 2, keepdims=False)
        up_mine = up_mine.reshape(shard, groups * fine)
    (
        normed_attend, qkv, lse, attn_mixed, attention_out, mix_all, small, meta_all, place,
        attend_full, output_full, got_mix, got_cot, cot_all, up_full, down_full,
    ) = front(groups, lanes, local, cap, slots, tokens, cotangent, meta, small, attend_weight, output_weight, up_mine, down_weight)
    doc_col = meta_all[:, 0].reshape(all_rows, 1)
    valid_all = meta_all[:, 1].reshape(all_rows, 1)
    attend_gain_row = small[:, 0].astype(f32)
    mixer_gain_row = small[:, 1].astype(f32)
    mix_cols = jnp.where((jnp.arange(SMALL) < 2)[None, :], 0, small)
    residual_mid = tokens.astype(f32) + attention_out
    mid_normed, mid_scale = norm_stats(residual_mid)
    normed_mix = (mid_normed * mixer_gain_row).astype(bf16)
    route = routes[:, 0]

    def give_back(partial):
        return mm(place, lane_swap(group_scatter(partial)))

    valid = valid_mask.astype(f32)[:, None]
    grad_layer = cotangent.astype(f32) * valid

    def coefficients(mix_rows):
        logits = mm(mix_rows, mix_cols)
        columns = jnp.arange(SMALL)[None, :]
        blend = soft_max(jnp.where((columns >= 2) & (columns < 4), logits, masked_score))
        router = soft_max(jnp.where((columns >= 4) & (columns < 4 + experts), logits, masked_score))
        return columns, blend, router

    columns, blend, _ = coefficients(mix_all)
    blend_0, blend_1 = blend[:, 2:3], blend[:, 3:4]
    grad_dense = (blend_1 * (cot_all.astype(f32) * valid_all.astype(f32))).astype(bf16)
    up_act, up_slope = gelu_both(mm(mix_all, up_full))
    up_act = up_act.astype(bf16)
    dense_part = mm(up_act, down_full)
    grad_up_act = mm(grad_dense, down_full, 1, 1)
    dense_dot = jnp.sum(up_act.astype(f32) * grad_up_act, axis=1, keepdims=True)
    grad_up_pre = (up_slope * grad_up_act).astype(bf16)
    dense_logits = (jnp.where(columns == 3, 1.0, 0.0) - jnp.where(columns == 2, 1.0, 0.0)) * (blend_0 * dense_dot)
    grad_mix_part = mm(grad_up_pre, up_full, 1, 1) + mm(dense_logits.astype(bf16), mix_cols, 1, 1)
    grad_small = mm(mix_all, dense_logits.astype(bf16), 0, 0)
    grad_up = mm(mix_all, grad_up_pre, 0, 0)
    grad_down = mm(up_act, grad_dense, 0, 0)

    def by_expert(received):
        split = received.reshape(lanes * groups, slots, width)[:, : local * cap]
        return split.reshape(lanes * groups, local, cap, width).transpose(1, 0, 2, 3).reshape(local, -1, width)

    def by_slot(values):
        split = values.reshape(local, lanes * groups, cap, width).transpose(1, 0, 2, 3)
        split = split.reshape(lanes * groups, local * cap, width)
        return jnp.pad(split, ((0, 0), (0, slots - local * cap), (0, 0))).reshape(-1, width)

    mix_e, cot_e = by_expert(got_mix), by_expert(got_cot)
    tok_parts, back_parts, up_grads, down_grads = [], [], [], []
    for e in range(local):
        _, blend, router = coefficients(mix_e[e])
        own = columns == 4 + group * local + e
        chosen = jnp.sum(jnp.where(own, router, 0.0), axis=1, keepdims=True)
        scale = blend[:, 2:3] * chosen
        grad_tok = (scale * cot_e[e].astype(f32)).astype(bf16)
        act, slope = gelu_both(mm(mix_e[e], expert_up[e]))
        act = act.astype(bf16)
        tok_parts.append((mm(act, expert_down[e])))
        grad_act = mm(grad_tok, expert_down[e], 1, 1)
        dot = jnp.sum(act.astype(f32) * grad_act, axis=1, keepdims=True)
        grad_hidden = (slope * grad_act).astype(bf16)
        logits = dot * (jnp.where(own, 1.0, 0.0) - router)
        logits += dot * blend[:, 3:4] * (jnp.where(columns == 2, 1.0, 0.0) - jnp.where(columns == 3, 1.0, 0.0))
        logits = logits.astype(bf16)
        back_parts.append(mm(grad_hidden, expert_up[e], 1, 1) + mm(logits, mix_cols, 1, 1))
        grad_small += mm(mix_e[e], logits, 0, 0)
        down_grads.append(mm(act, grad_tok, 0, 0))
        up_grads.append(mm(mix_e[e], grad_hidden, 0, 0))
    grad_expert_up, grad_expert_down = jnp.stack(up_grads), jnp.stack(down_grads)
    expert_back = give_back(by_slot(jnp.stack(back_parts)))
    expert_tok = give_back(by_slot(jnp.stack(tok_parts)))

    dense_out = group_scatter(dense_part).astype(f32)
    _, blend, router = coefficients(normed_mix)
    own = columns == 4 + route[:, None]
    chosen = jnp.sum(jnp.where(own, router, 0.0), axis=1, keepdims=True)
    ffn_out = blend[:, 2:3] * chosen * expert_tok + blend[:, 3:4] * dense_out
    layer_full = residual_mid + ffn_out
    sums = jnp.stack(
        [jnp.sum(valid * v * v) for v in (residual_mid, layer_full, attention_out, ffn_out)] + [jnp.sum(valid)])

    grad_mix = group_scatter(grad_mix_part).astype(f32) + expert_back
    grad_mid = grad_layer + norm_back(mid_normed, mid_scale, mixer_gain_row, grad_mix)
    mixer_gain_grad = jnp.sum(grad_mix * mid_normed, axis=0)
    grad_attn = grad_mid.astype(bf16)
    grad_output = mm(attn_mixed, grad_attn, 0, 0)
    grad_mixed = mm(grad_attn, output_full, 1, 1).astype(bf16)
    grad_heads = lax.all_to_all(grad_mixed, "narrow", split_axis=1, concat_axis=0, tiled=True)
    grad_qkv = attend_back(qkv, doc_col, lse, grad_heads)
    grad_attend = mm(normed_attend, grad_qkv, 0, 0)
    grad_normed = group_scatter(mm(grad_qkv, attend_full, 1, 1)).astype(f32)
    in_normed, in_scale = norm_stats(tokens.astype(f32))
    grad_tokens = (grad_mid + norm_back(in_normed, in_scale, attend_gain_row, grad_normed)).astype(bf16)
    attend_gain_grad = jnp.sum(grad_normed * in_normed, axis=0)

    grad_small = jnp.where(columns == 0, attend_gain_grad[:, None], jnp.where(columns == 1, mixer_gain_grad[:, None], grad_small))
    small_out = lax.psum(lax.psum_scatter(grad_small, "wide", scatter_dimension=0, tiled=True), "narrow")
    sums = lax.psum(sums, ("wide", "narrow"))
    root_means = jnp.sqrt(sums[:4] / (jnp.maximum(sums[4], 1.0) * width))

    def widen(part, parts):
        full = group_gather(part.astype(bf16)[None])
        full = full.reshape(lanes, part.shape[0], parts, -1)
        return full.transpose(1, 2, 0, 3).reshape(part.shape[0], -1).astype(f32)

    out_attend = widen(lane_scatter(grad_attend), 3)
    out_output = widen(lane_scatter(group_scatter(grad_output, axis=1)), 1)
    out_up = widen(lane_scatter(grad_up), groups)
    out_down = group_gather(lane_scatter(grad_down).astype(bf16)).astype(f32)
    return (
        layer_full.astype(bf16), grad_tokens, small_out[:, 0], out_attend, out_output, small_out[:, 1],
        small_out[:, 4 : 4 + experts], small_out[:, 2:4], out_up, out_down, grad_expert_up, grad_expert_down, root_means,
    )


def solution(mesh):
    both = ("wide", "narrow")
    row, vec, mat = P(both, None), P("wide"), P("wide", None)
    up, down = P("wide", None, "narrow"), P("wide", "narrow", None)
    return jax.shard_map(
        per_device,
        mesh=mesh,
        in_specs=(row, P(both), P(both), row, row, vec, mat, mat, vec, mat, mat, mat, mat, up, down),
        out_specs=(row, row, vec, mat, mat, vec, mat, mat, mat, mat, up, down, P()),
        check_vma=False,
    )
```

```python
import functools

import jax
import jax.numpy as jnp
from jax import lax
from jax.experimental import pallas as pl
from jax.experimental.pallas import tpu as pltpu
from jax.sharding import PartitionSpec as P

HEAD_DIM = 64
PAIR = 2 * HEAD_DIM
Q_TILE = 256
SMALL = 128
eps_norm = 1e-05
masked_score = -1e30
f32 = jnp.float32
bf16 = jnp.bfloat16


def mm(a, b, ca=1, cb=0):
    return lax.dot_general(a, b, (((ca,), (cb,)), ((), ())), preferred_element_type=f32)


def norm_stats(values):
    center = values - jnp.mean(values, axis=-1, keepdims=True)
    scale = lax.rsqrt(jnp.mean(center * center, axis=-1, keepdims=True) + eps_norm)
    return center * scale, scale


def norm_back(normed, scale, gain, grad):
    u = grad * gain
    return scale * (
        u
        - jnp.mean(u, axis=-1, keepdims=True)
        - normed * jnp.mean(u * normed, axis=-1, keepdims=True)
    )


GELU_A = 0.7978845608028654
GELU_B = 0.044715


def gelu(v):
    return 0.5 * v * (1.0 + jnp.tanh(GELU_A * (v + GELU_B * v * v * v)))


def gelu_both(v):
    t = jnp.tanh(GELU_A * (v + GELU_B * v * v * v))
    value = 0.5 * v * (1.0 + t)
    slope = 0.5 * (1.0 + t) + 0.5 * v * (1.0 - t * t) * (GELU_A * (1.0 + 3.0 * GELU_B * v * v))
    return value, slope


def soft_max(logits):
    shifted = jnp.exp(logits - jnp.max(logits, axis=-1, keepdims=True))
    return shifted / jnp.sum(shifted, axis=-1, keepdims=True)


def head_mask(half):
    lanes = lax.broadcasted_iota(jnp.int32, (1, PAIR), 1)
    return (lanes // HEAD_DIM) == half


def attend_tile(tile, qkv_ref, doc_cols, out_ref, lse_ref, mask_ref, vt_ref):
    cols = out_ref.shape[1]
    extent = (tile + 1) * Q_TILE
    here, seen = pl.ds(tile * Q_TILE, Q_TILE), pl.ds(0, extent)
    mask_tile(tile, doc_cols, mask_ref)

    def pair_step(pair, carry):
        q_cols = pl.ds(pl.multiple_of(pair * PAIR, PAIR), PAIR)
        k_cols = pl.ds(pl.multiple_of(cols + pair * PAIR, PAIR), PAIR)
        v_cols = pl.ds(pl.multiple_of(2 * cols + pair * PAIR, PAIR), PAIR)
        if tile == 0:
            vt_ref[pair] = qkv_ref[:, v_cols].T
        queries = qkv_ref[here, q_cols] * jnp.asarray(HEAD_DIM**-0.5, bf16)
        mixed = jnp.zeros((PAIR, Q_TILE), f32)
        for half in range(2):
            one = jnp.where(head_mask(half), queries, jnp.zeros_like(queries))
            scores = mm(qkv_ref[seen, k_cols], one, 1, 1) + mask_ref[seen, :]
            top = jnp.max(scores, axis=0, keepdims=True)
            shifted = jnp.exp(scores - top)
            total = jnp.sum(shifted, axis=0, keepdims=True)
            low = (shifted * (1.0 / total)).astype(bf16)
            lse_ref[pair, pl.ds(half, 1), here] = top + jnp.log(total)
            got = mm(vt_ref[pair, :, seen], low)
            sublanes = lax.broadcasted_iota(jnp.int32, (PAIR, 1), 0)
            mixed = jnp.where((sublanes // HEAD_DIM) == half, got, mixed)
        out_ref[here, q_cols] = mixed.T.astype(bf16)
        return carry

    lax.fori_loop(0, cols // PAIR, pair_step, 0)


def mask_tile(tile, doc_cols, mask_ref):
    row = (tile * Q_TILE + lax.broadcasted_iota(jnp.int32, (Q_TILE, Q_TILE), 1)).astype(f32)
    for block in range(tile + 1):
        allowed = doc_cols[block] >= row
        if block == tile:
            key = (tile * Q_TILE + lax.broadcasted_iota(jnp.int32, (Q_TILE, Q_TILE), 0)).astype(f32)
            allowed = allowed & (key <= row)
        mask_ref[pl.ds(block * Q_TILE, Q_TILE), :] = jnp.where(allowed, 0.0, masked_score)


def attend_back_kernel(qkv_ref, doc_ref, lse_ref, grad_ref, out_ref, mask_ref, dk_ref, dv_ref):
    rows, cols = grad_ref.shape
    pairs = cols // PAIR
    dk_ref[...] = jnp.zeros_like(dk_ref)
    dv_ref[...] = jnp.zeros_like(dv_ref)
    for tile in range(rows // Q_TILE):
        extent = (tile + 1) * Q_TILE
        here = pl.ds(tile * Q_TILE, Q_TILE)
        seen = pl.ds(0, extent)
        mask_tile(tile, [doc_ref[pl.ds(b * Q_TILE, Q_TILE), :] for b in range(tile + 1)], mask_ref)

        def pair_step(pair, carry):
            q_cols = pl.ds(pl.multiple_of(pair * PAIR, PAIR), PAIR)
            k_cols = pl.ds(pl.multiple_of(cols + pair * PAIR, PAIR), PAIR)
            v_cols = pl.ds(pl.multiple_of(2 * cols + pair * PAIR, PAIR), PAIR)
            queries = qkv_ref[here, q_cols] * jnp.asarray(HEAD_DIM**-0.5, bf16)
            keys, values = qkv_ref[seen, k_cols], qkv_ref[seen, v_cols]
            grads = grad_ref[here, q_cols]
            dq = jnp.zeros((PAIR, Q_TILE), f32)
            for half in range(2):
                on = head_mask(half)
                q_one = jnp.where(on, queries, jnp.zeros_like(queries))
                g_one = jnp.where(on, grads, jnp.zeros_like(grads))
                probs = jnp.exp(mm(keys, q_one, 1, 1) + mask_ref[seen, :] - lse_ref[pair, pl.ds(half, 1), here])
                dv_ref[pair, seen, :] += mm(probs.astype(bf16), g_one)
                back = mm(values, g_one, 1, 1)
                low = (probs * (back - jnp.sum(probs * back, axis=0, keepdims=True))).astype(bf16)
                dk_ref[pair, seen, :] += mm(low, q_one)
                got = mm(keys, low, 0, 0)
                sublanes = lax.broadcasted_iota(jnp.int32, (PAIR, 1), 0)
                dq = jnp.where((sublanes // HEAD_DIM) == half, got, dq)
            out_ref[here, q_cols] = (dq.T * HEAD_DIM**-0.5).astype(bf16)
            return carry

        lax.fori_loop(0, pairs, pair_step, 0)
    for pair in range(pairs):
        out_ref[:, cols + pair * PAIR : cols + (pair + 1) * PAIR] = dk_ref[pair].astype(bf16)
        out_ref[:, 2 * cols + pair * PAIR : 2 * cols + (pair + 1) * PAIR] = dv_ref[pair].astype(bf16)


def attend_back(qkv, doc_col, lse, grad):
    rows, cols = grad.shape
    vmem = pl.BlockSpec(memory_space=pltpu.VMEM)
    return pl.pallas_call(
        attend_back_kernel,
        out_shape=jax.ShapeDtypeStruct((rows, 3 * cols), bf16),
        in_specs=[vmem] * 4,
        out_specs=vmem,
        scratch_shapes=[
            pltpu.VMEM((rows, Q_TILE), f32),
            pltpu.VMEM((cols // PAIR, rows, PAIR), f32),
            pltpu.VMEM((cols // PAIR, rows, PAIR), f32),
        ],
        compiler_params=pltpu.CompilerParams(vmem_limit_bytes=56 * 2**20),
        cost_estimate=pl.CostEstimate(flops=20 * rows * rows * cols, bytes_accessed=16 * rows * cols, transcendentals=0),
        name="attend_back",
    )(qkv, doc_col, lse, grad)


MESH = pl.DeviceIdType.MESH


class Spot:
    def __init__(self, groups, lanes):
        self.W, self.L = groups, lanes
        self.X = 1 << ((groups.bit_length() - 1) // 2)
        self.Z, self.Y = groups // self.X, lanes // 2
        self.g, self.l = lax.axis_index("wide"), lax.axis_index("narrow")
        self.z, self.x = self.g // self.X, self.g % self.X
        self.y, self.c = self.l // 2, self.l % 2

    def zx_peer(self, dz, dx):
        return lax.rem(self.z + dz, self.Z) * self.X + lax.rem(self.x + dx, self.X)

    def z_peer(self, d):
        return self.zx_peer(d, 0)

    def x_peer(self, d):
        return self.zx_peer(0, d)

    def y_peer(self, d):
        return lax.rem(self.y + d, self.Y) * 2 + self.c

    def core_peer(self):
        return self.y * 2 + 1 - self.c

    def w_peer(self, d):
        return lax.rem(self.g + d, self.W)

    def l_peer(self, d):
        return lax.rem(self.l + d, self.L)

    def greet(self, lane_peers=True):
        barrier = pltpu.get_barrier_semaphore()
        met = self.L - 1
        for d in range(1, self.L):
            pl.semaphore_signal(barrier, 1, device_id=(self.g, self.l_peer(d)), device_id_type=MESH)
        if lane_peers:
            met += self.W - 1
            for d in range(1, self.W):
                pl.semaphore_signal(barrier, 1, device_id=(self.w_peer(d), self.l), device_id_type=MESH)
        pl.semaphore_wait(barrier, met)


def remote(src, dst, send_sem, recv_sem, group, lane):
    return pltpu.make_async_remote_copy(src, dst, send_sem, recv_sem, device_id=(group, lane), device_id_type=MESH)


class LaneGather:
    def __init__(self, spot, src, place, sems):
        self.s, self.src, self.place = spot, src, place
        self.z_sem, self.x_sem, self.r_sem, self.own_sem = sems

    @staticmethod
    def sems(W, X):
        dma = pltpu.SemaphoreType.DMA
        return [dma((W // X,)), dma((W // X, X)), dma((W,)), dma((1,))]

    def z_copy(self, d):
        s = self.s
        return remote(self.src, self.place(s.g), self.z_sem.at[d], self.r_sem.at[s.g], s.z_peer(d), s.l)

    def x_copy(self, d, e):
        s = self.s
        w = s.z_peer(d)
        src = self.src if d == 0 else self.place(w)
        return remote(src, self.place(w), self.x_sem.at[d, e], self.r_sem.at[w], s.x_peer(e), s.l)

    def got(self, w):
        s = self.s
        remote(self.src, self.place(w), self.z_sem.at[0], self.r_sem.at[w], s.x_peer(1), s.l).wait_recv()

    def own(self):
        return pltpu.make_async_copy(self.src, self.place(self.s.g), self.own_sem.at[0])

    def start(self):
        for d in range(1, self.s.Z):
            self.z_copy(d).start()
        for e in range(1, self.s.X):
            self.x_copy(0, e).start()
        self.own().start()

    def forward(self):
        for d in range(1, self.s.Z):
            self.got(self.s.z_peer(d))
            for e in range(1, self.s.X):
                self.x_copy(d, e).start()

    def arrive(self):
        s = self.s
        for d in range(s.Z):
            for e in range(1, s.X):
                self.got(s.zx_peer(d, e))
        self.own().wait()

    def sent(self):
        for d in range(1, self.s.Z):
            self.z_copy(d).wait_send()
        for d in range(self.s.Z):
            for e in range(1, self.s.X):
                self.x_copy(d, e).wait_send()


class GroupGather:
    def __init__(self, spot, src, place, sems, own=True):
        self.s, self.src, self.place, self.has_own = spot, src, place, own
        self.y_sem, self.c_sem, self.r_sem, self.own_sem = sems

    @staticmethod
    def sems(L):
        dma = pltpu.SemaphoreType.DMA
        return [dma((L // 2,)), dma((L // 2,)), dma((L,)), dma((1,))]

    def y_copy(self, d):
        s = self.s
        return remote(self.src, self.place(s.l), self.y_sem.at[d], self.r_sem.at[s.l], s.g, s.y_peer(d))

    def c_copy(self, d):
        s = self.s
        l = s.y_peer(d)
        src = self.src if d == 0 else self.place(l)
        return remote(src, self.place(l), self.c_sem.at[d], self.r_sem.at[l], s.g, s.core_peer())

    def got(self, l):
        s = self.s
        remote(self.src, self.place(l), self.y_sem.at[0], self.r_sem.at[l], s.g, s.core_peer()).wait_recv()

    def own(self):
        return pltpu.make_async_copy(self.src, self.place(self.s.l), self.own_sem.at[0])

    def start(self):
        for d in range(1, self.s.Y):
            self.y_copy(d).start()
        self.c_copy(0).start()
        if self.has_own:
            self.own().start()

    def forward(self):
        for d in range(1, self.s.Y):
            self.got(self.s.y_peer(d))
            self.c_copy(d).start()

    def arrive(self):
        s = self.s
        for d in range(s.Y):
            self.got(lax.rem(s.y + d, s.Y) * 2 + 1 - s.c)
        if self.has_own:
            self.own().wait()

    def sent(self):
        for d in range(1, self.s.Y):
            self.y_copy(d).wait_send()
        for d in range(self.s.Y):
            self.c_copy(d).wait_send()


class LaneSwap:
    def __init__(self, spot, src, dst, sems):
        self.s, self.src, self.dst = spot, src, dst
        self.s_sem, self.r_sem = sems

    @staticmethod
    def sems(W):
        return [pltpu.SemaphoreType.DMA((W,)), pltpu.SemaphoreType.DMA((W,))]

    def copy(self, d):
        s = self.s
        w = s.w_peer(d)
        return remote(self.src(w), self.dst(s.g), self.s_sem.at[d], self.r_sem.at[s.g], w, s.l)

    def own(self):
        return pltpu.make_async_copy(self.src(self.s.g), self.dst(self.s.g), self.s_sem.at[0])

    def start(self):
        for d in range(1, self.s.W):
            self.copy(d).start()
        self.own().start()

    def got(self, w):
        s = self.s
        remote(self.src(w), self.dst(w), self.s_sem.at[0], self.r_sem.at[w], s.w_peer(1), s.l).wait_recv()

    def arrive(self):
        for d in range(1, self.s.W):
            self.got(self.s.w_peer(self.s.W - d))
        self.own().wait()

    def sent(self):
        for d in range(1, self.s.W):
            self.copy(d).wait_send()


class GroupSwap:
    def __init__(self, spot, src, dst, sems):
        self.s, self.src, self.dst = spot, src, dst
        self.s_sem, self.r_sem = sems

    @staticmethod
    def sems(L):
        return [pltpu.SemaphoreType.DMA((L,)), pltpu.SemaphoreType.DMA((L,))]

    def copy(self, l):
        s = self.s
        return remote(self.src(l), self.dst(s.l), self.s_sem.at[l], self.r_sem.at[s.l], s.g, l)

    def own(self):
        s = self.s
        return pltpu.make_async_copy(self.src(s.l), self.dst(s.l), self.s_sem.at[s.l])

    def send(self, l):
        @pl.when(self.s.l == l)
        def _():
            self.own().start()

        @pl.when(self.s.l != l)
        def _():
            self.copy(l).start()

    def arrive(self):
        s = self.s
        for d in range(1, s.L):
            l = s.l_peer(d)
            remote(self.src(l), self.dst(l), self.s_sem.at[l], self.r_sem.at[l], s.g, l).wait_recv()
        self.own().wait()

    def sent(self):
        for d in range(1, self.s.L):
            self.copy(self.s.l_peer(d)).wait_send()


def rows_norm(src, gain, dst, count, step=64):
    def body(i, carry):
        at = pl.ds(pl.multiple_of(i * step, step), step)
        normed, _ = norm_stats(src[at, :].astype(f32))
        dst[at, :] = (normed * gain).astype(bf16)
        return carry

    lax.fori_loop(0, count // step, body, 0)


def front_kernel(
    groups, lanes, local, cap, slots,
    tokens, cot, meta, small, attend_w, output_w, up_w, down_w,
    normed_out, qkv, lse, attn_mixed, attention_out, mix_all, small_all, meta_all, place,
    attend_all, output_all, got_mix, got_cot, cot_all, up_all, down_all,
    tok_all, attend_mine, up_mine, mixed, mask, vt, packed_mix, packed_cot, stage_sem, spread_y, spread_c, spread_r, *sems,
):
    s = Spot(groups, lanes)
    rows, width = tokens.shape
    head_cols = width // lanes
    shard = attend_w.shape[0]
    depth = down_all.shape[0] // groups
    sems = list(sems)

    def take(n):
        out = sems[:n]
        del sems[:n]
        return out

    def blocks(ref, n):
        return lambda i: ref.at[pl.ds(pl.multiple_of(i * n, n), n)]

    def cols(i):
        return pl.ds(pl.multiple_of(i * head_cols, head_cols), head_cols)

    staged = [
        pltpu.make_async_copy(
            attend_w.at[:, pl.ds(pl.multiple_of(p * width + s.l * head_cols, head_cols), head_cols)],
            attend_mine.at[:, pl.ds(p * head_cols, head_cols)], stage_sem.at[p])
        for p in range(3)
    ]
    if up_w.shape[1] != up_mine.shape[1]:
        fine = up_mine.shape[1] // groups
        staged += [
            pltpu.make_async_copy(
                up_w.at[:, pl.ds(pl.multiple_of((w * lanes + s.l) * fine, fine), fine)],
                up_mine.at[:, pl.ds(w * fine, fine)], stage_sem.at[3 + w])
            for w in range(groups)
        ]
    else:
        staged += [pltpu.make_async_copy(up_w, up_mine, stage_sem.at[3])]
    for c in staged:
        c.start()

    tok = GroupGather(s, tokens, blocks(tok_all, rows), take(4))
    met = GroupGather(s, meta, lambda l: meta_all.at[l], take(4))
    cots = GroupGather(s, cot, blocks(cot_all, rows), take(4))
    mix = GroupGather(s, blocks(mix_all, rows)(s.l), blocks(mix_all, rows), take(4), own=False)
    outs = GroupGather(s, output_all.at[:, cols(s.l)], lambda l: output_all.at[:, cols(l)], take(4), own=False)
    cot_spread = GroupGather(s, got_cot.at[s.l], lambda l: got_cot.at[l], take(4), own=False)
    att = LaneGather(s, attend_mine, blocks(attend_all, shard), take(4))
    sml = LaneGather(s, small, blocks(small_all, shard), take(4))
    out = LaneGather(s, output_w.at[:, cols(s.l)],
                     lambda w: output_all.at[pl.ds(pl.multiple_of(w * shard, shard), shard), cols(s.l)], take(4))
    up = LaneGather(s, up_mine, blocks(up_all, shard), take(4))
    down = LaneGather(s, down_w.at[pl.ds(pl.multiple_of(s.l * depth, depth), depth)], blocks(down_all, depth), take(4))
    swap = GroupSwap(s, blocks(mixed, rows), lambda l: attn_mixed.at[:, cols(l)], take(2))
    mix_swap = LaneSwap(s, blocks(packed_mix, slots), lambda w: got_mix.at[s.l, w], take(2))
    cot_swap = LaneSwap(s, blocks(packed_cot, slots), lambda w: got_cot.at[s.l, w], take(2))

    def spread(d):
        w = s.w_peer(groups - d)
        return GroupGather(s, got_mix.at[s.l, w], lambda l: got_mix.at[l, w],
                           [spread_y.at[w], spread_c.at[w], spread_r.at[w], None], own=False)

    mix_spread = [spread(d) for d in range(groups)]

    s.greet()
    for c in staged[:3]:
        c.wait()
    sml.start()
    met.start()
    tok.start()
    att.start()
    for c in staged[3:]:
        c.wait()
    mine = meta[...].T
    valid, route = mine[:, 1:2], mine[:, 2:3].astype(jnp.int32)
    column = lax.broadcasted_iota(jnp.int32, (rows, SMALL), 1)
    hits = (column == route).astype(f32)
    earlier = lax.broadcasted_iota(jnp.int32, (rows, rows), 1) < lax.broadcasted_iota(jnp.int32, (rows, rows), 0)
    rank = jnp.sum(hits * mm(earlier.astype(f32).astype(bf16), hits.astype(bf16)), axis=1, keepdims=True).astype(jnp.int32)
    slot = (route // local) * slots + (route % local) * cap + rank
    spots = (slot == lax.broadcasted_iota(jnp.int32, (rows, groups * slots), 1)).astype(f32)
    place[...] = spots.astype(bf16)
    packed_cot[...] = mm((spots * valid).astype(bf16), cot[...], 0, 0).astype(bf16)
    sml.forward()
    met.forward()
    sml.arrive()
    met.arrive()
    tok.forward()
    att.forward()
    cots.start()
    tok.arrive()
    gains = small_all[...].astype(f32).T
    rows_norm(tok_all, gains[0:1, :], normed_out, rows * lanes)
    att.arrive()
    out.start()
    up.start()

    def project(i, carry):
        at = pl.ds(pl.multiple_of(i * Q_TILE, Q_TILE), Q_TILE)
        qkv[at, :] = mm(normed_out[at, :], attend_all[...]).astype(bf16)
        return carry

    lax.fori_loop(0, rows * lanes // Q_TILE, project, 0)
    out.forward()
    doc_cols = [meta_all[l].T[:, 0:1] for l in range(lanes)]
    for tile in range(lanes):
        attend_tile(tile, qkv, doc_cols, mixed, lse, mask, vt)
        swap.send(tile)
        if tile == 0:
            out.arrive()
            outs.start()
        if tile == 1:
            cots.forward()
    outs.forward()
    up.forward()
    down.start()
    outs.arrive()
    swap.arrive()
    attention_out[...] = mm(attn_mixed[...], output_all[...])
    gain = small_all[...].astype(f32).T[1:2, :]
    base = pl.multiple_of(s.l * rows, rows)

    def mid(i, carry):
        at = pl.ds(pl.multiple_of(i * 64, 64), 64)
        normed, _ = norm_stats(tokens[at, :].astype(f32) + attention_out[at, :])
        mix_all[pl.ds(pl.multiple_of(base + i * 64, 64), 64), :] = (normed * gain).astype(bf16)
        return carry

    lax.fori_loop(0, rows // 64, mid, 0)
    mix.start()
    packed_mix[...] = mm(place[...], mix_all[pl.ds(base, rows), :], 0, 0).astype(bf16)
    mix_swap.start()
    cot_swap.start()
    down.forward()
    mix.forward()
    for d in range(groups):
        if d:
            mix_swap.got(s.w_peer(groups - d))
        else:
            mix_swap.own().wait()
        mix_spread[d].start()
    cot_swap.arrive()
    cot_spread.start()
    for task in mix_spread:
        task.forward()
    cot_spread.forward()
    mix.arrive()
    for task in mix_spread:
        task.arrive()
    cot_spread.arrive()
    cots.arrive()
    up.arrive()
    down.arrive()
    for task in [tok, met, cots, mix, outs, cot_spread, att, sml, out, up, down, swap, mix_swap, cot_swap] + mix_spread:
        task.sent()


def front(groups, lanes, local, cap, slots, tokens, cot, meta, small, attend_w, output_w, up_w, down_w):
    rows, width = tokens.shape
    X = 1 << ((groups.bit_length() - 1) // 2)
    Y = lanes // 2
    everyone = rows * lanes
    head_cols = width // lanes
    hidden = down_w.shape[0] // lanes * groups
    shard = attend_w.shape[0]
    vmem, anywhere = pl.BlockSpec(memory_space=pltpu.VMEM), pl.BlockSpec(memory_space=pl.ANY)
    dma = pltpu.SemaphoreType.DMA
    of = jax.ShapeDtypeStruct
    sems = []
    for _ in range(6):
        sems += GroupGather.sems(lanes)
    for _ in range(5):
        sems += LaneGather.sems(groups, X)
    sems += GroupSwap.sems(lanes) + LaneSwap.sems(groups) + LaneSwap.sems(groups)
    outs = [
        (of((everyone, width), bf16), vmem),
        (of((everyone, 3 * head_cols), bf16), vmem),
        (of((head_cols // PAIR, 2, everyone), f32), vmem),
        (of((rows, width), bf16), vmem),
        (of((rows, width), f32), vmem),
        (of((everyone, width), bf16), vmem),
        (of((width, SMALL), bf16), vmem),
        (of((lanes, 8, rows), f32), vmem),
        (of((rows, groups * slots), bf16), vmem),
        (of((width, 3 * head_cols), bf16), vmem),
        (of((width, width), bf16), vmem),
        (of((lanes, groups, slots, width), bf16), anywhere),
        (of((lanes, groups, slots, width), bf16), anywhere),
        (of((everyone, width), bf16), anywhere),
        (of((width, hidden), bf16), anywhere),
        (of((hidden, width), bf16), anywhere),
    ]
    return pl.pallas_call(
        functools.partial(front_kernel, groups, lanes, local, cap, slots),
        out_shape=[o for o, _ in outs],
        in_specs=[vmem] * 4 + [anywhere] * 4,
        out_specs=[p for _, p in outs],
        scratch_shapes=[
            pltpu.VMEM((everyone, width), bf16),
            pltpu.VMEM((shard, 3 * head_cols), bf16),
            pltpu.VMEM((shard, hidden), bf16),
            pltpu.VMEM((everyone, head_cols), bf16),
            pltpu.VMEM((everyone, Q_TILE), f32),
            pltpu.VMEM((head_cols // PAIR, PAIR, everyone), bf16),
            pltpu.VMEM((groups * slots, width), bf16),
            pltpu.VMEM((groups * slots, width), bf16),
            dma((3 + groups,)),
            dma((groups, Y)),
            dma((groups, Y)),
            dma((groups, lanes)),
        ] + sems,
        compiler_params=pltpu.CompilerParams(collective_id=0, has_side_effects=True, vmem_limit_bytes=56 * 2**20),
        cost_estimate=pl.CostEstimate(flops=8 * 10**9, bytes_accessed=10**8, transcendentals=0),
        name="front",
    )(tokens, cot, meta, small, attend_w, output_w, up_w, down_w)


def add_rows(dst, sources, step=32):
    def body(i, carry):
        at = pl.ds(pl.multiple_of(i * step, step), step)
        total = sources[0][at, :].astype(f32)
        for ref in sources[1:]:
            total += ref[at, :].astype(f32)
        dst[at, :] = total.astype(dst.dtype)
        return carry

    lax.fori_loop(0, dst.shape[0] // step, body, 0)


class GroupScatter:
    def __init__(self, spot, part, held, from_core, from_y, sems, fine):
        self.s, self.part, self.from_core, self.from_y, self.fine = spot, part, from_core, from_y, fine
        self.staged = held is not None
        self.held = (lambda d: held.at[d]) if self.staged else (lambda d: part(spot.y_peer(d)))
        self.stage_sem, self.cs_sem, self.cr_sem, self.ys_sem, self.yr_sem = sems
        self.chunks = from_core.shape[1]

    @staticmethod
    def sems(L, chunks):
        dma = pltpu.SemaphoreType.DMA
        return [dma((L // 2,))] * 3 + [dma((L // 2, chunks))] * 2

    def stage(self, d):
        return pltpu.make_async_copy(self.part(self.s.y_peer(d)), self.held(d), self.stage_sem.at[d])

    def core_copy(self, d):
        s = self.s
        other = lax.rem(s.y + d, s.Y) * 2 + 1 - s.c
        return remote(self.part(other), self.from_core.at[d], self.cs_sem.at[d], self.cr_sem.at[d], s.g, s.core_peer())

    def y_copy(self, d, k):
        s = self.s
        src, dst = self.held(d), self.from_y.at[d - 1]
        if self.fine:
            src, dst = src.at[k], dst.at[k]
        return remote(src, dst, self.ys_sem.at[d, k], self.yr_sem.at[d, k], s.g, s.y_peer(d))

    def start(self):
        for d in range(self.s.Y):
            if self.staged:
                self.stage(d).start()
            self.core_copy(d).start()

    def ready(self):
        for d in range(self.s.Y):
            if self.staged:
                self.stage(d).wait()
            self.core_copy(d).wait_recv()

    def add(self, d, k):
        self.held(d)[k] = (self.held(d)[k].astype(f32) + self.from_core[d, k].astype(f32)).astype(bf16)

    def relay(self, k=0):
        for d in range(1, self.s.Y):
            if self.fine:
                self.add(d, k)
            else:

                def body(i, carry, d=d):
                    self.add(d, i)
                    return carry

                lax.fori_loop(0, self.chunks, body, 0)
            self.y_copy(d, k).start()

    def got(self, k=0):
        for d in range(1, self.s.Y):
            self.y_copy(d, k).wait_recv()

    def total(self, k):
        value = self.held(0)[k].astype(f32) + self.from_core[0, k].astype(f32)
        for d in range(1, self.s.Y):
            value += self.from_y[d - 1, k].astype(f32)
        return value

    def sent(self):
        for d in range(self.s.Y):
            self.core_copy(d).wait_send()
        for d in range(1, self.s.Y):
            for k in range(self.chunks if self.fine else 1):
                self.y_copy(d, k).wait_send()


class LaneScatter:
    def __init__(self, spot, part, held, from_x, from_z, sems):
        self.s, self.part, self.from_x, self.from_z = spot, part, from_x, from_z
        self.staged = held is not None
        self.held = (lambda d: held.at[d]) if self.staged else (lambda d: part(spot.z_peer(d)))
        self.stage_sem, self.xs_sem, self.xr_sem, self.zs_sem, self.zr_sem = sems

    @staticmethod
    def sems(W, X):
        dma = pltpu.SemaphoreType.DMA
        Z = W // X
        return [dma((Z,)), dma((X, Z)), dma((X, Z)), dma((Z,)), dma((Z,))]

    def stage(self, d):
        return pltpu.make_async_copy(self.part(self.s.z_peer(d)), self.held(d), self.stage_sem.at[d])

    def x_copy(self, e, d):
        s = self.s
        return remote(self.part(s.zx_peer(d, e)), self.from_x.at[e - 1, d], self.xs_sem.at[e, d], self.xr_sem.at[e, d],
                      s.x_peer(e), s.l)

    def z_copy(self, d):
        s = self.s
        return remote(self.held(d), self.from_z.at[d - 1], self.zs_sem.at[d], self.zr_sem.at[d], s.z_peer(d), s.l)

    def start(self):
        for d in [*range(1, self.s.Z), 0]:
            if self.staged:
                self.stage(d).start()
            for e in range(1, self.s.X):
                self.x_copy(e, d).start()

    def ready(self, d):
        if self.staged:
            self.stage(d).wait()
        for e in range(1, self.s.X):
            self.x_copy(e, d).wait_recv()

    def relay(self):
        for d in range(1, self.s.Z):
            self.ready(d)
            add_rows(self.held(d), [self.held(d)] + [self.from_x.at[e - 1, d] for e in range(1, self.s.X)])
            self.z_copy(d).start()

    def finish(self, dst):
        self.ready(0)
        for d in range(1, self.s.Z):
            self.z_copy(d).wait_recv()
        add_rows(dst, [self.held(0)] + [self.from_x.at[e - 1, 0] for e in range(1, self.s.X)]
                 + [self.from_z.at[d - 1] for d in range(1, self.s.Z)])

    def sent(self):
        for d in range(self.s.Z):
            for e in range(1, self.s.X):
                self.x_copy(e, d).wait_send()
        for d in range(1, self.s.Z):
            self.z_copy(d).wait_send()


def attend_back_tile(tile, qkv_ref, doc_cols, lse_ref, grad_ref, out_ref, mask_ref, dk_ref, dv_ref):
    cols = grad_ref.shape[1]
    extent = (tile + 1) * Q_TILE
    here, seen = pl.ds(tile * Q_TILE, Q_TILE), pl.ds(0, extent)
    mask_tile(tile, doc_cols, mask_ref)

    def pair_step(pair, carry):
        q_cols = pl.ds(pl.multiple_of(pair * PAIR, PAIR), PAIR)
        k_cols = pl.ds(pl.multiple_of(cols + pair * PAIR, PAIR), PAIR)
        v_cols = pl.ds(pl.multiple_of(2 * cols + pair * PAIR, PAIR), PAIR)
        queries = qkv_ref[here, q_cols] * jnp.asarray(HEAD_DIM**-0.5, bf16)
        keys, values = qkv_ref[seen, k_cols], qkv_ref[seen, v_cols]
        grads = grad_ref[here, q_cols]
        dq = jnp.zeros((PAIR, Q_TILE), f32)
        for half in range(2):
            on = head_mask(half)
            q_one = jnp.where(on, queries, jnp.zeros_like(queries))
            g_one = jnp.where(on, grads, jnp.zeros_like(grads))
            probs = jnp.exp(mm(keys, q_one, 1, 1) + mask_ref[seen, :] - lse_ref[pair, pl.ds(half, 1), here])
            dv_ref[pair, seen, :] += mm(probs.astype(bf16), g_one)
            back = mm(values, g_one, 1, 1)
            low = (probs * (back - jnp.sum(probs * back, axis=0, keepdims=True))).astype(bf16)
            dk_ref[pair, seen, :] += mm(low, q_one)
            got = mm(keys, low, 0, 0)
            sublanes = lax.broadcasted_iota(jnp.int32, (PAIR, 1), 0)
            dq = jnp.where((sublanes // HEAD_DIM) == half, got, dq)
        out_ref[here, q_cols] = (dq.T * HEAD_DIM**-0.5).astype(bf16)
        return carry

    lax.fori_loop(0, cols // PAIR, pair_step, 0)


def take_from(sems):
    sems = list(sems)

    def take(n):
        out = sems[:n]
        del sems[:n]
        return out

    return take


def picked(logits, first, count):
    columns = lax.broadcasted_iota(jnp.int32, logits.shape, 1)
    return soft_max(jnp.where((columns >= first) & (columns < first + count), logits, masked_score))


def back_kernel(
    groups, lanes, experts,
    tokens, cot, meta, small, attention_out, attn_mixed, place, meta_all, lse, grad_small,
    mix_part, dense_part, back_part, tok_part, grad_up, grad_down, qkv_in, output_in, attend_in, normed_in,
    layer_out, grad_tokens, small_out, all_attend, all_output, all_up, all_down,
    qkv, output_all, attend_all, normed, bk_h, bk_c, bk_y, tk_h, tk_c, tk_y, mx_h, mx_c, mx_y, dn_h, dn_c, dn_y,
    go, go_c, go_y, gn, gn_c, gn_y, up_h, up_x, up_z, dw_h, dw_x, dw_z, ga, ga_x, ga_z, gl, gl_x, gl_z,
    sm, sm_x, sm_z, sm_mine, sm_all, ret_back, got_back, ret_tok, got_tok, grad_mix, grad_mid, grad_attn, grad_mixed,
    grad_heads, grad_qkv, mask, dk, dv, valid_cols, mine_attend, mine_output, mine_up, mine_down, stage_sem, *sems,
):
    s = Spot(groups, lanes)
    rows, width = tokens.shape
    head_cols = width // lanes
    slots = place.shape[1] // groups
    shard = width // groups
    take = take_from(sems)
    step = 64

    def blocks(ref, n):
        return lambda i: ref.at[pl.ds(pl.multiple_of(i * n, n), n)]

    def cols(i):
        return pl.ds(pl.multiple_of(i * head_cols, head_cols), head_cols)

    loads = [
        pltpu.make_async_copy(src, dst, stage_sem.at[i])
        for i, (src, dst) in enumerate(
            [(output_in, output_all), (qkv_in, qkv), (attend_in, attend_all), (normed_in, normed)])
    ]
    bk = GroupScatter(s, lambda l: back_part.at[l], bk_h, bk_c, bk_y, take(5), True)
    tk = GroupScatter(s, lambda l: tok_part.at[l], tk_h, tk_c, tk_y, take(5), True)
    mx = GroupScatter(s, lambda l: mix_part.at[l], mx_h, mx_c, mx_y, take(5), False)
    dn = GroupScatter(s, lambda l: dense_part.at[l], dn_h, dn_c, dn_y, take(5), False)
    gos = GroupScatter(s, lambda l: go.at[l], None, go_c, go_y, take(5), False)
    gns = GroupScatter(s, lambda l: gn.at[l], None, gn_c, gn_y, take(5), False)
    ups = LaneScatter(s, blocks(grad_up, shard), up_h, up_x, up_z, take(5))
    dws = LaneScatter(s, blocks(grad_down, shard), dw_h, dw_x, dw_z, take(5))
    gas = LaneScatter(s, blocks(ga, shard), None, ga_x, ga_z, take(5))
    gls = LaneScatter(s, blocks(gl, shard), None, gl_x, gl_z, take(5))
    sms = LaneScatter(s, lambda w: sm.at[w], None, sm_x, sm_z, take(5))
    back_swap = LaneSwap(s, blocks(ret_back, slots), blocks(got_back, slots), take(2))
    tok_swap = LaneSwap(s, blocks(ret_tok, slots), blocks(got_tok, slots), take(2))
    heads = GroupSwap(s, lambda l: grad_mixed.at[:, cols(l)], blocks(grad_heads, rows), take(2))
    f_attend = GroupGather(s, mine_attend, lambda l: all_attend.at[l], take(4))
    f_output = GroupGather(s, mine_output, lambda l: all_output.at[l], take(4))
    f_up = GroupGather(s, mine_up, lambda l: all_up.at[l], take(4))
    f_down = GroupGather(s, mine_down, lambda l: all_down.at[l], take(4))
    f_small = GroupGather(s, sm_mine, lambda l: sm_all.at[l], take(4))
    order = [(d, s.w_peer(d)) for d in [*range(1, groups), 0]]

    def pass_on(scatter):
        for _, w in order:
            scatter.relay(w)

    def hand_back(scatter, swap, ret):
        for d, w in order:
            scatter.got(w)
            ret[pl.ds(pl.multiple_of(w * slots, slots), slots), :] = scatter.total(w).astype(bf16)
            if d:
                swap.copy(d).start()
            else:
                swap.own().start()

    def totals(scatter, dst):
        scatter.got()

        def body(k, carry):
            dst[pl.ds(pl.multiple_of(k * step, step), step), :] = scatter.total(k).astype(dst.dtype)
            return carry

        lax.fori_loop(0, scatter.chunks, body, 0)

    def over_rows(body, init):
        return lax.fori_loop(0, rows // step, lambda i, c: body(pl.ds(pl.multiple_of(i * step, step), step), c), init)

    s.greet()
    bk.start()
    mx.start()
    ups.start()
    for c in loads:
        c.start()
    dk[...] = jnp.zeros_like(dk)
    dv[...] = jnp.zeros_like(dv)
    gains = small[...].astype(f32).T
    mine = meta[...].T
    valid_cols[...] = jnp.broadcast_to(mine[:, 1:2], valid_cols.shape)
    bk.ready()
    pass_on(bk)
    mx.ready()
    mx.relay()
    dws.start()
    hand_back(bk, back_swap, ret_back)
    tk.start()
    dn.start()
    ups.relay()
    totals(mx, grad_mix)
    for c in loads:
        c.wait()
    back_swap.arrive()
    grad_mix[...] += mm(place[...], got_back[...])

    def mid(at, gain_sum):
        normed_v, scale = norm_stats(tokens[at, :].astype(f32) + attention_out[at, :])
        grad = grad_mix[at, :]
        value = cot[at, :].astype(f32) * valid_cols[at, 0:1] + norm_back(normed_v, scale, gains[1:2, :], grad)
        grad_mid[at, :] = value
        grad_attn[at, :] = value.astype(bf16)
        return gain_sum + jnp.sum(grad * normed_v, axis=0, keepdims=True)

    mixer_gain_grad = over_rows(mid, jnp.zeros((1, width), f32))
    grad_mixed[...] = mm(grad_attn[...], output_all[...], 1, 1).astype(bf16)
    for l in range(lanes):
        heads.send(l)

    def out_grad(m, carry):
        value = mm(attn_mixed[:, cols(m)], grad_attn[...], 0, 0).astype(bf16)
        parts = head_cols // step
        for l in range(lanes):
            go[l, pl.ds(m * parts, parts)] = value[:, l * head_cols : (l + 1) * head_cols].reshape(parts, step, head_cols)
        return carry

    lax.fori_loop(0, lanes, out_grad, 0)
    gos.start()
    tk.ready()
    dws.relay()
    heads.arrive()
    doc_cols = [meta_all[l].T[:, 0:1] for l in range(lanes)]
    for tile in range(lanes):
        attend_back_tile(tile, qkv, doc_cols, lse, grad_heads, grad_qkv, mask, dk, dv)
        if tile == 0:
            pass_on(tk)
        if tile == 1:
            gos.ready()
            gos.relay()
        if tile == 2:
            dn.ready()
            dn.relay()
    for pair in range(head_cols // PAIR):
        grad_qkv[:, head_cols + pair * PAIR : head_cols + (pair + 1) * PAIR] = dk[pair].astype(bf16)
        grad_qkv[:, 2 * head_cols + pair * PAIR : 2 * head_cols + (pair + 1) * PAIR] = dv[pair].astype(bf16)

    def weight_grad(m, carry):
        ga[pl.ds(pl.multiple_of(m * head_cols, head_cols), head_cols), :] = mm(normed[:, cols(m)], grad_qkv[...], 0, 0).astype(bf16)
        return carry

    lax.fori_loop(0, lanes, weight_grad, 0)
    gas.start()

    def rows_grad(l, carry):
        value = mm(grad_qkv[pl.ds(pl.multiple_of(l * rows, rows), rows), :], attend_all[...], 1, 1)
        gn[l] = value.astype(bf16).reshape(rows // step, step, width)
        return carry

    lax.fori_loop(0, lanes, rows_grad, 0)
    gns.start()
    hand_back(tk, tok_swap, ret_tok)
    gns.ready()
    gns.relay()
    totals(gos, gl)
    gls.start()
    ups.finish(mine_up)
    f_up.start()
    gas.relay()
    totals(dn, grad_mix)
    tok_swap.arrive()
    gls.relay()

    def layer(at, sums):
        attention = attention_out[at, :]
        residual = tokens[at, :].astype(f32) + attention
        normed_v, _ = norm_stats(residual)
        mix = (normed_v * gains[1:2, :]).astype(bf16)
        logits = mm(mix, small[...])
        blend, router = picked(logits, 2, 2), picked(logits, 4, experts)
        columns = lax.broadcasted_iota(jnp.int32, logits.shape, 1)
        route = valid_cols[at, 1:2].astype(jnp.int32)
        chosen = jnp.sum(jnp.where(columns == 4 + route, router, 0.0), axis=1, keepdims=True)
        ffn = blend[:, 2:3] * chosen * mm(place[at, :], got_tok[...]) + blend[:, 3:4] * grad_mix[at, :]
        full = residual + ffn
        layer_out[at, :] = full.astype(bf16)
        valid = valid_cols[at, 0:1]
        got = [jnp.sum(valid * v * v, axis=(0, 1), keepdims=True) for v in (residual, full, attention, ffn)]
        got.append(jnp.sum(valid, axis=(0, 1), keepdims=True))
        return tuple(a + b for a, b in zip(sums, got))

    lane_of = lax.broadcasted_iota(jnp.int32, valid_cols.shape, 1)
    valid_cols[...] = jnp.where(lane_of == 1, mine[:, 2:3], mine[:, 1:2])
    sums = over_rows(layer, tuple(jnp.zeros((1, 1), f32) for _ in range(5)))
    totals(gns, grad_mix)

    def first(at, gain_sum):
        normed_v, scale = norm_stats(tokens[at, :].astype(f32))
        grad = grad_mix[at, :]
        grad_tokens[at, :] = (grad_mid[at, :] + norm_back(normed_v, scale, gains[0:1, :], grad)).astype(bf16)
        return gain_sum + jnp.sum(grad * normed_v, axis=0, keepdims=True)

    attend_gain_grad = over_rows(first, jnp.zeros((1, width), f32))
    feature = lax.broadcasted_iota(jnp.int32, (SMALL, shard), 0)
    place_of = lax.broadcasted_iota(jnp.int32, (SMALL, shard), 1)
    tail = jnp.zeros((SMALL, shard), f32)
    for i, v in enumerate(sums):
        tail = jnp.where(place_of == i, v, tail)
    for w in range(groups):
        here = slice(w * shard, (w + 1) * shard)
        value = jnp.where(feature == SMALL - 1, tail, grad_small[:, here])
        value = jnp.where(feature == 0, attend_gain_grad[:, here], value)
        sm[w] = jnp.where(feature == 1, mixer_gain_grad[:, here], value)
    sms.start()
    f_up.forward()
    dws.finish(mine_down)
    f_down.start()
    sms.relay()
    gas.finish(mine_attend)
    f_attend.start()
    gls.finish(mine_output)
    f_output.start()
    sms.finish(sm_mine)
    f_small.start()
    gathers = [f_up, f_down, f_attend, f_output, f_small]
    for task in gathers[1:]:
        task.forward()
    for task in gathers:
        task.arrive()
    small_out[...] = sum([sm_all[l] for l in range(1, lanes)], sm_all[0])
    for task in [bk, tk, mx, dn, gos, gns, ups, dws, gas, gls, sms, back_swap, tok_swap, heads] + gathers:
        task.sent()


def back(groups, lanes, experts, slots, inputs, placed):
    tokens = inputs[0]
    rows, width = tokens.shape
    X = 1 << ((groups.bit_length() - 1) // 2)
    Y, Z = lanes // 2, groups // X
    everyone = rows * lanes
    head_cols = width // lanes
    shard = width // groups
    hidden = placed[4].shape[1]
    vmem, anywhere = pl.BlockSpec(memory_space=pltpu.VMEM), pl.BlockSpec(memory_space=pl.ANY)
    dma = pltpu.SemaphoreType.DMA
    of = jax.ShapeDtypeStruct
    pairs = head_cols // PAIR
    low = lambda *shape: pltpu.VMEM(shape, bf16)
    wide = lambda *shape: pltpu.VMEM(shape, f32)

    def group_bufs(c, r, n, held=True):
        return ([low(Y, c, r, n)] if held else [low(lanes, c, r, n)]) + [low(Y, c, r, n), low(Y - 1, c, r, n)]

    def lane_bufs(n, held=True):
        return ([low(Z, shard, n)] if held else [low(width, n)]) + [low(X - 1, Z, shard, n), low(Z - 1, shard, n)]

    scratch = [low(everyone, 3 * head_cols), low(width, width), low(width, 3 * head_cols), low(everyone, width)]
    scratch[0], scratch[1] = low(everyone, 3 * head_cols), low(width, width)
    scratch += group_bufs(groups, slots, width) * 2 + group_bufs(rows // 64, 64, width) * 2
    scratch += group_bufs(width // 64, 64, head_cols, False) + group_bufs(rows // 64, 64, width, False)
    scratch += lane_bufs(hidden) + lane_bufs(width) + lane_bufs(3 * head_cols, False) + lane_bufs(head_cols, False)
    scratch += [wide(groups, SMALL, shard), wide(X - 1, Z, SMALL, shard), wide(Z - 1, SMALL, shard)]
    scratch += [wide(SMALL, shard), wide(lanes, SMALL, shard)]
    scratch += [low(groups * slots, width)] * 4
    scratch += [wide(rows, width), wide(rows, width), low(rows, width), low(rows, width)]
    scratch += [low(everyone, head_cols), low(everyone, 3 * head_cols), wide(everyone, Q_TILE)]
    scratch += [wide(pairs, everyone, PAIR)] * 2 + [wide(rows, SMALL)]
    scratch += [low(shard, 3 * head_cols), low(shard, head_cols), low(shard, hidden), low(shard, width)]
    scratch += [dma((4,))]
    scratch += GroupScatter.sems(lanes, groups) * 2 + GroupScatter.sems(lanes, 1) * 4
    scratch += LaneScatter.sems(groups, X) * 5
    scratch += LaneSwap.sems(groups) * 2 + GroupSwap.sems(lanes)
    scratch += GroupGather.sems(lanes) * 5
    outs = [
        (of((rows, width), bf16), vmem),
        (of((rows, width), bf16), vmem),
        (of((SMALL, shard), f32), vmem),
        (of((lanes, shard, 3 * head_cols), bf16), anywhere),
        (of((lanes, shard, head_cols), bf16), anywhere),
        (of((lanes, shard, hidden), bf16), anywhere),
        (of((lanes, shard, width), bf16), anywhere),
    ]
    return pl.pallas_call(
        functools.partial(back_kernel, groups, lanes, experts),
        out_shape=[o for o, _ in outs],
        in_specs=[vmem] * len(inputs) + [anywhere] * len(placed),
        out_specs=[p for _, p in outs],
        scratch_shapes=scratch,
        compiler_params=pltpu.CompilerParams(collective_id=1, has_side_effects=True, vmem_limit_bytes=62 * 2**20),
        cost_estimate=pl.CostEstimate(flops=8 * 10**9, bytes_accessed=10**8, transcendentals=0),
        name="back",
    )(*inputs, *placed)


def lane_gather(part):
    return lax.all_gather(part, "wide", axis=0, tiled=True)


def lane_scatter(part):
    return lax.psum_scatter(part.astype(bf16), "wide", scatter_dimension=0, tiled=True)


def group_gather(part, axis=0):
    return lax.all_gather(part, "narrow", axis=axis, tiled=True)


def group_scatter(part, axis=0):
    return lax.psum_scatter(part.astype(bf16), "narrow", scatter_dimension=axis, tiled=True)


def lane_swap(part):
    return lax.all_to_all(part, "wide", split_axis=0, concat_axis=0, tiled=True)


def per_device(
    tokens, doc_ids, valid_mask, routes, cotangent, attend_gain, attend_weight, output_weight, mixer_gain,
    router_weight, blend_weight, up_weight, down_weight, expert_up, expert_down,
):
    rows, width = tokens.shape
    groups, lanes = lax.axis_size("wide"), lax.axis_size("narrow")
    group, lane = lax.axis_index("wide"), lax.axis_index("narrow")
    shard = attend_gain.shape[0]
    local = expert_up.shape[0]
    experts = local * groups
    hidden = up_weight.shape[1]
    fine = hidden // groups // lanes
    cap = max(2, (3 * rows + 2 * experts - 1) // (2 * experts))
    slots = -(-local * cap // 16) * 16
    all_rows = rows * lanes

    small = jnp.concatenate(
        [attend_gain[:, None], mixer_gain[:, None], blend_weight, router_weight,
         jnp.zeros((shard, SMALL - 4 - experts), bf16)], axis=1)
    meta = jnp.stack([doc_ids, valid_mask, routes[:, 0]]).astype(f32)
    meta = jnp.pad(meta, ((0, 5), (0, 0)))
    up_mine = up_weight
    if fine % 128:
        up_mine = lax.dynamic_index_in_dim(up_weight.reshape(shard, groups, lanes, fine), lane, 2, keepdims=False)
        up_mine = up_mine.reshape(shard, groups * fine)
    (
        normed_attend, qkv, lse, attn_mixed, attention_out, mix_all, small, meta_all, place,
        attend_full, output_full, got_mix, got_cot, cot_all, up_full, down_full,
    ) = front(groups, lanes, local, cap, slots, tokens, cotangent, meta, small, attend_weight, output_weight, up_mine, down_weight)
    doc_col = meta_all[:, 0].reshape(all_rows, 1)
    valid_all = meta_all[:, 1].reshape(all_rows, 1)
    attend_gain_row = small[:, 0].astype(f32)
    mixer_gain_row = small[:, 1].astype(f32)
    mix_cols = jnp.where((jnp.arange(SMALL) < 2)[None, :], 0, small)
    residual_mid = tokens.astype(f32) + attention_out
    mid_normed, mid_scale = norm_stats(residual_mid)
    normed_mix = (mid_normed * mixer_gain_row).astype(bf16)
    route = routes[:, 0]

    def give_back(partial):
        return mm(place, lane_swap(group_scatter(partial)))

    valid = valid_mask.astype(f32)[:, None]
    grad_layer = cotangent.astype(f32) * valid

    def coefficients(mix_rows):
        logits = mm(mix_rows, mix_cols)
        columns = jnp.arange(SMALL)[None, :]
        blend = soft_max(jnp.where((columns >= 2) & (columns < 4), logits, masked_score))
        router = soft_max(jnp.where((columns >= 4) & (columns < 4 + experts), logits, masked_score))
        return columns, blend, router

    columns, blend, _ = coefficients(mix_all)
    blend_0, blend_1 = blend[:, 2:3], blend[:, 3:4]
    grad_dense = (blend_1 * (cot_all.astype(f32) * valid_all.astype(f32))).astype(bf16)
    up_act, up_slope = gelu_both(mm(mix_all, up_full))
    up_act = up_act.astype(bf16)
    dense_part = mm(up_act, down_full)
    grad_up_act = mm(grad_dense, down_full, 1, 1)
    dense_dot = jnp.sum(up_act.astype(f32) * grad_up_act, axis=1, keepdims=True)
    grad_up_pre = (up_slope * grad_up_act).astype(bf16)
    dense_logits = (jnp.where(columns == 3, 1.0, 0.0) - jnp.where(columns == 2, 1.0, 0.0)) * (blend_0 * dense_dot)
    grad_mix_part = mm(grad_up_pre, up_full, 1, 1) + mm(dense_logits.astype(bf16), mix_cols, 1, 1)
    grad_small = mm(dense_logits.astype(bf16), mix_all, 0, 0)
    grad_up = mm(mix_all, grad_up_pre, 0, 0)
    grad_down = mm(up_act, grad_dense, 0, 0)

    def by_expert(received):
        split = received.reshape(lanes * groups, slots, width)[:, : local * cap]
        return split.reshape(lanes * groups, local, cap, width).transpose(1, 0, 2, 3).reshape(local, -1, width)

    def by_slot(values):
        split = values.reshape(local, lanes * groups, cap, width).transpose(1, 0, 2, 3)
        split = split.reshape(lanes * groups, local * cap, width)
        return jnp.pad(split, ((0, 0), (0, slots - local * cap), (0, 0))).reshape(-1, width)

    mix_e, cot_e = by_expert(got_mix), by_expert(got_cot)
    tok_parts, back_parts, up_grads, down_grads = [], [], [], []
    for e in range(local):
        _, blend, router = coefficients(mix_e[e])
        own = columns == 4 + group * local + e
        chosen = jnp.sum(jnp.where(own, router, 0.0), axis=1, keepdims=True)
        scale = blend[:, 2:3] * chosen
        grad_tok = (scale * cot_e[e].astype(f32)).astype(bf16)
        act, slope = gelu_both(mm(mix_e[e], expert_up[e]))
        act = act.astype(bf16)
        tok_parts.append((mm(act, expert_down[e])))
        grad_act = mm(grad_tok, expert_down[e], 1, 1)
        dot = jnp.sum(act.astype(f32) * grad_act, axis=1, keepdims=True)
        grad_hidden = (slope * grad_act).astype(bf16)
        logits = dot * (jnp.where(own, 1.0, 0.0) - router)
        logits += dot * blend[:, 3:4] * (jnp.where(columns == 2, 1.0, 0.0) - jnp.where(columns == 3, 1.0, 0.0))
        logits = logits.astype(bf16)
        back_parts.append(mm(grad_hidden, expert_up[e], 1, 1) + mm(logits, mix_cols, 1, 1))
        grad_small += mm(logits, mix_e[e], 0, 0)
        down_grads.append(mm(act, grad_tok, 0, 0))
        up_grads.append(mm(mix_e[e], grad_hidden, 0, 0))
    grad_expert_up, grad_expert_down = jnp.stack(up_grads), jnp.stack(down_grads)
    def widen(gathered, parts):
        full = gathered.reshape(lanes, shard, parts, -1)
        return full.transpose(1, 2, 0, 3).reshape(shard, -1).astype(f32)

    if all_rows * width <= 2**20 and shard % 128 == 0:
        def chunked(part):
            return part.astype(bf16).reshape(lanes, rows // 64, 64, width)

        def slotted(parts):
            return by_slot(jnp.stack(parts).astype(bf16)).reshape(lanes, groups, slots, width)

        layer_out, grad_tokens, small_out, out_attend, out_output, out_up, out_down = back(
            groups, lanes, experts, slots,
            (tokens, cotangent, meta, small, attention_out, attn_mixed, place, meta_all, lse, grad_small),
            (chunked(grad_mix_part), chunked(dense_part), slotted(back_parts), slotted(tok_parts), grad_up.astype(bf16),
             grad_down.astype(bf16), qkv, output_full, attend_full, normed_attend))
        sums, small_out = small_out[SMALL - 1], small_out.T
        root_means = jnp.sqrt(sums[:4] / (jnp.maximum(sums[4], 1.0) * width))
        return (
            layer_out, grad_tokens, small_out[:, 0], widen(out_attend, 3), widen(out_output, 1), small_out[:, 1],
            small_out[:, 4 : 4 + experts], small_out[:, 2:4], widen(out_up, groups),
            out_down.reshape(-1, width).astype(f32), grad_expert_up, grad_expert_down, root_means,
        )
    grad_small = grad_small.T
    expert_back = give_back(by_slot(jnp.stack(back_parts)))
    expert_tok = give_back(by_slot(jnp.stack(tok_parts)))

    dense_out = group_scatter(dense_part).astype(f32)
    _, blend, router = coefficients(normed_mix)
    own = columns == 4 + route[:, None]
    chosen = jnp.sum(jnp.where(own, router, 0.0), axis=1, keepdims=True)
    ffn_out = blend[:, 2:3] * chosen * expert_tok + blend[:, 3:4] * dense_out
    layer_full = residual_mid + ffn_out
    sums = jnp.stack(
        [jnp.sum(valid * v * v) for v in (residual_mid, layer_full, attention_out, ffn_out)] + [jnp.sum(valid)])

    grad_mix = group_scatter(grad_mix_part).astype(f32) + expert_back
    grad_mid = grad_layer + norm_back(mid_normed, mid_scale, mixer_gain_row, grad_mix)
    mixer_gain_grad = jnp.sum(grad_mix * mid_normed, axis=0)
    grad_attn = grad_mid.astype(bf16)
    grad_output = mm(attn_mixed, grad_attn, 0, 0)
    grad_mixed = mm(grad_attn, output_full, 1, 1).astype(bf16)
    grad_heads = lax.all_to_all(grad_mixed, "narrow", split_axis=1, concat_axis=0, tiled=True)
    grad_qkv = attend_back(qkv, doc_col, lse, grad_heads)
    grad_attend = mm(normed_attend, grad_qkv, 0, 0)
    grad_normed = group_scatter(mm(grad_qkv, attend_full, 1, 1)).astype(f32)
    in_normed, in_scale = norm_stats(tokens.astype(f32))
    grad_tokens = (grad_mid + norm_back(in_normed, in_scale, attend_gain_row, grad_normed)).astype(bf16)
    attend_gain_grad = jnp.sum(grad_normed * in_normed, axis=0)

    grad_small = jnp.where(columns == 0, attend_gain_grad[:, None], jnp.where(columns == 1, mixer_gain_grad[:, None], grad_small))
    small_out = lax.psum(lax.psum_scatter(grad_small, "wide", scatter_dimension=0, tiled=True), "narrow")
    sums = lax.psum(sums, ("wide", "narrow"))
    root_means = jnp.sqrt(sums[:4] / (jnp.maximum(sums[4], 1.0) * width))

    def share(part):
        return group_gather(part.astype(bf16)[None])

    out_attend = widen(share(lane_scatter(grad_attend)), 3)
    out_output = widen(share(lane_scatter(group_scatter(grad_output, axis=1))), 1)
    out_up = widen(share(lane_scatter(grad_up)), groups)
    out_down = group_gather(lane_scatter(grad_down).astype(bf16)).astype(f32)
    return (
        layer_full.astype(bf16), grad_tokens, small_out[:, 0], out_attend, out_output, small_out[:, 1],
        small_out[:, 4 : 4 + experts], small_out[:, 2:4], out_up, out_down, grad_expert_up, grad_expert_down, root_means,
    )


def solution(mesh):
    both = ("wide", "narrow")
    row, vec, mat = P(both, None), P("wide"), P("wide", None)
    up, down = P("wide", None, "narrow"), P("wide", "narrow", None)
    return jax.shard_map(
        per_device,
        mesh=mesh,
        in_specs=(row, P(both), P(both), row, row, vec, mat, mat, vec, mat, mat, mat, mat, up, down),
        out_specs=(row, row, vec, mat, mat, vec, mat, mat, mat, mat, up, down, P()),
        check_vma=False,
    )
```

```python
import functools

import jax
import jax.numpy as jnp
from jax import lax
from jax.experimental import pallas as pl
from jax.experimental.pallas import tpu as pltpu
from jax.sharding import PartitionSpec as P

HEAD_DIM = 64
PAIR = 2 * HEAD_DIM
Q_TILE = 256
SMALL = 128
eps_norm = 1e-05
masked_score = -1e30
f32 = jnp.float32
bf16 = jnp.bfloat16


def mm(a, b, ca=1, cb=0):
    return lax.dot_general(a, b, (((ca,), (cb,)), ((), ())), preferred_element_type=f32)


def norm_stats(values):
    center = values - jnp.mean(values, axis=-1, keepdims=True)
    scale = lax.rsqrt(jnp.mean(center * center, axis=-1, keepdims=True) + eps_norm)
    return center * scale, scale


def norm_back(normed, scale, gain, grad):
    u = grad * gain
    return scale * (
        u
        - jnp.mean(u, axis=-1, keepdims=True)
        - normed * jnp.mean(u * normed, axis=-1, keepdims=True)
    )


GELU_A = 0.7978845608028654
GELU_B = 0.044715


def gelu(v):
    return 0.5 * v * (1.0 + jnp.tanh(GELU_A * (v + GELU_B * v * v * v)))


def gelu_both(v):
    t = jnp.tanh(GELU_A * (v + GELU_B * v * v * v))
    value = 0.5 * v * (1.0 + t)
    slope = 0.5 * (1.0 + t) + 0.5 * v * (1.0 - t * t) * (GELU_A * (1.0 + 3.0 * GELU_B * v * v))
    return value, slope


def soft_max(logits):
    shifted = jnp.exp(logits - jnp.max(logits, axis=-1, keepdims=True))
    return shifted / jnp.sum(shifted, axis=-1, keepdims=True)


def head_mask(half):
    lanes = lax.broadcasted_iota(jnp.int32, (1, PAIR), 1)
    return (lanes // HEAD_DIM) == half


def attend_tile(tile, qkv_ref, doc_cols, out_ref, lse_ref, mask_ref, vt_ref):
    cols = out_ref.shape[1]
    extent = (tile + 1) * Q_TILE
    here, seen = pl.ds(tile * Q_TILE, Q_TILE), pl.ds(0, extent)
    mask_tile(tile, doc_cols, mask_ref)

    def pair_step(pair, carry):
        q_cols = pl.ds(pl.multiple_of(pair * PAIR, PAIR), PAIR)
        k_cols = pl.ds(pl.multiple_of(cols + pair * PAIR, PAIR), PAIR)
        v_cols = pl.ds(pl.multiple_of(2 * cols + pair * PAIR, PAIR), PAIR)
        if tile == 0:
            vt_ref[pair] = qkv_ref[:, v_cols].T
        queries = qkv_ref[here, q_cols] * jnp.asarray(HEAD_DIM**-0.5, bf16)
        mixed = jnp.zeros((PAIR, Q_TILE), f32)
        for half in range(2):
            one = jnp.where(head_mask(half), queries, jnp.zeros_like(queries))
            scores = mm(qkv_ref[seen, k_cols], one, 1, 1) + mask_ref[seen, :]
            top = jnp.max(scores, axis=0, keepdims=True)
            shifted = jnp.exp(scores - top)
            total = jnp.sum(shifted, axis=0, keepdims=True)
            low = (shifted * (1.0 / total)).astype(bf16)
            lse_ref[pair, pl.ds(half, 1), here] = top + jnp.log(total)
            got = mm(vt_ref[pair, :, seen], low)
            sublanes = lax.broadcasted_iota(jnp.int32, (PAIR, 1), 0)
            mixed = jnp.where((sublanes // HEAD_DIM) == half, got, mixed)
        out_ref[here, q_cols] = mixed.T.astype(bf16)
        return carry

    lax.fori_loop(0, cols // PAIR, pair_step, 0)


def mask_tile(tile, doc_cols, mask_ref):
    row = (tile * Q_TILE + lax.broadcasted_iota(jnp.int32, (Q_TILE, Q_TILE), 1)).astype(f32)
    for block in range(tile + 1):
        allowed = doc_cols[block] >= row
        if block == tile:
            key = (tile * Q_TILE + lax.broadcasted_iota(jnp.int32, (Q_TILE, Q_TILE), 0)).astype(f32)
            allowed = allowed & (key <= row)
        mask_ref[pl.ds(block * Q_TILE, Q_TILE), :] = jnp.where(allowed, 0.0, masked_score)


def attend_back_kernel(qkv_ref, doc_ref, lse_ref, grad_ref, out_ref, mask_ref, dk_ref, dv_ref):
    rows, cols = grad_ref.shape
    pairs = cols // PAIR
    dk_ref[...] = jnp.zeros_like(dk_ref)
    dv_ref[...] = jnp.zeros_like(dv_ref)
    for tile in range(rows // Q_TILE):
        extent = (tile + 1) * Q_TILE
        here = pl.ds(tile * Q_TILE, Q_TILE)
        seen = pl.ds(0, extent)
        mask_tile(tile, [doc_ref[pl.ds(b * Q_TILE, Q_TILE), :] for b in range(tile + 1)], mask_ref)

        def pair_step(pair, carry):
            q_cols = pl.ds(pl.multiple_of(pair * PAIR, PAIR), PAIR)
            k_cols = pl.ds(pl.multiple_of(cols + pair * PAIR, PAIR), PAIR)
            v_cols = pl.ds(pl.multiple_of(2 * cols + pair * PAIR, PAIR), PAIR)
            queries = qkv_ref[here, q_cols] * jnp.asarray(HEAD_DIM**-0.5, bf16)
            keys, values = qkv_ref[seen, k_cols], qkv_ref[seen, v_cols]
            grads = grad_ref[here, q_cols]
            dq = jnp.zeros((PAIR, Q_TILE), f32)
            for half in range(2):
                on = head_mask(half)
                q_one = jnp.where(on, queries, jnp.zeros_like(queries))
                g_one = jnp.where(on, grads, jnp.zeros_like(grads))
                probs = jnp.exp(mm(keys, q_one, 1, 1) + mask_ref[seen, :] - lse_ref[pair, pl.ds(half, 1), here])
                dv_ref[pair, seen, :] += mm(probs.astype(bf16), g_one)
                back = mm(values, g_one, 1, 1)
                low = (probs * (back - jnp.sum(probs * back, axis=0, keepdims=True))).astype(bf16)
                dk_ref[pair, seen, :] += mm(low, q_one)
                got = mm(keys, low, 0, 0)
                sublanes = lax.broadcasted_iota(jnp.int32, (PAIR, 1), 0)
                dq = jnp.where((sublanes // HEAD_DIM) == half, got, dq)
            out_ref[here, q_cols] = (dq.T * HEAD_DIM**-0.5).astype(bf16)
            return carry

        lax.fori_loop(0, pairs, pair_step, 0)
    for pair in range(pairs):
        out_ref[:, cols + pair * PAIR : cols + (pair + 1) * PAIR] = dk_ref[pair].astype(bf16)
        out_ref[:, 2 * cols + pair * PAIR : 2 * cols + (pair + 1) * PAIR] = dv_ref[pair].astype(bf16)


def attend_back(qkv, doc_col, lse, grad):
    rows, cols = grad.shape
    vmem = pl.BlockSpec(memory_space=pltpu.VMEM)
    return pl.pallas_call(
        attend_back_kernel,
        out_shape=jax.ShapeDtypeStruct((rows, 3 * cols), bf16),
        in_specs=[vmem] * 4,
        out_specs=vmem,
        scratch_shapes=[
            pltpu.VMEM((rows, Q_TILE), f32),
            pltpu.VMEM((cols // PAIR, rows, PAIR), f32),
            pltpu.VMEM((cols // PAIR, rows, PAIR), f32),
        ],
        compiler_params=pltpu.CompilerParams(vmem_limit_bytes=56 * 2**20),
        cost_estimate=pl.CostEstimate(flops=20 * rows * rows * cols, bytes_accessed=16 * rows * cols, transcendentals=0),
        name="attend_back",
    )(qkv, doc_col, lse, grad)


MESH = pl.DeviceIdType.MESH


class Spot:
    def __init__(self, groups, lanes):
        self.W, self.L = groups, lanes
        self.X = 1 << ((groups.bit_length() - 1) // 2)
        self.Z, self.Y = groups // self.X, lanes // 2
        self.g, self.l = lax.axis_index("wide"), lax.axis_index("narrow")
        self.z, self.x = self.g // self.X, self.g % self.X
        self.y, self.c = self.l // 2, self.l % 2

    def zx_peer(self, dz, dx):
        return lax.rem(self.z + dz, self.Z) * self.X + lax.rem(self.x + dx, self.X)

    def z_peer(self, d):
        return self.zx_peer(d, 0)

    def x_peer(self, d):
        return self.zx_peer(0, d)

    def y_peer(self, d):
        return lax.rem(self.y + d, self.Y) * 2 + self.c

    def core_peer(self):
        return self.y * 2 + 1 - self.c

    def w_peer(self, d):
        return lax.rem(self.g + d, self.W)

    def l_peer(self, d):
        return lax.rem(self.l + d, self.L)

    def greet(self, lane_peers=True):
        barrier = pltpu.get_barrier_semaphore()
        met = self.L - 1
        for d in range(1, self.L):
            pl.semaphore_signal(barrier, 1, device_id=(self.g, self.l_peer(d)), device_id_type=MESH)
        if lane_peers:
            met += self.W - 1
            for d in range(1, self.W):
                pl.semaphore_signal(barrier, 1, device_id=(self.w_peer(d), self.l), device_id_type=MESH)
        pl.semaphore_wait(barrier, met)


def remote(src, dst, send_sem, recv_sem, group, lane):
    return pltpu.make_async_remote_copy(src, dst, send_sem, recv_sem, device_id=(group, lane), device_id_type=MESH)


class LaneGather:
    def __init__(self, spot, src, place, sems):
        self.s, self.src, self.place = spot, src, place
        self.z_sem, self.x_sem, self.r_sem, self.own_sem = sems

    @staticmethod
    def sems(W, X):
        dma = pltpu.SemaphoreType.DMA
        return [dma((W // X,)), dma((W // X, X)), dma((W,)), dma((1,))]

    def z_copy(self, d):
        s = self.s
        return remote(self.src, self.place(s.g), self.z_sem.at[d], self.r_sem.at[s.g], s.z_peer(d), s.l)

    def x_copy(self, d, e):
        s = self.s
        w = s.z_peer(d)
        src = self.src if d == 0 else self.place(w)
        return remote(src, self.place(w), self.x_sem.at[d, e], self.r_sem.at[w], s.x_peer(e), s.l)

    def got(self, w):
        s = self.s
        remote(self.src, self.place(w), self.z_sem.at[0], self.r_sem.at[w], s.x_peer(1), s.l).wait_recv()

    def own(self):
        return pltpu.make_async_copy(self.src, self.place(self.s.g), self.own_sem.at[0])

    def start(self):
        for d in range(1, self.s.Z):
            self.z_copy(d).start()
        for e in range(1, self.s.X):
            self.x_copy(0, e).start()
        self.own().start()

    def forward(self):
        for d in range(1, self.s.Z):
            self.got(self.s.z_peer(d))
            for e in range(1, self.s.X):
                self.x_copy(d, e).start()

    def arrive(self):
        s = self.s
        for d in range(s.Z):
            for e in range(1, s.X):
                self.got(s.zx_peer(d, e))
        self.own().wait()

    def sent(self):
        for d in range(1, self.s.Z):
            self.z_copy(d).wait_send()
        for d in range(self.s.Z):
            for e in range(1, self.s.X):
                self.x_copy(d, e).wait_send()


class GroupGather:
    def __init__(self, spot, src, place, sems, own=True):
        self.s, self.src, self.place, self.has_own = spot, src, place, own
        self.y_sem, self.c_sem, self.r_sem, self.own_sem = sems

    @staticmethod
    def sems(L):
        dma = pltpu.SemaphoreType.DMA
        return [dma((L // 2,)), dma((L // 2,)), dma((L,)), dma((1,))]

    def y_copy(self, d):
        s = self.s
        return remote(self.src, self.place(s.l), self.y_sem.at[d], self.r_sem.at[s.l], s.g, s.y_peer(d))

    def c_copy(self, d):
        s = self.s
        l = s.y_peer(d)
        src = self.src if d == 0 else self.place(l)
        return remote(src, self.place(l), self.c_sem.at[d], self.r_sem.at[l], s.g, s.core_peer())

    def got(self, l):
        s = self.s
        remote(self.src, self.place(l), self.y_sem.at[0], self.r_sem.at[l], s.g, s.core_peer()).wait_recv()

    def own(self):
        return pltpu.make_async_copy(self.src, self.place(self.s.l), self.own_sem.at[0])

    def start(self):
        for d in range(1, self.s.Y):
            self.y_copy(d).start()
        self.c_copy(0).start()
        if self.has_own:
            self.own().start()

    def forward(self):
        for d in range(1, self.s.Y):
            self.got(self.s.y_peer(d))
            self.c_copy(d).start()

    def arrive(self):
        s = self.s
        for d in range(s.Y):
            self.got(lax.rem(s.y + d, s.Y) * 2 + 1 - s.c)
        if self.has_own:
            self.own().wait()

    def sent(self):
        for d in range(1, self.s.Y):
            self.y_copy(d).wait_send()
        for d in range(self.s.Y):
            self.c_copy(d).wait_send()


class LaneSwap:
    def __init__(self, spot, src, dst, sems):
        self.s, self.src, self.dst = spot, src, dst
        self.s_sem, self.r_sem = sems

    @staticmethod
    def sems(W):
        return [pltpu.SemaphoreType.DMA((W,)), pltpu.SemaphoreType.DMA((W,))]

    def copy(self, d):
        s = self.s
        w = s.w_peer(d)
        return remote(self.src(w), self.dst(s.g), self.s_sem.at[d], self.r_sem.at[s.g], w, s.l)

    def own(self):
        return pltpu.make_async_copy(self.src(self.s.g), self.dst(self.s.g), self.s_sem.at[0])

    def start(self):
        for d in range(1, self.s.W):
            self.copy(d).start()
        self.own().start()

    def got(self, w):
        s = self.s
        remote(self.src(w), self.dst(w), self.s_sem.at[0], self.r_sem.at[w], s.w_peer(1), s.l).wait_recv()

    def arrive(self):
        for d in range(1, self.s.W):
            self.got(self.s.w_peer(self.s.W - d))
        self.own().wait()

    def sent(self):
        for d in range(1, self.s.W):
            self.copy(d).wait_send()


class GroupSwap:
    def __init__(self, spot, src, dst, sems):
        self.s, self.src, self.dst = spot, src, dst
        self.s_sem, self.r_sem = sems

    @staticmethod
    def sems(L):
        return [pltpu.SemaphoreType.DMA((L,)), pltpu.SemaphoreType.DMA((L,))]

    def copy(self, l):
        s = self.s
        return remote(self.src(l), self.dst(s.l), self.s_sem.at[l], self.r_sem.at[s.l], s.g, l)

    def own(self):
        s = self.s
        return pltpu.make_async_copy(self.src(s.l), self.dst(s.l), self.s_sem.at[s.l])

    def send(self, l):
        @pl.when(self.s.l == l)
        def _():
            self.own().start()

        @pl.when(self.s.l != l)
        def _():
            self.copy(l).start()

    def arrive(self):
        s = self.s
        for d in range(1, s.L):
            l = s.l_peer(d)
            remote(self.src(l), self.dst(l), self.s_sem.at[l], self.r_sem.at[l], s.g, l).wait_recv()
        self.own().wait()

    def sent(self):
        for d in range(1, self.s.L):
            self.copy(self.s.l_peer(d)).wait_send()


def rows_norm(src, gain, dst, count, step=64):
    def body(i, carry):
        at = pl.ds(pl.multiple_of(i * step, step), step)
        normed, _ = norm_stats(src[at, :].astype(f32))
        dst[at, :] = (normed * gain).astype(bf16)
        return carry

    lax.fori_loop(0, count // step, body, 0)


def front_kernel(
    groups, lanes, local, cap, slots,
    tokens, cot, meta, small, attend_w, output_w, up_w, down_w,
    normed_out, qkv, lse, attn_mixed, attention_out, mix_all, small_all, meta_all, place,
    attend_all, output_all, packed_cot, got_mix, cot_all, up_all, down_all,
    tok_all, attend_mine, up_mine, mixed, mask, vt, packed_mix, stage_sem, spread_y, spread_c, spread_r, *sems,
):
    s = Spot(groups, lanes)
    rows, width = tokens.shape
    head_cols = width // lanes
    shard = attend_w.shape[0]
    depth = down_all.shape[0] // groups
    sems = list(sems)

    def take(n):
        out = sems[:n]
        del sems[:n]
        return out

    def blocks(ref, n):
        return lambda i: ref.at[pl.ds(pl.multiple_of(i * n, n), n)]

    def cols(i):
        return pl.ds(pl.multiple_of(i * head_cols, head_cols), head_cols)

    staged = [
        pltpu.make_async_copy(
            attend_w.at[:, pl.ds(pl.multiple_of(p * width + s.l * head_cols, head_cols), head_cols)],
            attend_mine.at[:, pl.ds(p * head_cols, head_cols)], stage_sem.at[p])
        for p in range(3)
    ]
    if up_w.shape[1] != up_mine.shape[1]:
        fine = up_mine.shape[1] // groups
        staged += [
            pltpu.make_async_copy(
                up_w.at[:, pl.ds(pl.multiple_of((w * lanes + s.l) * fine, fine), fine)],
                up_mine.at[:, pl.ds(w * fine, fine)], stage_sem.at[3 + w])
            for w in range(groups)
        ]
    else:
        staged += [pltpu.make_async_copy(up_w, up_mine, stage_sem.at[3])]
    for c in staged:
        c.start()

    tok = GroupGather(s, tokens, blocks(tok_all, rows), take(4))
    met = GroupGather(s, meta, lambda l: meta_all.at[l], take(4))
    cots = GroupGather(s, cot, blocks(cot_all, rows), take(4))
    mix = GroupGather(s, blocks(mix_all, rows)(s.l), blocks(mix_all, rows), take(4), own=False)
    outs = GroupGather(s, output_all.at[:, cols(s.l)], lambda l: output_all.at[:, cols(l)], take(4), own=False)
    att = LaneGather(s, attend_mine, blocks(attend_all, shard), take(4))
    sml = LaneGather(s, small, blocks(small_all, shard), take(4))
    out = LaneGather(s, output_w.at[:, cols(s.l)],
                     lambda w: output_all.at[pl.ds(pl.multiple_of(w * shard, shard), shard), cols(s.l)], take(4))
    up = LaneGather(s, up_mine, blocks(up_all, shard), take(4))
    down = LaneGather(s, down_w.at[pl.ds(pl.multiple_of(s.l * depth, depth), depth)], blocks(down_all, depth), take(4))
    swap = GroupSwap(s, blocks(mixed, rows), lambda l: attn_mixed.at[:, cols(l)], take(2))
    mix_swap = LaneSwap(s, blocks(packed_mix, slots), lambda w: got_mix.at[s.l, w], take(2))

    def spread(d):
        w = s.w_peer(groups - d)
        return GroupGather(s, got_mix.at[s.l, w], lambda l: got_mix.at[l, w],
                           [spread_y.at[w], spread_c.at[w], spread_r.at[w], None], own=False)

    mix_spread = [spread(d) for d in range(groups)]

    s.greet()
    for c in staged[:3]:
        c.wait()
    sml.start()
    met.start()
    tok.start()
    att.start()
    for c in staged[3:]:
        c.wait()
    mine = meta[...].T
    valid, route = mine[:, 1:2], mine[:, 2:3].astype(jnp.int32)
    column = lax.broadcasted_iota(jnp.int32, (rows, SMALL), 1)
    hits = (column == route).astype(f32)
    earlier = lax.broadcasted_iota(jnp.int32, (rows, rows), 1) < lax.broadcasted_iota(jnp.int32, (rows, rows), 0)
    rank = jnp.sum(hits * mm(earlier.astype(f32).astype(bf16), hits.astype(bf16)), axis=1, keepdims=True).astype(jnp.int32)
    slot = (route // local) * slots + (route % local) * cap + rank
    spots = (slot == lax.broadcasted_iota(jnp.int32, (rows, groups * slots), 1)).astype(f32)
    place[...] = spots.astype(bf16)
    packed_cot[...] = mm((spots * valid).astype(bf16), cot[...], 0, 0).astype(bf16)
    sml.forward()
    met.forward()
    sml.arrive()
    met.arrive()
    tok.forward()
    att.forward()
    cots.start()
    tok.arrive()
    gains = small_all[...].astype(f32).T
    rows_norm(tok_all, gains[0:1, :], normed_out, rows * lanes)
    att.arrive()
    out.start()
    up.start()

    def project(i, carry):
        at = pl.ds(pl.multiple_of(i * Q_TILE, Q_TILE), Q_TILE)
        qkv[at, :] = mm(normed_out[at, :], attend_all[...]).astype(bf16)
        return carry

    lax.fori_loop(0, rows * lanes // Q_TILE, project, 0)
    out.forward()
    doc_cols = [meta_all[l].T[:, 0:1] for l in range(lanes)]
    for tile in range(lanes):
        attend_tile(tile, qkv, doc_cols, mixed, lse, mask, vt)
        swap.send(tile)
        if tile == 0:
            out.arrive()
            outs.start()
        if tile == 1:
            cots.forward()
    outs.forward()
    up.forward()
    down.start()
    outs.arrive()
    swap.arrive()
    attention_out[...] = mm(attn_mixed[...], output_all[...])
    gain = small_all[...].astype(f32).T[1:2, :]
    base = pl.multiple_of(s.l * rows, rows)

    def mid(i, carry):
        at = pl.ds(pl.multiple_of(i * 64, 64), 64)
        normed, _ = norm_stats(tokens[at, :].astype(f32) + attention_out[at, :])
        mix_all[pl.ds(pl.multiple_of(base + i * 64, 64), 64), :] = (normed * gain).astype(bf16)
        return carry

    lax.fori_loop(0, rows // 64, mid, 0)
    mix.start()
    packed_mix[...] = mm(place[...], mix_all[pl.ds(base, rows), :], 0, 0).astype(bf16)
    mix_swap.start()
    down.forward()
    mix.forward()
    for d in range(groups):
        if d:
            mix_swap.got(s.w_peer(groups - d))
        else:
            mix_swap.own().wait()
        mix_spread[d].start()
    for task in mix_spread:
        task.forward()
    mix.arrive()
    for task in mix_spread:
        task.arrive()
    cots.arrive()
    up.arrive()
    down.arrive()
    for task in [tok, met, cots, mix, outs, att, sml, out, up, down, swap, mix_swap] + mix_spread:
        task.sent()


def front(groups, lanes, local, cap, slots, tokens, cot, meta, small, attend_w, output_w, up_w, down_w):
    rows, width = tokens.shape
    X = 1 << ((groups.bit_length() - 1) // 2)
    Y = lanes // 2
    everyone = rows * lanes
    head_cols = width // lanes
    hidden = down_w.shape[0] // lanes * groups
    shard = attend_w.shape[0]
    vmem, anywhere = pl.BlockSpec(memory_space=pltpu.VMEM), pl.BlockSpec(memory_space=pl.ANY)
    dma = pltpu.SemaphoreType.DMA
    of = jax.ShapeDtypeStruct
    sems = []
    for _ in range(5):
        sems += GroupGather.sems(lanes)
    for _ in range(5):
        sems += LaneGather.sems(groups, X)
    sems += GroupSwap.sems(lanes) + LaneSwap.sems(groups)
    outs = [
        (of((everyone, width), bf16), vmem),
        (of((everyone, 3 * head_cols), bf16), vmem),
        (of((head_cols // PAIR, 2, everyone), f32), vmem),
        (of((rows, width), bf16), vmem),
        (of((rows, width), f32), vmem),
        (of((everyone, width), bf16), vmem),
        (of((width, SMALL), bf16), vmem),
        (of((lanes, 8, rows), f32), vmem),
        (of((rows, groups * slots), bf16), vmem),
        (of((width, 3 * head_cols), bf16), vmem),
        (of((width, width), bf16), vmem),
        (of((groups * slots, width), bf16), vmem),
        (of((lanes, groups, slots, width), bf16), anywhere),
        (of((everyone, width), bf16), anywhere),
        (of((width, hidden), bf16), anywhere),
        (of((hidden, width), bf16), anywhere),
    ]
    return pl.pallas_call(
        functools.partial(front_kernel, groups, lanes, local, cap, slots),
        out_shape=[o for o, _ in outs],
        in_specs=[vmem] * 4 + [anywhere] * 4,
        out_specs=[p for _, p in outs],
        scratch_shapes=[
            pltpu.VMEM((everyone, width), bf16),
            pltpu.VMEM((shard, 3 * head_cols), bf16),
            pltpu.VMEM((shard, hidden), bf16),
            pltpu.VMEM((everyone, head_cols), bf16),
            pltpu.VMEM((everyone, Q_TILE), f32),
            pltpu.VMEM((head_cols // PAIR, PAIR, everyone), bf16),
            pltpu.VMEM((groups * slots, width), bf16),
            dma((3 + groups,)),
            dma((groups, Y)),
            dma((groups, Y)),
            dma((groups, lanes)),
        ] + sems,
        compiler_params=pltpu.CompilerParams(collective_id=0, has_side_effects=True, vmem_limit_bytes=56 * 2**20),
        cost_estimate=pl.CostEstimate(flops=8 * 10**9, bytes_accessed=10**8, transcendentals=0),
        name="front",
    )(tokens, cot, meta, small, attend_w, output_w, up_w, down_w)


def add_rows(dst, sources, step=32):
    def body(i, carry):
        at = pl.ds(pl.multiple_of(i * step, step), step)
        total = sources[0][at, :].astype(f32)
        for ref in sources[1:]:
            total += ref[at, :].astype(f32)
        dst[at, :] = total.astype(dst.dtype)
        return carry

    lax.fori_loop(0, dst.shape[0] // step, body, 0)


class GroupScatter:
    def __init__(self, spot, part, held, from_core, from_y, sems, fine):
        self.s, self.part, self.from_core, self.from_y, self.fine = spot, part, from_core, from_y, fine
        self.staged = held is not None
        self.held = (lambda d: held.at[d]) if self.staged else (lambda d: part(spot.y_peer(d)))
        self.stage_sem, self.cs_sem, self.cr_sem, self.ys_sem, self.yr_sem = sems
        self.chunks = from_core.shape[1]

    @staticmethod
    def sems(L, chunks):
        dma = pltpu.SemaphoreType.DMA
        return [dma((L // 2,))] * 3 + [dma((L // 2, chunks))] * 2

    def stage(self, d):
        return pltpu.make_async_copy(self.part(self.s.y_peer(d)), self.held(d), self.stage_sem.at[d])

    def core_copy(self, d):
        s = self.s
        other = lax.rem(s.y + d, s.Y) * 2 + 1 - s.c
        return remote(self.part(other), self.from_core.at[d], self.cs_sem.at[d], self.cr_sem.at[d], s.g, s.core_peer())

    def y_copy(self, d, k):
        s = self.s
        src, dst = self.held(d), self.from_y.at[d - 1]
        if self.fine:
            src, dst = src.at[k], dst.at[k]
        return remote(src, dst, self.ys_sem.at[d, k], self.yr_sem.at[d, k], s.g, s.y_peer(d))

    def start(self):
        for d in range(self.s.Y):
            if self.staged:
                self.stage(d).start()
            self.core_copy(d).start()

    def ready(self):
        for d in range(self.s.Y):
            if self.staged:
                self.stage(d).wait()
            self.core_copy(d).wait_recv()

    def add(self, d, k):
        self.held(d)[k] = (self.held(d)[k].astype(f32) + self.from_core[d, k].astype(f32)).astype(bf16)

    def relay(self, k=0):
        for d in range(1, self.s.Y):
            if self.fine:
                self.add(d, k)
            else:

                def body(i, carry, d=d):
                    self.add(d, i)
                    return carry

                lax.fori_loop(0, self.chunks, body, 0)
            self.y_copy(d, k).start()

    def got(self, k=0):
        for d in range(1, self.s.Y):
            self.y_copy(d, k).wait_recv()

    def total(self, k):
        value = self.held(0)[k].astype(f32) + self.from_core[0, k].astype(f32)
        for d in range(1, self.s.Y):
            value += self.from_y[d - 1, k].astype(f32)
        return value

    def sent(self):
        for d in range(self.s.Y):
            self.core_copy(d).wait_send()
        for d in range(1, self.s.Y):
            for k in range(self.chunks if self.fine else 1):
                self.y_copy(d, k).wait_send()


class LaneScatter:
    def __init__(self, spot, part, held, from_x, from_z, sems):
        self.s, self.part, self.from_x, self.from_z = spot, part, from_x, from_z
        self.staged = held is not None
        self.held = (lambda d: held.at[d]) if self.staged else (lambda d: part(spot.z_peer(d)))
        self.stage_sem, self.xs_sem, self.xr_sem, self.zs_sem, self.zr_sem = sems

    @staticmethod
    def sems(W, X):
        dma = pltpu.SemaphoreType.DMA
        Z = W // X
        return [dma((Z,)), dma((X, Z)), dma((X, Z)), dma((Z,)), dma((Z,))]

    def stage(self, d):
        return pltpu.make_async_copy(self.part(self.s.z_peer(d)), self.held(d), self.stage_sem.at[d])

    def x_copy(self, e, d):
        s = self.s
        return remote(self.part(s.zx_peer(d, e)), self.from_x.at[e - 1, d], self.xs_sem.at[e, d], self.xr_sem.at[e, d],
                      s.x_peer(e), s.l)

    def z_copy(self, d):
        s = self.s
        return remote(self.held(d), self.from_z.at[d - 1], self.zs_sem.at[d], self.zr_sem.at[d], s.z_peer(d), s.l)

    def start(self):
        for d in [*range(1, self.s.Z), 0]:
            if self.staged:
                self.stage(d).start()
            for e in range(1, self.s.X):
                self.x_copy(e, d).start()

    def ready(self, d):
        if self.staged:
            self.stage(d).wait()
        for e in range(1, self.s.X):
            self.x_copy(e, d).wait_recv()

    def relay(self):
        for d in range(1, self.s.Z):
            self.ready(d)
            add_rows(self.held(d), [self.held(d)] + [self.from_x.at[e - 1, d] for e in range(1, self.s.X)])
            self.z_copy(d).start()

    def finish(self, dst):
        self.ready(0)
        for d in range(1, self.s.Z):
            self.z_copy(d).wait_recv()
        add_rows(dst, [self.held(0)] + [self.from_x.at[e - 1, 0] for e in range(1, self.s.X)]
                 + [self.from_z.at[d - 1] for d in range(1, self.s.Z)])

    def fold(self, dst):
        for d in range(self.s.Z):
            self.ready(d)
            add_rows(dst.at[d], [self.held(d)] + [self.from_x.at[e - 1, d] for e in range(1, self.s.X)])

    def x_sent(self):
        for d in range(self.s.Z):
            for e in range(1, self.s.X):
                self.x_copy(e, d).wait_send()

    def sent(self):
        self.x_sent()
        for d in range(1, self.s.Z):
            self.z_copy(d).wait_send()


class ZScatter(LaneScatter):
    def __init__(self, spot, held, from_z, sems):
        self.s, self.held, self.from_z = spot, held, from_z
        self.zs_sem, self.zr_sem = sems

    def start(self):
        for d in range(1, self.s.Z):
            self.z_copy(d).start()

    def finish(self, dst):
        for d in range(1, self.s.Z):
            self.z_copy(d).wait_recv()
        add_rows(dst, [self.held(0)] + [self.from_z.at[d - 1] for d in range(1, self.s.Z)])

    def sent(self):
        for d in range(1, self.s.Z):
            self.z_copy(d).wait_send()


def attend_back_tile(tile, qkv_ref, doc_cols, lse_ref, grad_ref, out_ref, mask_ref, dk_ref, dv_ref):
    cols = grad_ref.shape[1]
    extent = (tile + 1) * Q_TILE
    here, seen = pl.ds(tile * Q_TILE, Q_TILE), pl.ds(0, extent)
    mask_tile(tile, doc_cols, mask_ref)

    def pair_step(pair, carry):
        q_cols = pl.ds(pl.multiple_of(pair * PAIR, PAIR), PAIR)
        k_cols = pl.ds(pl.multiple_of(cols + pair * PAIR, PAIR), PAIR)
        v_cols = pl.ds(pl.multiple_of(2 * cols + pair * PAIR, PAIR), PAIR)
        queries = qkv_ref[here, q_cols] * jnp.asarray(HEAD_DIM**-0.5, bf16)
        keys, values = qkv_ref[seen, k_cols], qkv_ref[seen, v_cols]
        grads = grad_ref[here, q_cols]
        dq = jnp.zeros((PAIR, Q_TILE), f32)
        for half in range(2):
            on = head_mask(half)
            q_one = jnp.where(on, queries, jnp.zeros_like(queries))
            g_one = jnp.where(on, grads, jnp.zeros_like(grads))
            probs = jnp.exp(mm(keys, q_one, 1, 1) + mask_ref[seen, :] - lse_ref[pair, pl.ds(half, 1), here])
            dv_ref[pair, seen, :] += mm(probs.astype(bf16), g_one)
            back = mm(values, g_one, 1, 1)
            low = (probs * (back - jnp.sum(probs * back, axis=0, keepdims=True))).astype(bf16)
            dk_ref[pair, seen, :] += mm(low, q_one)
            got = mm(keys, low, 0, 0)
            sublanes = lax.broadcasted_iota(jnp.int32, (PAIR, 1), 0)
            dq = jnp.where((sublanes // HEAD_DIM) == half, got, dq)
        out_ref[here, q_cols] = (dq.T * HEAD_DIM**-0.5).astype(bf16)
        return carry

    lax.fori_loop(0, cols // PAIR, pair_step, 0)


def take_from(sems):
    sems = list(sems)

    def take(n):
        out = sems[:n]
        del sems[:n]
        return out

    return take


def picked(logits, first, count):
    columns = lax.broadcasted_iota(jnp.int32, logits.shape, 1)
    return soft_max(jnp.where((columns >= first) & (columns < first + count), logits, masked_score))


def middle_kernel(
    groups, lanes, local, cap, experts,
    small, meta_all, place,
    mix_in, cot_in, up_in, down_in, got_mix_in, packed_cot, expert_up, expert_down,
    grad_mix, dense_out, grad_small, mine_up, down_half, tok_part, mix_e_out, grad_e_out, act_e_out, hidden_e_out,
    mix, cot, up, down, act, hidden, got_mix, got_cot, mix_e, grad_e, act_e, hidden_e, expert_in, expert_to,
    mx, mx_c, mx_y, dn, dn_c, dn_y, bk_c, bk_y, gu, gu_x, gu_z, gd, gd_x, ret_back, got_back, dots, coefs,
    load_sem, out_sem, spread_y, spread_c, spread_r, *sems,
):
    s = Spot(groups, lanes)
    everyone, width = mix.shape
    rows = everyone // lanes
    units = up.shape[1]
    slots = got_mix.shape[2]
    shard = width // groups
    rows_e = mix_e.shape[1]
    tile = 256
    step = 64
    take = take_from(sems)

    def blocks(ref, n):
        return lambda i: ref.at[pl.ds(pl.multiple_of(i * n, n), n)]

    def part(i, n=tile):
        return pl.ds(pl.multiple_of(i * n, n), n)

    def load(i, src, dst):
        return pltpu.make_async_copy(src, dst, load_sem.at[i])

    cot_swap = LaneSwap(s, blocks(packed_cot, slots), lambda w: got_cot.at[s.l, w], take(2))
    mxs = GroupScatter(s, lambda l: mx.at[l], None, mx_c, mx_y, take(5), False)
    dns = GroupScatter(s, lambda l: dn.at[l], None, dn_c, dn_y, take(5), False)
    bks = GroupScatter(s, lambda l: got_cot.at[l], None, bk_c, bk_y, take(5), True)
    ups = LaneScatter(s, blocks(gu, shard), None, gu_x, gu_z, take(5))
    dws = LaneScatter(s, blocks(gd, shard), None, gd_x, None, take(5))
    back_swap = LaneSwap(s, blocks(ret_back, slots), blocks(got_back, slots), take(2))
    order = [(d, s.w_peer(d)) for d in [*range(1, groups), 0]]

    def spread(w):
        return GroupGather(s, got_cot.at[s.l, w], lambda l: got_cot.at[l, w],
                           [spread_y.at[w], spread_c.at[w], spread_r.at[w], None], own=False)

    spreads = [(d, s.w_peer(groups - d)) for d in range(groups)]
    loads = [load(i, a, b) for i, (a, b) in enumerate([
        (mix_in, mix), (up_in, up), (cot_in, cot), (down_in, down), (got_mix_in, got_mix),
        (expert_up.at[0], expert_in), (expert_down.at[0], expert_to)])]
    more_loads = [load(7, expert_up.at[1], up), load(8, expert_down.at[1], down)]

    def branch(x, grad, w_in, w_to, act_ref, hidden_ref, count):
        dots[pl.ds(0, count), :] = jnp.zeros((count, SMALL), f32)

        def body(n, carry):
            value, slope = gelu_both(mm(x[...], w_in[:, part(n)]))
            value = value.astype(bf16)
            act_ref[pl.ds(0, count), part(n)] = value
            back = mm(grad[...], w_to[part(n), :], 1, 1)
            hidden_ref[pl.ds(0, count), part(n)] = (slope * back).astype(bf16)
            both = value.astype(f32) * back
            dots[pl.ds(0, count), :] += sum([both[:, i * SMALL : (i + 1) * SMALL] for i in range(1, tile // SMALL)], both[:, :SMALL])
            return carry

        lax.fori_loop(0, units // tile, body, 0)
        return jnp.sum(dots[pl.ds(0, count), :], axis=1, keepdims=True)

    s.greet()
    cot_swap.start()
    for c in loads:
        c.start()
    for c in loads[:4]:
        c.wait()
    columns = lax.broadcasted_iota(jnp.int32, (everyone, SMALL), 1)

    coefs[...] = picked(mm(mix[...], small[...]), 2, 2)
    for l in range(lanes):
        at = pl.ds(l * rows, rows)
        valid = meta_all[l].T[:, 1:2]
        cot[at, :] = (coefs[at, 3:4] * (cot[at, :].astype(f32) * valid)).astype(bf16)
    dot = branch(mix, cot, up, down, act, hidden, everyone)
    sign = jnp.where(columns == 3, 1.0, 0.0) - jnp.where(columns == 2, 1.0, 0.0)
    logits = (sign * (coefs[:, 2:3] * dot)).astype(bf16)
    grad_small[...] = mm(logits, mix[...], 0, 0)

    def up_grad(m, carry):
        gu[part(m), :] = mm(mix[:, part(m)], hidden[...], 0, 0).astype(bf16)
        return carry

    lax.fori_loop(0, width // tile, up_grad, 0)
    ups.start()
    for d, w in spreads:
        if d:
            cot_swap.got(w)
        else:
            cot_swap.own().wait()
        spread(w).start()

    def down_grad(m, carry):
        gd[part(m), :] = mm(act[:, part(m)], cot[...], 0, 0).astype(bf16)
        return carry

    lax.fori_loop(0, units // tile, down_grad, 0)
    dws.start()

    def mix_grad(n, carry):
        value = mm(hidden[...], up[part(n), :], 1, 1) + mm(logits, small[part(n), :], 1, 1)
        mx[:, :, :, part(n)] = value.astype(bf16).reshape(lanes, rows // step, step, tile)
        return carry

    lax.fori_loop(0, width // tile, mix_grad, 0)
    mxs.start()

    def out_part(n, carry):
        value = mm(act[...], down[:, part(n)])
        dn[:, :, :, part(n)] = value.astype(bf16).reshape(lanes, rows // step, step, tile)
        return carry

    lax.fori_loop(0, width // tile, out_part, 0)
    dns.start()
    for c in more_loads:
        c.start()
    for c in loads[4:]:
        c.wait()

    def apart(src, dst):
        def body(j, carry):
            pair = []
            for i in range(2):
                b = 2 * j + i
                pair.append(src[b // groups, b % groups].astype(f32))
            for e in range(local):
                both = [p[e * cap : (e + 1) * cap] for p in pair]
                dst[e, part(j, 2 * cap), :] = jnp.concatenate(both, axis=0).astype(bf16)
            return carry

        lax.fori_loop(0, lanes * groups // 2, body, 0)

    def together(sources, dst):
        def body(j, carry):
            values = [src[part(j, 2 * cap), :].astype(f32) for src in sources]
            for i in range(2):
                b = 2 * j + i
                dst[b // groups, b % groups] = jnp.concatenate([v[i * cap : (i + 1) * cap] for v in values], axis=0).astype(bf16)
            return carry

        lax.fori_loop(0, lanes * groups // 2, body, 0)

    apart(got_mix, mix_e)
    for _, w in spreads:
        spread(w).forward()
    mxs.ready()
    mxs.relay()
    for _, w in spreads:
        spread(w).arrive()
    apart(got_cot, grad_e)

    backs, toks = [act, hidden], [mix, cot]
    columns = lax.broadcasted_iota(jnp.int32, (rows_e, SMALL), 1)
    outs = []
    for e in range(local):
        w_in, w_to = (expert_in, expert_to) if e == 0 else (up, down)
        if e:
            for c in more_loads:
                c.wait()
        x, grad = mix_e.at[e], grad_e.at[e]
        scores = mm(x[...], small[...])
        blend, router = picked(scores, 2, 2), picked(scores, 4, experts)
        own = columns == 4 + s.g * local + e
        chosen = jnp.sum(jnp.where(own, router, 0.0), axis=1, keepdims=True)
        grad[...] = (blend[:, 2:3] * chosen * grad[...].astype(f32)).astype(bf16)
        shares = jnp.where(own, 1.0, 0.0) - router
        shares += blend[:, 3:4] * (jnp.where(columns == 2, 1.0, 0.0) - jnp.where(columns == 3, 1.0, 0.0))
        coefs[pl.ds(0, rows_e), :] = shares
        dot = branch(x, grad, w_in, w_to, act_e.at[e], hidden_e.at[e], rows_e)
        logits = (dot * coefs[pl.ds(0, rows_e), :]).astype(bf16)
        grad_small[...] += mm(logits, x[...], 0, 0)
        if e == 0:
            ups.relay()

        def rows_back(n, carry, e=e, w_in=w_in, logits=logits):
            value = mm(hidden_e[e], w_in[part(n), :], 1, 1) + mm(logits, small[part(n), :], 1, 1)
            backs[e][pl.ds(0, rows_e), part(n)] = value.astype(bf16)
            return carry

        lax.fori_loop(0, width // tile, rows_back, 0)
        if e == 0:
            dns.ready()
            dns.relay()
        if e == local - 1:
            for _, w in spreads:
                spread(w).sent()
            together([b.at[pl.ds(0, rows_e)] for b in backs], got_cot)
            bks.start()

        def rows_out(n, carry, e=e, w_to=w_to):
            toks[e][pl.ds(0, rows_e), part(n)] = mm(act_e[e], w_to[:, part(n)]).astype(bf16)
            return carry

        lax.fori_loop(0, width // tile, rows_out, 0)
        if e == local - 1:
            bks.ready()
            for _, w in order:
                bks.relay(w)
        for i, (a, b) in enumerate([(mix_e, mix_e_out), (grad_e, grad_e_out), (act_e, act_e_out), (hidden_e, hidden_e_out)]):
            outs.append(pltpu.make_async_copy(a.at[e], b.at[e], out_sem.at[4 * e + i]))
            outs[-1].start()
    together([t.at[pl.ds(0, rows_e)] for t in toks], got_mix)
    outs.append(pltpu.make_async_copy(got_mix, tok_part, out_sem.at[4 * local]))
    outs[-1].start()

    def totals(scatter, dst):
        scatter.got()

        def body(k, carry):
            dst[pl.ds(pl.multiple_of(k * step, step), step), :] = scatter.total(k).astype(dst.dtype)
            return carry

        lax.fori_loop(0, scatter.chunks, body, 0)

    totals(mxs, grad_mix)
    for d, w in order:
        bks.got(w)
        ret_back[pl.ds(pl.multiple_of(w * slots, slots), slots), :] = bks.total(w).astype(bf16)
        if d:
            back_swap.copy(d).start()
        else:
            back_swap.own().start()
    dws.fold(down_half)
    totals(dns, dense_out)
    ups.finish(mine_up)
    back_swap.arrive()
    grad_mix[...] += mm(place[...], got_back[...])
    for c in outs:
        c.wait()
    dws.x_sent()
    for task in [cot_swap, mxs, dns, bks, ups, back_swap]:
        task.sent()


def middle(groups, lanes, local, cap, experts, slots, inputs, placed):
    rows, width = inputs[2].shape[0], inputs[0].shape[0]
    X = 1 << ((groups.bit_length() - 1) // 2)
    Y, Z = lanes // 2, groups // X
    everyone = rows * lanes
    shard = width // groups
    units = placed[2].shape[1]
    rows_e = lanes * groups * cap
    vmem, anywhere = pl.BlockSpec(memory_space=pltpu.VMEM), pl.BlockSpec(memory_space=pl.ANY)
    dma = pltpu.SemaphoreType.DMA
    of = jax.ShapeDtypeStruct
    low = lambda *shape: pltpu.VMEM(shape, bf16)
    wide = lambda *shape: pltpu.VMEM(shape, f32)
    expert_rows = (local, rows_e, width)
    outs = [
        (of((rows, width), f32), vmem),
        (of((rows, width), bf16), vmem),
        (of((SMALL, width), f32), vmem),
        (of((shard, units), bf16), vmem),
        (of((Z, shard, width), bf16), vmem),
        (of((lanes, groups, slots, width), bf16), anywhere),
        (of(expert_rows, bf16), anywhere),
        (of(expert_rows, bf16), anywhere),
        (of((local, rows_e, units), bf16), anywhere),
        (of((local, rows_e, units), bf16), anywhere),
    ]
    scratch = [low(everyone, width), low(everyone, width), low(width, units), low(units, width)]
    scratch += [low(everyone, units), low(everyone, units)]
    scratch += [low(lanes, groups, slots, width)] * 2
    scratch += [low(*expert_rows), low(*expert_rows), low(local, rows_e, units), low(local, rows_e, units)]
    scratch += [low(width, units), low(units, width)]
    scratch += [low(lanes, rows // 64, 64, width), low(Y, rows // 64, 64, width), low(Y - 1, rows // 64, 64, width)] * 2
    scratch += [low(Y, groups, slots, width), low(Y - 1, groups, slots, width)]
    scratch += [low(width, units), low(X - 1, Z, shard, units), low(Z - 1, shard, units)]
    scratch += [low(units, width), low(X - 1, Z, shard, width)]
    scratch += [low(groups * slots, width)] * 2 + [wide(everyone, SMALL)] * 2
    scratch += [dma((9,)), dma((4 * local + 1,)), dma((groups, Y)), dma((groups, Y)), dma((groups, lanes))]
    scratch += LaneSwap.sems(groups) + GroupScatter.sems(lanes, 1) * 2 + GroupScatter.sems(lanes, groups)
    scratch += LaneScatter.sems(groups, X) * 2 + LaneSwap.sems(groups)
    return pl.pallas_call(
        functools.partial(middle_kernel, groups, lanes, local, cap, experts),
        out_shape=[o for o, _ in outs],
        in_specs=[vmem] * len(inputs) + [anywhere] * len(placed),
        out_specs=[p for _, p in outs],
        scratch_shapes=scratch,
        compiler_params=pltpu.CompilerParams(collective_id=2, has_side_effects=True, vmem_limit_bytes=62 * 2**20),
        cost_estimate=pl.CostEstimate(flops=35 * 10**9, bytes_accessed=10**8, transcendentals=0),
        name="middle",
    )(*inputs, *placed)


def back_kernel(
    groups, lanes, experts,
    tokens, cot, meta, small, attention_out, attn_mixed, place, meta_all, lse, grad_small, grad_mix_in, dense_out,
    mine_up, down_half, tok_part, qkv_in, output_in, attend_in, normed_in,
    layer_out, grad_tokens, small_out, all_attend, all_output, all_up, all_down,
    qkv, output_all, attend_all, normed, tk_h, tk_c, tk_y,
    go, go_c, go_y, gn, gn_c, gn_y, dw_z, ga, ga_x, ga_z, gl, gl_x, gl_z,
    sm, sm_x, sm_z, sm_mine, sm_all, ret_tok, got_tok, grad_mix, grad_mid, grad_attn, grad_mixed,
    grad_heads, grad_qkv, mask, dk, dv, valid_cols, mine_attend, mine_output, mine_down, stage_sem, *sems,
):
    s = Spot(groups, lanes)
    rows, width = tokens.shape
    head_cols = width // lanes
    slots = place.shape[1] // groups
    shard = width // groups
    take = take_from(sems)
    step = 64

    def blocks(ref, n):
        return lambda i: ref.at[pl.ds(pl.multiple_of(i * n, n), n)]

    def cols(i):
        return pl.ds(pl.multiple_of(i * head_cols, head_cols), head_cols)

    loads = [
        pltpu.make_async_copy(src, dst, stage_sem.at[i])
        for i, (src, dst) in enumerate(
            [(output_in, output_all), (qkv_in, qkv), (attend_in, attend_all), (normed_in, normed)])
    ]
    tk = GroupScatter(s, lambda l: tok_part.at[l], tk_h, tk_c, tk_y, take(5), True)
    gos = GroupScatter(s, lambda l: go.at[l], None, go_c, go_y, take(5), False)
    gns = GroupScatter(s, lambda l: gn.at[l], None, gn_c, gn_y, take(5), False)
    dws = ZScatter(s, lambda d: down_half.at[d], dw_z, take(2))
    gas = LaneScatter(s, blocks(ga, shard), None, ga_x, ga_z, take(5))
    gls = LaneScatter(s, blocks(gl, shard), None, gl_x, gl_z, take(5))
    sms = LaneScatter(s, lambda w: sm.at[w], None, sm_x, sm_z, take(5))
    tok_swap = LaneSwap(s, blocks(ret_tok, slots), blocks(got_tok, slots), take(2))
    heads = GroupSwap(s, lambda l: grad_mixed.at[:, cols(l)], blocks(grad_heads, rows), take(2))
    f_attend = GroupGather(s, mine_attend, lambda l: all_attend.at[l], take(4))
    f_output = GroupGather(s, mine_output, lambda l: all_output.at[l], take(4))
    f_up = GroupGather(s, mine_up, lambda l: all_up.at[l], take(4))
    f_down = GroupGather(s, mine_down, lambda l: all_down.at[l], take(4))
    f_small = GroupGather(s, sm_mine, lambda l: sm_all.at[l], take(4))
    order = [(d, s.w_peer(d)) for d in [*range(1, groups), 0]]

    def pass_on(scatter):
        for _, w in order:
            scatter.relay(w)

    def hand_back(scatter, swap, ret):
        for d, w in order:
            scatter.got(w)
            ret[pl.ds(pl.multiple_of(w * slots, slots), slots), :] = scatter.total(w).astype(bf16)
            if d:
                swap.copy(d).start()
            else:
                swap.own().start()

    def totals(scatter, dst):
        scatter.got()

        def body(k, carry):
            dst[pl.ds(pl.multiple_of(k * step, step), step), :] = scatter.total(k).astype(dst.dtype)
            return carry

        lax.fori_loop(0, scatter.chunks, body, 0)

    def over_rows(body, init):
        return lax.fori_loop(0, rows // step, lambda i, c: body(pl.ds(pl.multiple_of(i * step, step), step), c), init)

    s.greet()
    tk.start()
    dws.start()
    f_up.start()
    for c in loads:
        c.start()
    dk[...] = jnp.zeros_like(dk)
    dv[...] = jnp.zeros_like(dv)
    gains = small[...].astype(f32).T
    mine = meta[...].T
    valid_cols[...] = jnp.broadcast_to(mine[:, 1:2], valid_cols.shape)

    def mid(at, gain_sum):
        normed_v, scale = norm_stats(tokens[at, :].astype(f32) + attention_out[at, :])
        grad = grad_mix_in[at, :]
        value = cot[at, :].astype(f32) * valid_cols[at, 0:1] + norm_back(normed_v, scale, gains[1:2, :], grad)
        grad_mid[at, :] = value
        grad_attn[at, :] = value.astype(bf16)
        return gain_sum + jnp.sum(grad * normed_v, axis=0, keepdims=True)

    mixer_gain_grad = over_rows(mid, jnp.zeros((1, width), f32))
    loads[0].wait()
    grad_mixed[...] = mm(grad_attn[...], output_all[...], 1, 1).astype(bf16)
    for l in range(lanes):
        heads.send(l)

    def out_grad(m, carry):
        value = mm(attn_mixed[:, cols(m)], grad_attn[...], 0, 0).astype(bf16)
        parts = head_cols // step
        for l in range(lanes):
            go[l, pl.ds(m * parts, parts)] = value[:, l * head_cols : (l + 1) * head_cols].reshape(parts, step, head_cols)
        return carry

    lax.fori_loop(0, lanes, out_grad, 0)
    gos.start()
    tk.ready()
    for c in loads[1:]:
        c.wait()
    heads.arrive()
    doc_cols = [meta_all[l].T[:, 0:1] for l in range(lanes)]
    for tile in range(lanes):
        attend_back_tile(tile, qkv, doc_cols, lse, grad_heads, grad_qkv, mask, dk, dv)
        if tile == 0:
            pass_on(tk)
        if tile == 1:
            gos.ready()
            gos.relay()
        if tile == 2:
            f_up.forward()
    for pair in range(head_cols // PAIR):
        grad_qkv[:, head_cols + pair * PAIR : head_cols + (pair + 1) * PAIR] = dk[pair].astype(bf16)
        grad_qkv[:, 2 * head_cols + pair * PAIR : 2 * head_cols + (pair + 1) * PAIR] = dv[pair].astype(bf16)

    def weight_grad(m, carry):
        ga[pl.ds(pl.multiple_of(m * head_cols, head_cols), head_cols), :] = mm(normed[:, cols(m)], grad_qkv[...], 0, 0).astype(bf16)
        return carry

    lax.fori_loop(0, lanes, weight_grad, 0)
    gas.start()

    def rows_grad(l, carry):
        value = mm(grad_qkv[pl.ds(pl.multiple_of(l * rows, rows), rows), :], attend_all[...], 1, 1)
        gn[l] = value.astype(bf16).reshape(rows // step, step, width)
        return carry

    lax.fori_loop(0, lanes, rows_grad, 0)
    gns.start()
    hand_back(tk, tok_swap, ret_tok)
    gns.ready()
    gns.relay()
    totals(gos, gl)
    gls.start()
    gas.relay()
    tok_swap.arrive()
    gls.relay()

    def layer(at, sums):
        attention = attention_out[at, :]
        residual = tokens[at, :].astype(f32) + attention
        normed_v, _ = norm_stats(residual)
        mix = (normed_v * gains[1:2, :]).astype(bf16)
        logits = mm(mix, small[...])
        blend, router = picked(logits, 2, 2), picked(logits, 4, experts)
        columns = lax.broadcasted_iota(jnp.int32, logits.shape, 1)
        route = valid_cols[at, 1:2].astype(jnp.int32)
        chosen = jnp.sum(jnp.where(columns == 4 + route, router, 0.0), axis=1, keepdims=True)
        ffn = blend[:, 2:3] * chosen * mm(place[at, :], got_tok[...]) + blend[:, 3:4] * dense_out[at, :].astype(f32)
        full = residual + ffn
        layer_out[at, :] = full.astype(bf16)
        valid = valid_cols[at, 0:1]
        got = [jnp.sum(valid * v * v, axis=(0, 1), keepdims=True) for v in (residual, full, attention, ffn)]
        got.append(jnp.sum(valid, axis=(0, 1), keepdims=True))
        return tuple(a + b for a, b in zip(sums, got))

    lane_of = lax.broadcasted_iota(jnp.int32, valid_cols.shape, 1)
    valid_cols[...] = jnp.where(lane_of == 1, mine[:, 2:3], mine[:, 1:2])
    sums = over_rows(layer, tuple(jnp.zeros((1, 1), f32) for _ in range(5)))
    totals(gns, grad_mix)

    def first(at, gain_sum):
        normed_v, scale = norm_stats(tokens[at, :].astype(f32))
        grad = grad_mix[at, :]
        grad_tokens[at, :] = (grad_mid[at, :] + norm_back(normed_v, scale, gains[0:1, :], grad)).astype(bf16)
        return gain_sum + jnp.sum(grad * normed_v, axis=0, keepdims=True)

    attend_gain_grad = over_rows(first, jnp.zeros((1, width), f32))
    feature = lax.broadcasted_iota(jnp.int32, (SMALL, shard), 0)
    place_of = lax.broadcasted_iota(jnp.int32, (SMALL, shard), 1)
    tail = jnp.zeros((SMALL, shard), f32)
    for i, v in enumerate(sums):
        tail = jnp.where(place_of == i, v, tail)
    for w in range(groups):
        here = slice(w * shard, (w + 1) * shard)
        value = jnp.where(feature == SMALL - 1, tail, grad_small[:, here])
        value = jnp.where(feature == 0, attend_gain_grad[:, here], value)
        sm[w] = jnp.where(feature == 1, mixer_gain_grad[:, here], value)
    sms.start()
    dws.finish(mine_down)
    f_down.start()
    sms.relay()
    gas.finish(mine_attend)
    f_attend.start()
    gls.finish(mine_output)
    f_output.start()
    sms.finish(sm_mine)
    f_small.start()
    gathers = [f_up, f_down, f_attend, f_output, f_small]
    for task in gathers[1:]:
        task.forward()
    for task in gathers:
        task.arrive()
    small_out[...] = sum([sm_all[l] for l in range(1, lanes)], sm_all[0])
    for task in [tk, gos, gns, dws, gas, gls, sms, tok_swap, heads] + gathers:
        task.sent()


def back(groups, lanes, experts, slots, inputs, placed):
    tokens = inputs[0]
    rows, width = tokens.shape
    X = 1 << ((groups.bit_length() - 1) // 2)
    Y, Z = lanes // 2, groups // X
    everyone = rows * lanes
    head_cols = width // lanes
    shard = width // groups
    hidden = inputs[-2].shape[1]
    vmem, anywhere = pl.BlockSpec(memory_space=pltpu.VMEM), pl.BlockSpec(memory_space=pl.ANY)
    dma = pltpu.SemaphoreType.DMA
    of = jax.ShapeDtypeStruct
    pairs = head_cols // PAIR
    low = lambda *shape: pltpu.VMEM(shape, bf16)
    wide = lambda *shape: pltpu.VMEM(shape, f32)

    def group_bufs(c, r, n, held=True):
        return ([low(Y, c, r, n)] if held else [low(lanes, c, r, n)]) + [low(Y, c, r, n), low(Y - 1, c, r, n)]

    def lane_bufs(n, held=True):
        return ([low(Z, shard, n)] if held else [low(width, n)]) + [low(X - 1, Z, shard, n), low(Z - 1, shard, n)]

    scratch = [low(everyone, 3 * head_cols), low(width, width), low(width, 3 * head_cols), low(everyone, width)]
    scratch += group_bufs(groups, slots, width)
    scratch += group_bufs(width // 64, 64, head_cols, False) + group_bufs(rows // 64, 64, width, False)
    scratch += [low(Z - 1, shard, width)] + lane_bufs(3 * head_cols, False) + lane_bufs(head_cols, False)
    scratch += [wide(groups, SMALL, shard), wide(X - 1, Z, SMALL, shard), wide(Z - 1, SMALL, shard)]
    scratch += [wide(SMALL, shard), wide(lanes, SMALL, shard)]
    scratch += [low(groups * slots, width)] * 2
    scratch += [wide(rows, width), wide(rows, width), low(rows, width), low(rows, width)]
    scratch += [low(everyone, head_cols), low(everyone, 3 * head_cols), wide(everyone, Q_TILE)]
    scratch += [wide(pairs, everyone, PAIR)] * 2 + [wide(rows, SMALL)]
    scratch += [low(shard, 3 * head_cols), low(shard, head_cols), low(shard, width)]
    scratch += [dma((4,))]
    scratch += GroupScatter.sems(lanes, groups) + GroupScatter.sems(lanes, 1) * 2
    scratch += [dma((Z,))] * 2 + LaneScatter.sems(groups, X) * 3
    scratch += LaneSwap.sems(groups) + GroupSwap.sems(lanes)
    scratch += GroupGather.sems(lanes) * 5
    outs = [
        (of((rows, width), bf16), vmem),
        (of((rows, width), bf16), vmem),
        (of((SMALL, shard), f32), vmem),
        (of((lanes, shard, 3 * head_cols), bf16), anywhere),
        (of((lanes, shard, head_cols), bf16), anywhere),
        (of((lanes, shard, hidden), bf16), anywhere),
        (of((lanes, shard, width), bf16), anywhere),
    ]
    return pl.pallas_call(
        functools.partial(back_kernel, groups, lanes, experts),
        out_shape=[o for o, _ in outs],
        in_specs=[vmem] * len(inputs) + [anywhere] * len(placed),
        out_specs=[p for _, p in outs],
        scratch_shapes=scratch,
        compiler_params=pltpu.CompilerParams(collective_id=1, has_side_effects=True, vmem_limit_bytes=62 * 2**20),
        cost_estimate=pl.CostEstimate(flops=8 * 10**9, bytes_accessed=10**8, transcendentals=0),
        name="back",
    )(*inputs, *placed)


def lane_gather(part):
    return lax.all_gather(part, "wide", axis=0, tiled=True)


def lane_scatter(part):
    return lax.psum_scatter(part.astype(bf16), "wide", scatter_dimension=0, tiled=True)


def group_gather(part, axis=0):
    return lax.all_gather(part, "narrow", axis=axis, tiled=True)


def group_scatter(part, axis=0):
    return lax.psum_scatter(part.astype(bf16), "narrow", scatter_dimension=axis, tiled=True)


def lane_swap(part):
    return lax.all_to_all(part, "wide", split_axis=0, concat_axis=0, tiled=True)


def per_device(
    tokens, doc_ids, valid_mask, routes, cotangent, attend_gain, attend_weight, output_weight, mixer_gain,
    router_weight, blend_weight, up_weight, down_weight, expert_up, expert_down,
):
    rows, width = tokens.shape
    groups, lanes = lax.axis_size("wide"), lax.axis_size("narrow")
    group, lane = lax.axis_index("wide"), lax.axis_index("narrow")
    shard = attend_gain.shape[0]
    local = expert_up.shape[0]
    experts = local * groups
    hidden = up_weight.shape[1]
    fine = hidden // groups // lanes
    cap = max(2, (3 * rows + 2 * experts - 1) // (2 * experts))
    slots = -(-local * cap // 16) * 16
    all_rows = rows * lanes

    small = jnp.concatenate(
        [attend_gain[:, None], mixer_gain[:, None], blend_weight, router_weight,
         jnp.zeros((shard, SMALL - 4 - experts), bf16)], axis=1)
    meta_in = jnp.stack([doc_ids, valid_mask, routes[:, 0]]).astype(f32)
    meta_in = jnp.pad(meta_in, ((0, 5), (0, 0)))
    up_mine = up_weight
    if fine % 128:
        up_mine = lax.dynamic_index_in_dim(up_weight.reshape(shard, groups, lanes, fine), lane, 2, keepdims=False)
        up_mine = up_mine.reshape(shard, groups * fine)
    (
        normed_attend, qkv, lse, attn_mixed, attention_out, mix_all, small, meta_all, place,
        attend_full, output_full, packed_cot, got_mix, cot_all, up_full, down_full,
    ) = front(groups, lanes, local, cap, slots, tokens, cotangent, meta_in, small, attend_weight, output_weight, up_mine, down_weight)
    doc_col = meta_all[:, 0].reshape(all_rows, 1)
    valid_all = meta_all[:, 1].reshape(all_rows, 1)
    attend_gain_row = small[:, 0].astype(f32)
    mixer_gain_row = small[:, 1].astype(f32)
    mix_cols = jnp.where((jnp.arange(SMALL) < 2)[None, :], 0, small)
    residual_mid = tokens.astype(f32) + attention_out
    mid_normed, mid_scale = norm_stats(residual_mid)
    normed_mix = (mid_normed * mixer_gain_row).astype(bf16)
    route = routes[:, 0]

    def give_back(partial):
        return mm(place, lane_swap(group_scatter(partial)))

    valid = valid_mask.astype(f32)[:, None]
    grad_layer = cotangent.astype(f32) * valid

    def widen(gathered, parts):
        full = gathered.reshape(lanes, shard, parts, -1)
        return full.transpose(1, 2, 0, 3).reshape(shard, -1).astype(f32)

    if all_rows * width <= 2**20 and shard % 128 == 0 and cap % 8 == 0 and slots == local * cap and local == 2 and lanes * groups * cap <= all_rows:
        grad_mix, dense_out, grad_small, mine_up, down_half, tok_part, mix_e, grad_e, act_e, hidden_e = middle(
            groups, lanes, local, cap, experts, slots, (small, meta_all, place),
            (mix_all, cot_all, up_full, down_full, got_mix, packed_cot, expert_up, expert_down))
        layer_out, grad_tokens, small_out, out_attend, out_output, out_up, out_down = back(
            groups, lanes, experts, slots,
            (tokens, cotangent, meta_in, small, attention_out, attn_mixed, place, meta_all, lse, grad_small, grad_mix,
             dense_out, mine_up, down_half),
            (tok_part, qkv, output_full, attend_full, normed_attend))
        grad_expert_up = jnp.einsum("etd,etf->edf", mix_e, hidden_e, preferred_element_type=f32)
        grad_expert_down = jnp.einsum("etf,etd->efd", act_e, grad_e, preferred_element_type=f32)
        sums, small_out = small_out[SMALL - 1], small_out.T
        root_means = jnp.sqrt(sums[:4] / (jnp.maximum(sums[4], 1.0) * width))
        return (
            layer_out, grad_tokens, small_out[:, 0], widen(out_attend, 3), widen(out_output, 1), small_out[:, 1],
            small_out[:, 4 : 4 + experts], small_out[:, 2:4], widen(out_up, groups),
            out_down.reshape(-1, width).astype(f32), grad_expert_up, grad_expert_down, root_means,
        )

    got_cot = group_gather(lane_swap(packed_cot.reshape(groups, slots, width))[None])

    def coefficients(mix_rows):
        logits = mm(mix_rows, mix_cols)
        columns = jnp.arange(SMALL)[None, :]
        blend = soft_max(jnp.where((columns >= 2) & (columns < 4), logits, masked_score))
        router = soft_max(jnp.where((columns >= 4) & (columns < 4 + experts), logits, masked_score))
        return columns, blend, router

    columns, blend, _ = coefficients(mix_all)
    blend_0, blend_1 = blend[:, 2:3], blend[:, 3:4]
    grad_dense = (blend_1 * (cot_all.astype(f32) * valid_all.astype(f32))).astype(bf16)
    up_act, up_slope = gelu_both(mm(mix_all, up_full))
    up_act = up_act.astype(bf16)
    dense_part = mm(up_act, down_full)
    grad_up_act = mm(grad_dense, down_full, 1, 1)
    dense_dot = jnp.sum(up_act.astype(f32) * grad_up_act, axis=1, keepdims=True)
    grad_up_pre = (up_slope * grad_up_act).astype(bf16)
    dense_logits = (jnp.where(columns == 3, 1.0, 0.0) - jnp.where(columns == 2, 1.0, 0.0)) * (blend_0 * dense_dot)
    grad_mix_part = mm(grad_up_pre, up_full, 1, 1) + mm(dense_logits.astype(bf16), mix_cols, 1, 1)
    grad_small = mm(dense_logits.astype(bf16), mix_all, 0, 0)
    grad_up = mm(mix_all, grad_up_pre, 0, 0)
    grad_down = mm(up_act, grad_dense, 0, 0)

    def by_expert(received):
        split = received.reshape(lanes * groups, slots, width)[:, : local * cap]
        return split.reshape(lanes * groups, local, cap, width).transpose(1, 0, 2, 3).reshape(local, -1, width)

    def by_slot(values):
        split = values.reshape(local, lanes * groups, cap, width).transpose(1, 0, 2, 3)
        split = split.reshape(lanes * groups, local * cap, width)
        return jnp.pad(split, ((0, 0), (0, slots - local * cap), (0, 0))).reshape(-1, width)

    mix_e, cot_e = by_expert(got_mix), by_expert(got_cot)
    tok_parts, back_parts, up_grads, down_grads = [], [], [], []
    for e in range(local):
        _, blend, router = coefficients(mix_e[e])
        own = columns == 4 + group * local + e
        chosen = jnp.sum(jnp.where(own, router, 0.0), axis=1, keepdims=True)
        scale = blend[:, 2:3] * chosen
        grad_tok = (scale * cot_e[e].astype(f32)).astype(bf16)
        act, slope = gelu_both(mm(mix_e[e], expert_up[e]))
        act = act.astype(bf16)
        tok_parts.append((mm(act, expert_down[e])))
        grad_act = mm(grad_tok, expert_down[e], 1, 1)
        dot = jnp.sum(act.astype(f32) * grad_act, axis=1, keepdims=True)
        grad_hidden = (slope * grad_act).astype(bf16)
        logits = dot * (jnp.where(own, 1.0, 0.0) - router)
        logits += dot * blend[:, 3:4] * (jnp.where(columns == 2, 1.0, 0.0) - jnp.where(columns == 3, 1.0, 0.0))
        logits = logits.astype(bf16)
        back_parts.append(mm(grad_hidden, expert_up[e], 1, 1) + mm(logits, mix_cols, 1, 1))
        grad_small += mm(logits, mix_e[e], 0, 0)
        down_grads.append(mm(act, grad_tok, 0, 0))
        up_grads.append(mm(mix_e[e], grad_hidden, 0, 0))
    grad_expert_up, grad_expert_down = jnp.stack(up_grads), jnp.stack(down_grads)
    grad_small = grad_small.T
    expert_back = give_back(by_slot(jnp.stack(back_parts)))
    expert_tok = give_back(by_slot(jnp.stack(tok_parts)))

    dense_out = group_scatter(dense_part).astype(f32)
    _, blend, router = coefficients(normed_mix)
    own = columns == 4 + route[:, None]
    chosen = jnp.sum(jnp.where(own, router, 0.0), axis=1, keepdims=True)
    ffn_out = blend[:, 2:3] * chosen * expert_tok + blend[:, 3:4] * dense_out
    layer_full = residual_mid + ffn_out
    sums = jnp.stack(
        [jnp.sum(valid * v * v) for v in (residual_mid, layer_full, attention_out, ffn_out)] + [jnp.sum(valid)])

    grad_mix = group_scatter(grad_mix_part).astype(f32) + expert_back
    grad_mid = grad_layer + norm_back(mid_normed, mid_scale, mixer_gain_row, grad_mix)
    mixer_gain_grad = jnp.sum(grad_mix * mid_normed, axis=0)
    grad_attn = grad_mid.astype(bf16)
    grad_output = mm(attn_mixed, grad_attn, 0, 0)
    grad_mixed = mm(grad_attn, output_full, 1, 1).astype(bf16)
    grad_heads = lax.all_to_all(grad_mixed, "narrow", split_axis=1, concat_axis=0, tiled=True)
    grad_qkv = attend_back(qkv, doc_col, lse, grad_heads)
    grad_attend = mm(normed_attend, grad_qkv, 0, 0)
    grad_normed = group_scatter(mm(grad_qkv, attend_full, 1, 1)).astype(f32)
    in_normed, in_scale = norm_stats(tokens.astype(f32))
    grad_tokens = (grad_mid + norm_back(in_normed, in_scale, attend_gain_row, grad_normed)).astype(bf16)
    attend_gain_grad = jnp.sum(grad_normed * in_normed, axis=0)

    grad_small = jnp.where(columns == 0, attend_gain_grad[:, None], jnp.where(columns == 1, mixer_gain_grad[:, None], grad_small))
    small_out = lax.psum(lax.psum_scatter(grad_small, "wide", scatter_dimension=0, tiled=True), "narrow")
    sums = lax.psum(sums, ("wide", "narrow"))
    root_means = jnp.sqrt(sums[:4] / (jnp.maximum(sums[4], 1.0) * width))

    def share(part):
        return group_gather(part.astype(bf16)[None])

    out_attend = widen(share(lane_scatter(grad_attend)), 3)
    out_output = widen(share(lane_scatter(group_scatter(grad_output, axis=1))), 1)
    out_up = widen(share(lane_scatter(grad_up)), groups)
    out_down = group_gather(lane_scatter(grad_down).astype(bf16)).astype(f32)
    return (
        layer_full.astype(bf16), grad_tokens, small_out[:, 0], out_attend, out_output, small_out[:, 1],
        small_out[:, 4 : 4 + experts], small_out[:, 2:4], out_up, out_down, grad_expert_up, grad_expert_down, root_means,
    )


def solution(mesh):
    both = ("wide", "narrow")
    row, vec, mat = P(both, None), P("wide"), P("wide", None)
    up, down = P("wide", None, "narrow"), P("wide", "narrow", None)
    return jax.shard_map(
        per_device,
        mesh=mesh,
        in_specs=(row, P(both), P(both), row, row, vec, mat, mat, vec, mat, mat, mat, mat, up, down),
        out_specs=(row, row, vec, mat, mat, vec, mat, mat, mat, mat, up, down, P()),
        check_vma=False,
    )
```

```python
import functools

import jax
import jax.numpy as jnp
from jax import lax
from jax.experimental import pallas as pl
from jax.experimental.pallas import tpu as pltpu
from jax.sharding import PartitionSpec as P

HEAD_DIM = 64
PAIR = 2 * HEAD_DIM
Q_TILE = 256
SMALL = 128
eps_norm = 1e-05
masked_score = -1e30
f32 = jnp.float32
bf16 = jnp.bfloat16


def mm(a, b, ca=1, cb=0):
    return lax.dot_general(a, b, (((ca,), (cb,)), ((), ())), preferred_element_type=f32)


def norm_stats(values):
    center = values - jnp.mean(values, axis=-1, keepdims=True)
    scale = lax.rsqrt(jnp.mean(center * center, axis=-1, keepdims=True) + eps_norm)
    return center * scale, scale


def norm_back(normed, scale, gain, grad):
    u = grad * gain
    return scale * (
        u
        - jnp.mean(u, axis=-1, keepdims=True)
        - normed * jnp.mean(u * normed, axis=-1, keepdims=True)
    )


GELU_A = 0.7978845608028654
GELU_B = 0.044715


def gelu(v):
    return 0.5 * v * (1.0 + jnp.tanh(GELU_A * (v + GELU_B * v * v * v)))


def gelu_both(v):
    t = jnp.tanh(GELU_A * (v + GELU_B * v * v * v))
    value = 0.5 * v * (1.0 + t)
    slope = 0.5 * (1.0 + t) + 0.5 * v * (1.0 - t * t) * (GELU_A * (1.0 + 3.0 * GELU_B * v * v))
    return value, slope


def soft_max(logits):
    shifted = jnp.exp(logits - jnp.max(logits, axis=-1, keepdims=True))
    return shifted / jnp.sum(shifted, axis=-1, keepdims=True)


def head_mask(half):
    lanes = lax.broadcasted_iota(jnp.int32, (1, PAIR), 1)
    return (lanes // HEAD_DIM) == half


def attend_tile(tile, qkv_ref, doc_cols, out_ref, lse_ref, mask_ref, vt_ref):
    cols = out_ref.shape[1]
    extent = (tile + 1) * Q_TILE
    here, seen = pl.ds(tile * Q_TILE, Q_TILE), pl.ds(0, extent)
    mask_tile(tile, doc_cols, mask_ref)

    def pair_step(pair, carry):
        q_cols = pl.ds(pl.multiple_of(pair * PAIR, PAIR), PAIR)
        k_cols = pl.ds(pl.multiple_of(cols + pair * PAIR, PAIR), PAIR)
        v_cols = pl.ds(pl.multiple_of(2 * cols + pair * PAIR, PAIR), PAIR)
        if tile == 0:
            vt_ref[pair] = qkv_ref[:, v_cols].T
        queries = qkv_ref[here, q_cols] * jnp.asarray(HEAD_DIM**-0.5, bf16)
        mixed = jnp.zeros((PAIR, Q_TILE), f32)
        for half in range(2):
            one = jnp.where(head_mask(half), queries, jnp.zeros_like(queries))
            scores = mm(qkv_ref[seen, k_cols], one, 1, 1) + mask_ref[seen, :]
            top = jnp.max(scores, axis=0, keepdims=True)
            shifted = jnp.exp(scores - top)
            total = jnp.sum(shifted, axis=0, keepdims=True)
            low = (shifted * (1.0 / total)).astype(bf16)
            lse_ref[pair, pl.ds(half, 1), here] = top + jnp.log(total)
            got = mm(vt_ref[pair, :, seen], low)
            sublanes = lax.broadcasted_iota(jnp.int32, (PAIR, 1), 0)
            mixed = jnp.where((sublanes // HEAD_DIM) == half, got, mixed)
        out_ref[here, q_cols] = mixed.T.astype(bf16)
        return carry

    lax.fori_loop(0, cols // PAIR, pair_step, 0)


def mask_tile(tile, doc_cols, mask_ref):
    row = (tile * Q_TILE + lax.broadcasted_iota(jnp.int32, (Q_TILE, Q_TILE), 1)).astype(f32)
    for block in range(tile + 1):
        allowed = doc_cols[block] >= row
        if block == tile:
            key = (tile * Q_TILE + lax.broadcasted_iota(jnp.int32, (Q_TILE, Q_TILE), 0)).astype(f32)
            allowed = allowed & (key <= row)
        mask_ref[pl.ds(block * Q_TILE, Q_TILE), :] = jnp.where(allowed, 0.0, masked_score)


def attend_back_kernel(qkv_ref, doc_ref, lse_ref, grad_ref, out_ref, mask_ref, dk_ref, dv_ref):
    rows, cols = grad_ref.shape
    pairs = cols // PAIR
    dk_ref[...] = jnp.zeros_like(dk_ref)
    dv_ref[...] = jnp.zeros_like(dv_ref)
    for tile in range(rows // Q_TILE):
        extent = (tile + 1) * Q_TILE
        here = pl.ds(tile * Q_TILE, Q_TILE)
        seen = pl.ds(0, extent)
        mask_tile(tile, [doc_ref[pl.ds(b * Q_TILE, Q_TILE), :] for b in range(tile + 1)], mask_ref)

        def pair_step(pair, carry):
            q_cols = pl.ds(pl.multiple_of(pair * PAIR, PAIR), PAIR)
            k_cols = pl.ds(pl.multiple_of(cols + pair * PAIR, PAIR), PAIR)
            v_cols = pl.ds(pl.multiple_of(2 * cols + pair * PAIR, PAIR), PAIR)
            queries = qkv_ref[here, q_cols] * jnp.asarray(HEAD_DIM**-0.5, bf16)
            keys, values = qkv_ref[seen, k_cols], qkv_ref[seen, v_cols]
            grads = grad_ref[here, q_cols]
            dq = jnp.zeros((PAIR, Q_TILE), f32)
            for half in range(2):
                on = head_mask(half)
                q_one = jnp.where(on, queries, jnp.zeros_like(queries))
                g_one = jnp.where(on, grads, jnp.zeros_like(grads))
                probs = jnp.exp(mm(keys, q_one, 1, 1) + mask_ref[seen, :] - lse_ref[pair, pl.ds(half, 1), here])
                dv_ref[pair, seen, :] += mm(probs.astype(bf16), g_one)
                back = mm(values, g_one, 1, 1)
                low = (probs * (back - jnp.sum(probs * back, axis=0, keepdims=True))).astype(bf16)
                dk_ref[pair, seen, :] += mm(low, q_one)
                got = mm(keys, low, 0, 0)
                sublanes = lax.broadcasted_iota(jnp.int32, (PAIR, 1), 0)
                dq = jnp.where((sublanes // HEAD_DIM) == half, got, dq)
            out_ref[here, q_cols] = (dq.T * HEAD_DIM**-0.5).astype(bf16)
            return carry

        lax.fori_loop(0, pairs, pair_step, 0)
    for pair in range(pairs):
        out_ref[:, cols + pair * PAIR : cols + (pair + 1) * PAIR] = dk_ref[pair].astype(bf16)
        out_ref[:, 2 * cols + pair * PAIR : 2 * cols + (pair + 1) * PAIR] = dv_ref[pair].astype(bf16)


def attend_back(qkv, doc_col, lse, grad):
    rows, cols = grad.shape
    vmem = pl.BlockSpec(memory_space=pltpu.VMEM)
    return pl.pallas_call(
        attend_back_kernel,
        out_shape=jax.ShapeDtypeStruct((rows, 3 * cols), bf16),
        in_specs=[vmem] * 4,
        out_specs=vmem,
        scratch_shapes=[
            pltpu.VMEM((rows, Q_TILE), f32),
            pltpu.VMEM((cols // PAIR, rows, PAIR), f32),
            pltpu.VMEM((cols // PAIR, rows, PAIR), f32),
        ],
        compiler_params=pltpu.CompilerParams(vmem_limit_bytes=56 * 2**20),
        cost_estimate=pl.CostEstimate(flops=20 * rows * rows * cols, bytes_accessed=16 * rows * cols, transcendentals=0),
        name="attend_back",
    )(qkv, doc_col, lse, grad)


MESH = pl.DeviceIdType.MESH


class Spot:
    def __init__(self, groups, lanes):
        self.W, self.L = groups, lanes
        self.X = 1 << ((groups.bit_length() - 1) // 2)
        self.Z, self.Y = groups // self.X, lanes // 2
        self.g, self.l = lax.axis_index("wide"), lax.axis_index("narrow")
        self.z, self.x = self.g // self.X, self.g % self.X
        self.y, self.c = self.l // 2, self.l % 2

    def zx_peer(self, dz, dx):
        return lax.rem(self.z + dz, self.Z) * self.X + lax.rem(self.x + dx, self.X)

    def z_peer(self, d):
        return self.zx_peer(d, 0)

    def x_peer(self, d):
        return self.zx_peer(0, d)

    def y_peer(self, d):
        return lax.rem(self.y + d, self.Y) * 2 + self.c

    def core_peer(self):
        return self.y * 2 + 1 - self.c

    def w_peer(self, d):
        return lax.rem(self.g + d, self.W)

    def w_at(self, p):
        return lax.rem(self.g + 1 + p, self.W)

    def l_peer(self, d):
        return lax.rem(self.l + d, self.L)

    def greet(self, lane_peers=True):
        barrier = pltpu.get_barrier_semaphore()
        met = self.L - 1
        for d in range(1, self.L):
            pl.semaphore_signal(barrier, 1, device_id=(self.g, self.l_peer(d)), device_id_type=MESH)
        if lane_peers:
            met += self.W - 1
            for d in range(1, self.W):
                pl.semaphore_signal(barrier, 1, device_id=(self.w_peer(d), self.l), device_id_type=MESH)
        pl.semaphore_wait(barrier, met)


def remote(src, dst, send_sem, recv_sem, group, lane):
    return pltpu.make_async_remote_copy(src, dst, send_sem, recv_sem, device_id=(group, lane), device_id_type=MESH)


class LaneGather:
    def __init__(self, spot, src, place, sems):
        self.s, self.src, self.place = spot, src, place
        self.z_sem, self.x_sem, self.r_sem, self.own_sem = sems

    @staticmethod
    def sems(W, X):
        dma = pltpu.SemaphoreType.DMA
        return [dma((W // X,)), dma((W // X, X)), dma((W,)), dma((1,))]

    def z_copy(self, d):
        s = self.s
        return remote(self.src, self.place(s.g), self.z_sem.at[d], self.r_sem.at[s.g], s.z_peer(d), s.l)

    def x_copy(self, d, e):
        s = self.s
        w = s.z_peer(d)
        src = self.src if d == 0 else self.place(w)
        return remote(src, self.place(w), self.x_sem.at[d, e], self.r_sem.at[w], s.x_peer(e), s.l)

    def got(self, w):
        s = self.s
        remote(self.src, self.place(w), self.z_sem.at[0], self.r_sem.at[w], s.x_peer(1), s.l).wait_recv()

    def own(self):
        return pltpu.make_async_copy(self.src, self.place(self.s.g), self.own_sem.at[0])

    def start_z(self):
        for d in range(1, self.s.Z):
            self.z_copy(d).start()

    def start_x(self):
        for e in range(1, self.s.X):
            self.x_copy(0, e).start()
        self.own().start()

    def start(self):
        self.start_z()
        self.start_x()

    def forward(self):
        for d in range(1, self.s.Z):
            self.got(self.s.z_peer(d))
            for e in range(1, self.s.X):
                self.x_copy(d, e).start()

    def arrive(self):
        s = self.s
        for d in range(s.Z):
            for e in range(1, s.X):
                self.got(s.zx_peer(d, e))
        self.own().wait()

    def sent(self):
        for d in range(1, self.s.Z):
            self.z_copy(d).wait_send()
        for d in range(self.s.Z):
            for e in range(1, self.s.X):
                self.x_copy(d, e).wait_send()


class LineGather:
    def __init__(self, spot, src, place, sems):
        self.s, self.src, self.place = spot, src, place
        self.z_sem, self.x_sem, self.r_sem, self.own_sem = sems

    @staticmethod
    def sems(W, X):
        dma = pltpu.SemaphoreType.DMA
        return [dma((W // X, 2)), dma((W // X, 2, X)), dma((W,)), dma((1,))]

    def home(self, z):
        return self.place(z * self.s.X + self.s.x)

    def exists(self, z):
        return (z >= 0) & (z < self.s.Z)

    def z_copy(self, k, side):
        s, sign = self.s, 2 * side - 1
        z = s.z + sign * k
        src = self.src if k == 0 else self.home(z)
        return remote(src, self.home(z), self.z_sem.at[k, side], self.r_sem.at[z * s.X + s.x], (s.z - sign) * s.X + s.x, s.l)

    def x_copy(self, k, side, e):
        s = self.s
        z = s.z + (2 * side - 1) * k
        src = self.src if k == 0 else self.home(z)
        return remote(src, self.home(z), self.x_sem.at[k, side, e], self.r_sem.at[z * s.X + s.x], s.x_peer(e), s.l)

    def got(self, w):
        s = self.s
        remote(self.src, self.place(w), self.z_sem.at[0, 0], self.r_sem.at[w], s.x_peer(1), s.l).wait_recv()

    def own(self):
        return pltpu.make_async_copy(self.src, self.place(self.s.g), self.own_sem.at[0])

    def each(self, k, act):
        s = self.s
        for side in range(2):
            sign = 2 * side - 1
            onward = self.exists(s.z - sign)
            if k == 0:
                pl.when(onward)(lambda side=side: act(self.z_copy(0, side)))
                continue

            @pl.when(self.exists(s.z + sign * k))
            def _(side=side, sign=sign, onward=onward):
                if act is None:
                    self.got((s.z + sign * k) * s.X + s.x)
                go = (lambda c: c.start()) if act is None else act
                pl.when(onward)(lambda: go(self.z_copy(k, side)))
                for e in range(1, s.X):
                    go(self.x_copy(k, side, e))

    def start(self):
        self.each(0, lambda c: c.start())
        for e in range(1, self.s.X):
            self.x_copy(0, 0, e).start()
        self.own().start()

    def hop(self, k):
        self.each(k, None)

    def arrive(self):
        s = self.s
        for d in range(s.Z):
            for e in range(1, s.X):
                self.got(s.zx_peer(d, e))
        self.own().wait()

    def sent(self):
        for k in range(self.s.Z):
            self.each(k, lambda c: c.wait_send())
        for e in range(1, self.s.X):
            self.x_copy(0, 0, e).wait_send()


class GroupGather:
    def __init__(self, spot, src, place, sems, own=True):
        self.s, self.src, self.place, self.has_own = spot, src, place, own
        self.y_sem, self.c_sem, self.r_sem, self.own_sem = sems

    @staticmethod
    def sems(L):
        dma = pltpu.SemaphoreType.DMA
        return [dma((L // 2,)), dma((L // 2,)), dma((L,)), dma((1,))]

    def y_copy(self, d):
        s = self.s
        return remote(self.src, self.place(s.l), self.y_sem.at[d], self.r_sem.at[s.l], s.g, s.y_peer(d))

    def c_copy(self, d):
        s = self.s
        l = s.y_peer(d)
        src = self.src if d == 0 else self.place(l)
        return remote(src, self.place(l), self.c_sem.at[d], self.r_sem.at[l], s.g, s.core_peer())

    def got(self, l):
        s = self.s
        remote(self.src, self.place(l), self.y_sem.at[0], self.r_sem.at[l], s.g, s.core_peer()).wait_recv()

    def own(self):
        return pltpu.make_async_copy(self.src, self.place(self.s.l), self.own_sem.at[0])

    def start(self):
        for d in range(1, self.s.Y):
            self.y_copy(d).start()
        self.c_copy(0).start()
        if self.has_own:
            self.own().start()

    def forward(self):
        for d in range(1, self.s.Y):
            self.got(self.s.y_peer(d))
            self.c_copy(d).start()

    def arrive(self):
        s = self.s
        for d in range(s.Y):
            self.got(lax.rem(s.y + d, s.Y) * 2 + 1 - s.c)
        if self.has_own:
            self.own().wait()

    def sent(self):
        for d in range(1, self.s.Y):
            self.y_copy(d).wait_send()
        for d in range(self.s.Y):
            self.c_copy(d).wait_send()


class LaneSwap:
    def __init__(self, spot, src, dst, sems):
        self.s, self.src, self.dst = spot, src, dst
        self.s_sem, self.r_sem = sems

    @staticmethod
    def sems(W):
        return [pltpu.SemaphoreType.DMA((W,)), pltpu.SemaphoreType.DMA((W,))]

    def copy(self, d):
        s = self.s
        w = s.w_peer(d)
        return remote(self.src(w), self.dst(s.g), self.s_sem.at[d], self.r_sem.at[s.g], w, s.l)

    def own(self):
        return pltpu.make_async_copy(self.src(self.s.g), self.dst(self.s.g), self.s_sem.at[0])

    def start(self):
        for d in range(1, self.s.W):
            self.copy(d).start()
        self.own().start()

    def got(self, w):
        s = self.s
        remote(self.src(w), self.dst(w), self.s_sem.at[0], self.r_sem.at[w], s.w_peer(1), s.l).wait_recv()

    def arrive(self):
        for d in range(1, self.s.W):
            self.got(self.s.w_peer(self.s.W - d))
        self.own().wait()

    def sent(self):
        for d in range(1, self.s.W):
            self.copy(d).wait_send()


class GroupSwap:
    def __init__(self, spot, src, dst, sems):
        self.s, self.src, self.dst = spot, src, dst
        self.s_sem, self.r_sem = sems

    @staticmethod
    def sems(L):
        return [pltpu.SemaphoreType.DMA((L,)), pltpu.SemaphoreType.DMA((L,))]

    def copy(self, l):
        s = self.s
        return remote(self.src(l), self.dst(s.l), self.s_sem.at[l], self.r_sem.at[s.l], s.g, l)

    def own(self):
        s = self.s
        return pltpu.make_async_copy(self.src(s.l), self.dst(s.l), self.s_sem.at[s.l])

    def send(self, l):
        @pl.when(self.s.l == l)
        def _():
            self.own().start()

        @pl.when(self.s.l != l)
        def _():
            self.copy(l).start()

    def arrive(self):
        s = self.s
        for d in range(1, s.L):
            l = s.l_peer(d)
            remote(self.src(l), self.dst(l), self.s_sem.at[l], self.r_sem.at[l], s.g, l).wait_recv()
        self.own().wait()

    def sent(self):
        for d in range(1, self.s.L):
            self.copy(self.s.l_peer(d)).wait_send()


def rows_norm(src, gain, dst, count, step=64):
    def body(i, carry):
        at = pl.ds(pl.multiple_of(i * step, step), step)
        normed, _ = norm_stats(src[at, :].astype(f32))
        dst[at, :] = (normed * gain).astype(bf16)
        return carry

    lax.fori_loop(0, count // step, body, 0)


def front_kernel(
    groups, lanes, local, cap, slots,
    tokens, cot, meta, small, attend_w, output_w, up_w, down_w,
    lse, attn_mixed, attention_out, small_all, meta_all, place,
    normed_to, qkv_to, attend_to, output_to, mix_to, got_mix, cot_mine, cot_all, up_all, down_all,
    normed_out, qkv, attend_all, output_all, mix_all, tok_all, up_mine, mixed, mask, vt, packed_mix, packed_cot, out_sem, stage_sem, spread_y, spread_c, spread_r, *sems,
):
    s = Spot(groups, lanes)
    rows, width = tokens.shape
    head_cols = width // lanes
    shard = attend_w.shape[0]
    depth = down_all.shape[0] // groups
    sems = list(sems)

    def take(n):
        out = sems[:n]
        del sems[:n]
        return out

    def blocks(ref, n):
        return lambda i: ref.at[pl.ds(pl.multiple_of(i * n, n), n)]

    def cols(i):
        return pl.ds(pl.multiple_of(i * head_cols, head_cols), head_cols)

    staged = []
    if up_w.shape[1] != up_mine.shape[1]:
        fine = up_mine.shape[1] // groups
        staged += [
            pltpu.make_async_copy(
                up_w.at[:, pl.ds(pl.multiple_of((w * lanes + s.l) * fine, fine), fine)],
                up_mine.at[:, pl.ds(w * fine, fine)], stage_sem.at[w])
            for w in range(groups)
        ]
    else:
        staged += [pltpu.make_async_copy(up_w, up_mine, stage_sem.at[0])]
    for c in staged:
        c.start()

    tok = GroupGather(s, tokens, blocks(tok_all, rows), take(4))
    met = GroupGather(s, meta, lambda l: meta_all.at[l], take(4))
    cots = GroupGather(s, cot, blocks(cot_all, rows), take(4))
    mix = GroupGather(s, blocks(mix_all, rows)(s.l), blocks(mix_all, rows), take(4), own=False)
    outs = GroupGather(s, output_all.at[:, cols(s.l)], lambda l: output_all.at[:, cols(l)], take(4), own=False)
    atts = [
        LineGather(
            s, attend_w.at[:, pl.ds(pl.multiple_of(p * width + s.l * head_cols, head_cols), head_cols)],
            lambda w, p=p: attend_all.at[pl.ds(pl.multiple_of(w * shard, shard), shard), pl.ds(p * head_cols, head_cols)],
            take(4))
        for p in range(3)
    ]
    sml = LaneGather(s, small, blocks(small_all, shard), take(4))
    out = LineGather(s, output_w.at[:, cols(s.l)],
                     lambda w: output_all.at[pl.ds(pl.multiple_of(w * shard, shard), shard), cols(s.l)], take(4))
    up = LineGather(s, up_mine, blocks(up_all, shard), take(4))
    down = LineGather(s, down_w.at[pl.ds(pl.multiple_of(s.l * depth, depth), depth)], blocks(down_all, depth), take(4))
    swap = GroupSwap(s, blocks(mixed, rows), lambda l: attn_mixed.at[:, cols(l)], take(2))
    cot_swap = LaneSwap(s, blocks(packed_cot, slots), lambda w: cot_mine.at[w], take(2))
    mix_swap = LaneSwap(s, blocks(packed_mix, slots), lambda w: got_mix.at[s.l, w], take(2))

    def spread(d):
        w = s.w_peer(groups - d)
        return GroupGather(s, got_mix.at[s.l, w], lambda l: got_mix.at[l, w],
                           [spread_y.at[w], spread_c.at[w], spread_r.at[w], None], own=False)

    mix_spread = [spread(d) for d in range(groups)]

    s.greet()
    sml.start()
    met.start()
    tok.start()
    for att in atts:
        att.start()
    for c in staged:
        c.wait()
    mine = meta[...].T
    valid, route = mine[:, 1:2], mine[:, 2:3].astype(jnp.int32)
    column = lax.broadcasted_iota(jnp.int32, (rows, SMALL), 1)
    hits = (column == route).astype(f32)
    earlier = lax.broadcasted_iota(jnp.int32, (rows, rows), 1) < lax.broadcasted_iota(jnp.int32, (rows, rows), 0)
    rank = jnp.sum(hits * mm(earlier.astype(f32).astype(bf16), hits.astype(bf16)), axis=1, keepdims=True).astype(jnp.int32)
    slot = (route // local) * slots + (route % local) * cap + rank
    spots = (slot == lax.broadcasted_iota(jnp.int32, (rows, groups * slots), 1)).astype(f32)
    place[...] = spots.astype(bf16)
    packed_cot[...] = mm((spots * valid).astype(bf16), cot[...], 0, 0).astype(bf16)
    def give(ref, to, k):
        done.append(pltpu.make_async_copy(ref, to, out_sem.at[k]))
        done[-1].start()

    done = []
    sml.forward()
    for att in atts:
        att.hop(1)
    met.forward()
    tok.forward()
    cots.start()
    for k in range(2, s.Z):
        for att in atts:
            att.hop(k)
    out.start()
    up.start()
    sml.arrive()
    met.arrive()
    gains = small_all[...].astype(f32).T
    tok.arrive()
    rows_norm(tok_all, gains[0:1, :], normed_out, rows * lanes)
    give(normed_out, normed_to, 0)
    for att in atts:
        att.arrive()
    give(attend_all, attend_to, 1)

    def project(i, carry):
        at = pl.ds(pl.multiple_of(i * Q_TILE, Q_TILE), Q_TILE)
        qkv[at, :] = mm(normed_out[at, :], attend_all[...]).astype(bf16)
        return carry

    for k in range(1, s.Z - 1):
        out.hop(k)
    lax.fori_loop(0, rows * lanes // Q_TILE, project, 0)
    give(qkv, qkv_to, 2)
    out.hop(s.Z - 1)
    up.hop(1)
    doc_cols = [meta_all[l].T[:, 0:1] for l in range(lanes)]
    for tile in range(lanes):
        attend_tile(tile, qkv, doc_cols, mixed, lse, mask, vt)
        swap.send(tile)
        if tile == 0:
            out.arrive()
            outs.start()
        if tile == lanes - 3:
            up.hop(2)
            down.start()
        if tile == lanes - 2:
            for k in range(3, s.Z):
                up.hop(k)
            cots.forward()
    down.hop(1)
    outs.forward()
    outs.arrive()
    give(output_all, output_to, 3)
    swap.arrive()
    attention_out[...] = mm(attn_mixed[...], output_all[...])
    gain = small_all[...].astype(f32).T[1:2, :]
    base = pl.multiple_of(s.l * rows, rows)

    def mid(i, carry):
        at = pl.ds(pl.multiple_of(i * 64, 64), 64)
        normed, _ = norm_stats(tokens[at, :].astype(f32) + attention_out[at, :])
        mix_all[pl.ds(pl.multiple_of(base + i * 64, 64), 64), :] = (normed * gain).astype(bf16)
        return carry

    lax.fori_loop(0, rows // 64, mid, 0)
    mix.start()
    down.hop(2)
    packed_mix[...] = mm(place[...], mix_all[pl.ds(base, rows), :], 0, 0).astype(bf16)
    mix_swap.start()
    mix.forward()
    for k in range(3, s.Z):
        down.hop(k)
    for d in range(groups):
        if d:
            mix_swap.got(s.w_peer(groups - d))
        else:
            mix_swap.own().wait()
        mix_spread[d].start()
    cot_swap.start()
    mix.arrive()
    give(mix_all, mix_to, 4)
    for task in [tok, met, cots, outs, sml, out, up, swap, *atts]:
        task.sent()
    for task in mix_spread:
        task.forward()
    for task in mix_spread:
        task.arrive()
    cots.arrive()
    up.arrive()
    down.arrive()
    cot_swap.arrive()
    for c in done:
        c.wait()
    for task in [mix, down, mix_swap, cot_swap] + mix_spread:
        task.sent()


def front(groups, lanes, local, cap, slots, tokens, cot, meta, small, attend_w, output_w, up_w, down_w):
    rows, width = tokens.shape
    X = 1 << ((groups.bit_length() - 1) // 2)
    Y = lanes // 2
    everyone = rows * lanes
    head_cols = width // lanes
    hidden = down_w.shape[0] // lanes * groups
    shard = attend_w.shape[0]
    vmem, anywhere = pl.BlockSpec(memory_space=pltpu.VMEM), pl.BlockSpec(memory_space=pl.ANY)
    dma = pltpu.SemaphoreType.DMA
    of = jax.ShapeDtypeStruct
    sems = []
    for _ in range(5):
        sems += GroupGather.sems(lanes)
    for _ in range(3):
        sems += LineGather.sems(groups, X)
    sems += LaneGather.sems(groups, X)
    for _ in range(3):
        sems += LineGather.sems(groups, X)
    sems += GroupSwap.sems(lanes) + LaneSwap.sems(groups) * 2
    outs = [
        (of((head_cols // PAIR, 2, everyone), f32), vmem),
        (of((rows, width), bf16), vmem),
        (of((rows, width), f32), vmem),
        (of((width, SMALL), bf16), vmem),
        (of((lanes, 8, rows), f32), vmem),
        (of((rows, groups * slots), bf16), vmem),
    ]
    big = [(everyone, width), (everyone, 3 * head_cols), (width, 3 * head_cols), (width, width), (everyone, width)]
    outs += [(of(shape, bf16), anywhere) for shape in big]
    outs += [
        (of((lanes, groups, slots, width), bf16), anywhere),
        (of((groups, slots, width), bf16), anywhere),
        (of((everyone, width), bf16), anywhere),
        (of((width, hidden), bf16), anywhere),
        (of((hidden, width), bf16), anywhere),
    ]
    return pl.pallas_call(
        functools.partial(front_kernel, groups, lanes, local, cap, slots),
        out_shape=[o for o, _ in outs],
        in_specs=[vmem] * 4 + [anywhere] * 4,
        out_specs=[p for _, p in outs],
        scratch_shapes=[pltpu.VMEM(shape, bf16) for shape in big] + [
            pltpu.VMEM((everyone, width), bf16),
            pltpu.VMEM((shard, hidden), bf16),
            pltpu.VMEM((everyone, head_cols), bf16),
            pltpu.VMEM((everyone, Q_TILE), f32),
            pltpu.VMEM((head_cols // PAIR, PAIR, everyone), bf16),
            pltpu.VMEM((groups * slots, width), bf16),
            pltpu.VMEM((groups * slots, width), bf16),
            dma((5,)),
            dma((groups,)),
            dma((groups, Y)),
            dma((groups, Y)),
            dma((groups, lanes)),
        ] + sems,
        compiler_params=pltpu.CompilerParams(collective_id=0, has_side_effects=True, vmem_limit_bytes=56 * 2**20),
        cost_estimate=pl.CostEstimate(flops=8 * 10**9, bytes_accessed=10**8, transcendentals=0),
        name="front",
    )(tokens, cot, meta, small, attend_w, output_w, up_w, down_w)


def add_rows(dst, sources, step=32):
    def body(i, carry):
        at = pl.ds(pl.multiple_of(i * step, step), step)
        total = sources[0][at, :].astype(f32)
        for ref in sources[1:]:
            total += ref[at, :].astype(f32)
        dst[at, :] = total.astype(dst.dtype)
        return carry

    step = step if dst.shape[0] % step == 0 else dst.shape[0]
    lax.fori_loop(0, dst.shape[0] // step, body, 0)


class GroupScatter:
    def __init__(self, spot, part, held, from_core, from_y, sems, fine, chunks=None):
        self.s, self.part, self.from_core, self.from_y, self.fine = spot, part, from_core, from_y, fine
        self.staged = held is not None
        self.held = (lambda d: held.at[d]) if self.staged else (lambda d: part(spot.y_peer(d)))
        self.stage_sem, self.cs_sem, self.cr_sem, self.ys_sem, self.yr_sem = sems
        self.chunks = chunks or from_core.shape[1]

    @staticmethod
    def sems(L, chunks):
        dma = pltpu.SemaphoreType.DMA
        return [dma((L // 2,))] * 3 + [dma((L // 2, chunks))] * 2

    def stage(self, d):
        return pltpu.make_async_copy(self.part(self.s.y_peer(d)), self.held(d), self.stage_sem.at[d])

    def core_copy(self, d):
        s = self.s
        other = lax.rem(s.y + d, s.Y) * 2 + 1 - s.c
        return remote(self.part(other), self.from_core.at[d], self.cs_sem.at[d], self.cr_sem.at[d], s.g, s.core_peer())

    def y_copy(self, d, k):
        s = self.s
        src, dst = self.held(d), self.from_y.at[d - 1]
        if self.fine:
            src, dst = src.at[k], dst.at[k]
        return remote(src, dst, self.ys_sem.at[d, k], self.yr_sem.at[d, k], s.g, s.y_peer(d))

    def start(self):
        for d in range(self.s.Y):
            if self.staged:
                self.stage(d).start()
            self.core_copy(d).start()

    def ready(self):
        for d in range(self.s.Y):
            if self.staged:
                self.stage(d).wait()
            self.core_copy(d).wait_recv()

    def add(self, d, k):
        self.held(d)[k] = (self.held(d)[k].astype(f32) + self.from_core[d, k].astype(f32)).astype(bf16)

    def relay(self, k=0):
        for d in range(1, self.s.Y):
            if self.fine:
                self.add(d, k)
            else:

                def body(i, carry, d=d):
                    self.add(d, i)
                    return carry

                lax.fori_loop(0, self.chunks, body, 0)
            self.y_copy(d, k).start()

    def got(self, k=0):
        for d in range(1, self.s.Y):
            self.y_copy(d, k).wait_recv()

    def total(self, k):
        value = self.held(0)[k].astype(f32) + self.from_core[0, k].astype(f32)
        for d in range(1, self.s.Y):
            value += self.from_y[d - 1, k].astype(f32)
        return value

    def sent(self):
        for d in range(self.s.Y):
            self.core_copy(d).wait_send()
        for d in range(1, self.s.Y):
            for k in range(self.chunks if self.fine else 1):
                self.y_copy(d, k).wait_send()


class LaneScatter:
    def __init__(self, spot, part, held, from_x, from_z, sems):
        self.s, self.part, self.from_x, self.from_z = spot, part, from_x, from_z
        self.staged = held is not None
        self.held = (lambda d: held.at[d]) if self.staged else (lambda d: part(spot.z_peer(d)))
        self.stage_sem, self.xs_sem, self.xr_sem, self.zs_sem, self.zr_sem = sems

    @staticmethod
    def sems(W, X):
        dma = pltpu.SemaphoreType.DMA
        Z = W // X
        return [dma((Z,)), dma((X, Z)), dma((X, Z)), dma((Z,)), dma((Z,))]

    def stage(self, d):
        return pltpu.make_async_copy(self.part(self.s.z_peer(d)), self.held(d), self.stage_sem.at[d])

    def x_copy(self, e, d):
        s = self.s
        return remote(self.part(s.zx_peer(d, e)), self.from_x.at[e - 1, d], self.xs_sem.at[e, d], self.xr_sem.at[e, d],
                      s.x_peer(e), s.l)

    def z_copy(self, d):
        s = self.s
        return remote(self.held(d), self.from_z.at[d - 1], self.zs_sem.at[d], self.zr_sem.at[d], s.z_peer(d), s.l)

    def start(self):
        for d in [*range(1, self.s.Z), 0]:
            if self.staged:
                self.stage(d).start()
            for e in range(1, self.s.X):
                self.x_copy(e, d).start()

    def ready(self, d):
        if self.staged:
            self.stage(d).wait()
        for e in range(1, self.s.X):
            self.x_copy(e, d).wait_recv()

    def relay(self):
        for d in range(1, self.s.Z):
            self.ready(d)
            add_rows(self.held(d), [self.held(d)] + [self.from_x.at[e - 1, d] for e in range(1, self.s.X)])
            self.z_copy(d).start()

    def finish(self, dst):
        self.ready(0)
        for d in range(1, self.s.Z):
            self.z_copy(d).wait_recv()
        add_rows(dst, [self.held(0)] + [self.from_x.at[e - 1, 0] for e in range(1, self.s.X)]
                 + [self.from_z.at[d - 1] for d in range(1, self.s.Z)])

    def fold(self, dst):
        for d in range(self.s.Z):
            self.ready(d)
            add_rows(dst.at[d], [self.held(d)] + [self.from_x.at[e - 1, d] for e in range(1, self.s.X)])

    def x_sent(self):
        for d in range(self.s.Z):
            for e in range(1, self.s.X):
                self.x_copy(e, d).wait_send()

    def sent(self):
        self.x_sent()
        for d in range(1, self.s.Z):
            self.z_copy(d).wait_send()


class ZScatter(LaneScatter):
    def __init__(self, spot, held, from_z, sems):
        self.s, self.held, self.from_z = spot, held, from_z
        self.zs_sem, self.zr_sem = sems

    def start(self):
        for d in range(1, self.s.Z):
            self.z_copy(d).start()

    def finish(self, dst):
        for d in range(1, self.s.Z):
            self.z_copy(d).wait_recv()
        add_rows(dst, [self.held(0)] + [self.from_z.at[d - 1] for d in range(1, self.s.Z)])

    def sent(self):
        for d in range(1, self.s.Z):
            self.z_copy(d).wait_send()


def attend_back_tile(tile, qkv_ref, doc_cols, lse_ref, grad_ref, out_ref, mask_ref, dk_ref, dv_ref):
    cols = grad_ref.shape[1]
    extent = (tile + 1) * Q_TILE
    here, seen = pl.ds(tile * Q_TILE, Q_TILE), pl.ds(0, extent)
    mask_tile(tile, doc_cols, mask_ref)

    def pair_step(pair, carry):
        q_cols = pl.ds(pl.multiple_of(pair * PAIR, PAIR), PAIR)
        k_cols = pl.ds(pl.multiple_of(cols + pair * PAIR, PAIR), PAIR)
        v_cols = pl.ds(pl.multiple_of(2 * cols + pair * PAIR, PAIR), PAIR)
        queries = qkv_ref[here, q_cols] * jnp.asarray(HEAD_DIM**-0.5, bf16)
        keys, values = qkv_ref[seen, k_cols], qkv_ref[seen, v_cols]
        grads = grad_ref[here, q_cols]
        dq = jnp.zeros((PAIR, Q_TILE), f32)
        for half in range(2):
            on = head_mask(half)
            q_one = jnp.where(on, queries, jnp.zeros_like(queries))
            g_one = jnp.where(on, grads, jnp.zeros_like(grads))
            probs = jnp.exp(mm(keys, q_one, 1, 1) + mask_ref[seen, :] - lse_ref[pair, pl.ds(half, 1), here])
            dv_ref[pair, seen, :] += mm(probs.astype(bf16), g_one)
            back = mm(values, g_one, 1, 1)
            low = (probs * (back - jnp.sum(probs * back, axis=0, keepdims=True))).astype(bf16)
            dk_ref[pair, seen, :] += mm(low, q_one)
            got = mm(keys, low, 0, 0)
            sublanes = lax.broadcasted_iota(jnp.int32, (PAIR, 1), 0)
            dq = jnp.where((sublanes // HEAD_DIM) == half, got, dq)
        out_ref[here, q_cols] = (dq.T * HEAD_DIM**-0.5).astype(bf16)
        return carry

    lax.fori_loop(0, cols // PAIR, pair_step, 0)


def expert_grads_kernel(x_ref, hidden_ref, act_ref, grad_ref, up_ref, down_ref):
    up_ref[0] = mm(x_ref[0], hidden_ref[0], 0, 0)
    down_ref[0] = mm(act_ref[0], grad_ref[0], 0, 0)


def expert_grads(x, hidden, act, grad):
    local, rows, width = x.shape
    units = hidden.shape[2]
    tile = 256
    tall = lambda: pl.BlockSpec((1, rows, tile), lambda e, m: (e, 0, m))
    return pl.pallas_call(
        expert_grads_kernel,
        grid=(local, width // tile),
        out_shape=[jax.ShapeDtypeStruct((local, width, units), f32), jax.ShapeDtypeStruct((local, units, width), f32)],
        in_specs=[
            tall(), pl.BlockSpec((1, rows, units), lambda e, m: (e, 0, 0)),
            tall(), pl.BlockSpec((1, rows, width), lambda e, m: (e, 0, 0)),
        ],
        out_specs=[pl.BlockSpec((1, tile, units), lambda e, m: (e, m, 0)), pl.BlockSpec((1, tile, width), lambda e, m: (e, m, 0))],
        compiler_params=pltpu.CompilerParams(vmem_limit_bytes=40 * 2**20),
        cost_estimate=pl.CostEstimate(flops=4 * local * rows * width * units, bytes_accessed=3 * 10**7, transcendentals=0),
        name="expert_grads",
    )(x, hidden, act, grad)


def take_from(sems):
    sems = list(sems)

    def take(n):
        out = sems[:n]
        del sems[:n]
        return out

    return take


def picked(logits, first, count):
    columns = lax.broadcasted_iota(jnp.int32, logits.shape, 1)
    return soft_max(jnp.where((columns >= first) & (columns < first + count), logits, masked_score))


def middle_kernel(
    groups, lanes, local, cap, experts,
    small, meta_all, place,
    mix_in, cot_in, up_in, down_in, got_mix_in, cot_mine, expert_up, expert_down,
    grad_mix, dense_out, grad_small, mine_up, down_half, tok_part, mix_e_out, grad_e_out, act_e_out, hidden_e_out,
    mix, cot, up, down, act, hidden, got_mix, got_cot, mix_e, grad_e, act_e, hidden_e, expert_in, expert_to,
    mx, mx_c, mx_y, dn, dn_c, dn_y, bk_c, bk_y, gu, gu_x, gu_z, gd, gd_x, ret_back, got_back, dots, coefs,
    load_sem, out_sem, *sems,
):
    s = Spot(groups, lanes)
    everyone, width = mix.shape
    rows = everyone // lanes
    units = up.shape[1]
    slots = got_mix.shape[2]
    shard = width // groups
    rows_e = mix_e.shape[1]
    tile = 256
    step = 64
    take = take_from(sems)

    def blocks(ref, n):
        return lambda i: ref.at[pl.ds(pl.multiple_of(i * n, n), n)]

    def part(i, n=tile):
        return pl.ds(pl.multiple_of(i * n, n), n)

    def load(i, src, dst):
        return pltpu.make_async_copy(src, dst, load_sem.at[i])

    cot_spread = GroupGather(s, cot_mine, lambda l: got_cot.at[l], take(4))
    mxs = GroupScatter(s, lambda l: mx.at[l], None, mx_c, mx_y, take(5), False)
    dns = GroupScatter(s, lambda l: dn.at[l], None, dn_c, dn_y, take(5), False)
    near = groups // 2
    bks = [
        GroupScatter(s, lambda l, h=h: got_cot.at[l, pl.ds(h * near, near)], None, bk_c.at[h], bk_y.at[h], take(5), True, near)
        for h in range(2)
    ]
    ups = LaneScatter(s, blocks(gu, shard), None, gu_x, gu_z, take(5))
    dws = LaneScatter(s, blocks(gd, shard), None, gd_x, None, take(5))
    back_swap = LaneSwap(s, blocks(ret_back, slots), blocks(got_back, slots), take(2))

    loads = [load(i, a, b) for i, (a, b) in enumerate([
        (mix_in, mix), (up_in, up), (cot_in, cot), (down_in, down), (got_mix_in, got_mix),
        (expert_up.at[0], expert_in), (expert_down.at[0], expert_to)])]
    more_loads = [load(7, expert_up.at[1], up), load(8, expert_down.at[1], down)]

    def branch(x, grad, w_in, w_to, act_ref, hidden_ref, count):
        dots[pl.ds(0, count), :] = jnp.zeros((count, SMALL), f32)

        def body(n, carry):
            value, slope = gelu_both(mm(x[...], w_in[:, part(n)]))
            value = value.astype(bf16)
            act_ref[pl.ds(0, count), part(n)] = value
            back = mm(grad[...], w_to[part(n), :], 1, 1)
            hidden_ref[pl.ds(0, count), part(n)] = (slope * back).astype(bf16)
            both = value.astype(f32) * back
            dots[pl.ds(0, count), :] += sum([both[:, i * SMALL : (i + 1) * SMALL] for i in range(1, tile // SMALL)], both[:, :SMALL])
            return carry

        lax.fori_loop(0, units // tile, body, 0)
        return jnp.sum(dots[pl.ds(0, count), :], axis=1, keepdims=True)

    s.greet()
    cot_spread.start()
    for c in loads:
        c.start()
    for c in loads[:4]:
        c.wait()
    columns = lax.broadcasted_iota(jnp.int32, (everyone, SMALL), 1)

    coefs[...] = picked(mm(mix[...], small[...]), 2, 2)
    for l in range(lanes):
        at = pl.ds(l * rows, rows)
        valid = meta_all[l].T[:, 1:2]
        cot[at, :] = (coefs[at, 3:4] * (cot[at, :].astype(f32) * valid)).astype(bf16)
    dot = branch(mix, cot, up, down, act, hidden, everyone)
    sign = jnp.where(columns == 3, 1.0, 0.0) - jnp.where(columns == 2, 1.0, 0.0)
    logits = (sign * (coefs[:, 2:3] * dot)).astype(bf16)
    grad_small[...] = mm(logits, mix[...], 0, 0)

    def up_grad(m, carry):
        gu[part(m), :] = mm(mix[:, part(m)], hidden[...], 0, 0).astype(bf16)
        return carry

    lax.fori_loop(0, width // tile, up_grad, 0)
    ups.start()
    def down_grad(m, carry):
        gd[part(m), :] = mm(act[:, part(m)], cot[...], 0, 0).astype(bf16)
        return carry

    lax.fori_loop(0, units // tile, down_grad, 0)
    dws.start()

    def mix_grad(n, carry):
        value = mm(hidden[...], up[part(n), :], 1, 1) + mm(logits, small[part(n), :], 1, 1)
        mx[:, :, :, part(n)] = value.astype(bf16).reshape(lanes, rows // step, step, tile)
        return carry

    lax.fori_loop(0, width // tile, mix_grad, 0)
    mxs.start()

    def out_part(n, carry):
        value = mm(act[...], down[:, part(n)])
        dn[:, :, :, part(n)] = value.astype(bf16).reshape(lanes, rows // step, step, tile)
        return carry

    lax.fori_loop(0, width // tile, out_part, 0)
    dns.start()
    for c in more_loads:
        c.start()
    for c in loads[4:]:
        c.wait()

    def apart(src, dst):
        def body(j, carry):
            pair = []
            for i in range(2):
                b = 2 * j + i
                pair.append(src[b % lanes, s.w_at(b // lanes)].astype(f32))
            for e in range(local):
                both = [p[e * cap : (e + 1) * cap] for p in pair]
                dst[e, part(j, 2 * cap), :] = jnp.concatenate(both, axis=0).astype(bf16)
            return carry

        lax.fori_loop(0, lanes * groups // 2, body, 0)

    def together(sources, dst, first=0, last=lanes * groups // 2):
        def body(j, carry):
            values = [src[part(j, 2 * cap), :].astype(f32) for src in sources]
            for i in range(2):
                b = 2 * j + i
                dst[b % lanes, b // lanes] = jnp.concatenate([v[i * cap : (i + 1) * cap] for v in values], axis=0).astype(bf16)
            return carry

        lax.fori_loop(first, last, body, 0)

    apart(got_mix, mix_e)
    cot_spread.forward()
    mxs.ready()
    mxs.relay()
    cot_spread.arrive()
    apart(got_cot, grad_e)

    backs, toks = [act, hidden], [mix, cot]
    outs = []
    few = rows_e // 2
    columns = lax.broadcasted_iota(jnp.int32, (few, SMALL), 1)

    def rows_out(h, e):
        w_to = expert_to if e == 0 else down
        at = pl.ds(h * few, few)

        def body(n, carry):
            toks[e][at, part(n)] = mm(act_e[e, at, :], w_to[:, part(n)]).astype(bf16)
            return carry

        lax.fori_loop(0, width // tile, body, 0)

    for h in range(2):
        at = pl.ds(h * few, few)
        for e in range(local):
            w_in, w_to = (expert_in, expert_to) if e == 0 else (up, down)
            if h == 0 and e:
                for c in more_loads:
                    c.wait()
            x, grad = mix_e.at[e, at], grad_e.at[e, at]
            scores = mm(x[...], small[...])
            blend, router = picked(scores, 2, 2), picked(scores, 4, experts)
            own = columns == 4 + s.g * local + e
            chosen = jnp.sum(jnp.where(own, router, 0.0), axis=1, keepdims=True)
            grad[...] = (blend[:, 2:3] * chosen * grad[...].astype(f32)).astype(bf16)
            shares = jnp.where(own, 1.0, 0.0) - router
            shares += blend[:, 3:4] * (jnp.where(columns == 2, 1.0, 0.0) - jnp.where(columns == 3, 1.0, 0.0))
            coefs[pl.ds(0, few), :] = shares
            dot = branch(x, grad, w_in, w_to, act_e.at[e, at], hidden_e.at[e, at], few)
            logits = (dot * coefs[pl.ds(0, few), :]).astype(bf16)
            grad_small[...] += mm(logits, x[...], 0, 0)

            def rows_back(n, carry, e=e, w_in=w_in, logits=logits, at=at):
                value = mm(hidden_e[e, at, :], w_in[part(n), :], 1, 1) + mm(logits, small[part(n), :], 1, 1)
                backs[e][at, part(n)] = value.astype(bf16)
                return carry

            lax.fori_loop(0, width // tile, rows_back, 0)
            if h == 0 and e == 0:
                ups.relay()
                dns.ready()
                dns.relay()
            if h == 1 and e == 0:
                bks[0].ready()
                for k in range(near):
                    bks[0].relay(k)
        if h == 0:
            cot_spread.sent()
        together([b.at[pl.ds(0, rows_e)] for b in backs], got_cot, h * lanes * groups // 4, (h + 1) * lanes * groups // 4)
        bks[h].start()

    def hand_back(h):
        for k in range(near):
            p = h * near + k
            w = s.w_at(p)
            bks[h].got(k)
            ret_back[pl.ds(pl.multiple_of(w * slots, slots), slots), :] = bks[h].total(k).astype(bf16)
            if p < groups - 1:
                back_swap.copy(p + 1).start()
            else:
                back_swap.own().start()

    rows_out(0, 0)
    bks[1].ready()
    for k in range(near):
        bks[1].relay(k)
    hand_back(0)
    rows_out(0, 1)
    rows_out(1, 0)
    rows_out(1, 1)
    for e in range(local):
        for i, (a, b) in enumerate([(mix_e, mix_e_out), (grad_e, grad_e_out), (act_e, act_e_out), (hidden_e, hidden_e_out)]):
            outs.append(pltpu.make_async_copy(a.at[e], b.at[e], out_sem.at[4 * e + i]))
            outs[-1].start()
    together([t.at[pl.ds(0, rows_e)] for t in toks], got_mix)
    outs.append(pltpu.make_async_copy(got_mix, tok_part, out_sem.at[4 * local]))
    outs[-1].start()

    def totals(scatter, dst):
        scatter.got()

        def body(k, carry):
            dst[pl.ds(pl.multiple_of(k * step, step), step), :] = scatter.total(k).astype(dst.dtype)
            return carry

        lax.fori_loop(0, scatter.chunks, body, 0)

    totals(mxs, grad_mix)
    hand_back(1)
    dws.fold(down_half)
    totals(dns, dense_out)
    ups.finish(mine_up)
    back_swap.arrive()
    grad_mix[...] += mm(place[...], got_back[...])
    for c in outs:
        c.wait()
    dws.x_sent()
    for task in [mxs, dns, *bks, ups, back_swap]:
        task.sent()


def middle(groups, lanes, local, cap, experts, slots, inputs, placed):
    rows, width = inputs[2].shape[0], inputs[0].shape[0]
    X = 1 << ((groups.bit_length() - 1) // 2)
    Y, Z = lanes // 2, groups // X
    everyone = rows * lanes
    shard = width // groups
    units = placed[2].shape[1]
    rows_e = lanes * groups * cap
    vmem, anywhere = pl.BlockSpec(memory_space=pltpu.VMEM), pl.BlockSpec(memory_space=pl.ANY)
    dma = pltpu.SemaphoreType.DMA
    of = jax.ShapeDtypeStruct
    low = lambda *shape: pltpu.VMEM(shape, bf16)
    wide = lambda *shape: pltpu.VMEM(shape, f32)
    expert_rows = (local, rows_e, width)
    outs = [
        (of((rows, width), f32), vmem),
        (of((rows, width), bf16), vmem),
        (of((SMALL, width), f32), vmem),
        (of((shard, units), bf16), vmem),
        (of((Z, shard, width), bf16), vmem),
        (of((lanes, groups, slots, width), bf16), anywhere),
        (of(expert_rows, bf16), anywhere),
        (of(expert_rows, bf16), anywhere),
        (of((local, rows_e, units), bf16), anywhere),
        (of((local, rows_e, units), bf16), anywhere),
    ]
    scratch = [low(everyone, width), low(everyone, width), low(width, units), low(units, width)]
    scratch += [low(everyone, units), low(everyone, units)]
    scratch += [low(lanes, groups, slots, width)] * 2
    scratch += [low(*expert_rows), low(*expert_rows), low(local, rows_e, units), low(local, rows_e, units)]
    scratch += [low(width, units), low(units, width)]
    scratch += [low(lanes, rows // 64, 64, width), low(Y, rows // 64, 64, width), low(Y - 1, rows // 64, 64, width)] * 2
    scratch += [low(2, Y, groups // 2, slots, width), low(2, Y - 1, groups // 2, slots, width)]
    scratch += [low(width, units), low(X - 1, Z, shard, units), low(Z - 1, shard, units)]
    scratch += [low(units, width), low(X - 1, Z, shard, width)]
    scratch += [low(groups * slots, width)] * 2 + [wide(everyone, SMALL)] * 2
    scratch += [dma((9,)), dma((4 * local + 1,))]
    scratch += GroupGather.sems(lanes) + GroupScatter.sems(lanes, 1) * 2 + GroupScatter.sems(lanes, groups // 2) * 2
    scratch += LaneScatter.sems(groups, X) * 2 + LaneSwap.sems(groups)
    return pl.pallas_call(
        functools.partial(middle_kernel, groups, lanes, local, cap, experts),
        out_shape=[o for o, _ in outs],
        in_specs=[vmem] * len(inputs) + [anywhere] * len(placed),
        out_specs=[p for _, p in outs],
        scratch_shapes=scratch,
        compiler_params=pltpu.CompilerParams(collective_id=2, has_side_effects=True, vmem_limit_bytes=62 * 2**20),
        cost_estimate=pl.CostEstimate(flops=35 * 10**9, bytes_accessed=10**8, transcendentals=0),
        name="middle",
    )(*inputs, *placed)


def back_kernel(
    groups, lanes, experts,
    tokens, cot, meta, small, attention_out, attn_mixed, place, meta_all, lse, grad_small, grad_mix_in, dense_out,
    mine_up, down_half, tok_part, qkv_in, output_in, attend_in, normed_in,
    layer_out, grad_tokens, small_out, all_attend, all_output, all_up, all_down,
    qkv, output_all, attend_all, normed, tk_h, tk_c, tk_y,
    go, go_c, go_y, gn, gn_c, gn_y, dw_z, ga, ga_x, ga_z, gl, gl_x, gl_z,
    sm, sm_x, sm_z, sm_mine, sm_all, ret_tok, got_tok, grad_mix, grad_mid, grad_attn, grad_mixed,
    grad_heads, grad_qkv, mask, dk, dv, valid_cols, mine_attend, mine_output, mine_down, stage_sem, *sems,
):
    s = Spot(groups, lanes)
    rows, width = tokens.shape
    head_cols = width // lanes
    slots = place.shape[1] // groups
    shard = width // groups
    take = take_from(sems)
    step = 64

    def blocks(ref, n):
        return lambda i: ref.at[pl.ds(pl.multiple_of(i * n, n), n)]

    def cols(i):
        return pl.ds(pl.multiple_of(i * head_cols, head_cols), head_cols)

    loads = [
        pltpu.make_async_copy(src, dst, stage_sem.at[i])
        for i, (src, dst) in enumerate(
            [(output_in, output_all), (qkv_in, qkv), (attend_in, attend_all), (normed_in, normed)])
    ]
    tk = GroupScatter(s, lambda l: tok_part.at[l], tk_h, tk_c, tk_y, take(5), True)
    gos = GroupScatter(s, lambda l: go.at[l], None, go_c, go_y, take(5), False)
    gns = GroupScatter(s, lambda l: gn.at[l], None, gn_c, gn_y, take(5), False)
    dws = ZScatter(s, lambda d: down_half.at[d], dw_z, take(2))
    gas = [LaneScatter(s, blocks(ga.at[p], shard), None, ga_x.at[p], ga_z.at[p], take(5)) for p in range(3)]
    gls = LaneScatter(s, blocks(gl, shard), None, gl_x, gl_z, take(5))
    sms = LaneScatter(s, lambda w: sm.at[w], None, sm_x, sm_z, take(5))
    tok_swap = LaneSwap(s, blocks(ret_tok, slots), blocks(got_tok, slots), take(2))
    heads = GroupSwap(s, lambda l: grad_mixed.at[:, cols(l)], blocks(grad_heads, rows), take(2))
    f_attend = GroupGather(s, mine_attend, lambda l: all_attend.at[l], take(4))
    f_output = GroupGather(s, mine_output, lambda l: all_output.at[l], take(4))
    f_up = GroupGather(s, mine_up, lambda l: all_up.at[l], take(4))
    f_down = GroupGather(s, mine_down, lambda l: all_down.at[l], take(4))
    f_small = GroupGather(s, sm_mine, lambda l: sm_all.at[l], take(4))

    def pass_on(first, last):
        for p in range(first, last):
            tk.relay(p)

    def hand_back(first, last):
        for p in range(first, last):
            w = s.w_at(p)
            tk.got(p)
            ret_tok[pl.ds(pl.multiple_of(w * slots, slots), slots), :] = tk.total(p).astype(bf16)
            if p < groups - 1:
                tok_swap.copy(p + 1).start()
            else:
                tok_swap.own().start()

    def totals(scatter, dst):
        scatter.got()

        def body(k, carry):
            dst[pl.ds(pl.multiple_of(k * step, step), step), :] = scatter.total(k).astype(dst.dtype)
            return carry

        lax.fori_loop(0, scatter.chunks, body, 0)

    def over_rows(body, init):
        return lax.fori_loop(0, rows // step, lambda i, c: body(pl.ds(pl.multiple_of(i * step, step), step), c), init)

    s.greet()
    tk.start()
    dws.start()
    f_up.start()
    for c in loads:
        c.start()
    dk[...] = jnp.zeros_like(dk)
    dv[...] = jnp.zeros_like(dv)
    gains = small[...].astype(f32).T
    mine = meta[...].T
    valid_cols[...] = jnp.broadcast_to(mine[:, 1:2], valid_cols.shape)

    def mid(at, gain_sum):
        normed_v, scale = norm_stats(tokens[at, :].astype(f32) + attention_out[at, :])
        grad = grad_mix_in[at, :]
        value = cot[at, :].astype(f32) * valid_cols[at, 0:1] + norm_back(normed_v, scale, gains[1:2, :], grad)
        grad_mid[at, :] = value
        grad_attn[at, :] = value.astype(bf16)
        return gain_sum + jnp.sum(grad * normed_v, axis=0, keepdims=True)

    mixer_gain_grad = over_rows(mid, jnp.zeros((1, width), f32))
    loads[0].wait()
    grad_mixed[...] = mm(grad_attn[...], output_all[...], 1, 1).astype(bf16)
    for l in range(lanes):
        heads.send(l)

    def out_grad(m, carry):
        value = mm(attn_mixed[:, cols(m)], grad_attn[...], 0, 0).astype(bf16)
        parts = head_cols // step
        for l in range(lanes):
            go[l, pl.ds(m * parts, parts)] = value[:, l * head_cols : (l + 1) * head_cols].reshape(parts, step, head_cols)
        return carry

    lax.fori_loop(0, lanes, out_grad, 0)
    gos.start()
    for c in loads[1:]:
        c.wait()
    heads.arrive()
    tk.ready()
    pass_on(0, groups)
    doc_cols = [meta_all[l].T[:, 0:1] for l in range(lanes)]
    for tile in range(lanes):
        attend_back_tile(tile, qkv, doc_cols, lse, grad_heads, grad_qkv, mask, dk, dv)
        if tile == 0:
            gos.ready()
            gos.relay()
        if tile == 2:
            f_up.forward()
            hand_back(0, groups // 2)
    for pair in range(head_cols // PAIR):
        grad_qkv[:, head_cols + pair * PAIR : head_cols + (pair + 1) * PAIR] = dk[pair].astype(bf16)
        grad_qkv[:, 2 * head_cols + pair * PAIR : 2 * head_cols + (pair + 1) * PAIR] = dv[pair].astype(bf16)

    for p in range(3):

        def weight_grad(m, carry, p=p):
            value = mm(normed[:, cols(m)], grad_qkv[:, p * head_cols : (p + 1) * head_cols], 0, 0)
            ga[p, pl.ds(pl.multiple_of(m * head_cols, head_cols), head_cols), :] = value.astype(bf16)
            return carry

        lax.fori_loop(0, lanes, weight_grad, 0)
        gas[p].start()

    def rows_grad(l, carry):
        value = mm(grad_qkv[pl.ds(pl.multiple_of(l * rows, rows), rows), :], attend_all[...], 1, 1)
        gn[l] = value.astype(bf16).reshape(rows // step, step, width)
        return carry

    lax.fori_loop(0, lanes, rows_grad, 0)
    gns.start()
    gns.ready()
    gns.relay()
    hand_back(groups // 2, groups)
    gas[0].relay()
    totals(gos, gl)
    gls.start()
    gas[1].relay()
    gas[2].relay()
    tok_swap.arrive()

    def layer(at, sums):
        attention = attention_out[at, :]
        residual = tokens[at, :].astype(f32) + attention
        normed_v, _ = norm_stats(residual)
        mix = (normed_v * gains[1:2, :]).astype(bf16)
        logits = mm(mix, small[...])
        blend, router = picked(logits, 2, 2), picked(logits, 4, experts)
        columns = lax.broadcasted_iota(jnp.int32, logits.shape, 1)
        route = valid_cols[at, 1:2].astype(jnp.int32)
        chosen = jnp.sum(jnp.where(columns == 4 + route, router, 0.0), axis=1, keepdims=True)
        ffn = blend[:, 2:3] * chosen * mm(place[at, :], got_tok[...]) + blend[:, 3:4] * dense_out[at, :].astype(f32)
        full = residual + ffn
        layer_out[at, :] = full.astype(bf16)
        valid = valid_cols[at, 0:1]
        got = [jnp.sum(valid * v * v, axis=(0, 1), keepdims=True) for v in (residual, full, attention, ffn)]
        got.append(jnp.sum(valid, axis=(0, 1), keepdims=True))
        return tuple(a + b for a, b in zip(sums, got))

    lane_of = lax.broadcasted_iota(jnp.int32, valid_cols.shape, 1)
    valid_cols[...] = jnp.where(lane_of == 1, mine[:, 2:3], mine[:, 1:2])
    sums = over_rows(layer, tuple(jnp.zeros((1, 1), f32) for _ in range(5)))
    totals(gns, grad_mix)

    def first(at, gain_sum):
        normed_v, scale = norm_stats(tokens[at, :].astype(f32))
        grad = grad_mix[at, :]
        grad_tokens[at, :] = (grad_mid[at, :] + norm_back(normed_v, scale, gains[0:1, :], grad)).astype(bf16)
        return gain_sum + jnp.sum(grad * normed_v, axis=0, keepdims=True)

    attend_gain_grad = over_rows(first, jnp.zeros((1, width), f32))
    used = sm_mine.shape[0]
    feature = lax.broadcasted_iota(jnp.int32, (used, shard), 0)
    place_of = lax.broadcasted_iota(jnp.int32, (used, shard), 1)
    tail = jnp.zeros((used, shard), f32)
    for i, v in enumerate(sums):
        tail = jnp.where(place_of == i, v, tail)
    for w in range(groups):
        here = slice(w * shard, (w + 1) * shard)
        value = jnp.where(feature == used - 1, tail, grad_small[0:used, here])
        value = jnp.where(feature == 0, attend_gain_grad[:, here], value)
        sm[w] = jnp.where(feature == 1, mixer_gain_grad[:, here], value)
    sms.start()
    gls.relay()
    dws.finish(mine_down)
    f_down.start()
    sms.relay()
    for p in range(3):
        gas[p].finish(mine_attend.at[:, pl.ds(p * head_cols, head_cols)])
    f_attend.start()
    gls.finish(mine_output)
    f_output.start()
    sms.finish(sm_mine)
    f_small.start()
    gathers = [f_up, f_down, f_attend, f_output, f_small]
    for task in gathers[1:]:
        task.forward()
    for task in gathers:
        task.arrive()
    small_out[...] = sum([sm_all[l] for l in range(1, lanes)], sm_all[0])
    for task in [tk, gos, gns, dws, *gas, gls, sms, tok_swap, heads] + gathers:
        task.sent()


def back(groups, lanes, experts, slots, inputs, placed):
    tokens = inputs[0]
    rows, width = tokens.shape
    X = 1 << ((groups.bit_length() - 1) // 2)
    Y, Z = lanes // 2, groups // X
    everyone = rows * lanes
    head_cols = width // lanes
    shard = width // groups
    hidden = inputs[-2].shape[1]
    vmem, anywhere = pl.BlockSpec(memory_space=pltpu.VMEM), pl.BlockSpec(memory_space=pl.ANY)
    dma = pltpu.SemaphoreType.DMA
    of = jax.ShapeDtypeStruct
    pairs = head_cols // PAIR
    low = lambda *shape: pltpu.VMEM(shape, bf16)
    wide = lambda *shape: pltpu.VMEM(shape, f32)

    def group_bufs(c, r, n, held=True):
        return ([low(Y, c, r, n)] if held else [low(lanes, c, r, n)]) + [low(Y, c, r, n), low(Y - 1, c, r, n)]

    def lane_bufs(n, held=True):
        return ([low(Z, shard, n)] if held else [low(width, n)]) + [low(X - 1, Z, shard, n), low(Z - 1, shard, n)]

    scratch = [low(everyone, 3 * head_cols), low(width, width), low(width, 3 * head_cols), low(everyone, width)]
    scratch += group_bufs(groups, slots, width)
    scratch += group_bufs(width // 64, 64, head_cols, False) + group_bufs(rows // 64, 64, width, False)
    scratch += [low(Z - 1, shard, width)] + [low(3, width, head_cols), low(3, X - 1, Z, shard, head_cols), low(3, Z - 1, shard, head_cols)] + lane_bufs(head_cols, False)
    used = -(-(5 + experts) // 8) * 8
    scratch += [wide(groups, used, shard), wide(X - 1, Z, used, shard), wide(Z - 1, used, shard)]
    scratch += [wide(used, shard), wide(lanes, used, shard)]
    scratch += [low(groups * slots, width)] * 2
    scratch += [wide(rows, width), wide(rows, width), low(rows, width), low(rows, width)]
    scratch += [low(everyone, head_cols), low(everyone, 3 * head_cols), wide(everyone, Q_TILE)]
    scratch += [wide(pairs, everyone, PAIR)] * 2 + [wide(rows, SMALL)]
    scratch += [low(shard, 3 * head_cols), low(shard, head_cols), low(shard, width)]
    scratch += [dma((4,))]
    scratch += GroupScatter.sems(lanes, groups) + GroupScatter.sems(lanes, 1) * 2
    scratch += [dma((Z,))] * 2 + LaneScatter.sems(groups, X) * 5
    scratch += LaneSwap.sems(groups) + GroupSwap.sems(lanes)
    scratch += GroupGather.sems(lanes) * 5
    outs = [
        (of((rows, width), bf16), vmem),
        (of((rows, width), bf16), vmem),
        (of((used, shard), f32), vmem),
        (of((lanes, shard, 3 * head_cols), bf16), anywhere),
        (of((lanes, shard, head_cols), bf16), anywhere),
        (of((lanes, shard, hidden), bf16), anywhere),
        (of((lanes, shard, width), bf16), anywhere),
    ]
    return pl.pallas_call(
        functools.partial(back_kernel, groups, lanes, experts),
        out_shape=[o for o, _ in outs],
        in_specs=[vmem] * len(inputs) + [anywhere] * len(placed),
        out_specs=[p for _, p in outs],
        scratch_shapes=scratch,
        compiler_params=pltpu.CompilerParams(collective_id=1, has_side_effects=True, vmem_limit_bytes=62 * 2**20),
        cost_estimate=pl.CostEstimate(flops=8 * 10**9, bytes_accessed=10**8, transcendentals=0),
        name="back",
    )(*inputs, *placed)


def lane_gather(part):
    return lax.all_gather(part, "wide", axis=0, tiled=True)


def lane_scatter(part):
    return lax.psum_scatter(part.astype(bf16), "wide", scatter_dimension=0, tiled=True)


def group_gather(part, axis=0):
    return lax.all_gather(part, "narrow", axis=axis, tiled=True)


def group_scatter(part, axis=0):
    return lax.psum_scatter(part.astype(bf16), "narrow", scatter_dimension=axis, tiled=True)


def lane_swap(part):
    return lax.all_to_all(part, "wide", split_axis=0, concat_axis=0, tiled=True)


def per_device(
    tokens, doc_ids, valid_mask, routes, cotangent, attend_gain, attend_weight, output_weight, mixer_gain,
    router_weight, blend_weight, up_weight, down_weight, expert_up, expert_down,
):
    rows, width = tokens.shape
    groups, lanes = lax.axis_size("wide"), lax.axis_size("narrow")
    group, lane = lax.axis_index("wide"), lax.axis_index("narrow")
    shard = attend_gain.shape[0]
    local = expert_up.shape[0]
    experts = local * groups
    hidden = up_weight.shape[1]
    fine = hidden // groups // lanes
    cap = max(2, (3 * rows + 2 * experts - 1) // (2 * experts))
    slots = -(-local * cap // 16) * 16
    all_rows = rows * lanes

    small = jnp.concatenate(
        [attend_gain[:, None], mixer_gain[:, None], blend_weight, router_weight,
         jnp.zeros((shard, SMALL - 4 - experts), bf16)], axis=1)
    meta_in = jnp.stack([doc_ids, valid_mask, routes[:, 0]]).astype(f32)
    meta_in = jnp.pad(meta_in, ((0, 5), (0, 0)))
    up_mine = up_weight
    if fine % 128:
        up_mine = lax.dynamic_index_in_dim(up_weight.reshape(shard, groups, lanes, fine), lane, 2, keepdims=False)
        up_mine = up_mine.reshape(shard, groups * fine)
    (
        lse, attn_mixed, attention_out, small, meta_all, place, normed_attend, qkv, attend_full, output_full, mix_all,
        got_mix, cot_mine, cot_all, up_full, down_full,
    ) = front(groups, lanes, local, cap, slots, tokens, cotangent, meta_in, small, attend_weight, output_weight, up_mine, down_weight)
    doc_col = meta_all[:, 0].reshape(all_rows, 1)
    valid_all = meta_all[:, 1].reshape(all_rows, 1)
    attend_gain_row = small[:, 0].astype(f32)
    mixer_gain_row = small[:, 1].astype(f32)
    mix_cols = jnp.where((jnp.arange(SMALL) < 2)[None, :], 0, small)
    residual_mid = tokens.astype(f32) + attention_out
    mid_normed, mid_scale = norm_stats(residual_mid)
    normed_mix = (mid_normed * mixer_gain_row).astype(bf16)
    route = routes[:, 0]

    def give_back(partial):
        return mm(place, lane_swap(group_scatter(partial)))

    valid = valid_mask.astype(f32)[:, None]
    grad_layer = cotangent.astype(f32) * valid

    def widen(gathered, parts):
        full = gathered.reshape(lanes, shard, parts, -1)
        return full.transpose(1, 2, 0, 3).reshape(shard, -1).astype(f32)

    if all_rows * width <= 2**20 and shard % 128 == 0 and cap % 8 == 0 and slots == local * cap and local == 2 and width == groups * fine and lanes * groups * cap <= all_rows:
        grad_mix, dense_out, grad_small, mine_up, down_half, tok_part, mix_e, grad_e, act_e, hidden_e = middle(
            groups, lanes, local, cap, experts, slots, (small, meta_all, place),
            (mix_all, cot_all, up_full, down_full, got_mix, cot_mine, expert_up, expert_down))
        layer_out, grad_tokens, small_out, out_attend, out_output, out_up, out_down = back(
            groups, lanes, experts, slots,
            (tokens, cotangent, meta_in, small, attention_out, attn_mixed, place, meta_all, lse, grad_small, grad_mix,
             dense_out, mine_up, down_half),
            (tok_part, qkv, output_full, attend_full, normed_attend))
        grad_expert_up, grad_expert_down = expert_grads(mix_e, hidden_e, act_e, grad_e)
        sums, small_out = small_out[-1], small_out.T
        root_means = jnp.sqrt(sums[:4] / (jnp.maximum(sums[4], 1.0) * width))
        return (
            layer_out, grad_tokens, small_out[:, 0], widen(out_attend, 3), widen(out_output, 1), small_out[:, 1],
            small_out[:, 4 : 4 + experts], small_out[:, 2:4], widen(out_up, groups),
            out_down.reshape(-1, width).astype(f32), grad_expert_up, grad_expert_down, root_means,
        )

    got_cot = group_gather(cot_mine[None])

    def coefficients(mix_rows):
        logits = mm(mix_rows, mix_cols)
        columns = jnp.arange(SMALL)[None, :]
        blend = soft_max(jnp.where((columns >= 2) & (columns < 4), logits, masked_score))
        router = soft_max(jnp.where((columns >= 4) & (columns < 4 + experts), logits, masked_score))
        return columns, blend, router

    columns, blend, _ = coefficients(mix_all)
    blend_0, blend_1 = blend[:, 2:3], blend[:, 3:4]
    grad_dense = (blend_1 * (cot_all.astype(f32) * valid_all.astype(f32))).astype(bf16)
    up_act, up_slope = gelu_both(mm(mix_all, up_full))
    up_act = up_act.astype(bf16)
    dense_part = mm(up_act, down_full)
    grad_up_act = mm(grad_dense, down_full, 1, 1)
    dense_dot = jnp.sum(up_act.astype(f32) * grad_up_act, axis=1, keepdims=True)
    grad_up_pre = (up_slope * grad_up_act).astype(bf16)
    dense_logits = (jnp.where(columns == 3, 1.0, 0.0) - jnp.where(columns == 2, 1.0, 0.0)) * (blend_0 * dense_dot)
    grad_mix_part = mm(grad_up_pre, up_full, 1, 1) + mm(dense_logits.astype(bf16), mix_cols, 1, 1)
    grad_small = mm(dense_logits.astype(bf16), mix_all, 0, 0)
    grad_up = mm(mix_all, grad_up_pre, 0, 0)
    grad_down = mm(up_act, grad_dense, 0, 0)

    def by_expert(received):
        split = received.reshape(lanes * groups, slots, width)[:, : local * cap]
        return split.reshape(lanes * groups, local, cap, width).transpose(1, 0, 2, 3).reshape(local, -1, width)

    def by_slot(values):
        split = values.reshape(local, lanes * groups, cap, width).transpose(1, 0, 2, 3)
        split = split.reshape(lanes * groups, local * cap, width)
        return jnp.pad(split, ((0, 0), (0, slots - local * cap), (0, 0))).reshape(-1, width)

    mix_e, cot_e = by_expert(got_mix), by_expert(got_cot)
    tok_parts, back_parts, up_grads, down_grads = [], [], [], []
    for e in range(local):
        _, blend, router = coefficients(mix_e[e])
        own = columns == 4 + group * local + e
        chosen = jnp.sum(jnp.where(own, router, 0.0), axis=1, keepdims=True)
        scale = blend[:, 2:3] * chosen
        grad_tok = (scale * cot_e[e].astype(f32)).astype(bf16)
        act, slope = gelu_both(mm(mix_e[e], expert_up[e]))
        act = act.astype(bf16)
        tok_parts.append((mm(act, expert_down[e])))
        grad_act = mm(grad_tok, expert_down[e], 1, 1)
        dot = jnp.sum(act.astype(f32) * grad_act, axis=1, keepdims=True)
        grad_hidden = (slope * grad_act).astype(bf16)
        logits = dot * (jnp.where(own, 1.0, 0.0) - router)
        logits += dot * blend[:, 3:4] * (jnp.where(columns == 2, 1.0, 0.0) - jnp.where(columns == 3, 1.0, 0.0))
        logits = logits.astype(bf16)
        back_parts.append(mm(grad_hidden, expert_up[e], 1, 1) + mm(logits, mix_cols, 1, 1))
        grad_small += mm(logits, mix_e[e], 0, 0)
        down_grads.append(mm(act, grad_tok, 0, 0))
        up_grads.append(mm(mix_e[e], grad_hidden, 0, 0))
    grad_expert_up, grad_expert_down = jnp.stack(up_grads), jnp.stack(down_grads)
    grad_small = grad_small.T
    expert_back = give_back(by_slot(jnp.stack(back_parts)))
    expert_tok = give_back(by_slot(jnp.stack(tok_parts)))

    dense_out = group_scatter(dense_part).astype(f32)
    _, blend, router = coefficients(normed_mix)
    own = columns == 4 + route[:, None]
    chosen = jnp.sum(jnp.where(own, router, 0.0), axis=1, keepdims=True)
    ffn_out = blend[:, 2:3] * chosen * expert_tok + blend[:, 3:4] * dense_out
    layer_full = residual_mid + ffn_out
    sums = jnp.stack(
        [jnp.sum(valid * v * v) for v in (residual_mid, layer_full, attention_out, ffn_out)] + [jnp.sum(valid)])

    grad_mix = group_scatter(grad_mix_part).astype(f32) + expert_back
    grad_mid = grad_layer + norm_back(mid_normed, mid_scale, mixer_gain_row, grad_mix)
    mixer_gain_grad = jnp.sum(grad_mix * mid_normed, axis=0)
    grad_attn = grad_mid.astype(bf16)
    grad_output = mm(attn_mixed, grad_attn, 0, 0)
    grad_mixed = mm(grad_attn, output_full, 1, 1).astype(bf16)
    grad_heads = lax.all_to_all(grad_mixed, "narrow", split_axis=1, concat_axis=0, tiled=True)
    grad_qkv = attend_back(qkv, doc_col, lse, grad_heads)
    grad_attend = mm(normed_attend, grad_qkv, 0, 0)
    grad_normed = group_scatter(mm(grad_qkv, attend_full, 1, 1)).astype(f32)
    in_normed, in_scale = norm_stats(tokens.astype(f32))
    grad_tokens = (grad_mid + norm_back(in_normed, in_scale, attend_gain_row, grad_normed)).astype(bf16)
    attend_gain_grad = jnp.sum(grad_normed * in_normed, axis=0)

    grad_small = jnp.where(columns == 0, attend_gain_grad[:, None], jnp.where(columns == 1, mixer_gain_grad[:, None], grad_small))
    small_out = lax.psum(lax.psum_scatter(grad_small, "wide", scatter_dimension=0, tiled=True), "narrow")
    sums = lax.psum(sums, ("wide", "narrow"))
    root_means = jnp.sqrt(sums[:4] / (jnp.maximum(sums[4], 1.0) * width))

    def share(part):
        return group_gather(part.astype(bf16)[None])

    out_attend = widen(share(lane_scatter(grad_attend)), 3)
    out_output = widen(share(lane_scatter(group_scatter(grad_output, axis=1))), 1)
    out_up = widen(share(lane_scatter(grad_up)), groups)
    out_down = group_gather(lane_scatter(grad_down).astype(bf16)).astype(f32)
    return (
        layer_full.astype(bf16), grad_tokens, small_out[:, 0], out_attend, out_output, small_out[:, 1],
        small_out[:, 4 : 4 + experts], small_out[:, 2:4], out_up, out_down, grad_expert_up, grad_expert_down, root_means,
    )


def solution(mesh):
    both = ("wide", "narrow")
    row, vec, mat = P(both, None), P("wide"), P("wide", None)
    up, down = P("wide", None, "narrow"), P("wide", "narrow", None)
    return jax.shard_map(
        per_device,
        mesh=mesh,
        in_specs=(row, P(both), P(both), row, row, vec, mat, mat, vec, mat, mat, mat, mat, up, down),
        out_specs=(row, row, vec, mat, mat, vec, mat, mat, mat, mat, up, down, P()),
        check_vma=False,
    )
```

```python
import functools

import jax
import jax.numpy as jnp
from jax import lax
from jax.experimental import pallas as pl
from jax.experimental.pallas import tpu as pltpu
from jax.sharding import PartitionSpec as P

HEAD_DIM = 64
PAIR = 2 * HEAD_DIM
Q_TILE = 256
SMALL = 128
eps_norm = 1e-05
masked_score = -1e30
f32 = jnp.float32
bf16 = jnp.bfloat16


def mm(a, b, ca=1, cb=0):
    return lax.dot_general(a, b, (((ca,), (cb,)), ((), ())), preferred_element_type=f32)


def norm_stats(values):
    center = values - jnp.mean(values, axis=-1, keepdims=True)
    scale = lax.rsqrt(jnp.mean(center * center, axis=-1, keepdims=True) + eps_norm)
    return center * scale, scale


def norm_back(normed, scale, gain, grad):
    u = grad * gain
    return scale * (
        u
        - jnp.mean(u, axis=-1, keepdims=True)
        - normed * jnp.mean(u * normed, axis=-1, keepdims=True)
    )


GELU_A = 0.7978845608028654
GELU_B = 0.044715


def gelu(v):
    return 0.5 * v * (1.0 + jnp.tanh(GELU_A * (v + GELU_B * v * v * v)))


def gelu_both(v):
    t = jnp.tanh(GELU_A * (v + GELU_B * v * v * v))
    value = 0.5 * v * (1.0 + t)
    slope = 0.5 * (1.0 + t) + 0.5 * v * (1.0 - t * t) * (GELU_A * (1.0 + 3.0 * GELU_B * v * v))
    return value, slope


def soft_max(logits):
    shifted = jnp.exp(logits - jnp.max(logits, axis=-1, keepdims=True))
    return shifted / jnp.sum(shifted, axis=-1, keepdims=True)


def head_mask(half):
    lanes = lax.broadcasted_iota(jnp.int32, (1, PAIR), 1)
    return (lanes // HEAD_DIM) == half


def attend_tile(tile, qkv_ref, doc_cols, out_ref, lse_ref, mask_ref, vt_ref):
    cols = out_ref.shape[1]
    extent = (tile + 1) * Q_TILE
    here, seen = pl.ds(tile * Q_TILE, Q_TILE), pl.ds(0, extent)
    mask_tile(tile, doc_cols, mask_ref)

    def pair_step(pair, carry):
        q_cols = pl.ds(pl.multiple_of(pair * PAIR, PAIR), PAIR)
        k_cols = pl.ds(pl.multiple_of(cols + pair * PAIR, PAIR), PAIR)
        v_cols = pl.ds(pl.multiple_of(2 * cols + pair * PAIR, PAIR), PAIR)
        if tile == 0:
            vt_ref[pair] = qkv_ref[:, v_cols].T
        queries = qkv_ref[here, q_cols] * jnp.asarray(HEAD_DIM**-0.5, bf16)
        mixed = jnp.zeros((PAIR, Q_TILE), f32)
        for half in range(2):
            one = jnp.where(head_mask(half), queries, jnp.zeros_like(queries))
            scores = mm(qkv_ref[seen, k_cols], one, 1, 1) + mask_ref[seen, :]
            top = jnp.max(scores, axis=0, keepdims=True)
            shifted = jnp.exp(scores - top)
            total = jnp.sum(shifted, axis=0, keepdims=True)
            low = (shifted * (1.0 / total)).astype(bf16)
            lse_ref[pair, pl.ds(half, 1), here] = top + jnp.log(total)
            got = mm(vt_ref[pair, :, seen], low)
            sublanes = lax.broadcasted_iota(jnp.int32, (PAIR, 1), 0)
            mixed = jnp.where((sublanes // HEAD_DIM) == half, got, mixed)
        out_ref[here, q_cols] = mixed.T.astype(bf16)
        return carry

    lax.fori_loop(0, cols // PAIR, pair_step, 0)


def mask_tile(tile, doc_cols, mask_ref):
    row = (tile * Q_TILE + lax.broadcasted_iota(jnp.int32, (Q_TILE, Q_TILE), 1)).astype(f32)
    for block in range(tile + 1):
        allowed = doc_cols[block] >= row
        if block == tile:
            key = (tile * Q_TILE + lax.broadcasted_iota(jnp.int32, (Q_TILE, Q_TILE), 0)).astype(f32)
            allowed = allowed & (key <= row)
        mask_ref[pl.ds(block * Q_TILE, Q_TILE), :] = jnp.where(allowed, 0.0, masked_score)


def attend_back_kernel(qkv_ref, doc_ref, lse_ref, grad_ref, out_ref, mask_ref, dk_ref, dv_ref):
    rows, cols = grad_ref.shape
    pairs = cols // PAIR
    dk_ref[...] = jnp.zeros_like(dk_ref)
    dv_ref[...] = jnp.zeros_like(dv_ref)
    for tile in range(rows // Q_TILE):
        extent = (tile + 1) * Q_TILE
        here = pl.ds(tile * Q_TILE, Q_TILE)
        seen = pl.ds(0, extent)
        mask_tile(tile, [doc_ref[pl.ds(b * Q_TILE, Q_TILE), :] for b in range(tile + 1)], mask_ref)

        def pair_step(pair, carry):
            q_cols = pl.ds(pl.multiple_of(pair * PAIR, PAIR), PAIR)
            k_cols = pl.ds(pl.multiple_of(cols + pair * PAIR, PAIR), PAIR)
            v_cols = pl.ds(pl.multiple_of(2 * cols + pair * PAIR, PAIR), PAIR)
            queries = qkv_ref[here, q_cols] * jnp.asarray(HEAD_DIM**-0.5, bf16)
            keys, values = qkv_ref[seen, k_cols], qkv_ref[seen, v_cols]
            grads = grad_ref[here, q_cols]
            dq = jnp.zeros((PAIR, Q_TILE), f32)
            for half in range(2):
                on = head_mask(half)
                q_one = jnp.where(on, queries, jnp.zeros_like(queries))
                g_one = jnp.where(on, grads, jnp.zeros_like(grads))
                probs = jnp.exp(mm(keys, q_one, 1, 1) + mask_ref[seen, :] - lse_ref[pair, pl.ds(half, 1), here])
                dv_ref[pair, seen, :] += mm(probs.astype(bf16), g_one)
                back = mm(values, g_one, 1, 1)
                low = (probs * (back - jnp.sum(probs * back, axis=0, keepdims=True))).astype(bf16)
                dk_ref[pair, seen, :] += mm(low, q_one)
                got = mm(keys, low, 0, 0)
                sublanes = lax.broadcasted_iota(jnp.int32, (PAIR, 1), 0)
                dq = jnp.where((sublanes // HEAD_DIM) == half, got, dq)
            out_ref[here, q_cols] = (dq.T * HEAD_DIM**-0.5).astype(bf16)
            return carry

        lax.fori_loop(0, pairs, pair_step, 0)
    for pair in range(pairs):
        out_ref[:, cols + pair * PAIR : cols + (pair + 1) * PAIR] = dk_ref[pair].astype(bf16)
        out_ref[:, 2 * cols + pair * PAIR : 2 * cols + (pair + 1) * PAIR] = dv_ref[pair].astype(bf16)


def attend_back(qkv, doc_col, lse, grad):
    rows, cols = grad.shape
    vmem = pl.BlockSpec(memory_space=pltpu.VMEM)
    return pl.pallas_call(
        attend_back_kernel,
        out_shape=jax.ShapeDtypeStruct((rows, 3 * cols), bf16),
        in_specs=[vmem] * 4,
        out_specs=vmem,
        scratch_shapes=[
            pltpu.VMEM((rows, Q_TILE), f32),
            pltpu.VMEM((cols // PAIR, rows, PAIR), f32),
            pltpu.VMEM((cols // PAIR, rows, PAIR), f32),
        ],
        compiler_params=pltpu.CompilerParams(vmem_limit_bytes=56 * 2**20),
        cost_estimate=pl.CostEstimate(flops=20 * rows * rows * cols, bytes_accessed=16 * rows * cols, transcendentals=0),
        name="attend_back",
    )(qkv, doc_col, lse, grad)


MESH = pl.DeviceIdType.MESH


class Spot:
    def __init__(self, groups, lanes):
        self.W, self.L = groups, lanes
        self.X = 1 << ((groups.bit_length() - 1) // 2)
        self.Z, self.Y = groups // self.X, lanes // 2
        self.g, self.l = lax.axis_index("wide"), lax.axis_index("narrow")
        self.z, self.x = self.g // self.X, self.g % self.X
        self.y, self.c = self.l // 2, self.l % 2

    def zx_peer(self, dz, dx):
        return lax.rem(self.z + dz, self.Z) * self.X + lax.rem(self.x + dx, self.X)

    def z_peer(self, d):
        return self.zx_peer(d, 0)

    def x_peer(self, d):
        return self.zx_peer(0, d)

    def y_peer(self, d):
        return lax.rem(self.y + d, self.Y) * 2 + self.c

    def core_peer(self):
        return self.y * 2 + 1 - self.c

    def w_peer(self, d):
        return lax.rem(self.g + d, self.W)

    def w_at(self, p):
        return lax.rem(self.g + 1 + p, self.W)

    def l_peer(self, d):
        return lax.rem(self.l + d, self.L)

    def greet(self):
        barrier = pltpu.get_barrier_semaphore()
        for d in range(1, self.L):
            pl.semaphore_signal(barrier, 1, device_id=(self.g, self.l_peer(d)), device_id_type=MESH)
        for d in range(1, self.W):
            pl.semaphore_signal(barrier, 1, device_id=(self.w_peer(d), self.l), device_id_type=MESH)

    def met(self):
        pl.semaphore_wait(pltpu.get_barrier_semaphore(), self.L + self.W - 2)


def remote(src, dst, send_sem, recv_sem, group, lane):
    return pltpu.make_async_remote_copy(src, dst, send_sem, recv_sem, device_id=(group, lane), device_id_type=MESH)


class LaneGather:
    def __init__(self, spot, src, place, sems):
        self.s, self.src, self.place = spot, src, place
        self.z_sem, self.x_sem, self.r_sem, self.own_sem = sems

    @staticmethod
    def sems(W, X):
        dma = pltpu.SemaphoreType.DMA
        return [dma((W // X,)), dma((W // X, X)), dma((W,)), dma((1,))]

    def z_copy(self, d):
        s = self.s
        return remote(self.src, self.place(s.g), self.z_sem.at[d], self.r_sem.at[s.g], s.z_peer(d), s.l)

    def x_copy(self, d, e):
        s = self.s
        w = s.z_peer(d)
        src = self.src if d == 0 else self.place(w)
        return remote(src, self.place(w), self.x_sem.at[d, e], self.r_sem.at[w], s.x_peer(e), s.l)

    def got(self, w):
        s = self.s
        remote(self.src, self.place(w), self.z_sem.at[0], self.r_sem.at[w], s.x_peer(1), s.l).wait_recv()

    def own(self):
        return pltpu.make_async_copy(self.src, self.place(self.s.g), self.own_sem.at[0])

    def start_z(self):
        for d in range(1, self.s.Z):
            self.z_copy(d).start()

    def start_x(self):
        for e in range(1, self.s.X):
            self.x_copy(0, e).start()
        self.own().start()

    def start(self):
        self.start_z()
        self.start_x()

    def forward(self):
        for d in range(1, self.s.Z):
            self.got(self.s.z_peer(d))
            for e in range(1, self.s.X):
                self.x_copy(d, e).start()

    def arrive(self):
        s = self.s
        for d in range(s.Z):
            for e in range(1, s.X):
                self.got(s.zx_peer(d, e))
        self.own().wait()

    def sent(self):
        for d in range(1, self.s.Z):
            self.z_copy(d).wait_send()
        for d in range(self.s.Z):
            for e in range(1, self.s.X):
                self.x_copy(d, e).wait_send()


class LineGather:
    def __init__(self, spot, src, place, sems):
        self.s, self.src, self.place = spot, src, place
        self.z_sem, self.x_sem, self.r_sem, self.own_sem = sems

    @staticmethod
    def sems(W, X):
        dma = pltpu.SemaphoreType.DMA
        return [dma((W // X, 2)), dma((W // X, 2, X)), dma((W,)), dma((1,))]

    def home(self, z):
        return self.place(z * self.s.X + self.s.x)

    def exists(self, z):
        return (z >= 0) & (z < self.s.Z)

    def z_copy(self, k, side):
        s, sign = self.s, 2 * side - 1
        z = s.z + sign * k
        src = self.src if k == 0 else self.home(z)
        return remote(src, self.home(z), self.z_sem.at[k, side], self.r_sem.at[z * s.X + s.x], (s.z - sign) * s.X + s.x, s.l)

    def x_copy(self, k, side, e):
        s = self.s
        z = s.z + (2 * side - 1) * k
        src = self.src if k == 0 else self.home(z)
        return remote(src, self.home(z), self.x_sem.at[k, side, e], self.r_sem.at[z * s.X + s.x], s.x_peer(e), s.l)

    def got(self, w):
        s = self.s
        remote(self.src, self.place(w), self.z_sem.at[0, 0], self.r_sem.at[w], s.x_peer(1), s.l).wait_recv()

    def own(self):
        return pltpu.make_async_copy(self.src, self.place(self.s.g), self.own_sem.at[0])

    def each(self, k, act):
        s = self.s
        for side in range(2):
            sign = 2 * side - 1
            onward = self.exists(s.z - sign)
            if k == 0:
                pl.when(onward)(lambda side=side: act(self.z_copy(0, side)))
                continue

            @pl.when(self.exists(s.z + sign * k))
            def _(side=side, sign=sign, onward=onward):
                if act is None:
                    self.got((s.z + sign * k) * s.X + s.x)
                go = (lambda c: c.start()) if act is None else act
                pl.when(onward)(lambda: go(self.z_copy(k, side)))
                for e in range(1, s.X):
                    go(self.x_copy(k, side, e))

    def start(self):
        self.each(0, lambda c: c.start())
        for e in range(1, self.s.X):
            self.x_copy(0, 0, e).start()
        self.own().start()

    def hop(self, k):
        self.each(k, None)

    def arrive(self):
        s = self.s
        for d in range(s.Z):
            for e in range(1, s.X):
                self.got(s.zx_peer(d, e))
        self.own().wait()

    def sent(self):
        for k in range(self.s.Z):
            self.each(k, lambda c: c.wait_send())
        for e in range(1, self.s.X):
            self.x_copy(0, 0, e).wait_send()


class GroupGather:
    def __init__(self, spot, src, place, sems, own=True):
        self.s, self.src, self.place, self.has_own = spot, src, place, own
        self.y_sem, self.c_sem, self.r_sem, self.own_sem = sems

    @staticmethod
    def sems(L):
        dma = pltpu.SemaphoreType.DMA
        return [dma((L // 2,)), dma((L // 2,)), dma((L,)), dma((1,))]

    def y_copy(self, d):
        s = self.s
        return remote(self.src, self.place(s.l), self.y_sem.at[d], self.r_sem.at[s.l], s.g, s.y_peer(d))

    def c_copy(self, d):
        s = self.s
        l = s.y_peer(d)
        src = self.src if d == 0 else self.place(l)
        return remote(src, self.place(l), self.c_sem.at[d], self.r_sem.at[l], s.g, s.core_peer())

    def got(self, l):
        s = self.s
        remote(self.src, self.place(l), self.y_sem.at[0], self.r_sem.at[l], s.g, s.core_peer()).wait_recv()

    def own(self):
        return pltpu.make_async_copy(self.src, self.place(self.s.l), self.own_sem.at[0])

    def start(self):
        for d in range(1, self.s.Y):
            self.y_copy(d).start()
        self.c_copy(0).start()
        if self.has_own:
            self.own().start()

    def forward(self):
        for d in range(1, self.s.Y):
            self.got(self.s.y_peer(d))
            self.c_copy(d).start()

    def arrive(self):
        s = self.s
        for d in range(s.Y):
            self.got(lax.rem(s.y + d, s.Y) * 2 + 1 - s.c)
        if self.has_own:
            self.own().wait()

    def sent(self):
        for d in range(1, self.s.Y):
            self.y_copy(d).wait_send()
        for d in range(self.s.Y):
            self.c_copy(d).wait_send()


class LaneSwap:
    def __init__(self, spot, src, dst, sems, distances=None):
        self.s, self.src, self.dst = spot, src, dst
        self.distances = range(spot.W) if distances is None else distances
        self.s_sem, self.r_sem = sems

    @staticmethod
    def sems(W):
        return [pltpu.SemaphoreType.DMA((W,)), pltpu.SemaphoreType.DMA((W,))]

    def copy(self, d):
        s = self.s
        w = s.w_peer(d)
        return remote(self.src(w), self.dst(s.g), self.s_sem.at[d], self.r_sem.at[s.g], w, s.l)

    def own(self):
        return pltpu.make_async_copy(self.src(self.s.g), self.dst(self.s.g), self.s_sem.at[0])

    def start(self):
        for d in self.distances:
            if d:
                self.copy(d).start()
            else:
                self.own().start()

    def got(self, w):
        s = self.s
        remote(self.src(w), self.dst(w), self.s_sem.at[0], self.r_sem.at[w], s.w_peer(1), s.l).wait_recv()

    def arrive(self):
        for d in self.distances:
            self.due(d)

    def due(self, d):
        if d:
            self.got(self.s.w_peer(self.s.W - d))
        else:
            self.own().wait()

    def sent(self):
        for d in self.distances:
            if d:
                self.copy(d).wait_send()


class GroupSwap:
    def __init__(self, spot, src, dst, sems):
        self.s, self.src, self.dst = spot, src, dst
        self.s_sem, self.r_sem = sems

    @staticmethod
    def sems(L):
        return [pltpu.SemaphoreType.DMA((L,)), pltpu.SemaphoreType.DMA((L,))]

    def copy(self, l):
        s = self.s
        return remote(self.src(l), self.dst(s.l), self.s_sem.at[l], self.r_sem.at[s.l], s.g, l)

    def own(self):
        s = self.s
        return pltpu.make_async_copy(self.src(s.l), self.dst(s.l), self.s_sem.at[s.l])

    def send(self, l):
        @pl.when(self.s.l == l)
        def _():
            self.own().start()

        @pl.when(self.s.l != l)
        def _():
            self.copy(l).start()

    def arrive(self):
        s = self.s
        for d in range(1, s.L):
            l = s.l_peer(d)
            remote(self.src(l), self.dst(l), self.s_sem.at[l], self.r_sem.at[l], s.g, l).wait_recv()
        self.own().wait()

    def sent(self):
        for d in range(1, self.s.L):
            self.copy(self.s.l_peer(d)).wait_send()


def rows_norm(src, gain, dst, count, step=64):
    def body(i, carry):
        at = pl.ds(pl.multiple_of(i * step, step), step)
        normed, _ = norm_stats(src[at, :].astype(f32))
        dst[at, :] = (normed * gain).astype(bf16)
        return carry

    lax.fori_loop(0, count // step, body, 0)


def front_kernel(
    groups, lanes, local, cap, slots,
    tokens, cot, facts, mixers, attend_w, output_w, up_w, down_w,
    lse, attn_mixed, attention_out, small_all, meta_all, place,
    packed_cot, normed_to, qkv_to, attend_to, output_to, mix_to, got_mix, cot_mine, cot_all, up_all, down_all,
    normed_out, qkv, attend_all, output_all, mix_all, tok_all, up_mine, mixed, mask, vt, packed_mix, meta, small, out_sem, stage_sem, spread_y, spread_c, spread_r, *sems,
):
    s = Spot(groups, lanes)
    s.greet()
    rows, width = tokens.shape
    head_cols = width // lanes
    shard = attend_w.shape[0]
    depth = down_all.shape[0] // groups
    sems = list(sems)

    def take(n):
        out = sems[:n]
        del sems[:n]
        return out

    def blocks(ref, n):
        return lambda i: ref.at[pl.ds(pl.multiple_of(i * n, n), n)]

    def cols(i):
        return pl.ds(pl.multiple_of(i * head_cols, head_cols), head_cols)

    staged = []
    if up_w.shape[1] != up_mine.shape[1]:
        fine = up_mine.shape[1] // groups
        staged += [
            pltpu.make_async_copy(
                up_w.at[:, pl.ds(pl.multiple_of((w * lanes + s.l) * fine, fine), fine)],
                up_mine.at[:, pl.ds(w * fine, fine)], stage_sem.at[w])
            for w in range(groups)
        ]
    else:
        staged += [pltpu.make_async_copy(up_w, up_mine, stage_sem.at[0])]
    for c in staged:
        c.start()

    meta[...] = jnp.zeros_like(meta)
    meta[0 : facts.shape[0], :] = facts[...]
    known = mixers.shape[0]
    rest = jnp.zeros((SMALL - known, shard), f32)
    small[...] = jnp.concatenate([mixers[...].astype(f32), rest], axis=0).T.astype(bf16)
    tok = GroupGather(s, tokens, blocks(tok_all, rows), take(4))
    met = GroupGather(s, meta, lambda l: meta_all.at[l], take(4))
    cots = GroupGather(s, cot, blocks(cot_all, rows), take(4))
    mix = GroupGather(s, blocks(mix_all, rows)(s.l), blocks(mix_all, rows), take(4), own=False)
    outs = GroupGather(s, output_all.at[:, cols(s.l)], lambda l: output_all.at[:, cols(l)], take(4), own=False)
    atts = [
        LineGather(
            s, attend_w.at[:, pl.ds(pl.multiple_of(p * width + s.l * head_cols, head_cols), head_cols)],
            lambda w, p=p: attend_all.at[pl.ds(pl.multiple_of(w * shard, shard), shard), pl.ds(p * head_cols, head_cols)],
            take(4))
        for p in range(3)
    ]
    sml = LaneGather(s, small, blocks(small_all, shard), take(4))
    out = LineGather(s, output_w.at[:, cols(s.l)],
                     lambda w: output_all.at[pl.ds(pl.multiple_of(w * shard, shard), shard), cols(s.l)], take(4))
    up = LineGather(s, up_mine, blocks(up_all, shard), take(4))
    down = LineGather(s, down_w.at[pl.ds(pl.multiple_of(s.l * depth, depth), depth)], blocks(down_all, depth), take(4))
    swap = GroupSwap(s, blocks(mixed, rows), lambda l: attn_mixed.at[:, cols(l)], take(2))
    cot_swap = LaneSwap(s, blocks(packed_cot, slots), lambda w: cot_mine.at[w], take(2), range(groups // 2))
    mix_swap = LaneSwap(s, blocks(packed_mix, slots), lambda w: got_mix.at[s.l, w], take(2))

    def spread(d):
        w = s.w_peer(groups - d)
        return GroupGather(s, got_mix.at[s.l, w], lambda l: got_mix.at[l, w],
                           [spread_y.at[w], spread_c.at[w], spread_r.at[w], None], own=False)

    mix_spread = [spread(d) for d in range(groups)]

    s.met()
    sml.start()
    met.start()
    tok.start()
    for att in atts:
        att.start()
    for c in staged:
        c.wait()
    mine = meta[...].T
    valid, route = mine[:, 1:2], mine[:, 2:3].astype(jnp.int32)
    column = lax.broadcasted_iota(jnp.int32, (rows, SMALL), 1)
    hits = (column == route).astype(f32)
    earlier = lax.broadcasted_iota(jnp.int32, (rows, rows), 1) < lax.broadcasted_iota(jnp.int32, (rows, rows), 0)
    rank = jnp.sum(hits * mm(earlier.astype(f32).astype(bf16), hits.astype(bf16)), axis=1, keepdims=True).astype(jnp.int32)
    slot = (route // local) * slots + (route % local) * cap + rank
    spots = (slot == lax.broadcasted_iota(jnp.int32, (rows, groups * slots), 1)).astype(f32)
    place[...] = spots.astype(bf16)
    packed_cot[...] = mm((spots * valid).astype(bf16), cot[...], 0, 0).astype(bf16)
    def give(ref, to, k):
        done.append(pltpu.make_async_copy(ref, to, out_sem.at[k]))
        done[-1].start()

    done = []
    sml.forward()
    for att in atts:
        att.hop(1)
    met.forward()
    tok.forward()
    cots.start()
    for k in range(2, s.Z):
        for att in atts:
            att.hop(k)
    out.start()
    up.start()
    sml.arrive()
    met.arrive()
    gains = small_all[...].astype(f32).T
    tok.arrive()
    rows_norm(tok_all, gains[0:1, :], normed_out, rows * lanes)
    give(normed_out, normed_to, 0)
    for att in atts:
        att.arrive()
    give(attend_all, attend_to, 1)

    def project(i, carry):
        at = pl.ds(pl.multiple_of(i * Q_TILE, Q_TILE), Q_TILE)
        qkv[at, :] = mm(normed_out[at, :], attend_all[...]).astype(bf16)
        return carry

    for k in range(1, s.Z - 1):
        out.hop(k)
    lax.fori_loop(0, rows * lanes // Q_TILE, project, 0)
    give(qkv, qkv_to, 2)
    out.hop(s.Z - 1)
    up.hop(1)
    doc_cols = [meta_all[l].T[:, 0:1] for l in range(lanes)]
    for tile in range(lanes):
        attend_tile(tile, qkv, doc_cols, mixed, lse, mask, vt)
        swap.send(tile)
        if tile == 0:
            out.arrive()
            outs.start()
        if tile == lanes - 3:
            up.hop(2)
            down.start()
        if tile == lanes - 2:
            for k in range(3, s.Z):
                up.hop(k)
            cots.forward()
    down.hop(1)
    outs.forward()
    outs.arrive()
    give(output_all, output_to, 3)
    swap.arrive()
    attention_out[...] = mm(attn_mixed[...], output_all[...])
    gain = small_all[...].astype(f32).T[1:2, :]
    base = pl.multiple_of(s.l * rows, rows)

    def mid(i, carry):
        at = pl.ds(pl.multiple_of(i * 64, 64), 64)
        normed, _ = norm_stats(tokens[at, :].astype(f32) + attention_out[at, :])
        mix_all[pl.ds(pl.multiple_of(base + i * 64, 64), 64), :] = (normed * gain).astype(bf16)
        return carry

    lax.fori_loop(0, rows // 64, mid, 0)
    mix.start()
    down.hop(2)
    packed_mix[...] = mm(place[...], mix_all[pl.ds(base, rows), :], 0, 0).astype(bf16)
    mix_swap.start()
    mix.forward()
    for k in range(3, s.Z):
        down.hop(k)
    for d in range(groups):
        if d:
            mix_swap.got(s.w_peer(groups - d))
        else:
            mix_swap.own().wait()
        mix_spread[d].start()
    cot_swap.start()
    mix.arrive()
    give(mix_all, mix_to, 4)
    for task in [tok, met, cots, outs, sml, out, up, swap, *atts]:
        task.sent()
    for task in mix_spread:
        task.forward()
    for task in mix_spread:
        task.arrive()
    cots.arrive()
    up.arrive()
    down.arrive()
    cot_swap.arrive()
    for c in done:
        c.wait()
    for task in [mix, down, mix_swap, cot_swap] + mix_spread:
        task.sent()


def front(groups, lanes, local, cap, slots, tokens, cot, meta, small, attend_w, output_w, up_w, down_w):
    rows, width = tokens.shape
    X = 1 << ((groups.bit_length() - 1) // 2)
    Y = lanes // 2
    everyone = rows * lanes
    head_cols = width // lanes
    hidden = down_w.shape[0] // lanes * groups
    shard = attend_w.shape[0]
    vmem, anywhere = pl.BlockSpec(memory_space=pltpu.VMEM), pl.BlockSpec(memory_space=pl.ANY)
    dma = pltpu.SemaphoreType.DMA
    of = jax.ShapeDtypeStruct
    sems = []
    for _ in range(5):
        sems += GroupGather.sems(lanes)
    for _ in range(3):
        sems += LineGather.sems(groups, X)
    sems += LaneGather.sems(groups, X)
    for _ in range(3):
        sems += LineGather.sems(groups, X)
    sems += GroupSwap.sems(lanes) + LaneSwap.sems(groups) * 2
    outs = [
        (of((head_cols // PAIR, 2, everyone), f32), vmem),
        (of((rows, width), bf16), vmem),
        (of((rows, width), f32), vmem),
        (of((width, SMALL), bf16), vmem),
        (of((lanes, 8, rows), f32), vmem),
        (of((rows, groups * slots), bf16), vmem),
        (of((groups * slots, width), bf16), vmem),
    ]
    big = [(everyone, width), (everyone, 3 * head_cols), (width, 3 * head_cols), (width, width), (everyone, width)]
    outs += [(of(shape, bf16), anywhere) for shape in big]
    outs += [
        (of((lanes, groups, slots, width), bf16), anywhere),
        (of((groups, slots, width), bf16), anywhere),
        (of((everyone, width), bf16), anywhere),
        (of((width, hidden), bf16), anywhere),
        (of((hidden, width), bf16), anywhere),
    ]
    return pl.pallas_call(
        functools.partial(front_kernel, groups, lanes, local, cap, slots),
        out_shape=[o for o, _ in outs],
        in_specs=[vmem] * 4 + [anywhere] * 4,
        out_specs=[p for _, p in outs],
        scratch_shapes=[pltpu.VMEM(shape, bf16) for shape in big] + [
            pltpu.VMEM((everyone, width), bf16),
            pltpu.VMEM((shard, hidden), bf16),
            pltpu.VMEM((everyone, head_cols), bf16),
            pltpu.VMEM((everyone, Q_TILE), f32),
            pltpu.VMEM((head_cols // PAIR, PAIR, everyone), bf16),
            pltpu.VMEM((groups * slots, width), bf16),
            pltpu.VMEM((8, rows), f32),
            pltpu.VMEM((shard, SMALL), bf16),
            dma((5,)),
            dma((groups,)),
            dma((groups, Y)),
            dma((groups, Y)),
            dma((groups, lanes)),
        ] + sems,
        compiler_params=pltpu.CompilerParams(collective_id=0, has_side_effects=True, vmem_limit_bytes=56 * 2**20),
        cost_estimate=pl.CostEstimate(flops=8 * 10**9, bytes_accessed=10**8, transcendentals=0),
        name="front",
    )(tokens, cot, meta, small, attend_w, output_w, up_w, down_w)


def add_rows(dst, sources, step=32):
    def body(i, carry):
        at = pl.ds(pl.multiple_of(i * step, step), step)
        total = sources[0][at, :].astype(f32)
        for ref in sources[1:]:
            total += ref[at, :].astype(f32)
        dst[at, :] = total.astype(dst.dtype)
        return carry

    step = step if dst.shape[0] % step == 0 else dst.shape[0]
    lax.fori_loop(0, dst.shape[0] // step, body, 0)


class GroupScatter:
    def __init__(self, spot, part, held, from_core, from_y, sems, fine, chunks=None):
        self.s, self.part, self.from_core, self.from_y, self.fine = spot, part, from_core, from_y, fine
        self.staged = held is not None
        self.held = (lambda d: held.at[d]) if self.staged else (lambda d: part(spot.y_peer(d)))
        self.stage_sem, self.cs_sem, self.cr_sem, self.ys_sem, self.yr_sem = sems
        self.chunks = chunks or from_core.shape[1]

    @staticmethod
    def sems(L, chunks):
        dma = pltpu.SemaphoreType.DMA
        return [dma((L // 2,))] * 3 + [dma((L // 2, chunks))] * 2

    def stage(self, d):
        return pltpu.make_async_copy(self.part(self.s.y_peer(d)), self.held(d), self.stage_sem.at[d])

    def core_copy(self, d):
        s = self.s
        other = lax.rem(s.y + d, s.Y) * 2 + 1 - s.c
        return remote(self.part(other), self.from_core.at[d], self.cs_sem.at[d], self.cr_sem.at[d], s.g, s.core_peer())

    def y_copy(self, d, k):
        s = self.s
        src, dst = self.held(d), self.from_y.at[d - 1]
        if self.fine:
            src, dst = src.at[k], dst.at[k]
        return remote(src, dst, self.ys_sem.at[d, k], self.yr_sem.at[d, k], s.g, s.y_peer(d))

    def start(self):
        for d in range(self.s.Y):
            if self.staged:
                self.stage(d).start()
            self.core_copy(d).start()

    def ready(self):
        for d in range(self.s.Y):
            if self.staged:
                self.stage(d).wait()
            self.core_copy(d).wait_recv()

    def add(self, d, k):
        self.held(d)[k] = (self.held(d)[k].astype(f32) + self.from_core[d, k].astype(f32)).astype(bf16)

    def relay(self, k=0):
        for d in range(1, self.s.Y):
            if self.fine:
                self.add(d, k)
            else:

                def body(i, carry, d=d):
                    self.add(d, i)
                    return carry

                lax.fori_loop(0, self.chunks, body, 0)
            self.y_copy(d, k).start()

    def got(self, k=0):
        for d in range(1, self.s.Y):
            self.y_copy(d, k).wait_recv()

    def total(self, k):
        value = self.held(0)[k].astype(f32) + self.from_core[0, k].astype(f32)
        for d in range(1, self.s.Y):
            value += self.from_y[d - 1, k].astype(f32)
        return value

    def sent(self):
        for d in range(self.s.Y):
            self.core_copy(d).wait_send()
        for d in range(1, self.s.Y):
            for k in range(self.chunks if self.fine else 1):
                self.y_copy(d, k).wait_send()


class LaneScatter:
    def __init__(self, spot, part, held, from_x, from_z, sems):
        self.s, self.part, self.from_x, self.from_z = spot, part, from_x, from_z
        self.staged = held is not None
        self.held = (lambda d: held.at[d]) if self.staged else (lambda d: part(spot.z_peer(d)))
        self.stage_sem, self.xs_sem, self.xr_sem, self.zs_sem, self.zr_sem = sems

    @staticmethod
    def sems(W, X):
        dma = pltpu.SemaphoreType.DMA
        Z = W // X
        return [dma((Z,)), dma((X, Z)), dma((X, Z)), dma((Z,)), dma((Z,))]

    def stage(self, d):
        return pltpu.make_async_copy(self.part(self.s.z_peer(d)), self.held(d), self.stage_sem.at[d])

    def x_copy(self, e, d):
        s = self.s
        return remote(self.part(s.zx_peer(d, e)), self.from_x.at[e - 1, d], self.xs_sem.at[e, d], self.xr_sem.at[e, d],
                      s.x_peer(e), s.l)

    def z_copy(self, d):
        s = self.s
        return remote(self.held(d), self.from_z.at[d - 1], self.zs_sem.at[d], self.zr_sem.at[d], s.z_peer(d), s.l)

    def start(self):
        for d in [*range(1, self.s.Z), 0]:
            if self.staged:
                self.stage(d).start()
            for e in range(1, self.s.X):
                self.x_copy(e, d).start()

    def ready(self, d):
        if self.staged:
            self.stage(d).wait()
        for e in range(1, self.s.X):
            self.x_copy(e, d).wait_recv()

    def relay(self):
        for d in range(1, self.s.Z):
            self.ready(d)
            add_rows(self.held(d), [self.held(d)] + [self.from_x.at[e - 1, d] for e in range(1, self.s.X)])
            self.z_copy(d).start()

    def finish(self, dst):
        self.ready(0)
        for d in range(1, self.s.Z):
            self.z_copy(d).wait_recv()
        add_rows(dst, [self.held(0)] + [self.from_x.at[e - 1, 0] for e in range(1, self.s.X)]
                 + [self.from_z.at[d - 1] for d in range(1, self.s.Z)])

    def fold(self, dst):
        for d in range(self.s.Z):
            self.ready(d)
            add_rows(dst.at[d], [self.held(d)] + [self.from_x.at[e - 1, d] for e in range(1, self.s.X)])

    def x_sent(self):
        for d in range(self.s.Z):
            for e in range(1, self.s.X):
                self.x_copy(e, d).wait_send()

    def sent(self):
        self.x_sent()
        for d in range(1, self.s.Z):
            self.z_copy(d).wait_send()


class ZScatter(LaneScatter):
    def __init__(self, spot, held, from_z, sems):
        self.s, self.held, self.from_z = spot, held, from_z
        self.zs_sem, self.zr_sem = sems

    def start(self):
        for d in range(1, self.s.Z):
            self.z_copy(d).start()

    def finish(self, dst):
        for d in range(1, self.s.Z):
            self.z_copy(d).wait_recv()
        add_rows(dst, [self.held(0)] + [self.from_z.at[d - 1] for d in range(1, self.s.Z)])

    def sent(self):
        for d in range(1, self.s.Z):
            self.z_copy(d).wait_send()


def attend_back_tile(tile, qkv_ref, doc_cols, lse_ref, grad_ref, out_ref, mask_ref, dk_ref, dv_ref):
    cols = grad_ref.shape[1]
    extent = (tile + 1) * Q_TILE
    here, seen = pl.ds(tile * Q_TILE, Q_TILE), pl.ds(0, extent)
    mask_tile(tile, doc_cols, mask_ref)

    def pair_step(pair, carry):
        q_cols = pl.ds(pl.multiple_of(pair * PAIR, PAIR), PAIR)
        k_cols = pl.ds(pl.multiple_of(cols + pair * PAIR, PAIR), PAIR)
        v_cols = pl.ds(pl.multiple_of(2 * cols + pair * PAIR, PAIR), PAIR)
        queries = qkv_ref[here, q_cols] * jnp.asarray(HEAD_DIM**-0.5, bf16)
        keys, values = qkv_ref[seen, k_cols], qkv_ref[seen, v_cols]
        grads = grad_ref[here, q_cols]
        dq = jnp.zeros((PAIR, Q_TILE), f32)
        for half in range(2):
            on = head_mask(half)
            q_one = jnp.where(on, queries, jnp.zeros_like(queries))
            g_one = jnp.where(on, grads, jnp.zeros_like(grads))
            probs = jnp.exp(mm(keys, q_one, 1, 1) + mask_ref[seen, :] - lse_ref[pair, pl.ds(half, 1), here])
            dv_ref[pair, seen, :] += mm(probs.astype(bf16), g_one)
            back = mm(values, g_one, 1, 1)
            low = (probs * (back - jnp.sum(probs * back, axis=0, keepdims=True))).astype(bf16)
            dk_ref[pair, seen, :] += mm(low, q_one)
            got = mm(keys, low, 0, 0)
            sublanes = lax.broadcasted_iota(jnp.int32, (PAIR, 1), 0)
            dq = jnp.where((sublanes // HEAD_DIM) == half, got, dq)
        out_ref[here, q_cols] = (dq.T * HEAD_DIM**-0.5).astype(bf16)
        return carry

    lax.fori_loop(0, cols // PAIR, pair_step, 0)


def finish_kernel(
    x_ref, hidden_ref, act_ref, grad_ref, attend_ref, output_ref, up_ref, down_ref, small_ref, layer_ref, tokens_ref,
    expert_up, expert_down, attend_out, output_out, up_out, down_out, layer_out, tokens_out, gain_0, gain_1, blend, router, root,
):
    expert_up[0] = mm(x_ref[0], hidden_ref[0], 0, 0)
    expert_down[0] = mm(act_ref[0], grad_ref[0], 0, 0)
    lanes, _, units = up_ref.shape
    width = output_out.shape[1]
    for ref, out, parts in ((attend_ref, attend_out, 3), (output_ref, output_out, 1), (up_ref, up_out, units // SMALL)):
        n = ref.shape[2] // parts
        for p in range(parts):
            for l in range(lanes):
                out[:, (p * lanes + l) * n : (p * lanes + l + 1) * n] = ref[l, :, p * n : (p + 1) * n].astype(f32)
    down_out[...] = down_ref[...].astype(f32)
    layer_out[...] = layer_ref[...]
    tokens_out[...] = tokens_ref[...]
    small = small_ref[...]
    gain_0[...] = small[0:1]
    gain_1[...] = small[1:2]
    blend[...] = small[2:4]
    router[...] = small[4 : 4 + router.shape[0]]
    sums = small[small.shape[0] - 1 :]
    root[...] = jnp.sqrt(sums / (jnp.maximum(sums[:, 4:5], 1.0) * width))[:, 0:4]


def finish(experts, x, hidden, act, grad, attend_all, output_all, up_all, down_all, small, layer, tokens):
    local, rows, width = x.shape
    units = hidden.shape[2]
    lanes, shard, _ = up_all.shape
    tile = 256
    steps = local * width // tile
    turns = width // tile
    down_all = down_all.reshape(-1, width)
    count = lambda n: n // steps
    of = jax.ShapeDtypeStruct
    tall = pl.BlockSpec((1, rows, tile), lambda e, m: (e, 0, m))
    whole = lambda n: pl.BlockSpec((1, rows, n), lambda e, m: (e, 0, 0))
    thin = lambda a: pl.BlockSpec((lanes, count(shard), a.shape[2]), lambda e, m: (0, e * turns + m, 0))
    flat = lambda n, c: pl.BlockSpec((count(n), c), lambda e, m: (e * turns + m, 0))
    fixed = lambda *s: pl.BlockSpec(s, lambda e, m: (0, 0))
    outs = [
        (of((local, width, units), f32), pl.BlockSpec((1, tile, units), lambda e, m: (e, m, 0))),
        (of((local, units, width), f32), pl.BlockSpec((1, tile, width), lambda e, m: (e, m, 0))),
        (of((shard, 3 * width), f32), flat(shard, 3 * width)),
        (of((shard, width), f32), flat(shard, width)),
        (of((shard, lanes * units), f32), flat(shard, lanes * units)),
        (of(down_all.shape, f32), flat(*down_all.shape)),
        (of(layer.shape, bf16), flat(*layer.shape)),
        (of(tokens.shape, bf16), flat(*tokens.shape)),
        (of((1, shard), f32), fixed(1, shard)),
        (of((1, shard), f32), fixed(1, shard)),
        (of((2, shard), f32), fixed(2, shard)),
        (of((experts, shard), f32), fixed(experts, shard)),
        (of((1, 4), f32), fixed(1, 4)),
    ]
    return pl.pallas_call(
        finish_kernel,
        grid=(local, turns),
        out_shape=[o for o, _ in outs],
        in_specs=[
            tall, whole(units), tall, whole(width), thin(attend_all), thin(output_all), thin(up_all),
            flat(*down_all.shape), fixed(*small.shape), flat(*layer.shape), flat(*tokens.shape),
        ],
        out_specs=[p for _, p in outs],
        compiler_params=pltpu.CompilerParams(vmem_limit_bytes=63 * 2**20),
        cost_estimate=pl.CostEstimate(flops=4 * local * rows * width * units, bytes_accessed=4 * 10**7, transcendentals=0),
        name="finish",
    )(x, hidden, act, grad, attend_all, output_all, up_all, down_all, small, layer, tokens)


def take_from(sems):
    sems = list(sems)

    def take(n):
        out = sems[:n]
        del sems[:n]
        return out

    return take


def picked(logits, first, count):
    columns = lax.broadcasted_iota(jnp.int32, logits.shape, 1)
    return soft_max(jnp.where((columns >= first) & (columns < first + count), logits, masked_score))


def middle_kernel(
    groups, lanes, local, cap, experts,
    small, meta_all, place,
    mix_in, cot_in, up_in, down_in, got_mix_in, cot_mine, packed_cot, expert_up, expert_down,
    grad_mix, dense_out, grad_small, mine_up, down_half, tok_part, mix_e_out, grad_e_out, act_e_out, hidden_e_out,
    mix, cot, up, down, act, hidden, got_mix, got_cot, mix_e, grad_e, act_e, hidden_e, expert_in, expert_to,
    mx, mx_c, mx_y, dn, dn_c, dn_y, bk_c, bk_y, gu, gu_x, gu_z, gd, gd_x, ret_back, got_back, dots, coefs,
    load_sem, out_sem, spread_y, spread_c, spread_r, spread_o, *sems,
):
    s = Spot(groups, lanes)
    s.greet()
    everyone, width = mix.shape
    rows = everyone // lanes
    units = up.shape[1]
    slots = got_mix.shape[2]
    shard = width // groups
    rows_e = mix_e.shape[1]
    tile = 256
    step = 64
    take = take_from(sems)

    def blocks(ref, n):
        return lambda i: ref.at[pl.ds(pl.multiple_of(i * n, n), n)]

    def part(i, n=tile):
        return pl.ds(pl.multiple_of(i * n, n), n)

    def load(i, src, dst):
        return pltpu.make_async_copy(src, dst, load_sem.at[i])

    cot_swap = LaneSwap(s, blocks(packed_cot, slots), lambda w: got_cot.at[s.l, w], take(2), range(groups // 2, groups))

    def spread(d):
        w = s.w_peer(groups - d)
        first = d < groups // 2
        return GroupGather(s, cot_mine.at[w] if first else got_cot.at[s.l, w], lambda l: got_cot.at[l, w],
                           [spread_y.at[w], spread_c.at[w], spread_r.at[w], spread_o.at[w]], own=first)

    cot_spread = [spread(d) for d in range(groups)]
    mxs = GroupScatter(s, lambda l: mx.at[l], None, mx_c, mx_y, take(5), False)
    dns = GroupScatter(s, lambda l: dn.at[l], None, dn_c, dn_y, take(5), False)
    near = groups // 2
    bks = [
        GroupScatter(s, lambda l, h=h: got_cot.at[l, pl.ds(h * near, near)], None, bk_c.at[h], bk_y.at[h], take(5), True, near)
        for h in range(2)
    ]
    ups = LaneScatter(s, blocks(gu, shard), None, gu_x, gu_z, take(5))
    dws = LaneScatter(s, blocks(gd, shard), None, gd_x, None, take(5))
    back_swap = LaneSwap(s, blocks(ret_back, slots), blocks(got_back, slots), take(2))

    loads = [load(i, a, b) for i, (a, b) in enumerate([
        (mix_in, mix), (up_in, up), (cot_in, cot), (down_in, down), (got_mix_in, got_mix),
        (expert_up.at[0], expert_in), (expert_down.at[0], expert_to)])]
    more_loads = [load(7, expert_up.at[1], up), load(8, expert_down.at[1], down)]

    def branch(x, grad, w_in, w_to, act_ref, hidden_ref, count):
        dots[pl.ds(0, count), :] = jnp.zeros((count, SMALL), f32)

        def body(n, carry):
            value, slope = gelu_both(mm(x[...], w_in[:, part(n)]))
            value = value.astype(bf16)
            act_ref[pl.ds(0, count), part(n)] = value
            back = mm(grad[...], w_to[part(n), :], 1, 1)
            hidden_ref[pl.ds(0, count), part(n)] = (slope * back).astype(bf16)
            both = value.astype(f32) * back
            dots[pl.ds(0, count), :] += sum([both[:, i * SMALL : (i + 1) * SMALL] for i in range(1, tile // SMALL)], both[:, :SMALL])
            return carry

        lax.fori_loop(0, units // tile, body, 0)
        return jnp.sum(dots[pl.ds(0, count), :], axis=1, keepdims=True)

    for c in loads[:4]:
        c.start()
    s.met()
    cot_swap.start()
    for task in cot_spread[: groups // 2]:
        task.start()
    for c in loads[4:]:
        c.start()
    for c in loads[:4]:
        c.wait()
    columns = lax.broadcasted_iota(jnp.int32, (everyone, SMALL), 1)

    coefs[...] = picked(mm(mix[...], small[...]), 2, 2)
    for l in range(lanes):
        at = pl.ds(l * rows, rows)
        valid = meta_all[l].T[:, 1:2]
        cot[at, :] = (coefs[at, 3:4] * (cot[at, :].astype(f32) * valid)).astype(bf16)
    dot = branch(mix, cot, up, down, act, hidden, everyone)
    for d in range(groups // 2, groups):
        cot_swap.due(d)
        cot_spread[d].start()
    sign = jnp.where(columns == 3, 1.0, 0.0) - jnp.where(columns == 2, 1.0, 0.0)
    logits = (sign * (coefs[:, 2:3] * dot)).astype(bf16)
    grad_small[...] = mm(logits, mix[...], 0, 0)

    def up_grad(m, carry):
        gu[part(m), :] = mm(mix[:, part(m)], hidden[...], 0, 0).astype(bf16)
        return carry

    lax.fori_loop(0, width // tile, up_grad, 0)
    ups.start()
    def down_grad(m, carry):
        gd[part(m), :] = mm(act[:, part(m)], cot[...], 0, 0).astype(bf16)
        return carry

    lax.fori_loop(0, units // tile, down_grad, 0)
    dws.start()

    def mix_grad(n, carry):
        value = mm(hidden[...], up[part(n), :], 1, 1) + mm(logits, small[part(n), :], 1, 1)
        mx[:, :, :, part(n)] = value.astype(bf16).reshape(lanes, rows // step, step, tile)
        return carry

    lax.fori_loop(0, width // tile, mix_grad, 0)
    mxs.start()

    def out_part(n, carry):
        value = mm(act[...], down[:, part(n)])
        dn[:, :, :, part(n)] = value.astype(bf16).reshape(lanes, rows // step, step, tile)
        return carry

    lax.fori_loop(0, width // tile, out_part, 0)
    dns.start()
    for c in more_loads:
        c.start()
    for c in loads[4:]:
        c.wait()

    def apart(src, dst):
        def body(j, carry):
            pair = []
            for i in range(2):
                b = 2 * j + i
                pair.append(src[b % lanes, s.w_at(b // lanes)].astype(f32))
            for e in range(local):
                both = [p[e * cap : (e + 1) * cap] for p in pair]
                dst[e, part(j, 2 * cap), :] = jnp.concatenate(both, axis=0).astype(bf16)
            return carry

        lax.fori_loop(0, lanes * groups // 2, body, 0)

    def together(sources, dst, first=0, last=lanes * groups // 2):
        def body(j, carry):
            values = [src[part(j, 2 * cap), :].astype(f32) for src in sources]
            for i in range(2):
                b = 2 * j + i
                dst[b % lanes, b // lanes] = jnp.concatenate([v[i * cap : (i + 1) * cap] for v in values], axis=0).astype(bf16)
            return carry

        lax.fori_loop(first, last, body, 0)

    apart(got_mix, mix_e)
    for task in cot_spread:
        task.forward()
    mxs.ready()
    mxs.relay()
    for task in cot_spread:
        task.arrive()
    apart(got_cot, grad_e)

    backs, toks = [act, hidden], [mix, cot]
    outs = []
    few = rows_e // 2
    columns = lax.broadcasted_iota(jnp.int32, (few, SMALL), 1)

    def rows_out(h, e):
        w_to = expert_to if e == 0 else down
        at = pl.ds(h * few, few)

        def body(n, carry):
            toks[e][at, part(n)] = mm(act_e[e, at, :], w_to[:, part(n)]).astype(bf16)
            return carry

        lax.fori_loop(0, width // tile, body, 0)

    for h in range(2):
        at = pl.ds(h * few, few)
        for e in range(local):
            w_in, w_to = (expert_in, expert_to) if e == 0 else (up, down)
            if h == 0 and e:
                for c in more_loads:
                    c.wait()
            x, grad = mix_e.at[e, at], grad_e.at[e, at]
            scores = mm(x[...], small[...])
            blend, router = picked(scores, 2, 2), picked(scores, 4, experts)
            own = columns == 4 + s.g * local + e
            chosen = jnp.sum(jnp.where(own, router, 0.0), axis=1, keepdims=True)
            grad[...] = (blend[:, 2:3] * chosen * grad[...].astype(f32)).astype(bf16)
            shares = jnp.where(own, 1.0, 0.0) - router
            shares += blend[:, 3:4] * (jnp.where(columns == 2, 1.0, 0.0) - jnp.where(columns == 3, 1.0, 0.0))
            coefs[pl.ds(0, few), :] = shares
            dot = branch(x, grad, w_in, w_to, act_e.at[e, at], hidden_e.at[e, at], few)
            logits = (dot * coefs[pl.ds(0, few), :]).astype(bf16)
            grad_small[...] += mm(logits, x[...], 0, 0)

            def rows_back(n, carry, e=e, w_in=w_in, logits=logits, at=at):
                value = mm(hidden_e[e, at, :], w_in[part(n), :], 1, 1) + mm(logits, small[part(n), :], 1, 1)
                backs[e][at, part(n)] = value.astype(bf16)
                return carry

            lax.fori_loop(0, width // tile, rows_back, 0)
            if h == 0 and e == 0:
                ups.relay()
                dns.ready()
                dns.relay()
            if h == 1 and e == 0:
                bks[0].ready()
                for k in range(near):
                    bks[0].relay(k)
        if h == 0:
            for task in cot_spread:
                task.sent()
        together([b.at[pl.ds(0, rows_e)] for b in backs], got_cot, h * lanes * groups // 4, (h + 1) * lanes * groups // 4)
        bks[h].start()

    def hand_back(h):
        for k in range(near):
            p = h * near + k
            w = s.w_at(p)
            bks[h].got(k)
            ret_back[pl.ds(pl.multiple_of(w * slots, slots), slots), :] = bks[h].total(k).astype(bf16)
            if p < groups - 1:
                back_swap.copy(p + 1).start()
            else:
                back_swap.own().start()

    rows_out(0, 0)
    bks[1].ready()
    for k in range(near):
        bks[1].relay(k)
    hand_back(0)
    rows_out(0, 1)
    rows_out(1, 0)
    rows_out(1, 1)
    for e in range(local):
        for i, (a, b) in enumerate([(mix_e, mix_e_out), (grad_e, grad_e_out), (act_e, act_e_out), (hidden_e, hidden_e_out)]):
            outs.append(pltpu.make_async_copy(a.at[e], b.at[e], out_sem.at[4 * e + i]))
            outs[-1].start()
    together([t.at[pl.ds(0, rows_e)] for t in toks], got_mix)
    outs.append(pltpu.make_async_copy(got_mix, tok_part, out_sem.at[4 * local]))
    outs[-1].start()

    def totals(scatter, dst):
        scatter.got()

        def body(k, carry):
            dst[pl.ds(pl.multiple_of(k * step, step), step), :] = scatter.total(k).astype(dst.dtype)
            return carry

        lax.fori_loop(0, scatter.chunks, body, 0)

    totals(mxs, grad_mix)
    hand_back(1)
    dws.fold(down_half)
    totals(dns, dense_out)
    ups.finish(mine_up)
    back_swap.arrive()
    grad_mix[...] += mm(place[...], got_back[...])
    for c in outs:
        c.wait()
    dws.x_sent()
    for task in [cot_swap, mxs, dns, *bks, ups, back_swap]:
        task.sent()


def middle(groups, lanes, local, cap, experts, slots, inputs, placed):
    rows, width = inputs[2].shape[0], inputs[0].shape[0]
    X = 1 << ((groups.bit_length() - 1) // 2)
    Y, Z = lanes // 2, groups // X
    everyone = rows * lanes
    shard = width // groups
    units = placed[2].shape[1]
    rows_e = lanes * groups * cap
    vmem, anywhere = pl.BlockSpec(memory_space=pltpu.VMEM), pl.BlockSpec(memory_space=pl.ANY)
    dma = pltpu.SemaphoreType.DMA
    of = jax.ShapeDtypeStruct
    low = lambda *shape: pltpu.VMEM(shape, bf16)
    wide = lambda *shape: pltpu.VMEM(shape, f32)
    expert_rows = (local, rows_e, width)
    outs = [
        (of((rows, width), f32), vmem),
        (of((rows, width), bf16), vmem),
        (of((SMALL, width), f32), vmem),
        (of((shard, units), bf16), vmem),
        (of((Z, shard, width), bf16), vmem),
        (of((lanes, groups, slots, width), bf16), anywhere),
        (of(expert_rows, bf16), anywhere),
        (of(expert_rows, bf16), anywhere),
        (of((local, rows_e, units), bf16), anywhere),
        (of((local, rows_e, units), bf16), anywhere),
    ]
    scratch = [low(everyone, width), low(everyone, width), low(width, units), low(units, width)]
    scratch += [low(everyone, units), low(everyone, units)]
    scratch += [low(lanes, groups, slots, width)] * 2
    scratch += [low(*expert_rows), low(*expert_rows), low(local, rows_e, units), low(local, rows_e, units)]
    scratch += [low(width, units), low(units, width)]
    scratch += [low(lanes, rows // 64, 64, width), low(Y, rows // 64, 64, width), low(Y - 1, rows // 64, 64, width)] * 2
    scratch += [low(2, Y, groups // 2, slots, width), low(2, Y - 1, groups // 2, slots, width)]
    scratch += [low(width, units), low(X - 1, Z, shard, units), low(Z - 1, shard, units)]
    scratch += [low(units, width), low(X - 1, Z, shard, width)]
    scratch += [low(groups * slots, width)] * 2 + [wide(everyone, SMALL)] * 2
    scratch += [dma((9,)), dma((4 * local + 1,)), dma((groups, Y)), dma((groups, Y)), dma((groups, lanes)), dma((groups, 1))]
    scratch += LaneSwap.sems(groups) + GroupScatter.sems(lanes, 1) * 2 + GroupScatter.sems(lanes, groups // 2) * 2
    scratch += LaneScatter.sems(groups, X) * 2 + LaneSwap.sems(groups)
    return pl.pallas_call(
        functools.partial(middle_kernel, groups, lanes, local, cap, experts),
        out_shape=[o for o, _ in outs],
        in_specs=[vmem] * len(inputs) + [anywhere] * len(placed),
        out_specs=[p for _, p in outs],
        scratch_shapes=scratch,
        compiler_params=pltpu.CompilerParams(collective_id=2, has_side_effects=True, vmem_limit_bytes=62 * 2**20),
        cost_estimate=pl.CostEstimate(flops=35 * 10**9, bytes_accessed=10**8, transcendentals=0),
        name="middle",
    )(*inputs, *placed)


def back_kernel(
    groups, lanes, experts,
    tokens, cot, small, attention_out, attn_mixed, place, meta_all, lse, grad_small, grad_mix_in, dense_out,
    mine_up, down_half, tok_part, qkv_in, output_in, attend_in, normed_in,
    layer_out, grad_tokens, small_out, all_attend, all_output, all_up, all_down,
    qkv, output_all, attend_all, normed, tk_h, tk_c, tk_y,
    go, go_c, go_y, gn, gn_c, gn_y, dw_z, ga, ga_x, ga_z, gl, gl_x, gl_z,
    sm, sm_x, sm_z, sm_mine, sm_all, ret_tok, got_tok, grad_mix, grad_mid, grad_attn, grad_mixed,
    grad_heads, grad_qkv, mask, dk, dv, valid_cols, mine_attend, mine_output, mine_down, stage_sem, *sems,
):
    s = Spot(groups, lanes)
    s.greet()
    rows, width = tokens.shape
    head_cols = width // lanes
    slots = place.shape[1] // groups
    shard = width // groups
    take = take_from(sems)
    step = 64

    def blocks(ref, n):
        return lambda i: ref.at[pl.ds(pl.multiple_of(i * n, n), n)]

    def cols(i):
        return pl.ds(pl.multiple_of(i * head_cols, head_cols), head_cols)

    loads = [
        pltpu.make_async_copy(src, dst, stage_sem.at[i])
        for i, (src, dst) in enumerate(
            [(output_in, output_all), (qkv_in, qkv), (attend_in, attend_all), (normed_in, normed)])
    ]
    tk = GroupScatter(s, lambda l: tok_part.at[l], tk_h, tk_c, tk_y, take(5), True)
    gos = GroupScatter(s, lambda l: go.at[l], None, go_c, go_y, take(5), False)
    gns = GroupScatter(s, lambda l: gn.at[l], None, gn_c, gn_y, take(5), False)
    dws = ZScatter(s, lambda d: down_half.at[d], dw_z, take(2))
    gas = [LaneScatter(s, blocks(ga.at[p], shard), None, ga_x.at[p], ga_z.at[p], take(5)) for p in range(3)]
    gls = LaneScatter(s, blocks(gl, shard), None, gl_x, gl_z, take(5))
    sms = LaneScatter(s, lambda w: sm.at[w], None, sm_x, sm_z, take(5))
    tok_swap = LaneSwap(s, blocks(ret_tok, slots), blocks(got_tok, slots), take(2))
    heads = GroupSwap(s, lambda l: grad_mixed.at[:, cols(l)], blocks(grad_heads, rows), take(2))
    f_attend = GroupGather(s, mine_attend, lambda l: all_attend.at[l], take(4))
    f_output = GroupGather(s, mine_output, lambda l: all_output.at[l], take(4))
    f_up = GroupGather(s, mine_up, lambda l: all_up.at[l], take(4))
    f_down = GroupGather(s, mine_down, lambda l: all_down.at[l], take(4))
    f_small = GroupGather(s, sm_mine, lambda l: sm_all.at[l], take(4))

    def pass_on(first, last):
        for p in range(first, last):
            tk.relay(p)

    def hand_back(first, last):
        for p in range(first, last):
            w = s.w_at(p)
            tk.got(p)
            ret_tok[pl.ds(pl.multiple_of(w * slots, slots), slots), :] = tk.total(p).astype(bf16)
            if p < groups - 1:
                tok_swap.copy(p + 1).start()
            else:
                tok_swap.own().start()

    def totals(scatter, dst):
        scatter.got()

        def body(k, carry):
            dst[pl.ds(pl.multiple_of(k * step, step), step), :] = scatter.total(k).astype(dst.dtype)
            return carry

        lax.fori_loop(0, scatter.chunks, body, 0)

    def over_rows(body, init):
        return lax.fori_loop(0, rows // step, lambda i, c: body(pl.ds(pl.multiple_of(i * step, step), step), c), init)

    for c in loads:
        c.start()
    dk[...] = jnp.zeros_like(dk)
    dv[...] = jnp.zeros_like(dv)
    gains = small[...].astype(f32).T
    mine = meta_all[s.l].T
    valid_cols[...] = jnp.broadcast_to(mine[:, 1:2], valid_cols.shape)

    def mid(at, gain_sum):
        normed_v, scale = norm_stats(tokens[at, :].astype(f32) + attention_out[at, :])
        grad = grad_mix_in[at, :]
        value = cot[at, :].astype(f32) * valid_cols[at, 0:1] + norm_back(normed_v, scale, gains[1:2, :], grad)
        grad_mid[at, :] = value
        grad_attn[at, :] = value.astype(bf16)
        return gain_sum + jnp.sum(grad * normed_v, axis=0, keepdims=True)

    mixer_gain_grad = over_rows(mid, jnp.zeros((1, width), f32))
    loads[0].wait()
    grad_mixed[...] = mm(grad_attn[...], output_all[...], 1, 1).astype(bf16)
    s.met()
    for l in range(lanes):
        heads.send(l)
    tk.start()
    dws.start()

    def out_grad(m, carry):
        value = mm(attn_mixed[:, cols(m)], grad_attn[...], 0, 0).astype(bf16)
        parts = head_cols // step
        for l in range(lanes):
            go[l, pl.ds(m * parts, parts)] = value[:, l * head_cols : (l + 1) * head_cols].reshape(parts, step, head_cols)
        return carry

    lax.fori_loop(0, lanes, out_grad, 0)
    gos.start()
    for c in loads[1:]:
        c.wait()
    heads.arrive()
    tk.ready()
    pass_on(0, groups)
    f_up.start()
    doc_cols = [meta_all[l].T[:, 0:1] for l in range(lanes)]
    for tile in range(lanes):
        attend_back_tile(tile, qkv, doc_cols, lse, grad_heads, grad_qkv, mask, dk, dv)
        if tile == 0:
            gos.ready()
            gos.relay()
        if tile == 2:
            hand_back(0, groups // 2)
    for pair in range(head_cols // PAIR):
        grad_qkv[:, head_cols + pair * PAIR : head_cols + (pair + 1) * PAIR] = dk[pair].astype(bf16)
        grad_qkv[:, 2 * head_cols + pair * PAIR : 2 * head_cols + (pair + 1) * PAIR] = dv[pair].astype(bf16)

    for p in range(3):

        def weight_grad(m, carry, p=p):
            value = mm(normed[:, cols(m)], grad_qkv[:, p * head_cols : (p + 1) * head_cols], 0, 0)
            ga[p, pl.ds(pl.multiple_of(m * head_cols, head_cols), head_cols), :] = value.astype(bf16)
            return carry

        lax.fori_loop(0, lanes, weight_grad, 0)
        gas[p].start()

    def rows_grad(l, carry):
        value = mm(grad_qkv[pl.ds(pl.multiple_of(l * rows, rows), rows), :], attend_all[...], 1, 1)
        gn[l] = value.astype(bf16).reshape(rows // step, step, width)
        return carry

    lax.fori_loop(0, lanes, rows_grad, 0)
    gns.start()
    gns.ready()
    gns.relay()
    hand_back(groups // 2, groups)
    gas[0].relay()
    totals(gos, gl)
    gls.start()
    gas[1].relay()
    gas[2].relay()
    f_up.forward()
    tok_swap.arrive()

    def layer(at, sums):
        attention = attention_out[at, :]
        residual = tokens[at, :].astype(f32) + attention
        normed_v, _ = norm_stats(residual)
        mix = (normed_v * gains[1:2, :]).astype(bf16)
        logits = mm(mix, small[...])
        blend, router = picked(logits, 2, 2), picked(logits, 4, experts)
        columns = lax.broadcasted_iota(jnp.int32, logits.shape, 1)
        route = valid_cols[at, 1:2].astype(jnp.int32)
        chosen = jnp.sum(jnp.where(columns == 4 + route, router, 0.0), axis=1, keepdims=True)
        ffn = blend[:, 2:3] * chosen * mm(place[at, :], got_tok[...]) + blend[:, 3:4] * dense_out[at, :].astype(f32)
        full = residual + ffn
        layer_out[at, :] = full.astype(bf16)
        valid = valid_cols[at, 0:1]
        got = [jnp.sum(valid * v * v, axis=(0, 1), keepdims=True) for v in (residual, full, attention, ffn)]
        got.append(jnp.sum(valid, axis=(0, 1), keepdims=True))
        return tuple(a + b for a, b in zip(sums, got))

    lane_of = lax.broadcasted_iota(jnp.int32, valid_cols.shape, 1)
    valid_cols[...] = jnp.where(lane_of == 1, mine[:, 2:3], mine[:, 1:2])
    sums = over_rows(layer, tuple(jnp.zeros((1, 1), f32) for _ in range(5)))
    totals(gns, grad_mix)

    def first(at, gain_sum):
        normed_v, scale = norm_stats(tokens[at, :].astype(f32))
        grad = grad_mix[at, :]
        grad_tokens[at, :] = (grad_mid[at, :] + norm_back(normed_v, scale, gains[0:1, :], grad)).astype(bf16)
        return gain_sum + jnp.sum(grad * normed_v, axis=0, keepdims=True)

    attend_gain_grad = over_rows(first, jnp.zeros((1, width), f32))
    used = sm_mine.shape[0]
    feature = lax.broadcasted_iota(jnp.int32, (used, shard), 0)
    place_of = lax.broadcasted_iota(jnp.int32, (used, shard), 1)
    tail = jnp.zeros((used, shard), f32)
    for i, v in enumerate(sums):
        tail = jnp.where(place_of == i, v, tail)
    for w in range(groups):
        here = slice(w * shard, (w + 1) * shard)
        value = jnp.where(feature == used - 1, tail, grad_small[0:used, here])
        value = jnp.where(feature == 0, attend_gain_grad[:, here], value)
        sm[w] = jnp.where(feature == 1, mixer_gain_grad[:, here], value)
    sms.start()
    gls.relay()
    dws.finish(mine_down)
    f_down.start()
    sms.relay()
    for p in range(3):
        gas[p].finish(mine_attend.at[:, pl.ds(p * head_cols, head_cols)])
    f_attend.start()
    gls.finish(mine_output)
    f_output.start()
    sms.finish(sm_mine)
    f_small.start()
    gathers = [f_up, f_down, f_attend, f_output, f_small]
    for task in gathers[1:]:
        task.forward()
    for task in gathers:
        task.arrive()
    small_out[...] = sum([sm_all[l] for l in range(1, lanes)], sm_all[0])
    for task in [tk, gos, gns, dws, *gas, gls, sms, tok_swap, heads] + gathers:
        task.sent()


def back(groups, lanes, experts, slots, inputs, placed):
    tokens = inputs[0]
    rows, width = tokens.shape
    X = 1 << ((groups.bit_length() - 1) // 2)
    Y, Z = lanes // 2, groups // X
    everyone = rows * lanes
    head_cols = width // lanes
    shard = width // groups
    hidden = inputs[-2].shape[1]
    vmem, anywhere = pl.BlockSpec(memory_space=pltpu.VMEM), pl.BlockSpec(memory_space=pl.ANY)
    dma = pltpu.SemaphoreType.DMA
    of = jax.ShapeDtypeStruct
    pairs = head_cols // PAIR
    low = lambda *shape: pltpu.VMEM(shape, bf16)
    wide = lambda *shape: pltpu.VMEM(shape, f32)

    def group_bufs(c, r, n, held=True):
        return ([low(Y, c, r, n)] if held else [low(lanes, c, r, n)]) + [low(Y, c, r, n), low(Y - 1, c, r, n)]

    def lane_bufs(n, held=True):
        return ([low(Z, shard, n)] if held else [low(width, n)]) + [low(X - 1, Z, shard, n), low(Z - 1, shard, n)]

    scratch = [low(everyone, 3 * head_cols), low(width, width), low(width, 3 * head_cols), low(everyone, width)]
    scratch += group_bufs(groups, slots, width)
    scratch += group_bufs(width // 64, 64, head_cols, False) + group_bufs(rows // 64, 64, width, False)
    scratch += [low(Z - 1, shard, width)] + [low(3, width, head_cols), low(3, X - 1, Z, shard, head_cols), low(3, Z - 1, shard, head_cols)] + lane_bufs(head_cols, False)
    used = -(-(5 + experts) // 8) * 8
    scratch += [wide(groups, used, shard), wide(X - 1, Z, used, shard), wide(Z - 1, used, shard)]
    scratch += [wide(used, shard), wide(lanes, used, shard)]
    scratch += [low(groups * slots, width)] * 2
    scratch += [wide(rows, width), wide(rows, width), low(rows, width), low(rows, width)]
    scratch += [low(everyone, head_cols), low(everyone, 3 * head_cols), wide(everyone, Q_TILE)]
    scratch += [wide(pairs, everyone, PAIR)] * 2 + [wide(rows, SMALL)]
    scratch += [low(shard, 3 * head_cols), low(shard, head_cols), low(shard, width)]
    scratch += [dma((4,))]
    scratch += GroupScatter.sems(lanes, groups) + GroupScatter.sems(lanes, 1) * 2
    scratch += [dma((Z,))] * 2 + LaneScatter.sems(groups, X) * 5
    scratch += LaneSwap.sems(groups) + GroupSwap.sems(lanes)
    scratch += GroupGather.sems(lanes) * 5
    outs = [
        (of((rows, width), bf16), vmem),
        (of((rows, width), bf16), vmem),
        (of((used, shard), f32), vmem),
        (of((lanes, shard, 3 * head_cols), bf16), anywhere),
        (of((lanes, shard, head_cols), bf16), anywhere),
        (of((lanes, shard, hidden), bf16), anywhere),
        (of((lanes, shard, width), bf16), anywhere),
    ]
    return pl.pallas_call(
        functools.partial(back_kernel, groups, lanes, experts),
        out_shape=[o for o, _ in outs],
        in_specs=[vmem] * len(inputs) + [anywhere] * len(placed),
        out_specs=[p for _, p in outs],
        scratch_shapes=scratch,
        compiler_params=pltpu.CompilerParams(collective_id=1, has_side_effects=True, vmem_limit_bytes=62 * 2**20),
        cost_estimate=pl.CostEstimate(flops=8 * 10**9, bytes_accessed=10**8, transcendentals=0),
        name="back",
    )(*inputs, *placed)


def lane_gather(part):
    return lax.all_gather(part, "wide", axis=0, tiled=True)


def lane_scatter(part):
    return lax.psum_scatter(part.astype(bf16), "wide", scatter_dimension=0, tiled=True)


def group_gather(part, axis=0):
    return lax.all_gather(part, "narrow", axis=axis, tiled=True)


def group_scatter(part, axis=0):
    return lax.psum_scatter(part.astype(bf16), "narrow", scatter_dimension=axis, tiled=True)


def lane_swap(part):
    return lax.all_to_all(part, "wide", split_axis=0, concat_axis=0, tiled=True)


def per_device(
    tokens, doc_ids, valid_mask, routes, cotangent, attend_gain, attend_weight, output_weight, mixer_gain,
    router_weight, blend_weight, up_weight, down_weight, expert_up, expert_down,
):
    rows, width = tokens.shape
    groups, lanes = lax.axis_size("wide"), lax.axis_size("narrow")
    group, lane = lax.axis_index("wide"), lax.axis_index("narrow")
    shard = attend_gain.shape[0]
    local = expert_up.shape[0]
    experts = local * groups
    hidden = up_weight.shape[1]
    fine = hidden // groups // lanes
    cap = max(2, (3 * rows + 2 * experts - 1) // (2 * experts))
    slots = -(-local * cap // 16) * 16
    all_rows = rows * lanes

    mixers = jnp.concatenate([attend_gain[None], mixer_gain[None], blend_weight.T, router_weight.T])
    facts = jnp.stack([doc_ids, valid_mask, routes[:, 0]]).astype(f32)
    up_mine = up_weight
    if fine % 128:
        up_mine = lax.dynamic_index_in_dim(up_weight.reshape(shard, groups, lanes, fine), lane, 2, keepdims=False)
        up_mine = up_mine.reshape(shard, groups * fine)
    (
        lse, attn_mixed, attention_out, small, meta_all, place, packed_cot, normed_attend, qkv, attend_full, output_full, mix_all,
        got_mix, cot_mine, cot_all, up_full, down_full,
    ) = front(groups, lanes, local, cap, slots, tokens, cotangent, facts, mixers, attend_weight, output_weight, up_mine, down_weight)
    doc_col = meta_all[:, 0].reshape(all_rows, 1)
    valid_all = meta_all[:, 1].reshape(all_rows, 1)
    attend_gain_row = small[:, 0].astype(f32)
    mixer_gain_row = small[:, 1].astype(f32)
    mix_cols = jnp.where((jnp.arange(SMALL) < 2)[None, :], 0, small)
    residual_mid = tokens.astype(f32) + attention_out
    mid_normed, mid_scale = norm_stats(residual_mid)
    normed_mix = (mid_normed * mixer_gain_row).astype(bf16)
    route = routes[:, 0]

    def give_back(partial):
        return mm(place, lane_swap(group_scatter(partial)))

    valid = valid_mask.astype(f32)[:, None]
    grad_layer = cotangent.astype(f32) * valid

    def widen(gathered, parts):
        full = gathered.reshape(lanes, shard, parts, -1)
        return full.transpose(1, 2, 0, 3).reshape(shard, -1).astype(f32)

    if all_rows * width <= 2**20 and shard % 128 == 0 and cap % 8 == 0 and slots == local * cap and local == 2 and fine == 128 and width == groups * fine and lanes * groups * cap <= all_rows:
        grad_mix, dense_out, grad_small, mine_up, down_half, tok_part, mix_e, grad_e, act_e, hidden_e = middle(
            groups, lanes, local, cap, experts, slots, (small, meta_all, place),
            (mix_all, cot_all, up_full, down_full, got_mix, cot_mine, packed_cot, expert_up, expert_down))
        layer_out, grad_tokens, small_out, out_attend, out_output, out_up, out_down = back(
            groups, lanes, experts, slots,
            (tokens, cotangent, small, attention_out, attn_mixed, place, meta_all, lse, grad_small, grad_mix,
             dense_out, mine_up, down_half),
            (tok_part, qkv, output_full, attend_full, normed_attend))
        (
            grad_expert_up, grad_expert_down, out_attend, out_output, out_up, out_down, layer_out, grad_tokens, gain_0, gain_1,
            out_blend, out_router, root,
        ) = finish(
            experts, mix_e, hidden_e, act_e, grad_e, out_attend, out_output, out_up, out_down, small_out, layer_out, grad_tokens)
        return (
            layer_out, grad_tokens, gain_0.reshape(shard), out_attend, out_output, gain_1.reshape(shard), out_router.T,
            out_blend.T, out_up, out_down, grad_expert_up, grad_expert_down, root.reshape(4),
        )

    got_cot = group_gather(lane_swap(packed_cot.reshape(groups, slots, width))[None])

    def coefficients(mix_rows):
        logits = mm(mix_rows, mix_cols)
        columns = jnp.arange(SMALL)[None, :]
        blend = soft_max(jnp.where((columns >= 2) & (columns < 4), logits, masked_score))
        router = soft_max(jnp.where((columns >= 4) & (columns < 4 + experts), logits, masked_score))
        return columns, blend, router

    columns, blend, _ = coefficients(mix_all)
    blend_0, blend_1 = blend[:, 2:3], blend[:, 3:4]
    grad_dense = (blend_1 * (cot_all.astype(f32) * valid_all.astype(f32))).astype(bf16)
    up_act, up_slope = gelu_both(mm(mix_all, up_full))
    up_act = up_act.astype(bf16)
    dense_part = mm(up_act, down_full)
    grad_up_act = mm(grad_dense, down_full, 1, 1)
    dense_dot = jnp.sum(up_act.astype(f32) * grad_up_act, axis=1, keepdims=True)
    grad_up_pre = (up_slope * grad_up_act).astype(bf16)
    dense_logits = (jnp.where(columns == 3, 1.0, 0.0) - jnp.where(columns == 2, 1.0, 0.0)) * (blend_0 * dense_dot)
    grad_mix_part = mm(grad_up_pre, up_full, 1, 1) + mm(dense_logits.astype(bf16), mix_cols, 1, 1)
    grad_small = mm(dense_logits.astype(bf16), mix_all, 0, 0)
    grad_up = mm(mix_all, grad_up_pre, 0, 0)
    grad_down = mm(up_act, grad_dense, 0, 0)

    def by_expert(received):
        split = received.reshape(lanes * groups, slots, width)[:, : local * cap]
        return split.reshape(lanes * groups, local, cap, width).transpose(1, 0, 2, 3).reshape(local, -1, width)

    def by_slot(values):
        split = values.reshape(local, lanes * groups, cap, width).transpose(1, 0, 2, 3)
        split = split.reshape(lanes * groups, local * cap, width)
        return jnp.pad(split, ((0, 0), (0, slots - local * cap), (0, 0))).reshape(-1, width)

    mix_e, cot_e = by_expert(got_mix), by_expert(got_cot)
    tok_parts, back_parts, up_grads, down_grads = [], [], [], []
    for e in range(local):
        _, blend, router = coefficients(mix_e[e])
        own = columns == 4 + group * local + e
        chosen = jnp.sum(jnp.where(own, router, 0.0), axis=1, keepdims=True)
        scale = blend[:, 2:3] * chosen
        grad_tok = (scale * cot_e[e].astype(f32)).astype(bf16)
        act, slope = gelu_both(mm(mix_e[e], expert_up[e]))
        act = act.astype(bf16)
        tok_parts.append((mm(act, expert_down[e])))
        grad_act = mm(grad_tok, expert_down[e], 1, 1)
        dot = jnp.sum(act.astype(f32) * grad_act, axis=1, keepdims=True)
        grad_hidden = (slope * grad_act).astype(bf16)
        logits = dot * (jnp.where(own, 1.0, 0.0) - router)
        logits += dot * blend[:, 3:4] * (jnp.where(columns == 2, 1.0, 0.0) - jnp.where(columns == 3, 1.0, 0.0))
        logits = logits.astype(bf16)
        back_parts.append(mm(grad_hidden, expert_up[e], 1, 1) + mm(logits, mix_cols, 1, 1))
        grad_small += mm(logits, mix_e[e], 0, 0)
        down_grads.append(mm(act, grad_tok, 0, 0))
        up_grads.append(mm(mix_e[e], grad_hidden, 0, 0))
    grad_expert_up, grad_expert_down = jnp.stack(up_grads), jnp.stack(down_grads)
    grad_small = grad_small.T
    expert_back = give_back(by_slot(jnp.stack(back_parts)))
    expert_tok = give_back(by_slot(jnp.stack(tok_parts)))

    dense_out = group_scatter(dense_part).astype(f32)
    _, blend, router = coefficients(normed_mix)
    own = columns == 4 + route[:, None]
    chosen = jnp.sum(jnp.where(own, router, 0.0), axis=1, keepdims=True)
    ffn_out = blend[:, 2:3] * chosen * expert_tok + blend[:, 3:4] * dense_out
    layer_full = residual_mid + ffn_out
    sums = jnp.stack(
        [jnp.sum(valid * v * v) for v in (residual_mid, layer_full, attention_out, ffn_out)] + [jnp.sum(valid)])

    grad_mix = group_scatter(grad_mix_part).astype(f32) + expert_back
    grad_mid = grad_layer + norm_back(mid_normed, mid_scale, mixer_gain_row, grad_mix)
    mixer_gain_grad = jnp.sum(grad_mix * mid_normed, axis=0)
    grad_attn = grad_mid.astype(bf16)
    grad_output = mm(attn_mixed, grad_attn, 0, 0)
    grad_mixed = mm(grad_attn, output_full, 1, 1).astype(bf16)
    grad_heads = lax.all_to_all(grad_mixed, "narrow", split_axis=1, concat_axis=0, tiled=True)
    grad_qkv = attend_back(qkv, doc_col, lse, grad_heads)
    grad_attend = mm(normed_attend, grad_qkv, 0, 0)
    grad_normed = group_scatter(mm(grad_qkv, attend_full, 1, 1)).astype(f32)
    in_normed, in_scale = norm_stats(tokens.astype(f32))
    grad_tokens = (grad_mid + norm_back(in_normed, in_scale, attend_gain_row, grad_normed)).astype(bf16)
    attend_gain_grad = jnp.sum(grad_normed * in_normed, axis=0)

    grad_small = jnp.where(columns == 0, attend_gain_grad[:, None], jnp.where(columns == 1, mixer_gain_grad[:, None], grad_small))
    small_out = lax.psum(lax.psum_scatter(grad_small, "wide", scatter_dimension=0, tiled=True), "narrow")
    sums = lax.psum(sums, ("wide", "narrow"))
    root_means = jnp.sqrt(sums[:4] / (jnp.maximum(sums[4], 1.0) * width))

    def share(part):
        return group_gather(part.astype(bf16)[None])

    out_attend = widen(share(lane_scatter(grad_attend)), 3)
    out_output = widen(share(lane_scatter(group_scatter(grad_output, axis=1))), 1)
    out_up = widen(share(lane_scatter(grad_up)), groups)
    out_down = group_gather(lane_scatter(grad_down).astype(bf16)).astype(f32)
    return (
        layer_full.astype(bf16), grad_tokens, small_out[:, 0], out_attend, out_output, small_out[:, 1],
        small_out[:, 4 : 4 + experts], small_out[:, 2:4], out_up, out_down, grad_expert_up, grad_expert_down, root_means,
    )


def solution(mesh):
    both = ("wide", "narrow")
    row, vec, mat = P(both, None), P("wide"), P("wide", None)
    up, down = P("wide", None, "narrow"), P("wide", "narrow", None)
    return jax.shard_map(
        per_device,
        mesh=mesh,
        in_specs=(row, P(both), P(both), row, row, vec, mat, mat, vec, mat, mat, mat, mat, up, down),
        out_specs=(row, row, vec, mat, mat, vec, mat, mat, mat, mat, up, down, P()),
        check_vma=False,
    )
```

```python
import functools

import jax
import jax.numpy as jnp
from jax import lax
from jax.experimental import pallas as pl
from jax.experimental.pallas import tpu as pltpu
from jax.sharding import PartitionSpec as P

HEAD_DIM = 64
PAIR = 2 * HEAD_DIM
Q_TILE = 256
SMALL = 128
eps_norm = 1e-05
masked_score = -1e30
f32 = jnp.float32
bf16 = jnp.bfloat16


def mm(a, b, ca=1, cb=0):
    return lax.dot_general(a, b, (((ca,), (cb,)), ((), ())), preferred_element_type=f32)


def norm_stats(values):
    center = values - jnp.mean(values, axis=-1, keepdims=True)
    scale = lax.rsqrt(jnp.mean(center * center, axis=-1, keepdims=True) + eps_norm)
    return center * scale, scale


def norm_back(normed, scale, gain, grad):
    u = grad * gain
    return scale * (
        u
        - jnp.mean(u, axis=-1, keepdims=True)
        - normed * jnp.mean(u * normed, axis=-1, keepdims=True)
    )


GELU_A = 0.7978845608028654
GELU_B = 0.044715


def gelu(v):
    return 0.5 * v * (1.0 + jnp.tanh(GELU_A * (v + GELU_B * v * v * v)))


def gelu_both(v):
    t = jnp.tanh(GELU_A * (v + GELU_B * v * v * v))
    value = 0.5 * v * (1.0 + t)
    slope = 0.5 * (1.0 + t) + 0.5 * v * (1.0 - t * t) * (GELU_A * (1.0 + 3.0 * GELU_B * v * v))
    return value, slope


def soft_max(logits):
    shifted = jnp.exp(logits - jnp.max(logits, axis=-1, keepdims=True))
    return shifted / jnp.sum(shifted, axis=-1, keepdims=True)


def head_mask(half):
    lanes = lax.broadcasted_iota(jnp.int32, (1, PAIR), 1)
    return (lanes // HEAD_DIM) == half


def attend_tile(tile, qkv_ref, doc_cols, out_ref, lse_ref, mask_ref, vt_ref):
    cols = out_ref.shape[1]
    extent = (tile + 1) * Q_TILE
    here, seen = pl.ds(tile * Q_TILE, Q_TILE), pl.ds(0, extent)
    mask_tile(tile, doc_cols, mask_ref)

    def pair_step(pair, carry):
        q_cols = pl.ds(pl.multiple_of(pair * PAIR, PAIR), PAIR)
        k_cols = pl.ds(pl.multiple_of(cols + pair * PAIR, PAIR), PAIR)
        v_cols = pl.ds(pl.multiple_of(2 * cols + pair * PAIR, PAIR), PAIR)
        if tile == 0:
            vt_ref[pair] = qkv_ref[:, v_cols].T
        queries = qkv_ref[here, q_cols] * jnp.asarray(HEAD_DIM**-0.5, bf16)
        mixed = jnp.zeros((PAIR, Q_TILE), f32)
        for half in range(2):
            one = jnp.where(head_mask(half), queries, jnp.zeros_like(queries))
            scores = mm(qkv_ref[seen, k_cols], one, 1, 1) + mask_ref[seen, :]
            top = jnp.max(scores, axis=0, keepdims=True)
            shifted = jnp.exp(scores - top)
            total = jnp.sum(shifted, axis=0, keepdims=True)
            low = (shifted * (1.0 / total)).astype(bf16)
            lse_ref[pair, pl.ds(half, 1), here] = top + jnp.log(total)
            got = mm(vt_ref[pair, :, seen], low)
            sublanes = lax.broadcasted_iota(jnp.int32, (PAIR, 1), 0)
            mixed = jnp.where((sublanes // HEAD_DIM) == half, got, mixed)
        out_ref[here, q_cols] = mixed.T.astype(bf16)
        return carry

    lax.fori_loop(0, cols // PAIR, pair_step, 0)


def mask_tile(tile, doc_cols, mask_ref):
    row = (tile * Q_TILE + lax.broadcasted_iota(jnp.int32, (Q_TILE, Q_TILE), 1)).astype(f32)
    for block in range(tile + 1):
        allowed = doc_cols[block] >= row
        if block == tile:
            key = (tile * Q_TILE + lax.broadcasted_iota(jnp.int32, (Q_TILE, Q_TILE), 0)).astype(f32)
            allowed = allowed & (key <= row)
        mask_ref[pl.ds(block * Q_TILE, Q_TILE), :] = jnp.where(allowed, 0.0, masked_score)


def attend_back_kernel(qkv_ref, doc_ref, lse_ref, grad_ref, out_ref, mask_ref, dk_ref, dv_ref):
    rows, cols = grad_ref.shape
    pairs = cols // PAIR
    dk_ref[...] = jnp.zeros_like(dk_ref)
    dv_ref[...] = jnp.zeros_like(dv_ref)
    for tile in range(rows // Q_TILE):
        extent = (tile + 1) * Q_TILE
        here = pl.ds(tile * Q_TILE, Q_TILE)
        seen = pl.ds(0, extent)
        mask_tile(tile, [doc_ref[pl.ds(b * Q_TILE, Q_TILE), :] for b in range(tile + 1)], mask_ref)

        def pair_step(pair, carry):
            q_cols = pl.ds(pl.multiple_of(pair * PAIR, PAIR), PAIR)
            k_cols = pl.ds(pl.multiple_of(cols + pair * PAIR, PAIR), PAIR)
            v_cols = pl.ds(pl.multiple_of(2 * cols + pair * PAIR, PAIR), PAIR)
            queries = qkv_ref[here, q_cols] * jnp.asarray(HEAD_DIM**-0.5, bf16)
            keys, values = qkv_ref[seen, k_cols], qkv_ref[seen, v_cols]
            grads = grad_ref[here, q_cols]
            dq = jnp.zeros((PAIR, Q_TILE), f32)
            for half in range(2):
                on = head_mask(half)
                q_one = jnp.where(on, queries, jnp.zeros_like(queries))
                g_one = jnp.where(on, grads, jnp.zeros_like(grads))
                probs = jnp.exp(mm(keys, q_one, 1, 1) + mask_ref[seen, :] - lse_ref[pair, pl.ds(half, 1), here])
                dv_ref[pair, seen, :] += mm(probs.astype(bf16), g_one)
                back = mm(values, g_one, 1, 1)
                low = (probs * (back - jnp.sum(probs * back, axis=0, keepdims=True))).astype(bf16)
                dk_ref[pair, seen, :] += mm(low, q_one)
                got = mm(keys, low, 0, 0)
                sublanes = lax.broadcasted_iota(jnp.int32, (PAIR, 1), 0)
                dq = jnp.where((sublanes // HEAD_DIM) == half, got, dq)
            out_ref[here, q_cols] = (dq.T * HEAD_DIM**-0.5).astype(bf16)
            return carry

        lax.fori_loop(0, pairs, pair_step, 0)
    for pair in range(pairs):
        out_ref[:, cols + pair * PAIR : cols + (pair + 1) * PAIR] = dk_ref[pair].astype(bf16)
        out_ref[:, 2 * cols + pair * PAIR : 2 * cols + (pair + 1) * PAIR] = dv_ref[pair].astype(bf16)


def attend_back(qkv, doc_col, lse, grad):
    rows, cols = grad.shape
    vmem = pl.BlockSpec(memory_space=pltpu.VMEM)
    return pl.pallas_call(
        attend_back_kernel,
        out_shape=jax.ShapeDtypeStruct((rows, 3 * cols), bf16),
        in_specs=[vmem] * 4,
        out_specs=vmem,
        scratch_shapes=[
            pltpu.VMEM((rows, Q_TILE), f32),
            pltpu.VMEM((cols // PAIR, rows, PAIR), f32),
            pltpu.VMEM((cols // PAIR, rows, PAIR), f32),
        ],
        compiler_params=pltpu.CompilerParams(vmem_limit_bytes=56 * 2**20),
        cost_estimate=pl.CostEstimate(flops=20 * rows * rows * cols, bytes_accessed=16 * rows * cols, transcendentals=0),
        name="attend_back",
    )(qkv, doc_col, lse, grad)


MESH = pl.DeviceIdType.MESH


class Spot:
    def __init__(self, groups, lanes):
        self.W, self.L = groups, lanes
        self.X = 1 << ((groups.bit_length() - 1) // 2)
        self.Z, self.Y = groups // self.X, lanes // 2
        self.g, self.l = lax.axis_index("wide"), lax.axis_index("narrow")
        self.z, self.x = self.g // self.X, self.g % self.X
        self.y, self.c = self.l // 2, self.l % 2

    def zx_peer(self, dz, dx):
        return lax.rem(self.z + dz, self.Z) * self.X + lax.rem(self.x + dx, self.X)

    def z_peer(self, d):
        return self.zx_peer(d, 0)

    def x_peer(self, d):
        return self.zx_peer(0, d)

    def y_peer(self, d):
        return lax.rem(self.y + d, self.Y) * 2 + self.c

    def core_peer(self):
        return self.y * 2 + 1 - self.c

    def w_peer(self, d):
        return lax.rem(self.g + d, self.W)

    def w_at(self, p):
        return lax.rem(self.g + 1 + p, self.W)

    def l_peer(self, d):
        return lax.rem(self.l + d, self.L)

    def greet(self):
        barrier = pltpu.get_barrier_semaphore()
        for d in range(1, self.L):
            pl.semaphore_signal(barrier, 1, device_id=(self.g, self.l_peer(d)), device_id_type=MESH)
        for d in range(1, self.W):
            pl.semaphore_signal(barrier, 1, device_id=(self.w_peer(d), self.l), device_id_type=MESH)

    def met(self):
        pl.semaphore_wait(pltpu.get_barrier_semaphore(), self.L + self.W - 2)


def remote(src, dst, send_sem, recv_sem, group, lane):
    return pltpu.make_async_remote_copy(src, dst, send_sem, recv_sem, device_id=(group, lane), device_id_type=MESH)


class LaneGather:
    def __init__(self, spot, src, place, sems):
        self.s, self.src, self.place = spot, src, place
        self.z_sem, self.x_sem, self.r_sem, self.own_sem = sems

    @staticmethod
    def sems(W, X):
        dma = pltpu.SemaphoreType.DMA
        return [dma((W // X,)), dma((W // X, X)), dma((W,)), dma((1,))]

    def z_copy(self, d):
        s = self.s
        return remote(self.src, self.place(s.g), self.z_sem.at[d], self.r_sem.at[s.g], s.z_peer(d), s.l)

    def x_copy(self, d, e):
        s = self.s
        w = s.z_peer(d)
        src = self.src if d == 0 else self.place(w)
        return remote(src, self.place(w), self.x_sem.at[d, e], self.r_sem.at[w], s.x_peer(e), s.l)

    def got(self, w):
        s = self.s
        remote(self.src, self.place(w), self.z_sem.at[0], self.r_sem.at[w], s.x_peer(1), s.l).wait_recv()

    def own(self):
        return pltpu.make_async_copy(self.src, self.place(self.s.g), self.own_sem.at[0])

    def start_z(self):
        for d in range(1, self.s.Z):
            self.z_copy(d).start()

    def start_x(self):
        for e in range(1, self.s.X):
            self.x_copy(0, e).start()
        self.own().start()

    def start(self):
        self.start_z()
        self.start_x()

    def forward(self):
        for d in range(1, self.s.Z):
            self.got(self.s.z_peer(d))
            for e in range(1, self.s.X):
                self.x_copy(d, e).start()

    def arrive(self):
        s = self.s
        for d in range(s.Z):
            for e in range(1, s.X):
                self.got(s.zx_peer(d, e))
        self.own().wait()

    def sent(self):
        for d in range(1, self.s.Z):
            self.z_copy(d).wait_send()
        for d in range(self.s.Z):
            for e in range(1, self.s.X):
                self.x_copy(d, e).wait_send()


class LineGather:
    def __init__(self, spot, src, place, sems):
        self.s, self.src, self.place = spot, src, place
        self.z_sem, self.x_sem, self.r_sem, self.own_sem = sems

    @staticmethod
    def sems(W, X):
        dma = pltpu.SemaphoreType.DMA
        return [dma((W // X, 2)), dma((W // X, 2, X)), dma((W,)), dma((1,))]

    def home(self, z):
        return self.place(z * self.s.X + self.s.x)

    def exists(self, z):
        return (z >= 0) & (z < self.s.Z)

    def z_copy(self, k, side):
        s, sign = self.s, 2 * side - 1
        z = s.z + sign * k
        src = self.src if k == 0 else self.home(z)
        return remote(src, self.home(z), self.z_sem.at[k, side], self.r_sem.at[z * s.X + s.x], (s.z - sign) * s.X + s.x, s.l)

    def x_copy(self, k, side, e):
        s = self.s
        z = s.z + (2 * side - 1) * k
        src = self.src if k == 0 else self.home(z)
        return remote(src, self.home(z), self.x_sem.at[k, side, e], self.r_sem.at[z * s.X + s.x], s.x_peer(e), s.l)

    def got(self, w):
        s = self.s
        remote(self.src, self.place(w), self.z_sem.at[0, 0], self.r_sem.at[w], s.x_peer(1), s.l).wait_recv()

    def own(self):
        return pltpu.make_async_copy(self.src, self.place(self.s.g), self.own_sem.at[0])

    def each(self, k, act):
        s = self.s
        for side in range(2):
            sign = 2 * side - 1
            onward = self.exists(s.z - sign)
            if k == 0:
                pl.when(onward)(lambda side=side: act(self.z_copy(0, side)))
                continue

            @pl.when(self.exists(s.z + sign * k))
            def _(side=side, sign=sign, onward=onward):
                if act is None:
                    self.got((s.z + sign * k) * s.X + s.x)
                go = (lambda c: c.start()) if act is None else act
                pl.when(onward)(lambda: go(self.z_copy(k, side)))
                for e in range(1, s.X):
                    go(self.x_copy(k, side, e))

    def start(self):
        self.each(0, lambda c: c.start())
        for e in range(1, self.s.X):
            self.x_copy(0, 0, e).start()
        self.own().start()

    def hop(self, k):
        self.each(k, None)

    def arrive(self):
        s = self.s
        for d in range(s.Z):
            for e in range(1, s.X):
                self.got(s.zx_peer(d, e))
        self.own().wait()

    def sent(self):
        for k in range(self.s.Z):
            self.each(k, lambda c: c.wait_send())
        for e in range(1, self.s.X):
            self.x_copy(0, 0, e).wait_send()


class GroupGather:
    def __init__(self, spot, src, place, sems, own=True):
        self.s, self.src, self.place, self.has_own = spot, src, place, own
        self.y_sem, self.c_sem, self.r_sem, self.own_sem = sems

    @staticmethod
    def sems(L):
        dma = pltpu.SemaphoreType.DMA
        return [dma((L // 2,)), dma((L // 2,)), dma((L,)), dma((1,))]

    def y_copy(self, d):
        s = self.s
        return remote(self.src, self.place(s.l), self.y_sem.at[d], self.r_sem.at[s.l], s.g, s.y_peer(d))

    def c_copy(self, d):
        s = self.s
        l = s.y_peer(d)
        src = self.src if d == 0 else self.place(l)
        return remote(src, self.place(l), self.c_sem.at[d], self.r_sem.at[l], s.g, s.core_peer())

    def got(self, l):
        s = self.s
        remote(self.src, self.place(l), self.y_sem.at[0], self.r_sem.at[l], s.g, s.core_peer()).wait_recv()

    def own(self):
        return pltpu.make_async_copy(self.src, self.place(self.s.l), self.own_sem.at[0])

    def start(self):
        for d in range(1, self.s.Y):
            self.y_copy(d).start()
        self.c_copy(0).start()
        if self.has_own:
            self.own().start()

    def forward(self):
        for d in range(1, self.s.Y):
            self.got(self.s.y_peer(d))
            self.c_copy(d).start()

    def arrive(self):
        s = self.s
        for d in range(s.Y):
            self.got(lax.rem(s.y + d, s.Y) * 2 + 1 - s.c)
        if self.has_own:
            self.own().wait()

    def sent(self):
        for d in range(1, self.s.Y):
            self.y_copy(d).wait_send()
        for d in range(self.s.Y):
            self.c_copy(d).wait_send()


class LaneSwap:
    def __init__(self, spot, src, dst, sems, distances=None):
        self.s, self.src, self.dst = spot, src, dst
        self.distances = range(spot.W) if distances is None else distances
        self.s_sem, self.r_sem = sems

    @staticmethod
    def sems(W):
        return [pltpu.SemaphoreType.DMA((W,)), pltpu.SemaphoreType.DMA((W,))]

    def copy(self, d):
        s = self.s
        w = s.w_peer(d)
        return remote(self.src(w), self.dst(s.g), self.s_sem.at[d], self.r_sem.at[s.g], w, s.l)

    def own(self):
        return pltpu.make_async_copy(self.src(self.s.g), self.dst(self.s.g), self.s_sem.at[0])

    def start(self):
        for d in self.distances:
            if d:
                self.copy(d).start()
            else:
                self.own().start()

    def got(self, w):
        s = self.s
        remote(self.src(w), self.dst(w), self.s_sem.at[0], self.r_sem.at[w], s.w_peer(1), s.l).wait_recv()

    def arrive(self):
        for d in self.distances:
            self.due(d)

    def due(self, d):
        if d:
            self.got(self.s.w_peer(self.s.W - d))
        else:
            self.own().wait()

    def sent(self):
        for d in self.distances:
            if d:
                self.copy(d).wait_send()


class GroupSwap:
    def __init__(self, spot, src, dst, sems):
        self.s, self.src, self.dst = spot, src, dst
        self.s_sem, self.r_sem = sems

    @staticmethod
    def sems(L):
        return [pltpu.SemaphoreType.DMA((L,)), pltpu.SemaphoreType.DMA((L,))]

    def copy(self, l):
        s = self.s
        return remote(self.src(l), self.dst(s.l), self.s_sem.at[l], self.r_sem.at[s.l], s.g, l)

    def own(self):
        s = self.s
        return pltpu.make_async_copy(self.src(s.l), self.dst(s.l), self.s_sem.at[s.l])

    def send(self, l):
        @pl.when(self.s.l == l)
        def _():
            self.own().start()

        @pl.when(self.s.l != l)
        def _():
            self.copy(l).start()

    def arrive(self):
        s = self.s
        for d in range(1, s.L):
            l = s.l_peer(d)
            remote(self.src(l), self.dst(l), self.s_sem.at[l], self.r_sem.at[l], s.g, l).wait_recv()
        self.own().wait()

    def sent(self):
        for d in range(1, self.s.L):
            self.copy(self.s.l_peer(d)).wait_send()


def rows_norm(src, gain, dst, count, step=64):
    def body(i, carry):
        at = pl.ds(pl.multiple_of(i * step, step), step)
        normed, _ = norm_stats(src[at, :].astype(f32))
        dst[at, :] = (normed * gain).astype(bf16)
        return carry

    lax.fori_loop(0, count // step, body, 0)


def front_kernel(
    groups, lanes, local, cap, slots,
    tokens, cot, facts, mixers, attend_w, output_w, up_w, down_w,
    lse, attn_mixed, attention_out, small_all, meta_all, place,
    packed_cot, normed_to, qkv_to, attend_to, output_to, mix_to, got_mix, cot_mine, cot_all, up_all, down_all,
    normed_out, qkv, attend_all, output_all, mix_all, tok_all, up_mine, mixed, mask, vt, packed_mix, meta, small, out_sem, stage_sem, spread_y, spread_c, spread_r, *sems,
):
    s = Spot(groups, lanes)
    s.greet()
    rows, width = tokens.shape
    head_cols = width // lanes
    shard = attend_w.shape[0]
    depth = down_all.shape[0] // groups
    sems = list(sems)

    def take(n):
        out = sems[:n]
        del sems[:n]
        return out

    def blocks(ref, n):
        return lambda i: ref.at[pl.ds(pl.multiple_of(i * n, n), n)]

    def cols(i):
        return pl.ds(pl.multiple_of(i * head_cols, head_cols), head_cols)

    staged = []
    if up_w.shape[1] != up_mine.shape[1]:
        fine = up_mine.shape[1] // groups
        staged += [
            pltpu.make_async_copy(
                up_w.at[:, pl.ds(pl.multiple_of((w * lanes + s.l) * fine, fine), fine)],
                up_mine.at[:, pl.ds(w * fine, fine)], stage_sem.at[w])
            for w in range(groups)
        ]
    else:
        staged += [pltpu.make_async_copy(up_w, up_mine, stage_sem.at[0])]
    for c in staged:
        c.start()

    meta[...] = jnp.zeros_like(meta)
    meta[0 : facts.shape[0], :] = facts[...]
    known = mixers.shape[0]
    rest = jnp.zeros((SMALL - known, shard), f32)
    small[...] = jnp.concatenate([mixers[...].astype(f32), rest], axis=0).T.astype(bf16)
    tok = GroupGather(s, tokens, blocks(tok_all, rows), take(4))
    met = GroupGather(s, meta, lambda l: meta_all.at[l], take(4))
    cots = GroupGather(s, cot, blocks(cot_all, rows), take(4))
    mix = GroupGather(s, blocks(mix_all, rows)(s.l), blocks(mix_all, rows), take(4), own=False)
    outs = GroupGather(s, output_all.at[:, cols(s.l)], lambda l: output_all.at[:, cols(l)], take(4), own=False)
    atts = [
        LineGather(
            s, attend_w.at[:, pl.ds(pl.multiple_of(p * width + s.l * head_cols, head_cols), head_cols)],
            lambda w, p=p: attend_all.at[pl.ds(pl.multiple_of(w * shard, shard), shard), pl.ds(p * head_cols, head_cols)],
            take(4))
        for p in range(3)
    ]
    sml = LaneGather(s, small, blocks(small_all, shard), take(4))
    out = LineGather(s, output_w.at[:, cols(s.l)],
                     lambda w: output_all.at[pl.ds(pl.multiple_of(w * shard, shard), shard), cols(s.l)], take(4))
    up = LineGather(s, up_mine, blocks(up_all, shard), take(4))
    down = LineGather(s, down_w.at[pl.ds(pl.multiple_of(s.l * depth, depth), depth)], blocks(down_all, depth), take(4))
    swap = GroupSwap(s, blocks(mixed, rows), lambda l: attn_mixed.at[:, cols(l)], take(2))
    cot_swap = LaneSwap(s, blocks(packed_cot, slots), lambda w: cot_mine.at[w], take(2), range(groups // 2))
    mix_swap = LaneSwap(s, blocks(packed_mix, slots), lambda w: got_mix.at[s.l, w], take(2))

    def spread(d):
        w = s.w_peer(groups - d)
        return GroupGather(s, got_mix.at[s.l, w], lambda l: got_mix.at[l, w],
                           [spread_y.at[w], spread_c.at[w], spread_r.at[w], None], own=False)

    mix_spread = [spread(d) for d in range(groups)]

    s.met()
    sml.start()
    met.start()
    tok.start()
    for att in atts:
        att.start()
    for c in staged:
        c.wait()
    mine = meta[...].T
    valid, route = mine[:, 1:2], mine[:, 2:3].astype(jnp.int32)
    column = lax.broadcasted_iota(jnp.int32, (rows, SMALL), 1)
    hits = (column == route).astype(f32)
    earlier = lax.broadcasted_iota(jnp.int32, (rows, rows), 1) < lax.broadcasted_iota(jnp.int32, (rows, rows), 0)
    rank = jnp.sum(hits * mm(earlier.astype(f32).astype(bf16), hits.astype(bf16)), axis=1, keepdims=True).astype(jnp.int32)
    slot = (route // local) * slots + (route % local) * cap + rank
    spots = (slot == lax.broadcasted_iota(jnp.int32, (rows, groups * slots), 1)).astype(f32)
    place[...] = spots.astype(bf16)
    packed_cot[...] = mm((spots * valid).astype(bf16), cot[...], 0, 0).astype(bf16)
    def give(ref, to, k):
        done.append(pltpu.make_async_copy(ref, to, out_sem.at[k]))
        done[-1].start()

    done = []
    sml.forward()
    for att in atts:
        att.hop(1)
    met.forward()
    for att in atts:
        att.hop(2)
    tok.forward()
    cots.start()
    for k in range(3, s.Z):
        for att in atts:
            att.hop(k)
    out.start()
    up.start()
    sml.arrive()
    met.arrive()
    gains = small_all[...].astype(f32).T
    tok.arrive()
    rows_norm(tok_all, gains[0:1, :], normed_out, rows * lanes)
    give(normed_out, normed_to, 0)
    for att in atts:
        att.arrive()
    give(attend_all, attend_to, 1)

    def project(i, carry):
        at = pl.ds(pl.multiple_of(i * Q_TILE, Q_TILE), Q_TILE)
        qkv[at, :] = mm(normed_out[at, :], attend_all[...]).astype(bf16)
        return carry

    out.hop(1)
    lax.fori_loop(0, rows * lanes // Q_TILE, project, 0)
    give(qkv, qkv_to, 2)
    out.hop(2)
    up.hop(1)
    doc_cols = [meta_all[l].T[:, 0:1] for l in range(lanes)]
    for tile in range(lanes):
        attend_tile(tile, qkv, doc_cols, mixed, lse, mask, vt)
        swap.send(tile)
        if tile == 0:
            for k in range(3, s.Z):
                out.hop(k)
        if tile == lanes - 3:
            out.arrive()
            outs.start()
            up.hop(2)
            down.start()
        if tile == lanes - 2:
            cots.forward()
    for k in range(3, s.Z):
        up.hop(k)
    down.hop(1)
    outs.forward()
    outs.arrive()
    give(output_all, output_to, 3)
    swap.arrive()
    attention_out[...] = mm(attn_mixed[...], output_all[...])
    gain = small_all[...].astype(f32).T[1:2, :]
    base = pl.multiple_of(s.l * rows, rows)

    def mid(i, carry):
        at = pl.ds(pl.multiple_of(i * 64, 64), 64)
        normed, _ = norm_stats(tokens[at, :].astype(f32) + attention_out[at, :])
        mix_all[pl.ds(pl.multiple_of(base + i * 64, 64), 64), :] = (normed * gain).astype(bf16)
        return carry

    lax.fori_loop(0, rows // 64, mid, 0)
    mix.start()
    packed_mix[...] = mm(place[...], mix_all[pl.ds(base, rows), :], 0, 0).astype(bf16)
    mix_swap.start()
    down.hop(2)
    mix.forward()
    for k in range(3, s.Z):
        down.hop(k)
    for d in range(groups):
        if d:
            mix_swap.got(s.w_peer(groups - d))
        else:
            mix_swap.own().wait()
        mix_spread[d].start()
    cot_swap.start()
    mix.arrive()
    give(mix_all, mix_to, 4)
    for task in [tok, met, cots, outs, sml, out, up, swap, *atts]:
        task.sent()
    for task in mix_spread:
        task.forward()
    for task in mix_spread:
        task.arrive()
    cots.arrive()
    up.arrive()
    down.arrive()
    cot_swap.arrive()
    for c in done:
        c.wait()
    for task in [mix, down, mix_swap, cot_swap] + mix_spread:
        task.sent()


def front(groups, lanes, local, cap, slots, tokens, cot, meta, small, attend_w, output_w, up_w, down_w):
    rows, width = tokens.shape
    X = 1 << ((groups.bit_length() - 1) // 2)
    Y = lanes // 2
    everyone = rows * lanes
    head_cols = width // lanes
    hidden = down_w.shape[0] // lanes * groups
    shard = attend_w.shape[0]
    vmem, anywhere = pl.BlockSpec(memory_space=pltpu.VMEM), pl.BlockSpec(memory_space=pl.ANY)
    dma = pltpu.SemaphoreType.DMA
    of = jax.ShapeDtypeStruct
    sems = []
    for _ in range(5):
        sems += GroupGather.sems(lanes)
    for _ in range(3):
        sems += LineGather.sems(groups, X)
    sems += LaneGather.sems(groups, X)
    for _ in range(3):
        sems += LineGather.sems(groups, X)
    sems += GroupSwap.sems(lanes) + LaneSwap.sems(groups) * 2
    outs = [
        (of((head_cols // PAIR, 2, everyone), f32), vmem),
        (of((rows, width), bf16), vmem),
        (of((rows, width), f32), vmem),
        (of((width, SMALL), bf16), vmem),
        (of((lanes, 8, rows), f32), vmem),
        (of((rows, groups * slots), bf16), vmem),
        (of((groups * slots, width), bf16), vmem),
    ]
    big = [(everyone, width), (everyone, 3 * head_cols), (width, 3 * head_cols), (width, width), (everyone, width)]
    outs += [(of(shape, bf16), anywhere) for shape in big]
    outs += [
        (of((lanes, groups, slots, width), bf16), anywhere),
        (of((groups, slots, width), bf16), anywhere),
        (of((everyone, width), bf16), anywhere),
        (of((width, hidden), bf16), anywhere),
        (of((hidden, width), bf16), anywhere),
    ]
    return pl.pallas_call(
        functools.partial(front_kernel, groups, lanes, local, cap, slots),
        out_shape=[o for o, _ in outs],
        in_specs=[vmem] * 4 + [anywhere] * 4,
        out_specs=[p for _, p in outs],
        scratch_shapes=[pltpu.VMEM(shape, bf16) for shape in big] + [
            pltpu.VMEM((everyone, width), bf16),
            pltpu.VMEM((shard, hidden), bf16),
            pltpu.VMEM((everyone, head_cols), bf16),
            pltpu.VMEM((everyone, Q_TILE), f32),
            pltpu.VMEM((head_cols // PAIR, PAIR, everyone), bf16),
            pltpu.VMEM((groups * slots, width), bf16),
            pltpu.VMEM((8, rows), f32),
            pltpu.VMEM((shard, SMALL), bf16),
            dma((5,)),
            dma((groups,)),
            dma((groups, Y)),
            dma((groups, Y)),
            dma((groups, lanes)),
        ] + sems,
        compiler_params=pltpu.CompilerParams(collective_id=0, has_side_effects=True, vmem_limit_bytes=56 * 2**20),
        cost_estimate=pl.CostEstimate(flops=8 * 10**9, bytes_accessed=10**8, transcendentals=0),
        name="front",
    )(tokens, cot, meta, small, attend_w, output_w, up_w, down_w)


def add_rows(dst, sources, step=32):
    def body(i, carry):
        at = pl.ds(pl.multiple_of(i * step, step), step)
        total = sources[0][at, :].astype(f32)
        for ref in sources[1:]:
            total += ref[at, :].astype(f32)
        dst[at, :] = total.astype(dst.dtype)
        return carry

    step = step if dst.shape[0] % step == 0 else dst.shape[0]
    lax.fori_loop(0, dst.shape[0] // step, body, 0)


class GroupScatter:
    def __init__(self, spot, part, held, from_core, from_y, sems, fine, chunks=None):
        self.s, self.part, self.from_core, self.from_y, self.fine = spot, part, from_core, from_y, fine
        self.staged = held is not None
        self.held = (lambda d: held.at[d]) if self.staged else (lambda d: part(spot.y_peer(d)))
        self.stage_sem, self.cs_sem, self.cr_sem, self.ys_sem, self.yr_sem = sems
        self.chunks = chunks or from_core.shape[1]

    @staticmethod
    def sems(L, chunks):
        dma = pltpu.SemaphoreType.DMA
        return [dma((L // 2,))] * 3 + [dma((L // 2, chunks))] * 2

    def stage(self, d):
        return pltpu.make_async_copy(self.part(self.s.y_peer(d)), self.held(d), self.stage_sem.at[d])

    def core_copy(self, d):
        s = self.s
        other = lax.rem(s.y + d, s.Y) * 2 + 1 - s.c
        return remote(self.part(other), self.from_core.at[d], self.cs_sem.at[d], self.cr_sem.at[d], s.g, s.core_peer())

    def y_copy(self, d, k):
        s = self.s
        src, dst = self.held(d), self.from_y.at[d - 1]
        if self.fine:
            src, dst = src.at[k], dst.at[k]
        return remote(src, dst, self.ys_sem.at[d, k], self.yr_sem.at[d, k], s.g, s.y_peer(d))

    def start(self):
        for d in range(self.s.Y):
            if self.staged:
                self.stage(d).start()
            self.core_copy(d).start()

    def ready(self):
        for d in range(self.s.Y):
            if self.staged:
                self.stage(d).wait()
            self.core_copy(d).wait_recv()

    def add(self, d, k):
        self.held(d)[k] = (self.held(d)[k].astype(f32) + self.from_core[d, k].astype(f32)).astype(bf16)

    def relay(self, k=0):
        for d in range(1, self.s.Y):
            if self.fine:
                self.add(d, k)
            else:

                def body(i, carry, d=d):
                    self.add(d, i)
                    return carry

                lax.fori_loop(0, self.chunks, body, 0)
            self.y_copy(d, k).start()

    def got(self, k=0):
        for d in range(1, self.s.Y):
            self.y_copy(d, k).wait_recv()

    def total(self, k):
        value = self.held(0)[k].astype(f32) + self.from_core[0, k].astype(f32)
        for d in range(1, self.s.Y):
            value += self.from_y[d - 1, k].astype(f32)
        return value

    def sent(self):
        for d in range(self.s.Y):
            self.core_copy(d).wait_send()
        for d in range(1, self.s.Y):
            for k in range(self.chunks if self.fine else 1):
                self.y_copy(d, k).wait_send()


class LaneScatter:
    def __init__(self, spot, part, held, from_x, from_z, sems):
        self.s, self.part, self.from_x, self.from_z = spot, part, from_x, from_z
        self.staged = held is not None
        self.held = (lambda d: held.at[d]) if self.staged else (lambda d: part(spot.z_peer(d)))
        self.stage_sem, self.xs_sem, self.xr_sem, self.zs_sem, self.zr_sem = sems

    @staticmethod
    def sems(W, X):
        dma = pltpu.SemaphoreType.DMA
        Z = W // X
        return [dma((Z,)), dma((X, Z)), dma((X, Z)), dma((Z,)), dma((Z,))]

    def stage(self, d):
        return pltpu.make_async_copy(self.part(self.s.z_peer(d)), self.held(d), self.stage_sem.at[d])

    def x_copy(self, e, d):
        s = self.s
        return remote(self.part(s.zx_peer(d, e)), self.from_x.at[e - 1, d], self.xs_sem.at[e, d], self.xr_sem.at[e, d],
                      s.x_peer(e), s.l)

    def z_copy(self, d):
        s = self.s
        return remote(self.held(d), self.from_z.at[d - 1], self.zs_sem.at[d], self.zr_sem.at[d], s.z_peer(d), s.l)

    def start(self):
        for d in [*range(1, self.s.Z), 0]:
            if self.staged:
                self.stage(d).start()
            for e in range(1, self.s.X):
                self.x_copy(e, d).start()

    def ready(self, d):
        if self.staged:
            self.stage(d).wait()
        for e in range(1, self.s.X):
            self.x_copy(e, d).wait_recv()

    def relay(self):
        for d in range(1, self.s.Z):
            self.ready(d)
            add_rows(self.held(d), [self.held(d)] + [self.from_x.at[e - 1, d] for e in range(1, self.s.X)])
            self.z_copy(d).start()

    def finish(self, dst):
        self.ready(0)
        for d in range(1, self.s.Z):
            self.z_copy(d).wait_recv()
        add_rows(dst, [self.held(0)] + [self.from_x.at[e - 1, 0] for e in range(1, self.s.X)]
                 + [self.from_z.at[d - 1] for d in range(1, self.s.Z)])

    def fold(self, dst):
        for d in range(self.s.Z):
            self.ready(d)
            add_rows(dst.at[d], [self.held(d)] + [self.from_x.at[e - 1, d] for e in range(1, self.s.X)])

    def x_sent(self):
        for d in range(self.s.Z):
            for e in range(1, self.s.X):
                self.x_copy(e, d).wait_send()

    def sent(self):
        self.x_sent()
        for d in range(1, self.s.Z):
            self.z_copy(d).wait_send()


class ZScatter(LaneScatter):
    def __init__(self, spot, held, from_z, sems):
        self.s, self.held, self.from_z = spot, held, from_z
        self.zs_sem, self.zr_sem = sems

    def start(self):
        for d in range(1, self.s.Z):
            self.z_copy(d).start()

    def finish(self, dst):
        for d in range(1, self.s.Z):
            self.z_copy(d).wait_recv()
        add_rows(dst, [self.held(0)] + [self.from_z.at[d - 1] for d in range(1, self.s.Z)])

    def sent(self):
        for d in range(1, self.s.Z):
            self.z_copy(d).wait_send()


def attend_back_tile(tile, qkv_ref, doc_cols, lse_ref, grad_ref, out_ref, mask_ref, dk_ref, dv_ref):
    cols = grad_ref.shape[1]
    extent = (tile + 1) * Q_TILE
    here, seen = pl.ds(tile * Q_TILE, Q_TILE), pl.ds(0, extent)
    mask_tile(tile, doc_cols, mask_ref)

    def pair_step(pair, carry):
        q_cols = pl.ds(pl.multiple_of(pair * PAIR, PAIR), PAIR)
        k_cols = pl.ds(pl.multiple_of(cols + pair * PAIR, PAIR), PAIR)
        v_cols = pl.ds(pl.multiple_of(2 * cols + pair * PAIR, PAIR), PAIR)
        queries = qkv_ref[here, q_cols] * jnp.asarray(HEAD_DIM**-0.5, bf16)
        keys, values = qkv_ref[seen, k_cols], qkv_ref[seen, v_cols]
        grads = grad_ref[here, q_cols]
        dq = jnp.zeros((PAIR, Q_TILE), f32)
        for half in range(2):
            on = head_mask(half)
            q_one = jnp.where(on, queries, jnp.zeros_like(queries))
            g_one = jnp.where(on, grads, jnp.zeros_like(grads))
            probs = jnp.exp(mm(keys, q_one, 1, 1) + mask_ref[seen, :] - lse_ref[pair, pl.ds(half, 1), here])
            dv_ref[pair, seen, :] += mm(probs.astype(bf16), g_one)
            back = mm(values, g_one, 1, 1)
            low = (probs * (back - jnp.sum(probs * back, axis=0, keepdims=True))).astype(bf16)
            dk_ref[pair, seen, :] += mm(low, q_one)
            got = mm(keys, low, 0, 0)
            sublanes = lax.broadcasted_iota(jnp.int32, (PAIR, 1), 0)
            dq = jnp.where((sublanes // HEAD_DIM) == half, got, dq)
        out_ref[here, q_cols] = (dq.T * HEAD_DIM**-0.5).astype(bf16)
        return carry

    lax.fori_loop(0, cols // PAIR, pair_step, 0)


def finish_kernel(
    up_grads, down_grads, attend_ref, output_ref, up_ref, down_ref, small_ref, layer_ref, tokens_ref,
    expert_up, expert_down, attend_out, output_out, up_out, down_out, layer_out, tokens_out, gain_0, gain_1, blend, router, root,
):
    expert_up[...] = up_grads[...].astype(f32)
    expert_down[...] = down_grads[...].astype(f32)
    lanes, _, units = up_ref.shape
    width = output_out.shape[1]
    for ref, out, parts in ((attend_ref, attend_out, 3), (output_ref, output_out, 1), (up_ref, up_out, units // SMALL)):
        n = ref.shape[2] // parts
        for p in range(parts):
            for l in range(lanes):
                out[:, (p * lanes + l) * n : (p * lanes + l + 1) * n] = ref[l, :, p * n : (p + 1) * n].astype(f32)
    down_out[...] = down_ref[...].astype(f32)
    layer_out[...] = layer_ref[...]
    tokens_out[...] = tokens_ref[...]
    small = small_ref[...]
    gain_0[...] = small[0:1]
    gain_1[...] = small[1:2]
    blend[...] = small[2:4]
    router[...] = small[4 : 4 + router.shape[0]]
    sums = small[small.shape[0] - 1 :]
    root[...] = jnp.sqrt(sums / (jnp.maximum(sums[:, 4:5], 1.0) * width))[:, 0:4]


def finish(experts, up_grads, down_grads, attend_all, output_all, up_all, down_all, small, layer, tokens):
    local, width, units = up_grads.shape
    lanes, shard, _ = up_all.shape
    tile = 256
    steps = local * width // tile
    turns = width // tile
    down_all = down_all.reshape(-1, width)
    count = lambda n: n // steps
    of = jax.ShapeDtypeStruct
    tall = lambda n: pl.BlockSpec((1, tile, n), lambda e, m: (e, m, 0))
    thin = lambda a: pl.BlockSpec((lanes, count(shard), a.shape[2]), lambda e, m: (0, e * turns + m, 0))
    flat = lambda n, c: pl.BlockSpec((count(n), c), lambda e, m: (e * turns + m, 0))
    fixed = lambda *s: pl.BlockSpec(s, lambda e, m: (0, 0))
    outs = [
        (of((local, width, units), f32), pl.BlockSpec((1, tile, units), lambda e, m: (e, m, 0))),
        (of((local, units, width), f32), pl.BlockSpec((1, tile, width), lambda e, m: (e, m, 0))),
        (of((shard, 3 * width), f32), flat(shard, 3 * width)),
        (of((shard, width), f32), flat(shard, width)),
        (of((shard, lanes * units), f32), flat(shard, lanes * units)),
        (of(down_all.shape, f32), flat(*down_all.shape)),
        (of(layer.shape, bf16), flat(*layer.shape)),
        (of(tokens.shape, bf16), flat(*tokens.shape)),
        (of((1, shard), f32), fixed(1, shard)),
        (of((1, shard), f32), fixed(1, shard)),
        (of((2, shard), f32), fixed(2, shard)),
        (of((experts, shard), f32), fixed(experts, shard)),
        (of((1, 4), f32), fixed(1, 4)),
    ]
    return pl.pallas_call(
        finish_kernel,
        grid=(local, turns),
        out_shape=[o for o, _ in outs],
        in_specs=[
            tall(units), tall(width), thin(attend_all), thin(output_all), thin(up_all),
            flat(*down_all.shape), fixed(*small.shape), flat(*layer.shape), flat(*tokens.shape),
        ],
        out_specs=[p for _, p in outs],
        compiler_params=pltpu.CompilerParams(vmem_limit_bytes=63 * 2**20),
        cost_estimate=pl.CostEstimate(flops=0, bytes_accessed=4 * 10**7, transcendentals=0),
        name="finish",
    )(up_grads, down_grads, attend_all, output_all, up_all, down_all, small, layer, tokens)


def take_from(sems):
    sems = list(sems)

    def take(n):
        out = sems[:n]
        del sems[:n]
        return out

    return take


def picked(logits, first, count):
    columns = lax.broadcasted_iota(jnp.int32, logits.shape, 1)
    return soft_max(jnp.where((columns >= first) & (columns < first + count), logits, masked_score))


def middle_kernel(
    groups, lanes, local, cap, experts,
    small, meta_all, place,
    mix_in, cot_in, up_in, down_in, got_mix_in, cot_mine, packed_cot, expert_up, expert_down,
    grad_mix, dense_out, grad_small, mine_up, down_half, tok_part, up_grads, down_grads,
    mix, cot, up, down, act, hidden, got_mix, got_cot, mix_e, grad_e, act_e, hidden_e, expert_in, expert_to,
    mx, mx_c, mx_y, dn, dn_c, dn_y, bk_c, bk_y, gu, gu_x, gu_z, gd, gd_x, ret_back, got_back, dots, coefs,
    load_sem, out_sem, spread_y, spread_c, spread_r, spread_o, *sems,
):
    s = Spot(groups, lanes)
    s.greet()
    everyone, width = mix.shape
    rows = everyone // lanes
    units = up.shape[1]
    slots = got_mix.shape[2]
    shard = width // groups
    rows_e = mix_e.shape[1]
    tile = 256
    step = 64
    take = take_from(sems)

    def blocks(ref, n):
        return lambda i: ref.at[pl.ds(pl.multiple_of(i * n, n), n)]

    def part(i, n=tile):
        return pl.ds(pl.multiple_of(i * n, n), n)

    def load(i, src, dst):
        return pltpu.make_async_copy(src, dst, load_sem.at[i])

    cot_swap = LaneSwap(s, blocks(packed_cot, slots), lambda w: got_cot.at[s.l, w], take(2), range(groups // 2, groups))

    def spread(d):
        w = s.w_peer(groups - d)
        first = d < groups // 2
        return GroupGather(s, cot_mine.at[w] if first else got_cot.at[s.l, w], lambda l: got_cot.at[l, w],
                           [spread_y.at[w], spread_c.at[w], spread_r.at[w], spread_o.at[w]], own=first)

    cot_spread = [spread(d) for d in range(groups)]
    mxs = GroupScatter(s, lambda l: mx.at[l], None, mx_c, mx_y, take(5), False)
    dns = GroupScatter(s, lambda l: dn.at[l], None, dn_c, dn_y, take(5), False)
    near = groups // 2
    bks = [
        GroupScatter(s, lambda l, h=h: got_cot.at[l, pl.ds(h * near, near)], None, bk_c.at[h], bk_y.at[h], take(5), True, near)
        for h in range(2)
    ]
    ups = LaneScatter(s, blocks(gu, shard), None, gu_x, gu_z, take(5))
    dws = LaneScatter(s, blocks(gd, shard), None, gd_x, None, take(5))
    back_swap = LaneSwap(s, blocks(ret_back, slots), blocks(got_back, slots), take(2))

    loads = [load(i, a, b) for i, (a, b) in enumerate([
        (mix_in, mix), (up_in, up), (cot_in, cot), (down_in, down), (got_mix_in, got_mix),
        (expert_up.at[0], expert_in), (expert_down.at[0], expert_to)])]
    more_loads = [load(7, expert_up.at[1], up), load(8, expert_down.at[1], down)]

    def branch(x, grad, w_in, w_to, act_ref, hidden_ref, count):
        dots[pl.ds(0, count), :] = jnp.zeros((count, SMALL), f32)

        def body(n, carry):
            value, slope = gelu_both(mm(x[...], w_in[:, part(n)]))
            value = value.astype(bf16)
            act_ref[pl.ds(0, count), part(n)] = value
            back = mm(grad[...], w_to[part(n), :], 1, 1)
            hidden_ref[pl.ds(0, count), part(n)] = (slope * back).astype(bf16)
            both = value.astype(f32) * back
            dots[pl.ds(0, count), :] += sum([both[:, i * SMALL : (i + 1) * SMALL] for i in range(1, tile // SMALL)], both[:, :SMALL])
            return carry

        lax.fori_loop(0, units // tile, body, 0)
        return jnp.sum(dots[pl.ds(0, count), :], axis=1, keepdims=True)

    for c in loads[:4]:
        c.start()
    s.met()
    cot_swap.start()
    for task in cot_spread[: groups // 2]:
        task.start()
    for c in loads[4:]:
        c.start()
    for c in loads[:4]:
        c.wait()
    columns = lax.broadcasted_iota(jnp.int32, (everyone, SMALL), 1)

    coefs[...] = picked(mm(mix[...], small[...]), 2, 2)
    for l in range(lanes):
        at = pl.ds(l * rows, rows)
        valid = meta_all[l].T[:, 1:2]
        cot[at, :] = (coefs[at, 3:4] * (cot[at, :].astype(f32) * valid)).astype(bf16)
    dot = branch(mix, cot, up, down, act, hidden, everyone)
    for d in range(groups // 2, groups):
        cot_swap.due(d)
        cot_spread[d].start()
    sign = jnp.where(columns == 3, 1.0, 0.0) - jnp.where(columns == 2, 1.0, 0.0)
    logits = (sign * (coefs[:, 2:3] * dot)).astype(bf16)
    grad_small[...] = mm(logits, mix[...], 0, 0)

    def up_grad(m, carry):
        gu[part(m), :] = mm(mix[:, part(m)], hidden[...], 0, 0).astype(bf16)
        return carry

    lax.fori_loop(0, width // tile, up_grad, 0)
    ups.start()
    def down_grad(m, carry):
        gd[part(m), :] = mm(act[:, part(m)], cot[...], 0, 0).astype(bf16)
        return carry

    lax.fori_loop(0, units // tile, down_grad, 0)
    dws.start()

    def mix_grad(n, carry):
        value = mm(hidden[...], up[part(n), :], 1, 1) + mm(logits, small[part(n), :], 1, 1)
        mx[:, :, :, part(n)] = value.astype(bf16).reshape(lanes, rows // step, step, tile)
        return carry

    lax.fori_loop(0, width // tile, mix_grad, 0)
    mxs.start()

    def out_part(n, carry):
        value = mm(act[...], down[:, part(n)])
        dn[:, :, :, part(n)] = value.astype(bf16).reshape(lanes, rows // step, step, tile)
        return carry

    lax.fori_loop(0, width // tile, out_part, 0)
    dns.start()
    for c in more_loads:
        c.start()
    for c in loads[4:]:
        c.wait()

    def apart(src, dst):
        def body(j, carry):
            pair = []
            for i in range(2):
                b = 2 * j + i
                pair.append(src[b % lanes, s.w_at(b // lanes)].astype(f32))
            for e in range(local):
                both = [p[e * cap : (e + 1) * cap] for p in pair]
                dst[e, part(j, 2 * cap), :] = jnp.concatenate(both, axis=0).astype(bf16)
            return carry

        lax.fori_loop(0, lanes * groups // 2, body, 0)

    def together(sources, dst, first=0, last=lanes * groups // 2):
        def body(j, carry):
            values = [src[part(j, 2 * cap), :].astype(f32) for src in sources]
            for i in range(2):
                b = 2 * j + i
                dst[b % lanes, b // lanes] = jnp.concatenate([v[i * cap : (i + 1) * cap] for v in values], axis=0).astype(bf16)
            return carry

        lax.fori_loop(first, last, body, 0)

    apart(got_mix, mix_e)
    for task in cot_spread:
        task.forward()
    mxs.ready()
    mxs.relay()
    for task in cot_spread:
        task.arrive()
    apart(got_cot, grad_e)

    backs, toks = [act, hidden], [mix, cot]
    outs = []
    few = rows_e // 2
    columns = lax.broadcasted_iota(jnp.int32, (few, SMALL), 1)

    def rows_out(h, e):
        w_to = expert_to if e == 0 else down
        at = pl.ds(h * few, few)

        def body(n, carry):
            toks[e][at, part(n)] = mm(act_e[e, at, :], w_to[:, part(n)]).astype(bf16)
            return carry

        lax.fori_loop(0, width // tile, body, 0)

    for h in range(2):
        at = pl.ds(h * few, few)
        for e in range(local):
            w_in, w_to = (expert_in, expert_to) if e == 0 else (up, down)
            if h == 0 and e:
                for c in more_loads:
                    c.wait()
            x, grad = mix_e.at[e, at], grad_e.at[e, at]
            scores = mm(x[...], small[...])
            blend, router = picked(scores, 2, 2), picked(scores, 4, experts)
            own = columns == 4 + s.g * local + e
            chosen = jnp.sum(jnp.where(own, router, 0.0), axis=1, keepdims=True)
            grad[...] = (blend[:, 2:3] * chosen * grad[...].astype(f32)).astype(bf16)
            shares = jnp.where(own, 1.0, 0.0) - router
            shares += blend[:, 3:4] * (jnp.where(columns == 2, 1.0, 0.0) - jnp.where(columns == 3, 1.0, 0.0))
            coefs[pl.ds(0, few), :] = shares
            dot = branch(x, grad, w_in, w_to, act_e.at[e, at], hidden_e.at[e, at], few)
            logits = (dot * coefs[pl.ds(0, few), :]).astype(bf16)
            grad_small[...] += mm(logits, x[...], 0, 0)

            def rows_back(n, carry, e=e, w_in=w_in, logits=logits, at=at):
                value = mm(hidden_e[e, at, :], w_in[part(n), :], 1, 1) + mm(logits, small[part(n), :], 1, 1)
                backs[e][at, part(n)] = value.astype(bf16)
                return carry

            lax.fori_loop(0, width // tile, rows_back, 0)
            if h == 0 and e == 0:
                ups.relay()
                dns.ready()
                dns.relay()
            if h == 1 and e == 0:
                bks[0].ready()
                for k in range(near):
                    bks[0].relay(k)
        if h == 0:
            for task in cot_spread:
                task.sent()
        together([b.at[pl.ds(0, rows_e)] for b in backs], got_cot, h * lanes * groups // 4, (h + 1) * lanes * groups // 4)
        bks[h].start()

    def hand_back(h):
        for k in range(near):
            p = h * near + k
            w = s.w_at(p)
            bks[h].got(k)
            ret_back[pl.ds(pl.multiple_of(w * slots, slots), slots), :] = bks[h].total(k).astype(bf16)
            if p < groups - 1:
                back_swap.copy(p + 1).start()
            else:
                back_swap.own().start()

    rows_out(0, 0)
    bks[1].ready()
    for k in range(near):
        bks[1].relay(k)
    hand_back(0)
    rows_out(0, 1)
    rows_out(1, 0)
    rows_out(1, 1)

    def weight_grads(e):
        up_to, down_to = (expert_in, expert_to) if e == 0 else (up, down)

        def body(m, carry):
            up_to[part(m), :] = mm(mix_e[e, :, part(m)], hidden_e[e], 0, 0).astype(bf16)
            down_to[part(m), :] = mm(act_e[e, :, part(m)], grad_e[e], 0, 0).astype(bf16)
            return carry

        lax.fori_loop(0, width // tile, body, 0)
        for i, (a, b) in enumerate([(up_to, up_grads), (down_to, down_grads)]):
            outs.append(pltpu.make_async_copy(a, b.at[e], out_sem.at[2 * e + i]))
            outs[-1].start()

    together([t.at[pl.ds(0, rows_e)] for t in toks], got_mix)
    outs.append(pltpu.make_async_copy(got_mix, tok_part, out_sem.at[4 * local]))
    outs[-1].start()

    def totals(scatter, dst):
        scatter.got()

        def body(k, carry):
            dst[pl.ds(pl.multiple_of(k * step, step), step), :] = scatter.total(k).astype(dst.dtype)
            return carry

        lax.fori_loop(0, scatter.chunks, body, 0)

    totals(mxs, grad_mix)
    weight_grads(0)
    hand_back(1)
    weight_grads(1)
    dws.fold(down_half)
    totals(dns, dense_out)
    ups.finish(mine_up)
    back_swap.arrive()
    grad_mix[...] += mm(place[...], got_back[...])
    for c in outs:
        c.wait()
    dws.x_sent()
    for task in [cot_swap, mxs, dns, *bks, ups, back_swap]:
        task.sent()


def middle(groups, lanes, local, cap, experts, slots, inputs, placed):
    rows, width = inputs[2].shape[0], inputs[0].shape[0]
    X = 1 << ((groups.bit_length() - 1) // 2)
    Y, Z = lanes // 2, groups // X
    everyone = rows * lanes
    shard = width // groups
    units = placed[2].shape[1]
    rows_e = lanes * groups * cap
    vmem, anywhere = pl.BlockSpec(memory_space=pltpu.VMEM), pl.BlockSpec(memory_space=pl.ANY)
    dma = pltpu.SemaphoreType.DMA
    of = jax.ShapeDtypeStruct
    low = lambda *shape: pltpu.VMEM(shape, bf16)
    wide = lambda *shape: pltpu.VMEM(shape, f32)
    expert_rows = (local, rows_e, width)
    outs = [
        (of((rows, width), f32), vmem),
        (of((rows, width), bf16), vmem),
        (of((SMALL, width), f32), vmem),
        (of((shard, units), bf16), vmem),
        (of((Z, shard, width), bf16), vmem),
        (of((lanes, groups, slots, width), bf16), anywhere),
        (of((local, width, units), bf16), anywhere),
        (of((local, units, width), bf16), anywhere),
    ]
    scratch = [low(everyone, width), low(everyone, width), low(width, units), low(units, width)]
    scratch += [low(everyone, units), low(everyone, units)]
    scratch += [low(lanes, groups, slots, width)] * 2
    scratch += [low(*expert_rows), low(*expert_rows), low(local, rows_e, units), low(local, rows_e, units)]
    scratch += [low(width, units), low(units, width)]
    scratch += [low(lanes, rows // 64, 64, width), low(Y, rows // 64, 64, width), low(Y - 1, rows // 64, 64, width)] * 2
    scratch += [low(2, Y, groups // 2, slots, width), low(2, Y - 1, groups // 2, slots, width)]
    scratch += [low(width, units), low(X - 1, Z, shard, units), low(Z - 1, shard, units)]
    scratch += [low(units, width), low(X - 1, Z, shard, width)]
    scratch += [low(groups * slots, width)] * 2 + [wide(everyone, SMALL)] * 2
    scratch += [dma((9,)), dma((4 * local + 1,)), dma((groups, Y)), dma((groups, Y)), dma((groups, lanes)), dma((groups, 1))]
    scratch += LaneSwap.sems(groups) + GroupScatter.sems(lanes, 1) * 2 + GroupScatter.sems(lanes, groups // 2) * 2
    scratch += LaneScatter.sems(groups, X) * 2 + LaneSwap.sems(groups)
    return pl.pallas_call(
        functools.partial(middle_kernel, groups, lanes, local, cap, experts),
        out_shape=[o for o, _ in outs],
        in_specs=[vmem] * len(inputs) + [anywhere] * len(placed),
        out_specs=[p for _, p in outs],
        scratch_shapes=scratch,
        compiler_params=pltpu.CompilerParams(collective_id=2, has_side_effects=True, vmem_limit_bytes=62 * 2**20),
        cost_estimate=pl.CostEstimate(flops=35 * 10**9, bytes_accessed=10**8, transcendentals=0),
        name="middle",
    )(*inputs, *placed)


def back_kernel(
    groups, lanes, experts,
    tokens, cot, small, attention_out, attn_mixed, place, meta_all, lse, grad_small, grad_mix_in, dense_out,
    mine_up, down_half, tok_part, qkv_in, output_in, attend_in, normed_in,
    layer_out, grad_tokens, small_out, all_attend, all_output, all_up, all_down,
    qkv, output_all, attend_all, normed, tk_h, tk_c, tk_y,
    go, go_c, go_y, gn, gn_c, gn_y, dw_z, ga, ga_x, ga_z, gl, gl_x, gl_z,
    sm, sm_x, sm_z, sm_mine, sm_all, ret_tok, got_tok, grad_mix, grad_mid, grad_attn, grad_mixed,
    grad_heads, grad_qkv, mask, dk, dv, valid_cols, mine_attend, mine_output, mine_down, stage_sem, *sems,
):
    s = Spot(groups, lanes)
    s.greet()
    rows, width = tokens.shape
    head_cols = width // lanes
    slots = place.shape[1] // groups
    shard = width // groups
    take = take_from(sems)
    step = 64

    def blocks(ref, n):
        return lambda i: ref.at[pl.ds(pl.multiple_of(i * n, n), n)]

    def cols(i):
        return pl.ds(pl.multiple_of(i * head_cols, head_cols), head_cols)

    loads = [
        pltpu.make_async_copy(src, dst, stage_sem.at[i])
        for i, (src, dst) in enumerate(
            [(output_in, output_all), (qkv_in, qkv), (attend_in, attend_all), (normed_in, normed)])
    ]
    tk = GroupScatter(s, lambda l: tok_part.at[l], tk_h, tk_c, tk_y, take(5), True)
    gos = GroupScatter(s, lambda l: go.at[l], None, go_c, go_y, take(5), False)
    gns = GroupScatter(s, lambda l: gn.at[l], None, gn_c, gn_y, take(5), False)
    dws = ZScatter(s, lambda d: down_half.at[d], dw_z, take(2))
    gas = [LaneScatter(s, blocks(ga.at[p], shard), None, ga_x.at[p], ga_z.at[p], take(5)) for p in range(3)]
    gls = LaneScatter(s, blocks(gl, shard), None, gl_x, gl_z, take(5))
    sms = LaneScatter(s, lambda w: sm.at[w], None, sm_x, sm_z, take(5))
    tok_swap = LaneSwap(s, blocks(ret_tok, slots), blocks(got_tok, slots), take(2))
    heads = GroupSwap(s, lambda l: grad_mixed.at[:, cols(l)], blocks(grad_heads, rows), take(2))
    f_attend = GroupGather(s, mine_attend, lambda l: all_attend.at[l], take(4))
    f_output = GroupGather(s, mine_output, lambda l: all_output.at[l], take(4))
    f_up = GroupGather(s, mine_up, lambda l: all_up.at[l], take(4))
    f_down = GroupGather(s, mine_down, lambda l: all_down.at[l], take(4))
    f_small = GroupGather(s, sm_mine, lambda l: sm_all.at[l], take(4))

    def pass_on(first, last):
        for p in range(first, last):
            tk.relay(p)

    def hand_back(first, last):
        for p in range(first, last):
            w = s.w_at(p)
            tk.got(p)
            ret_tok[pl.ds(pl.multiple_of(w * slots, slots), slots), :] = tk.total(p).astype(bf16)
            if p < groups - 1:
                tok_swap.copy(p + 1).start()
            else:
                tok_swap.own().start()

    def totals(scatter, dst):
        scatter.got()

        def body(k, carry):
            dst[pl.ds(pl.multiple_of(k * step, step), step), :] = scatter.total(k).astype(dst.dtype)
            return carry

        lax.fori_loop(0, scatter.chunks, body, 0)

    def over_rows(body, init):
        return lax.fori_loop(0, rows // step, lambda i, c: body(pl.ds(pl.multiple_of(i * step, step), step), c), init)

    for c in loads:
        c.start()
    dk[...] = jnp.zeros_like(dk)
    dv[...] = jnp.zeros_like(dv)
    gains = small[...].astype(f32).T
    mine = meta_all[s.l].T
    valid_cols[...] = jnp.broadcast_to(mine[:, 1:2], valid_cols.shape)

    def mid(at, gain_sum):
        normed_v, scale = norm_stats(tokens[at, :].astype(f32) + attention_out[at, :])
        grad = grad_mix_in[at, :]
        value = cot[at, :].astype(f32) * valid_cols[at, 0:1] + norm_back(normed_v, scale, gains[1:2, :], grad)
        grad_mid[at, :] = value
        grad_attn[at, :] = value.astype(bf16)
        return gain_sum + jnp.sum(grad * normed_v, axis=0, keepdims=True)

    mixer_gain_grad = over_rows(mid, jnp.zeros((1, width), f32))
    loads[0].wait()
    grad_mixed[...] = mm(grad_attn[...], output_all[...], 1, 1).astype(bf16)
    s.met()
    for l in range(lanes):
        heads.send(l)
    tk.start()
    dws.start()

    def out_grad(m, carry):
        value = mm(attn_mixed[:, cols(m)], grad_attn[...], 0, 0).astype(bf16)
        parts = head_cols // step
        for l in range(lanes):
            go[l, pl.ds(m * parts, parts)] = value[:, l * head_cols : (l + 1) * head_cols].reshape(parts, step, head_cols)
        return carry

    lax.fori_loop(0, lanes, out_grad, 0)
    gos.start()
    for c in loads[1:]:
        c.wait()
    heads.arrive()
    tk.ready()
    pass_on(0, groups)
    f_up.start()
    doc_cols = [meta_all[l].T[:, 0:1] for l in range(lanes)]
    for tile in range(lanes):
        attend_back_tile(tile, qkv, doc_cols, lse, grad_heads, grad_qkv, mask, dk, dv)
        if tile == 0:
            gos.ready()
            gos.relay()
        if tile == 2:
            hand_back(0, groups // 2)
    for pair in range(head_cols // PAIR):
        grad_qkv[:, head_cols + pair * PAIR : head_cols + (pair + 1) * PAIR] = dk[pair].astype(bf16)
        grad_qkv[:, 2 * head_cols + pair * PAIR : 2 * head_cols + (pair + 1) * PAIR] = dv[pair].astype(bf16)

    for p in range(3):

        def weight_grad(m, carry, p=p):
            value = mm(normed[:, cols(m)], grad_qkv[:, p * head_cols : (p + 1) * head_cols], 0, 0)
            ga[p, pl.ds(pl.multiple_of(m * head_cols, head_cols), head_cols), :] = value.astype(bf16)
            return carry

        lax.fori_loop(0, lanes, weight_grad, 0)
        gas[p].start()

    def rows_grad(l, carry):
        value = mm(grad_qkv[pl.ds(pl.multiple_of(l * rows, rows), rows), :], attend_all[...], 1, 1)
        gn[l] = value.astype(bf16).reshape(rows // step, step, width)
        return carry

    lax.fori_loop(0, lanes, rows_grad, 0)
    gns.start()
    gns.ready()
    gns.relay()
    hand_back(groups // 2, groups)
    gas[0].relay()
    totals(gos, gl)
    gls.start()
    gas[1].relay()
    gas[2].relay()
    f_up.forward()
    tok_swap.arrive()

    def layer(at, sums):
        attention = attention_out[at, :]
        residual = tokens[at, :].astype(f32) + attention
        normed_v, _ = norm_stats(residual)
        mix = (normed_v * gains[1:2, :]).astype(bf16)
        logits = mm(mix, small[...])
        blend, router = picked(logits, 2, 2), picked(logits, 4, experts)
        columns = lax.broadcasted_iota(jnp.int32, logits.shape, 1)
        route = valid_cols[at, 1:2].astype(jnp.int32)
        chosen = jnp.sum(jnp.where(columns == 4 + route, router, 0.0), axis=1, keepdims=True)
        ffn = blend[:, 2:3] * chosen * mm(place[at, :], got_tok[...]) + blend[:, 3:4] * dense_out[at, :].astype(f32)
        full = residual + ffn
        layer_out[at, :] = full.astype(bf16)
        valid = valid_cols[at, 0:1]
        got = [jnp.sum(valid * v * v, axis=(0, 1), keepdims=True) for v in (residual, full, attention, ffn)]
        got.append(jnp.sum(valid, axis=(0, 1), keepdims=True))
        return tuple(a + b for a, b in zip(sums, got))

    lane_of = lax.broadcasted_iota(jnp.int32, valid_cols.shape, 1)
    valid_cols[...] = jnp.where(lane_of == 1, mine[:, 2:3], mine[:, 1:2])
    sums = over_rows(layer, tuple(jnp.zeros((1, 1), f32) for _ in range(5)))
    totals(gns, grad_mix)

    def first(at, gain_sum):
        normed_v, scale = norm_stats(tokens[at, :].astype(f32))
        grad = grad_mix[at, :]
        grad_tokens[at, :] = (grad_mid[at, :] + norm_back(normed_v, scale, gains[0:1, :], grad)).astype(bf16)
        return gain_sum + jnp.sum(grad * normed_v, axis=0, keepdims=True)

    attend_gain_grad = over_rows(first, jnp.zeros((1, width), f32))
    used = sm_mine.shape[0]
    feature = lax.broadcasted_iota(jnp.int32, (used, shard), 0)
    place_of = lax.broadcasted_iota(jnp.int32, (used, shard), 1)
    tail = jnp.zeros((used, shard), f32)
    for i, v in enumerate(sums):
        tail = jnp.where(place_of == i, v, tail)
    for w in range(groups):
        here = slice(w * shard, (w + 1) * shard)
        value = jnp.where(feature == used - 1, tail, grad_small[0:used, here])
        value = jnp.where(feature == 0, attend_gain_grad[:, here], value)
        sm[w] = jnp.where(feature == 1, mixer_gain_grad[:, here], value)
    sms.start()
    gls.relay()
    dws.finish(mine_down)
    f_down.start()
    sms.relay()
    for p in range(3):
        gas[p].finish(mine_attend.at[:, pl.ds(p * head_cols, head_cols)])
    f_attend.start()
    gls.finish(mine_output)
    f_output.start()
    sms.finish(sm_mine)
    f_small.start()
    gathers = [f_up, f_down, f_attend, f_output, f_small]
    for task in gathers[1:]:
        task.forward()
    for task in gathers:
        task.arrive()
    small_out[...] = sum([sm_all[l] for l in range(1, lanes)], sm_all[0])
    for task in [tk, gos, gns, dws, *gas, gls, sms, tok_swap, heads] + gathers:
        task.sent()


def back(groups, lanes, experts, slots, inputs, placed):
    tokens = inputs[0]
    rows, width = tokens.shape
    X = 1 << ((groups.bit_length() - 1) // 2)
    Y, Z = lanes // 2, groups // X
    everyone = rows * lanes
    head_cols = width // lanes
    shard = width // groups
    hidden = inputs[-2].shape[1]
    vmem, anywhere = pl.BlockSpec(memory_space=pltpu.VMEM), pl.BlockSpec(memory_space=pl.ANY)
    dma = pltpu.SemaphoreType.DMA
    of = jax.ShapeDtypeStruct
    pairs = head_cols // PAIR
    low = lambda *shape: pltpu.VMEM(shape, bf16)
    wide = lambda *shape: pltpu.VMEM(shape, f32)

    def group_bufs(c, r, n, held=True):
        return ([low(Y, c, r, n)] if held else [low(lanes, c, r, n)]) + [low(Y, c, r, n), low(Y - 1, c, r, n)]

    def lane_bufs(n, held=True):
        return ([low(Z, shard, n)] if held else [low(width, n)]) + [low(X - 1, Z, shard, n), low(Z - 1, shard, n)]

    scratch = [low(everyone, 3 * head_cols), low(width, width), low(width, 3 * head_cols), low(everyone, width)]
    scratch += group_bufs(groups, slots, width)
    scratch += group_bufs(width // 64, 64, head_cols, False) + group_bufs(rows // 64, 64, width, False)
    scratch += [low(Z - 1, shard, width)] + [low(3, width, head_cols), low(3, X - 1, Z, shard, head_cols), low(3, Z - 1, shard, head_cols)] + lane_bufs(head_cols, False)
    used = -(-(5 + experts) // 8) * 8
    scratch += [wide(groups, used, shard), wide(X - 1, Z, used, shard), wide(Z - 1, used, shard)]
    scratch += [wide(used, shard), wide(lanes, used, shard)]
    scratch += [low(groups * slots, width)] * 2
    scratch += [wide(rows, width), wide(rows, width), low(rows, width), low(rows, width)]
    scratch += [low(everyone, head_cols), low(everyone, 3 * head_cols), wide(everyone, Q_TILE)]
    scratch += [wide(pairs, everyone, PAIR)] * 2 + [wide(rows, SMALL)]
    scratch += [low(shard, 3 * head_cols), low(shard, head_cols), low(shard, width)]
    scratch += [dma((4,))]
    scratch += GroupScatter.sems(lanes, groups) + GroupScatter.sems(lanes, 1) * 2
    scratch += [dma((Z,))] * 2 + LaneScatter.sems(groups, X) * 5
    scratch += LaneSwap.sems(groups) + GroupSwap.sems(lanes)
    scratch += GroupGather.sems(lanes) * 5
    outs = [
        (of((rows, width), bf16), vmem),
        (of((rows, width), bf16), vmem),
        (of((used, shard), f32), vmem),
        (of((lanes, shard, 3 * head_cols), bf16), anywhere),
        (of((lanes, shard, head_cols), bf16), anywhere),
        (of((lanes, shard, hidden), bf16), anywhere),
        (of((lanes, shard, width), bf16), anywhere),
    ]
    return pl.pallas_call(
        functools.partial(back_kernel, groups, lanes, experts),
        out_shape=[o for o, _ in outs],
        in_specs=[vmem] * len(inputs) + [anywhere] * len(placed),
        out_specs=[p for _, p in outs],
        scratch_shapes=scratch,
        compiler_params=pltpu.CompilerParams(collective_id=1, has_side_effects=True, vmem_limit_bytes=62 * 2**20),
        cost_estimate=pl.CostEstimate(flops=8 * 10**9, bytes_accessed=10**8, transcendentals=0),
        name="back",
    )(*inputs, *placed)


def lane_gather(part):
    return lax.all_gather(part, "wide", axis=0, tiled=True)


def lane_scatter(part):
    return lax.psum_scatter(part.astype(bf16), "wide", scatter_dimension=0, tiled=True)


def group_gather(part, axis=0):
    return lax.all_gather(part, "narrow", axis=axis, tiled=True)


def group_scatter(part, axis=0):
    return lax.psum_scatter(part.astype(bf16), "narrow", scatter_dimension=axis, tiled=True)


def lane_swap(part):
    return lax.all_to_all(part, "wide", split_axis=0, concat_axis=0, tiled=True)


def per_device(
    tokens, doc_ids, valid_mask, routes, cotangent, attend_gain, attend_weight, output_weight, mixer_gain,
    router_weight, blend_weight, up_weight, down_weight, expert_up, expert_down,
):
    rows, width = tokens.shape
    groups, lanes = lax.axis_size("wide"), lax.axis_size("narrow")
    group, lane = lax.axis_index("wide"), lax.axis_index("narrow")
    shard = attend_gain.shape[0]
    local = expert_up.shape[0]
    experts = local * groups
    hidden = up_weight.shape[1]
    fine = hidden // groups // lanes
    cap = max(2, (3 * rows + 2 * experts - 1) // (2 * experts))
    slots = -(-local * cap // 16) * 16
    all_rows = rows * lanes

    mixers = jnp.concatenate([attend_gain[None], mixer_gain[None], blend_weight.T, router_weight.T])
    facts = jnp.stack([doc_ids, valid_mask, routes[:, 0]]).astype(f32)
    up_mine = up_weight
    if fine % 128:
        up_mine = lax.dynamic_index_in_dim(up_weight.reshape(shard, groups, lanes, fine), lane, 2, keepdims=False)
        up_mine = up_mine.reshape(shard, groups * fine)
    (
        lse, attn_mixed, attention_out, small, meta_all, place, packed_cot, normed_attend, qkv, attend_full, output_full, mix_all,
        got_mix, cot_mine, cot_all, up_full, down_full,
    ) = front(groups, lanes, local, cap, slots, tokens, cotangent, facts, mixers, attend_weight, output_weight, up_mine, down_weight)
    doc_col = meta_all[:, 0].reshape(all_rows, 1)
    valid_all = meta_all[:, 1].reshape(all_rows, 1)
    attend_gain_row = small[:, 0].astype(f32)
    mixer_gain_row = small[:, 1].astype(f32)
    mix_cols = jnp.where((jnp.arange(SMALL) < 2)[None, :], 0, small)
    residual_mid = tokens.astype(f32) + attention_out
    mid_normed, mid_scale = norm_stats(residual_mid)
    normed_mix = (mid_normed * mixer_gain_row).astype(bf16)
    route = routes[:, 0]

    def give_back(partial):
        return mm(place, lane_swap(group_scatter(partial)))

    valid = valid_mask.astype(f32)[:, None]
    grad_layer = cotangent.astype(f32) * valid

    def widen(gathered, parts):
        full = gathered.reshape(lanes, shard, parts, -1)
        return full.transpose(1, 2, 0, 3).reshape(shard, -1).astype(f32)

    if all_rows * width <= 2**20 and shard % 128 == 0 and cap % 8 == 0 and slots == local * cap and local == 2 and fine == 128 and width == groups * fine and lanes * groups * cap <= all_rows:
        grad_mix, dense_out, grad_small, mine_up, down_half, tok_part, up_grads, down_grads = middle(
            groups, lanes, local, cap, experts, slots, (small, meta_all, place),
            (mix_all, cot_all, up_full, down_full, got_mix, cot_mine, packed_cot, expert_up, expert_down))
        layer_out, grad_tokens, small_out, out_attend, out_output, out_up, out_down = back(
            groups, lanes, experts, slots,
            (tokens, cotangent, small, attention_out, attn_mixed, place, meta_all, lse, grad_small, grad_mix,
             dense_out, mine_up, down_half),
            (tok_part, qkv, output_full, attend_full, normed_attend))
        (
            grad_expert_up, grad_expert_down, out_attend, out_output, out_up, out_down, layer_out, grad_tokens, gain_0, gain_1,
            out_blend, out_router, root,
        ) = finish(
            experts, up_grads, down_grads, out_attend, out_output, out_up, out_down, small_out, layer_out, grad_tokens)
        return (
            layer_out, grad_tokens, gain_0.reshape(shard), out_attend, out_output, gain_1.reshape(shard), out_router.T,
            out_blend.T, out_up, out_down, grad_expert_up, grad_expert_down, root.reshape(4),
        )

    got_cot = group_gather(lane_swap(packed_cot.reshape(groups, slots, width))[None])

    def coefficients(mix_rows):
        logits = mm(mix_rows, mix_cols)
        columns = jnp.arange(SMALL)[None, :]
        blend = soft_max(jnp.where((columns >= 2) & (columns < 4), logits, masked_score))
        router = soft_max(jnp.where((columns >= 4) & (columns < 4 + experts), logits, masked_score))
        return columns, blend, router

    columns, blend, _ = coefficients(mix_all)
    blend_0, blend_1 = blend[:, 2:3], blend[:, 3:4]
    grad_dense = (blend_1 * (cot_all.astype(f32) * valid_all.astype(f32))).astype(bf16)
    up_act, up_slope = gelu_both(mm(mix_all, up_full))
    up_act = up_act.astype(bf16)
    dense_part = mm(up_act, down_full)
    grad_up_act = mm(grad_dense, down_full, 1, 1)
    dense_dot = jnp.sum(up_act.astype(f32) * grad_up_act, axis=1, keepdims=True)
    grad_up_pre = (up_slope * grad_up_act).astype(bf16)
    dense_logits = (jnp.where(columns == 3, 1.0, 0.0) - jnp.where(columns == 2, 1.0, 0.0)) * (blend_0 * dense_dot)
    grad_mix_part = mm(grad_up_pre, up_full, 1, 1) + mm(dense_logits.astype(bf16), mix_cols, 1, 1)
    grad_small = mm(dense_logits.astype(bf16), mix_all, 0, 0)
    grad_up = mm(mix_all, grad_up_pre, 0, 0)
    grad_down = mm(up_act, grad_dense, 0, 0)

    def by_expert(received):
        split = received.reshape(lanes * groups, slots, width)[:, : local * cap]
        return split.reshape(lanes * groups, local, cap, width).transpose(1, 0, 2, 3).reshape(local, -1, width)

    def by_slot(values):
        split = values.reshape(local, lanes * groups, cap, width).transpose(1, 0, 2, 3)
        split = split.reshape(lanes * groups, local * cap, width)
        return jnp.pad(split, ((0, 0), (0, slots - local * cap), (0, 0))).reshape(-1, width)

    mix_e, cot_e = by_expert(got_mix), by_expert(got_cot)
    tok_parts, back_parts, up_grads, down_grads = [], [], [], []
    for e in range(local):
        _, blend, router = coefficients(mix_e[e])
        own = columns == 4 + group * local + e
        chosen = jnp.sum(jnp.where(own, router, 0.0), axis=1, keepdims=True)
        scale = blend[:, 2:3] * chosen
        grad_tok = (scale * cot_e[e].astype(f32)).astype(bf16)
        act, slope = gelu_both(mm(mix_e[e], expert_up[e]))
        act = act.astype(bf16)
        tok_parts.append((mm(act, expert_down[e])))
        grad_act = mm(grad_tok, expert_down[e], 1, 1)
        dot = jnp.sum(act.astype(f32) * grad_act, axis=1, keepdims=True)
        grad_hidden = (slope * grad_act).astype(bf16)
        logits = dot * (jnp.where(own, 1.0, 0.0) - router)
        logits += dot * blend[:, 3:4] * (jnp.where(columns == 2, 1.0, 0.0) - jnp.where(columns == 3, 1.0, 0.0))
        logits = logits.astype(bf16)
        back_parts.append(mm(grad_hidden, expert_up[e], 1, 1) + mm(logits, mix_cols, 1, 1))
        grad_small += mm(logits, mix_e[e], 0, 0)
        down_grads.append(mm(act, grad_tok, 0, 0))
        up_grads.append(mm(mix_e[e], grad_hidden, 0, 0))
    grad_expert_up, grad_expert_down = jnp.stack(up_grads), jnp.stack(down_grads)
    grad_small = grad_small.T
    expert_back = give_back(by_slot(jnp.stack(back_parts)))
    expert_tok = give_back(by_slot(jnp.stack(tok_parts)))

    dense_out = group_scatter(dense_part).astype(f32)
    _, blend, router = coefficients(normed_mix)
    own = columns == 4 + route[:, None]
    chosen = jnp.sum(jnp.where(own, router, 0.0), axis=1, keepdims=True)
    ffn_out = blend[:, 2:3] * chosen * expert_tok + blend[:, 3:4] * dense_out
    layer_full = residual_mid + ffn_out
    sums = jnp.stack(
        [jnp.sum(valid * v * v) for v in (residual_mid, layer_full, attention_out, ffn_out)] + [jnp.sum(valid)])

    grad_mix = group_scatter(grad_mix_part).astype(f32) + expert_back
    grad_mid = grad_layer + norm_back(mid_normed, mid_scale, mixer_gain_row, grad_mix)
    mixer_gain_grad = jnp.sum(grad_mix * mid_normed, axis=0)
    grad_attn = grad_mid.astype(bf16)
    grad_output = mm(attn_mixed, grad_attn, 0, 0)
    grad_mixed = mm(grad_attn, output_full, 1, 1).astype(bf16)
    grad_heads = lax.all_to_all(grad_mixed, "narrow", split_axis=1, concat_axis=0, tiled=True)
    grad_qkv = attend_back(qkv, doc_col, lse, grad_heads)
    grad_attend = mm(normed_attend, grad_qkv, 0, 0)
    grad_normed = group_scatter(mm(grad_qkv, attend_full, 1, 1)).astype(f32)
    in_normed, in_scale = norm_stats(tokens.astype(f32))
    grad_tokens = (grad_mid + norm_back(in_normed, in_scale, attend_gain_row, grad_normed)).astype(bf16)
    attend_gain_grad = jnp.sum(grad_normed * in_normed, axis=0)

    grad_small = jnp.where(columns == 0, attend_gain_grad[:, None], jnp.where(columns == 1, mixer_gain_grad[:, None], grad_small))
    small_out = lax.psum(lax.psum_scatter(grad_small, "wide", scatter_dimension=0, tiled=True), "narrow")
    sums = lax.psum(sums, ("wide", "narrow"))
    root_means = jnp.sqrt(sums[:4] / (jnp.maximum(sums[4], 1.0) * width))

    def share(part):
        return group_gather(part.astype(bf16)[None])

    out_attend = widen(share(lane_scatter(grad_attend)), 3)
    out_output = widen(share(lane_scatter(group_scatter(grad_output, axis=1))), 1)
    out_up = widen(share(lane_scatter(grad_up)), groups)
    out_down = group_gather(lane_scatter(grad_down).astype(bf16)).astype(f32)
    return (
        layer_full.astype(bf16), grad_tokens, small_out[:, 0], out_attend, out_output, small_out[:, 1],
        small_out[:, 4 : 4 + experts], small_out[:, 2:4], out_up, out_down, grad_expert_up, grad_expert_down, root_means,
    )


def solution(mesh):
    both = ("wide", "narrow")
    row, vec, mat = P(both, None), P("wide"), P("wide", None)
    up, down = P("wide", None, "narrow"), P("wide", "narrow", None)
    return jax.shard_map(
        per_device,
        mesh=mesh,
        in_specs=(row, P(both), P(both), row, row, vec, mat, mat, vec, mat, mat, mat, mat, up, down),
        out_specs=(row, row, vec, mat, mat, vec, mat, mat, mat, mat, up, down, P()),
        check_vma=False,
    )
```

```python
import functools

import jax
import jax.numpy as jnp
from jax import lax
from jax.experimental import pallas as pl
from jax.experimental.pallas import tpu as pltpu
from jax.sharding import PartitionSpec as P

HEAD_DIM = 64
PAIR = 2 * HEAD_DIM
Q_TILE = 256
SMALL = 128
eps_norm = 1e-05
masked_score = -1e30
f32 = jnp.float32
bf16 = jnp.bfloat16


def mm(a, b, ca=1, cb=0):
    return lax.dot_general(a, b, (((ca,), (cb,)), ((), ())), preferred_element_type=f32)


def norm_stats(values):
    center = values - jnp.mean(values, axis=-1, keepdims=True)
    scale = lax.rsqrt(jnp.mean(center * center, axis=-1, keepdims=True) + eps_norm)
    return center * scale, scale


def norm_back(normed, scale, gain, grad):
    u = grad * gain
    return scale * (
        u
        - jnp.mean(u, axis=-1, keepdims=True)
        - normed * jnp.mean(u * normed, axis=-1, keepdims=True)
    )


GELU_A = 0.7978845608028654
GELU_B = 0.044715


def gelu(v):
    return 0.5 * v * (1.0 + jnp.tanh(GELU_A * (v + GELU_B * v * v * v)))


def gelu_both(v):
    t = jnp.tanh(GELU_A * (v + GELU_B * v * v * v))
    value = 0.5 * v * (1.0 + t)
    slope = 0.5 * (1.0 + t) + 0.5 * v * (1.0 - t * t) * (GELU_A * (1.0 + 3.0 * GELU_B * v * v))
    return value, slope


def soft_max(logits):
    shifted = jnp.exp(logits - jnp.max(logits, axis=-1, keepdims=True))
    return shifted / jnp.sum(shifted, axis=-1, keepdims=True)


def head_mask(half):
    lanes = lax.broadcasted_iota(jnp.int32, (1, PAIR), 1)
    return (lanes // HEAD_DIM) == half


def attend_tile(tile, qkv_ref, doc_cols, out_ref, lse_ref, mask_ref, vt_ref):
    cols = out_ref.shape[1]
    extent = (tile + 1) * Q_TILE
    here, seen = pl.ds(tile * Q_TILE, Q_TILE), pl.ds(0, extent)
    mask_tile(tile, doc_cols, mask_ref)

    def pair_step(pair, carry):
        q_cols = pl.ds(pl.multiple_of(pair * PAIR, PAIR), PAIR)
        k_cols = pl.ds(pl.multiple_of(cols + pair * PAIR, PAIR), PAIR)
        v_cols = pl.ds(pl.multiple_of(2 * cols + pair * PAIR, PAIR), PAIR)
        if tile == 0:
            vt_ref[pair] = qkv_ref[:, v_cols].T
        queries = qkv_ref[here, q_cols] * jnp.asarray(HEAD_DIM**-0.5, bf16)
        mixed = jnp.zeros((PAIR, Q_TILE), f32)
        for half in range(2):
            one = jnp.where(head_mask(half), queries, jnp.zeros_like(queries))
            scores = mm(qkv_ref[seen, k_cols], one, 1, 1) + mask_ref[seen, :]
            top = jnp.max(scores, axis=0, keepdims=True)
            shifted = jnp.exp(scores - top)
            total = jnp.sum(shifted, axis=0, keepdims=True)
            low = (shifted * (1.0 / total)).astype(bf16)
            lse_ref[pair, pl.ds(half, 1), here] = top + jnp.log(total)
            got = mm(vt_ref[pair, :, seen], low)
            sublanes = lax.broadcasted_iota(jnp.int32, (PAIR, 1), 0)
            mixed = jnp.where((sublanes // HEAD_DIM) == half, got, mixed)
        out_ref[here, q_cols] = mixed.T.astype(bf16)
        return carry

    lax.fori_loop(0, cols // PAIR, pair_step, 0)


def mask_tile(tile, doc_cols, mask_ref):
    row = (tile * Q_TILE + lax.broadcasted_iota(jnp.int32, (Q_TILE, Q_TILE), 1)).astype(f32)
    for block in range(tile + 1):
        allowed = doc_cols[block] >= row
        if block == tile:
            key = (tile * Q_TILE + lax.broadcasted_iota(jnp.int32, (Q_TILE, Q_TILE), 0)).astype(f32)
            allowed = allowed & (key <= row)
        mask_ref[pl.ds(block * Q_TILE, Q_TILE), :] = jnp.where(allowed, 0.0, masked_score)


def attend_back_kernel(qkv_ref, doc_ref, lse_ref, grad_ref, out_ref, mask_ref, dk_ref, dv_ref):
    rows, cols = grad_ref.shape
    pairs = cols // PAIR
    dk_ref[...] = jnp.zeros_like(dk_ref)
    dv_ref[...] = jnp.zeros_like(dv_ref)
    for tile in range(rows // Q_TILE):
        extent = (tile + 1) * Q_TILE
        here = pl.ds(tile * Q_TILE, Q_TILE)
        seen = pl.ds(0, extent)
        mask_tile(tile, [doc_ref[pl.ds(b * Q_TILE, Q_TILE), :] for b in range(tile + 1)], mask_ref)

        def pair_step(pair, carry):
            q_cols = pl.ds(pl.multiple_of(pair * PAIR, PAIR), PAIR)
            k_cols = pl.ds(pl.multiple_of(cols + pair * PAIR, PAIR), PAIR)
            v_cols = pl.ds(pl.multiple_of(2 * cols + pair * PAIR, PAIR), PAIR)
            queries = qkv_ref[here, q_cols] * jnp.asarray(HEAD_DIM**-0.5, bf16)
            keys, values = qkv_ref[seen, k_cols], qkv_ref[seen, v_cols]
            grads = grad_ref[here, q_cols]
            dq = jnp.zeros((PAIR, Q_TILE), f32)
            for half in range(2):
                on = head_mask(half)
                q_one = jnp.where(on, queries, jnp.zeros_like(queries))
                g_one = jnp.where(on, grads, jnp.zeros_like(grads))
                probs = jnp.exp(mm(keys, q_one, 1, 1) + mask_ref[seen, :] - lse_ref[pair, pl.ds(half, 1), here])
                dv_ref[pair, seen, :] += mm(probs.astype(bf16), g_one)
                back = mm(values, g_one, 1, 1)
                low = (probs * (back - jnp.sum(probs * back, axis=0, keepdims=True))).astype(bf16)
                dk_ref[pair, seen, :] += mm(low, q_one)
                got = mm(keys, low, 0, 0)
                sublanes = lax.broadcasted_iota(jnp.int32, (PAIR, 1), 0)
                dq = jnp.where((sublanes // HEAD_DIM) == half, got, dq)
            out_ref[here, q_cols] = (dq.T * HEAD_DIM**-0.5).astype(bf16)
            return carry

        lax.fori_loop(0, pairs, pair_step, 0)
    for pair in range(pairs):
        out_ref[:, cols + pair * PAIR : cols + (pair + 1) * PAIR] = dk_ref[pair].astype(bf16)
        out_ref[:, 2 * cols + pair * PAIR : 2 * cols + (pair + 1) * PAIR] = dv_ref[pair].astype(bf16)


def attend_back(qkv, doc_col, lse, grad):
    rows, cols = grad.shape
    vmem = pl.BlockSpec(memory_space=pltpu.VMEM)
    return pl.pallas_call(
        attend_back_kernel,
        out_shape=jax.ShapeDtypeStruct((rows, 3 * cols), bf16),
        in_specs=[vmem] * 4,
        out_specs=vmem,
        scratch_shapes=[
            pltpu.VMEM((rows, Q_TILE), f32),
            pltpu.VMEM((cols // PAIR, rows, PAIR), f32),
            pltpu.VMEM((cols // PAIR, rows, PAIR), f32),
        ],
        compiler_params=pltpu.CompilerParams(vmem_limit_bytes=56 * 2**20),
        cost_estimate=pl.CostEstimate(flops=20 * rows * rows * cols, bytes_accessed=16 * rows * cols, transcendentals=0),
        name="attend_back",
    )(qkv, doc_col, lse, grad)


MESH = pl.DeviceIdType.MESH


class Spot:
    def __init__(self, groups, lanes):
        self.W, self.L = groups, lanes
        self.X = 1 << ((groups.bit_length() - 1) // 2)
        self.Z, self.Y = groups // self.X, lanes // 2
        self.g, self.l = lax.axis_index("wide"), lax.axis_index("narrow")
        self.z, self.x = self.g // self.X, self.g % self.X
        self.y, self.c = self.l // 2, self.l % 2

    def zx_peer(self, dz, dx):
        return lax.rem(self.z + dz, self.Z) * self.X + lax.rem(self.x + dx, self.X)

    def z_peer(self, d):
        return self.zx_peer(d, 0)

    def x_peer(self, d):
        return self.zx_peer(0, d)

    def y_peer(self, d):
        return lax.rem(self.y + d, self.Y) * 2 + self.c

    def core_peer(self):
        return self.y * 2 + 1 - self.c

    def w_peer(self, d):
        return lax.rem(self.g + d, self.W)

    def w_at(self, p):
        return lax.rem(self.g + 1 + p, self.W)

    def l_peer(self, d):
        return lax.rem(self.l + d, self.L)

    def greet(self):
        barrier = pltpu.get_barrier_semaphore()
        for d in range(1, self.L):
            pl.semaphore_signal(barrier, 1, device_id=(self.g, self.l_peer(d)), device_id_type=MESH)
        for d in range(1, self.W):
            pl.semaphore_signal(barrier, 1, device_id=(self.w_peer(d), self.l), device_id_type=MESH)

    def met(self):
        pl.semaphore_wait(pltpu.get_barrier_semaphore(), self.L + self.W - 2)


def remote(src, dst, send_sem, recv_sem, group, lane):
    return pltpu.make_async_remote_copy(src, dst, send_sem, recv_sem, device_id=(group, lane), device_id_type=MESH)


class LaneGather:
    def __init__(self, spot, src, place, sems):
        self.s, self.src, self.place = spot, src, place
        self.z_sem, self.x_sem, self.r_sem, self.own_sem = sems

    @staticmethod
    def sems(W, X):
        dma = pltpu.SemaphoreType.DMA
        return [dma((W // X,)), dma((W // X, X)), dma((W,)), dma((1,))]

    def z_copy(self, d):
        s = self.s
        return remote(self.src, self.place(s.g), self.z_sem.at[d], self.r_sem.at[s.g], s.z_peer(d), s.l)

    def x_copy(self, d, e):
        s = self.s
        w = s.z_peer(d)
        src = self.src if d == 0 else self.place(w)
        return remote(src, self.place(w), self.x_sem.at[d, e], self.r_sem.at[w], s.x_peer(e), s.l)

    def got(self, w):
        s = self.s
        remote(self.src, self.place(w), self.z_sem.at[0], self.r_sem.at[w], s.x_peer(1), s.l).wait_recv()

    def own(self):
        return pltpu.make_async_copy(self.src, self.place(self.s.g), self.own_sem.at[0])

    def start_z(self):
        for d in range(1, self.s.Z):
            self.z_copy(d).start()

    def start_x(self):
        for e in range(1, self.s.X):
            self.x_copy(0, e).start()
        self.own().start()

    def start(self):
        self.start_z()
        self.start_x()

    def forward(self):
        for d in range(1, self.s.Z):
            self.got(self.s.z_peer(d))
            for e in range(1, self.s.X):
                self.x_copy(d, e).start()

    def arrive(self):
        s = self.s
        for d in range(s.Z):
            for e in range(1, s.X):
                self.got(s.zx_peer(d, e))
        self.own().wait()

    def sent(self):
        for d in range(1, self.s.Z):
            self.z_copy(d).wait_send()
        for d in range(self.s.Z):
            for e in range(1, self.s.X):
                self.x_copy(d, e).wait_send()


class LineGather:
    def __init__(self, spot, src, place, sems):
        self.s, self.src, self.place = spot, src, place
        self.z_sem, self.x_sem, self.r_sem, self.own_sem = sems

    @staticmethod
    def sems(W, X):
        dma = pltpu.SemaphoreType.DMA
        return [dma((W // X, 2)), dma((W // X, 2, X)), dma((W,)), dma((1,))]

    def home(self, z):
        return self.place(z * self.s.X + self.s.x)

    def exists(self, z):
        return (z >= 0) & (z < self.s.Z)

    def z_copy(self, k, side):
        s, sign = self.s, 2 * side - 1
        z = s.z + sign * k
        src = self.src if k == 0 else self.home(z)
        return remote(src, self.home(z), self.z_sem.at[k, side], self.r_sem.at[z * s.X + s.x], (s.z - sign) * s.X + s.x, s.l)

    def x_copy(self, k, side, e):
        s = self.s
        z = s.z + (2 * side - 1) * k
        src = self.src if k == 0 else self.home(z)
        return remote(src, self.home(z), self.x_sem.at[k, side, e], self.r_sem.at[z * s.X + s.x], s.x_peer(e), s.l)

    def got(self, w):
        s = self.s
        remote(self.src, self.place(w), self.z_sem.at[0, 0], self.r_sem.at[w], s.x_peer(1), s.l).wait_recv()

    def own(self):
        return pltpu.make_async_copy(self.src, self.place(self.s.g), self.own_sem.at[0])

    def each(self, k, act):
        s = self.s
        for side in range(2):
            sign = 2 * side - 1
            onward = self.exists(s.z - sign)
            if k == 0:
                pl.when(onward)(lambda side=side: act(self.z_copy(0, side)))
                continue

            @pl.when(self.exists(s.z + sign * k))
            def _(side=side, sign=sign, onward=onward):
                if act is None:
                    self.got((s.z + sign * k) * s.X + s.x)
                go = (lambda c: c.start()) if act is None else act
                pl.when(onward)(lambda: go(self.z_copy(k, side)))
                for e in range(1, s.X):
                    go(self.x_copy(k, side, e))

    def start(self):
        self.each(0, lambda c: c.start())
        for e in range(1, self.s.X):
            self.x_copy(0, 0, e).start()
        self.own().start()

    def hop(self, k):
        self.each(k, None)

    def arrive(self):
        s = self.s
        for d in range(s.Z):
            for e in range(1, s.X):
                self.got(s.zx_peer(d, e))
        self.own().wait()

    def sent(self):
        for k in range(self.s.Z):
            self.each(k, lambda c: c.wait_send())
        for e in range(1, self.s.X):
            self.x_copy(0, 0, e).wait_send()


class GroupGather:
    def __init__(self, spot, src, place, sems, own=True):
        self.s, self.src, self.place, self.has_own = spot, src, place, own
        self.y_sem, self.c_sem, self.r_sem, self.own_sem = sems

    @staticmethod
    def sems(L):
        dma = pltpu.SemaphoreType.DMA
        return [dma((L // 2,)), dma((L // 2,)), dma((L,)), dma((1,))]

    def y_copy(self, d):
        s = self.s
        return remote(self.src, self.place(s.l), self.y_sem.at[d], self.r_sem.at[s.l], s.g, s.y_peer(d))

    def c_copy(self, d):
        s = self.s
        l = s.y_peer(d)
        src = self.src if d == 0 else self.place(l)
        return remote(src, self.place(l), self.c_sem.at[d], self.r_sem.at[l], s.g, s.core_peer())

    def got(self, l):
        s = self.s
        remote(self.src, self.place(l), self.y_sem.at[0], self.r_sem.at[l], s.g, s.core_peer()).wait_recv()

    def own(self):
        return pltpu.make_async_copy(self.src, self.place(self.s.l), self.own_sem.at[0])

    def start(self):
        for d in range(1, self.s.Y):
            self.y_copy(d).start()
        self.c_copy(0).start()
        if self.has_own:
            self.own().start()

    def forward(self):
        for d in range(1, self.s.Y):
            self.got(self.s.y_peer(d))
            self.c_copy(d).start()

    def arrive(self):
        s = self.s
        for d in range(s.Y):
            self.got(lax.rem(s.y + d, s.Y) * 2 + 1 - s.c)
        if self.has_own:
            self.own().wait()

    def sent(self):
        for d in range(1, self.s.Y):
            self.y_copy(d).wait_send()
        for d in range(self.s.Y):
            self.c_copy(d).wait_send()


class LaneSwap:
    def __init__(self, spot, src, dst, sems, distances=None):
        self.s, self.src, self.dst = spot, src, dst
        self.distances = range(spot.W) if distances is None else distances
        self.s_sem, self.r_sem = sems

    @staticmethod
    def sems(W):
        return [pltpu.SemaphoreType.DMA((W,)), pltpu.SemaphoreType.DMA((W,))]

    def copy(self, d):
        s = self.s
        w = s.w_peer(d)
        return remote(self.src(w), self.dst(s.g), self.s_sem.at[d], self.r_sem.at[s.g], w, s.l)

    def own(self):
        return pltpu.make_async_copy(self.src(self.s.g), self.dst(self.s.g), self.s_sem.at[0])

    def start(self):
        for d in self.distances:
            if d:
                self.copy(d).start()
            else:
                self.own().start()

    def got(self, w):
        s = self.s
        remote(self.src(w), self.dst(w), self.s_sem.at[0], self.r_sem.at[w], s.w_peer(1), s.l).wait_recv()

    def arrive(self):
        for d in self.distances:
            self.due(d)

    def due(self, d):
        if d:
            self.got(self.s.w_peer(self.s.W - d))
        else:
            self.own().wait()

    def sent(self):
        for d in self.distances:
            if d:
                self.copy(d).wait_send()


class GroupSwap:
    def __init__(self, spot, src, dst, sems):
        self.s, self.src, self.dst = spot, src, dst
        self.s_sem, self.r_sem = sems

    @staticmethod
    def sems(L):
        return [pltpu.SemaphoreType.DMA((L,)), pltpu.SemaphoreType.DMA((L,))]

    def copy(self, l):
        s = self.s
        return remote(self.src(l), self.dst(s.l), self.s_sem.at[l], self.r_sem.at[s.l], s.g, l)

    def own(self):
        s = self.s
        return pltpu.make_async_copy(self.src(s.l), self.dst(s.l), self.s_sem.at[s.l])

    def send(self, l):
        @pl.when(self.s.l == l)
        def _():
            self.own().start()

        @pl.when(self.s.l != l)
        def _():
            self.copy(l).start()

    def arrive(self):
        s = self.s
        for d in range(1, s.L):
            l = s.l_peer(d)
            remote(self.src(l), self.dst(l), self.s_sem.at[l], self.r_sem.at[l], s.g, l).wait_recv()
        self.own().wait()

    def sent(self):
        for d in range(1, self.s.L):
            self.copy(self.s.l_peer(d)).wait_send()


def rows_norm(src, gain, dst, count, step=64):
    def body(i, carry):
        at = pl.ds(pl.multiple_of(i * step, step), step)
        normed, _ = norm_stats(src[at, :].astype(f32))
        dst[at, :] = (normed * gain).astype(bf16)
        return carry

    lax.fori_loop(0, count // step, body, 0)


def front_kernel(
    groups, lanes, local, cap, slots,
    tokens, cot, docs, valids, chosen, gain_0, gain_1, blend, router, attend_w, output_w, up_w, down_w,
    lse, attn_mixed, attention_out, small_all, meta_all, place,
    packed_cot, normed_to, qkv_to, attend_to, output_to, mix_to, got_mix, cot_mine, cot_all, up_all, down_all,
    normed_out, qkv, attend_all, output_all, mix_all, tok_all, up_mine, mixed, mask, vt, packed_mix, meta, small, out_sem, stage_sem, spread_y, spread_c, spread_r, *sems,
):
    s = Spot(groups, lanes)
    s.greet()
    rows, width = tokens.shape
    head_cols = width // lanes
    shard = attend_w.shape[0]
    depth = down_all.shape[0] // groups
    sems = list(sems)

    def take(n):
        out = sems[:n]
        del sems[:n]
        return out

    def blocks(ref, n):
        return lambda i: ref.at[pl.ds(pl.multiple_of(i * n, n), n)]

    def cols(i):
        return pl.ds(pl.multiple_of(i * head_cols, head_cols), head_cols)

    staged = []
    if up_w.shape[1] != up_mine.shape[1]:
        fine = up_mine.shape[1] // groups
        staged += [
            pltpu.make_async_copy(
                up_w.at[:, pl.ds(pl.multiple_of((w * lanes + s.l) * fine, fine), fine)],
                up_mine.at[:, pl.ds(w * fine, fine)], stage_sem.at[w])
            for w in range(groups)
        ]
    else:
        staged += [pltpu.make_async_copy(up_w, up_mine, stage_sem.at[0])]
    for c in staged:
        c.start()

    meta[...] = jnp.zeros_like(meta)
    for n, ref in enumerate((docs, valids, chosen)):
        meta[n : n + 1, :] = ref[...].astype(f32)
    known = [ref[...].astype(f32) for ref in (gain_0, gain_1, blend, router)]
    rest = jnp.zeros((SMALL - sum(v.shape[0] for v in known), shard), f32)
    small[...] = jnp.concatenate(known + [rest], axis=0).T.astype(bf16)
    tok = GroupGather(s, tokens, blocks(tok_all, rows), take(4))
    met = GroupGather(s, meta, lambda l: meta_all.at[l], take(4))
    cots = GroupGather(s, cot, blocks(cot_all, rows), take(4))
    mix = GroupGather(s, blocks(mix_all, rows)(s.l), blocks(mix_all, rows), take(4), own=False)
    outs = GroupGather(s, output_all.at[:, cols(s.l)], lambda l: output_all.at[:, cols(l)], take(4), own=False)
    atts = [
        LineGather(
            s, attend_w.at[:, pl.ds(pl.multiple_of(p * width + s.l * head_cols, head_cols), head_cols)],
            lambda w, p=p: attend_all.at[pl.ds(pl.multiple_of(w * shard, shard), shard), pl.ds(p * head_cols, head_cols)],
            take(4))
        for p in range(3)
    ]
    sml = LaneGather(s, small, blocks(small_all, shard), take(4))
    out = LineGather(s, output_w.at[:, cols(s.l)],
                     lambda w: output_all.at[pl.ds(pl.multiple_of(w * shard, shard), shard), cols(s.l)], take(4))
    up = LineGather(s, up_mine, blocks(up_all, shard), take(4))
    down = LineGather(s, down_w.at[pl.ds(pl.multiple_of(s.l * depth, depth), depth)], blocks(down_all, depth), take(4))
    swap = GroupSwap(s, blocks(mixed, rows), lambda l: attn_mixed.at[:, cols(l)], take(2))
    cot_swap = LaneSwap(s, blocks(packed_cot, slots), lambda w: cot_mine.at[w], take(2), range(groups // 2))
    mix_swap = LaneSwap(s, blocks(packed_mix, slots), lambda w: got_mix.at[s.l, w], take(2))

    def spread(d):
        w = s.w_peer(groups - d)
        return GroupGather(s, got_mix.at[s.l, w], lambda l: got_mix.at[l, w],
                           [spread_y.at[w], spread_c.at[w], spread_r.at[w], None], own=False)

    mix_spread = [spread(d) for d in range(groups)]

    s.met()
    sml.start()
    met.start()
    tok.start()
    for att in atts:
        att.start()
    for c in staged:
        c.wait()
    mine = meta[...].T
    valid, route = mine[:, 1:2], mine[:, 2:3].astype(jnp.int32)
    column = lax.broadcasted_iota(jnp.int32, (rows, SMALL), 1)
    hits = (column == route).astype(f32)
    earlier = lax.broadcasted_iota(jnp.int32, (rows, rows), 1) < lax.broadcasted_iota(jnp.int32, (rows, rows), 0)
    rank = jnp.sum(hits * mm(earlier.astype(f32).astype(bf16), hits.astype(bf16)), axis=1, keepdims=True).astype(jnp.int32)
    slot = (route // local) * slots + (route % local) * cap + rank
    spots = (slot == lax.broadcasted_iota(jnp.int32, (rows, groups * slots), 1)).astype(f32)
    place[...] = spots.astype(bf16)
    packed_cot[...] = mm((spots * valid).astype(bf16), cot[...], 0, 0).astype(bf16)
    def give(ref, to, k):
        done.append(pltpu.make_async_copy(ref, to, out_sem.at[k]))
        done[-1].start()

    done = []
    sml.forward()
    for att in atts:
        att.hop(1)
    met.forward()
    for att in atts:
        att.hop(2)
    tok.forward()
    cots.start()
    for k in range(3, s.Z):
        for att in atts:
            att.hop(k)
    out.start()
    up.start()
    sml.arrive()
    met.arrive()
    gains = small_all[...].astype(f32).T
    tok.arrive()
    rows_norm(tok_all, gains[0:1, :], normed_out, rows * lanes)
    give(normed_out, normed_to, 0)
    for att in atts:
        att.arrive()
    give(attend_all, attend_to, 1)

    def project(i, carry):
        at = pl.ds(pl.multiple_of(i * Q_TILE, Q_TILE), Q_TILE)
        qkv[at, :] = mm(normed_out[at, :], attend_all[...]).astype(bf16)
        return carry

    out.hop(1)
    lax.fori_loop(0, rows * lanes // Q_TILE, project, 0)
    give(qkv, qkv_to, 2)
    out.hop(2)
    up.hop(1)
    doc_cols = [meta_all[l].T[:, 0:1] for l in range(lanes)]
    for tile in range(lanes):
        attend_tile(tile, qkv, doc_cols, mixed, lse, mask, vt)
        swap.send(tile)
        if tile == 0:
            for k in range(3, s.Z):
                out.hop(k)
        if tile == lanes - 3:
            out.arrive()
            outs.start()
            up.hop(2)
            down.start()
        if tile == lanes - 2:
            cots.forward()
    for k in range(3, s.Z):
        up.hop(k)
    down.hop(1)
    outs.forward()
    outs.arrive()
    give(output_all, output_to, 3)
    swap.arrive()
    attention_out[...] = mm(attn_mixed[...], output_all[...])
    gain = small_all[...].astype(f32).T[1:2, :]
    base = pl.multiple_of(s.l * rows, rows)

    def mid(i, carry):
        at = pl.ds(pl.multiple_of(i * 64, 64), 64)
        normed, _ = norm_stats(tokens[at, :].astype(f32) + attention_out[at, :])
        mix_all[pl.ds(pl.multiple_of(base + i * 64, 64), 64), :] = (normed * gain).astype(bf16)
        return carry

    lax.fori_loop(0, rows // 64, mid, 0)
    mix.start()
    packed_mix[...] = mm(place[...], mix_all[pl.ds(base, rows), :], 0, 0).astype(bf16)
    mix_swap.start()
    down.hop(2)
    mix.forward()
    for k in range(3, s.Z):
        down.hop(k)
    for d in range(groups):
        if d:
            mix_swap.got(s.w_peer(groups - d))
        else:
            mix_swap.own().wait()
        mix_spread[d].start()
    cot_swap.start()
    mix.arrive()
    give(mix_all, mix_to, 4)
    for task in [tok, met, cots, outs, sml, out, up, swap, *atts]:
        task.sent()
    for task in mix_spread:
        task.forward()
    for task in mix_spread:
        task.arrive()
    cots.arrive()
    up.arrive()
    down.arrive()
    cot_swap.arrive()
    for c in done:
        c.wait()
    for task in [mix, down, mix_swap, cot_swap] + mix_spread:
        task.sent()


def front(groups, lanes, local, cap, slots, tokens, cot, little, attend_w, output_w, up_w, down_w):
    rows, width = tokens.shape
    X = 1 << ((groups.bit_length() - 1) // 2)
    Y = lanes // 2
    everyone = rows * lanes
    head_cols = width // lanes
    hidden = down_w.shape[0] // lanes * groups
    shard = attend_w.shape[0]
    vmem, anywhere = pl.BlockSpec(memory_space=pltpu.VMEM), pl.BlockSpec(memory_space=pl.ANY)
    dma = pltpu.SemaphoreType.DMA
    of = jax.ShapeDtypeStruct
    sems = []
    for _ in range(5):
        sems += GroupGather.sems(lanes)
    for _ in range(3):
        sems += LineGather.sems(groups, X)
    sems += LaneGather.sems(groups, X)
    for _ in range(3):
        sems += LineGather.sems(groups, X)
    sems += GroupSwap.sems(lanes) + LaneSwap.sems(groups) * 2
    outs = [
        (of((head_cols // PAIR, 2, everyone), f32), vmem),
        (of((rows, width), bf16), vmem),
        (of((rows, width), f32), vmem),
        (of((width, SMALL), bf16), vmem),
        (of((lanes, 8, rows), f32), vmem),
        (of((rows, groups * slots), bf16), vmem),
        (of((groups * slots, width), bf16), vmem),
    ]
    big = [(everyone, width), (everyone, 3 * head_cols), (width, 3 * head_cols), (width, width), (everyone, width)]
    outs += [(of(shape, bf16), anywhere) for shape in big]
    outs += [
        (of((lanes, groups, slots, width), bf16), anywhere),
        (of((groups, slots, width), bf16), anywhere),
        (of((everyone, width), bf16), anywhere),
        (of((width, hidden), bf16), anywhere),
        (of((hidden, width), bf16), anywhere),
    ]
    return pl.pallas_call(
        functools.partial(front_kernel, groups, lanes, local, cap, slots),
        out_shape=[o for o, _ in outs],
        in_specs=[vmem] * (2 + len(little)) + [anywhere] * 4,
        out_specs=[p for _, p in outs],
        scratch_shapes=[pltpu.VMEM(shape, bf16) for shape in big] + [
            pltpu.VMEM((everyone, width), bf16),
            pltpu.VMEM((shard, hidden), bf16),
            pltpu.VMEM((everyone, head_cols), bf16),
            pltpu.VMEM((everyone, Q_TILE), f32),
            pltpu.VMEM((head_cols // PAIR, PAIR, everyone), bf16),
            pltpu.VMEM((groups * slots, width), bf16),
            pltpu.VMEM((8, rows), f32),
            pltpu.VMEM((shard, SMALL), bf16),
            dma((5,)),
            dma((groups,)),
            dma((groups, Y)),
            dma((groups, Y)),
            dma((groups, lanes)),
        ] + sems,
        compiler_params=pltpu.CompilerParams(collective_id=0, has_side_effects=True, vmem_limit_bytes=56 * 2**20),
        cost_estimate=pl.CostEstimate(flops=8 * 10**9, bytes_accessed=10**8, transcendentals=0),
        name="front",
    )(tokens, cot, *little, attend_w, output_w, up_w, down_w)


def add_rows(dst, sources, step=32):
    def body(i, carry):
        at = pl.ds(pl.multiple_of(i * step, step), step)
        total = sources[0][at, :].astype(f32)
        for ref in sources[1:]:
            total += ref[at, :].astype(f32)
        dst[at, :] = total.astype(dst.dtype)
        return carry

    step = step if dst.shape[0] % step == 0 else dst.shape[0]
    lax.fori_loop(0, dst.shape[0] // step, body, 0)


class GroupScatter:
    def __init__(self, spot, part, held, from_core, from_y, sems, fine, chunks=None):
        self.s, self.part, self.from_core, self.from_y, self.fine = spot, part, from_core, from_y, fine
        self.staged = held is not None
        self.held = (lambda d: held.at[d]) if self.staged else (lambda d: part(spot.y_peer(d)))
        self.stage_sem, self.cs_sem, self.cr_sem, self.ys_sem, self.yr_sem = sems
        self.chunks = chunks or from_core.shape[1]

    @staticmethod
    def sems(L, chunks):
        dma = pltpu.SemaphoreType.DMA
        return [dma((L // 2,))] * 3 + [dma((L // 2, chunks))] * 2

    def stage(self, d):
        return pltpu.make_async_copy(self.part(self.s.y_peer(d)), self.held(d), self.stage_sem.at[d])

    def core_copy(self, d):
        s = self.s
        other = lax.rem(s.y + d, s.Y) * 2 + 1 - s.c
        return remote(self.part(other), self.from_core.at[d], self.cs_sem.at[d], self.cr_sem.at[d], s.g, s.core_peer())

    def y_copy(self, d, k):
        s = self.s
        src, dst = self.held(d), self.from_y.at[d - 1]
        if self.fine:
            src, dst = src.at[k], dst.at[k]
        return remote(src, dst, self.ys_sem.at[d, k], self.yr_sem.at[d, k], s.g, s.y_peer(d))

    def start(self):
        for d in range(self.s.Y):
            if self.staged:
                self.stage(d).start()
            self.core_copy(d).start()

    def ready(self):
        for d in range(self.s.Y):
            if self.staged:
                self.stage(d).wait()
            self.core_copy(d).wait_recv()

    def add(self, d, k):
        self.held(d)[k] = (self.held(d)[k].astype(f32) + self.from_core[d, k].astype(f32)).astype(bf16)

    def relay(self, k=0):
        for d in range(1, self.s.Y):
            if self.fine:
                self.add(d, k)
            else:

                def body(i, carry, d=d):
                    self.add(d, i)
                    return carry

                lax.fori_loop(0, self.chunks, body, 0)
            self.y_copy(d, k).start()

    def got(self, k=0):
        for d in range(1, self.s.Y):
            self.y_copy(d, k).wait_recv()

    def total(self, k):
        value = self.held(0)[k].astype(f32) + self.from_core[0, k].astype(f32)
        for d in range(1, self.s.Y):
            value += self.from_y[d - 1, k].astype(f32)
        return value

    def sent(self):
        for d in range(self.s.Y):
            self.core_copy(d).wait_send()
        for d in range(1, self.s.Y):
            for k in range(self.chunks if self.fine else 1):
                self.y_copy(d, k).wait_send()


class LaneScatter:
    def __init__(self, spot, part, held, from_x, from_z, sems):
        self.s, self.part, self.from_x, self.from_z = spot, part, from_x, from_z
        self.staged = held is not None
        self.held = (lambda d: held.at[d]) if self.staged else (lambda d: part(spot.z_peer(d)))
        self.stage_sem, self.xs_sem, self.xr_sem, self.zs_sem, self.zr_sem = sems

    @staticmethod
    def sems(W, X):
        dma = pltpu.SemaphoreType.DMA
        Z = W // X
        return [dma((Z,)), dma((X, Z)), dma((X, Z)), dma((Z,)), dma((Z,))]

    def stage(self, d):
        return pltpu.make_async_copy(self.part(self.s.z_peer(d)), self.held(d), self.stage_sem.at[d])

    def x_copy(self, e, d):
        s = self.s
        return remote(self.part(s.zx_peer(d, e)), self.from_x.at[e - 1, d], self.xs_sem.at[e, d], self.xr_sem.at[e, d],
                      s.x_peer(e), s.l)

    def z_copy(self, d):
        s = self.s
        return remote(self.held(d), self.from_z.at[d - 1], self.zs_sem.at[d], self.zr_sem.at[d], s.z_peer(d), s.l)

    def start(self):
        for d in [*range(1, self.s.Z), 0]:
            if self.staged:
                self.stage(d).start()
            for e in range(1, self.s.X):
                self.x_copy(e, d).start()

    def ready(self, d):
        if self.staged:
            self.stage(d).wait()
        for e in range(1, self.s.X):
            self.x_copy(e, d).wait_recv()

    def relay(self):
        for d in range(1, self.s.Z):
            self.ready(d)
            add_rows(self.held(d), [self.held(d)] + [self.from_x.at[e - 1, d] for e in range(1, self.s.X)])
            self.z_copy(d).start()

    def finish(self, dst):
        self.ready(0)
        for d in range(1, self.s.Z):
            self.z_copy(d).wait_recv()
        add_rows(dst, [self.held(0)] + [self.from_x.at[e - 1, 0] for e in range(1, self.s.X)]
                 + [self.from_z.at[d - 1] for d in range(1, self.s.Z)])

    def fold(self, dst):
        for d in range(self.s.Z):
            self.ready(d)
            add_rows(dst.at[d], [self.held(d)] + [self.from_x.at[e - 1, d] for e in range(1, self.s.X)])

    def x_sent(self):
        for d in range(self.s.Z):
            for e in range(1, self.s.X):
                self.x_copy(e, d).wait_send()

    def sent(self):
        self.x_sent()
        for d in range(1, self.s.Z):
            self.z_copy(d).wait_send()


class ZScatter(LaneScatter):
    def __init__(self, spot, held, from_z, sems):
        self.s, self.held, self.from_z = spot, held, from_z
        self.zs_sem, self.zr_sem = sems

    def start(self):
        for d in range(1, self.s.Z):
            self.z_copy(d).start()

    def finish(self, dst):
        for d in range(1, self.s.Z):
            self.z_copy(d).wait_recv()
        add_rows(dst, [self.held(0)] + [self.from_z.at[d - 1] for d in range(1, self.s.Z)])

    def sent(self):
        for d in range(1, self.s.Z):
            self.z_copy(d).wait_send()


def attend_back_tile(tile, qkv_ref, doc_cols, lse_ref, grad_ref, out_ref, mask_ref, dk_ref, dv_ref):
    cols = grad_ref.shape[1]
    extent = (tile + 1) * Q_TILE
    here, seen = pl.ds(tile * Q_TILE, Q_TILE), pl.ds(0, extent)
    mask_tile(tile, doc_cols, mask_ref)

    def pair_step(pair, carry):
        q_cols = pl.ds(pl.multiple_of(pair * PAIR, PAIR), PAIR)
        k_cols = pl.ds(pl.multiple_of(cols + pair * PAIR, PAIR), PAIR)
        v_cols = pl.ds(pl.multiple_of(2 * cols + pair * PAIR, PAIR), PAIR)
        queries = qkv_ref[here, q_cols] * jnp.asarray(HEAD_DIM**-0.5, bf16)
        keys, values = qkv_ref[seen, k_cols], qkv_ref[seen, v_cols]
        grads = grad_ref[here, q_cols]
        dq = jnp.zeros((PAIR, Q_TILE), f32)
        for half in range(2):
            on = head_mask(half)
            q_one = jnp.where(on, queries, jnp.zeros_like(queries))
            g_one = jnp.where(on, grads, jnp.zeros_like(grads))
            probs = jnp.exp(mm(keys, q_one, 1, 1) + mask_ref[seen, :] - lse_ref[pair, pl.ds(half, 1), here])
            dv_ref[pair, seen, :] += mm(probs.astype(bf16), g_one)
            back = mm(values, g_one, 1, 1)
            low = (probs * (back - jnp.sum(probs * back, axis=0, keepdims=True))).astype(bf16)
            dk_ref[pair, seen, :] += mm(low, q_one)
            got = mm(keys, low, 0, 0)
            sublanes = lax.broadcasted_iota(jnp.int32, (PAIR, 1), 0)
            dq = jnp.where((sublanes // HEAD_DIM) == half, got, dq)
        out_ref[here, q_cols] = (dq.T * HEAD_DIM**-0.5).astype(bf16)
        return carry

    lax.fori_loop(0, cols // PAIR, pair_step, 0)


def finish_kernel(
    up_grads, down_grads, attend_ref, output_ref, up_ref, down_ref, small_ref, layer_ref, tokens_ref,
    expert_up, expert_down, attend_out, output_out, up_out, down_out, layer_out, tokens_out, gain_0, gain_1, blend, router, root,
):
    expert_up[...] = up_grads[...].astype(f32)
    expert_down[...] = down_grads[...].astype(f32)
    lanes, _, units = up_ref.shape
    width = output_out.shape[1]
    for ref, out, parts in ((attend_ref, attend_out, 3), (output_ref, output_out, 1), (up_ref, up_out, units // SMALL)):
        n = ref.shape[2] // parts
        for p in range(parts):
            for l in range(lanes):
                out[:, (p * lanes + l) * n : (p * lanes + l + 1) * n] = ref[l, :, p * n : (p + 1) * n].astype(f32)
    down_out[...] = down_ref[...].astype(f32)
    layer_out[...] = layer_ref[...]
    tokens_out[...] = tokens_ref[...]
    small = small_ref[...]
    gain_0[...] = small[0:1]
    gain_1[...] = small[1:2]
    blend[...] = small[2:4]
    router[...] = small[4 : 4 + router.shape[0]]
    sums = small[small.shape[0] - 1 :]
    root[...] = jnp.sqrt(sums / (jnp.maximum(sums[:, 4:5], 1.0) * width))[:, 0:4]


def finish(experts, up_grads, down_grads, attend_all, output_all, up_all, down_all, small, layer, tokens):
    local, width, units = up_grads.shape
    lanes, shard, _ = up_all.shape
    tile = 256
    steps = local * width // tile
    turns = width // tile
    down_all = down_all.reshape(-1, width)
    count = lambda n: n // steps
    of = jax.ShapeDtypeStruct
    tall = lambda n: pl.BlockSpec((1, tile, n), lambda e, m: (e, m, 0))
    thin = lambda a: pl.BlockSpec((lanes, count(shard), a.shape[2]), lambda e, m: (0, e * turns + m, 0))
    flat = lambda n, c: pl.BlockSpec((count(n), c), lambda e, m: (e * turns + m, 0))
    fixed = lambda *s: pl.BlockSpec(s, lambda e, m: (0, 0))
    outs = [
        (of((local, width, units), f32), pl.BlockSpec((1, tile, units), lambda e, m: (e, m, 0))),
        (of((local, units, width), f32), pl.BlockSpec((1, tile, width), lambda e, m: (e, m, 0))),
        (of((shard, 3 * width), f32), flat(shard, 3 * width)),
        (of((shard, width), f32), flat(shard, width)),
        (of((shard, lanes * units), f32), flat(shard, lanes * units)),
        (of(down_all.shape, f32), flat(*down_all.shape)),
        (of(layer.shape, bf16), flat(*layer.shape)),
        (of(tokens.shape, bf16), flat(*tokens.shape)),
        (of((1, shard), f32), fixed(1, shard)),
        (of((1, shard), f32), fixed(1, shard)),
        (of((2, shard), f32), fixed(2, shard)),
        (of((experts, shard), f32), fixed(experts, shard)),
        (of((1, 4), f32), fixed(1, 4)),
    ]
    return pl.pallas_call(
        finish_kernel,
        grid=(local, turns),
        out_shape=[o for o, _ in outs],
        in_specs=[
            tall(units), tall(width), thin(attend_all), thin(output_all), thin(up_all),
            flat(*down_all.shape), fixed(*small.shape), flat(*layer.shape), flat(*tokens.shape),
        ],
        out_specs=[p for _, p in outs],
        compiler_params=pltpu.CompilerParams(vmem_limit_bytes=63 * 2**20),
        cost_estimate=pl.CostEstimate(flops=0, bytes_accessed=4 * 10**7, transcendentals=0),
        name="finish",
    )(up_grads, down_grads, attend_all, output_all, up_all, down_all, small, layer, tokens)


def take_from(sems):
    sems = list(sems)

    def take(n):
        out = sems[:n]
        del sems[:n]
        return out

    return take


def picked(logits, first, count):
    columns = lax.broadcasted_iota(jnp.int32, logits.shape, 1)
    return soft_max(jnp.where((columns >= first) & (columns < first + count), logits, masked_score))


def middle_kernel(
    groups, lanes, local, cap, experts,
    small, meta_all, place,
    mix_in, cot_in, up_in, down_in, got_mix_in, cot_mine, packed_cot, expert_up, expert_down,
    grad_mix, dense_out, grad_small, mine_up, down_half, tok_part, up_grads, down_grads,
    mix, cot, up, down, act, hidden, got_mix, got_cot, mix_e, grad_e, act_e, hidden_e, expert_in, expert_to,
    mx, mx_c, mx_y, dn, dn_c, dn_y, bk_c, bk_y, gu, gu_x, gu_z, gd, gd_x, ret_back, got_back, dots, coefs,
    load_sem, out_sem, spread_y, spread_c, spread_r, spread_o, *sems,
):
    s = Spot(groups, lanes)
    s.greet()
    everyone, width = mix.shape
    rows = everyone // lanes
    units = up.shape[1]
    slots = got_mix.shape[2]
    shard = width // groups
    rows_e = mix_e.shape[1]
    tile = 256
    step = 64
    take = take_from(sems)

    def blocks(ref, n):
        return lambda i: ref.at[pl.ds(pl.multiple_of(i * n, n), n)]

    def part(i, n=tile):
        return pl.ds(pl.multiple_of(i * n, n), n)

    def load(i, src, dst):
        return pltpu.make_async_copy(src, dst, load_sem.at[i])

    cot_swap = LaneSwap(s, blocks(packed_cot, slots), lambda w: got_cot.at[s.l, w], take(2), range(groups // 2, groups))

    def spread(d):
        w = s.w_peer(groups - d)
        first = d < groups // 2
        return GroupGather(s, cot_mine.at[w] if first else got_cot.at[s.l, w], lambda l: got_cot.at[l, w],
                           [spread_y.at[w], spread_c.at[w], spread_r.at[w], spread_o.at[w]], own=first)

    cot_spread = [spread(d) for d in range(groups)]
    mxs = GroupScatter(s, lambda l: mx.at[l], None, mx_c, mx_y, take(5), False)
    dns = GroupScatter(s, lambda l: dn.at[l], None, dn_c, dn_y, take(5), False)
    near = groups // 2
    bks = [
        GroupScatter(s, lambda l, h=h: got_cot.at[l, pl.ds(h * near, near)], None, bk_c.at[h], bk_y.at[h], take(5), True, near)
        for h in range(2)
    ]
    ups = LaneScatter(s, blocks(gu, shard), None, gu_x, gu_z, take(5))
    dws = LaneScatter(s, blocks(gd, shard), None, gd_x, None, take(5))
    back_swap = LaneSwap(s, blocks(ret_back, slots), blocks(got_back, slots), take(2))

    loads = [load(i, a, b) for i, (a, b) in enumerate([
        (mix_in, mix), (up_in, up), (cot_in, cot), (down_in, down), (got_mix_in, got_mix),
        (expert_up.at[0], expert_in), (expert_down.at[0], expert_to)])]
    more_loads = [load(7, expert_up.at[1], up), load(8, expert_down.at[1], down)]

    def branch(x, grad, w_in, w_to, act_ref, hidden_ref, count):
        dots[pl.ds(0, count), :] = jnp.zeros((count, SMALL), f32)

        def body(n, carry):
            value, slope = gelu_both(mm(x[...], w_in[:, part(n)]))
            value = value.astype(bf16)
            act_ref[pl.ds(0, count), part(n)] = value
            back = mm(grad[...], w_to[part(n), :], 1, 1)
            hidden_ref[pl.ds(0, count), part(n)] = (slope * back).astype(bf16)
            both = value.astype(f32) * back
            dots[pl.ds(0, count), :] += sum([both[:, i * SMALL : (i + 1) * SMALL] for i in range(1, tile // SMALL)], both[:, :SMALL])
            return carry

        lax.fori_loop(0, units // tile, body, 0)
        return jnp.sum(dots[pl.ds(0, count), :], axis=1, keepdims=True)

    for c in loads[:4]:
        c.start()
    s.met()
    cot_swap.start()
    for task in cot_spread[: groups // 2]:
        task.start()
    for c in loads[4:]:
        c.start()
    for c in loads[:4]:
        c.wait()
    columns = lax.broadcasted_iota(jnp.int32, (everyone, SMALL), 1)

    coefs[...] = picked(mm(mix[...], small[...]), 2, 2)
    for l in range(lanes):
        at = pl.ds(l * rows, rows)
        valid = meta_all[l].T[:, 1:2]
        cot[at, :] = (coefs[at, 3:4] * (cot[at, :].astype(f32) * valid)).astype(bf16)
    dot = branch(mix, cot, up, down, act, hidden, everyone)
    for d in range(groups // 2, groups):
        cot_swap.due(d)
        cot_spread[d].start()
    sign = jnp.where(columns == 3, 1.0, 0.0) - jnp.where(columns == 2, 1.0, 0.0)
    logits = (sign * (coefs[:, 2:3] * dot)).astype(bf16)
    grad_small[...] = mm(logits, mix[...], 0, 0)

    def up_grad(m, carry):
        gu[part(m), :] = mm(mix[:, part(m)], hidden[...], 0, 0).astype(bf16)
        return carry

    lax.fori_loop(0, width // tile, up_grad, 0)
    ups.start()
    def down_grad(m, carry):
        gd[part(m), :] = mm(act[:, part(m)], cot[...], 0, 0).astype(bf16)
        return carry

    lax.fori_loop(0, units // tile, down_grad, 0)
    dws.start()

    def mix_grad(n, carry):
        value = mm(hidden[...], up[part(n), :], 1, 1) + mm(logits, small[part(n), :], 1, 1)
        mx[:, :, :, part(n)] = value.astype(bf16).reshape(lanes, rows // step, step, tile)
        return carry

    lax.fori_loop(0, width // tile, mix_grad, 0)
    mxs.start()

    def out_part(n, carry):
        value = mm(act[...], down[:, part(n)])
        dn[:, :, :, part(n)] = value.astype(bf16).reshape(lanes, rows // step, step, tile)
        return carry

    lax.fori_loop(0, width // tile, out_part, 0)
    dns.start()
    for c in more_loads:
        c.start()
    for c in loads[4:]:
        c.wait()

    def apart(src, dst):
        def body(j, carry):
            pair = []
            for i in range(2):
                b = 2 * j + i
                pair.append(src[b % lanes, s.w_at(b // lanes)].astype(f32))
            for e in range(local):
                both = [p[e * cap : (e + 1) * cap] for p in pair]
                dst[e, part(j, 2 * cap), :] = jnp.concatenate(both, axis=0).astype(bf16)
            return carry

        lax.fori_loop(0, lanes * groups // 2, body, 0)

    def together(sources, dst, first=0, last=lanes * groups // 2):
        def body(j, carry):
            values = [src[part(j, 2 * cap), :].astype(f32) for src in sources]
            for i in range(2):
                b = 2 * j + i
                dst[b % lanes, b // lanes] = jnp.concatenate([v[i * cap : (i + 1) * cap] for v in values], axis=0).astype(bf16)
            return carry

        lax.fori_loop(first, last, body, 0)

    apart(got_mix, mix_e)
    for task in cot_spread:
        task.forward()
    mxs.ready()
    mxs.relay()
    for task in cot_spread:
        task.arrive()
    apart(got_cot, grad_e)

    backs, toks = [act, hidden], [mix, cot]
    outs = []
    few = rows_e // 2
    columns = lax.broadcasted_iota(jnp.int32, (few, SMALL), 1)

    def rows_out(h, e):
        w_to = expert_to if e == 0 else down
        at = pl.ds(h * few, few)

        def body(n, carry):
            toks[e][at, part(n)] = mm(act_e[e, at, :], w_to[:, part(n)]).astype(bf16)
            return carry

        lax.fori_loop(0, width // tile, body, 0)

    for h in range(2):
        at = pl.ds(h * few, few)
        for e in range(local):
            w_in, w_to = (expert_in, expert_to) if e == 0 else (up, down)
            if h == 0 and e:
                for c in more_loads:
                    c.wait()
            x, grad = mix_e.at[e, at], grad_e.at[e, at]
            scores = mm(x[...], small[...])
            blend, router = picked(scores, 2, 2), picked(scores, 4, experts)
            own = columns == 4 + s.g * local + e
            chosen = jnp.sum(jnp.where(own, router, 0.0), axis=1, keepdims=True)
            grad[...] = (blend[:, 2:3] * chosen * grad[...].astype(f32)).astype(bf16)
            shares = jnp.where(own, 1.0, 0.0) - router
            shares += blend[:, 3:4] * (jnp.where(columns == 2, 1.0, 0.0) - jnp.where(columns == 3, 1.0, 0.0))
            coefs[pl.ds(0, few), :] = shares
            dot = branch(x, grad, w_in, w_to, act_e.at[e, at], hidden_e.at[e, at], few)
            logits = (dot * coefs[pl.ds(0, few), :]).astype(bf16)
            grad_small[...] += mm(logits, x[...], 0, 0)

            def rows_back(n, carry, e=e, w_in=w_in, logits=logits, at=at):
                value = mm(hidden_e[e, at, :], w_in[part(n), :], 1, 1) + mm(logits, small[part(n), :], 1, 1)
                backs[e][at, part(n)] = value.astype(bf16)
                return carry

            lax.fori_loop(0, width // tile, rows_back, 0)
            if h == 0 and e == 0:
                ups.relay()
                dns.ready()
                dns.relay()
            if h == 1 and e == 0:
                bks[0].ready()
                for k in range(near):
                    bks[0].relay(k)
        if h == 0:
            for task in cot_spread:
                task.sent()
        together([b.at[pl.ds(0, rows_e)] for b in backs], got_cot, h * lanes * groups // 4, (h + 1) * lanes * groups // 4)
        bks[h].start()

    def hand_back(h):
        for k in range(near):
            p = h * near + k
            w = s.w_at(p)
            bks[h].got(k)
            ret_back[pl.ds(pl.multiple_of(w * slots, slots), slots), :] = bks[h].total(k).astype(bf16)
            if p < groups - 1:
                back_swap.copy(p + 1).start()
            else:
                back_swap.own().start()

    rows_out(0, 0)
    bks[1].ready()
    for k in range(near):
        bks[1].relay(k)
    hand_back(0)
    rows_out(0, 1)
    rows_out(1, 0)
    rows_out(1, 1)

    def weight_grads(e, which=(0, 1)):
        up_to, down_to = (expert_in, expert_to) if e == 0 else (up, down)

        pieces = [(up_to, up_grads, mix_e, hidden_e), (down_to, down_grads, act_e, grad_e)]
        for i in which:
            to, out, left, right = pieces[i]

            def body(m, carry, to=to, left=left, right=right):
                to[part(m), :] = mm(left[e, :, part(m)], right[e], 0, 0).astype(bf16)
                return carry

            lax.fori_loop(0, width // tile, body, 0)
            outs.append(pltpu.make_async_copy(to, out.at[e], out_sem.at[2 * e + i]))
            outs[-1].start()

    together([t.at[pl.ds(0, rows_e)] for t in toks], got_mix)
    outs.append(pltpu.make_async_copy(got_mix, tok_part, out_sem.at[4 * local]))
    outs[-1].start()

    def totals(scatter, dst):
        scatter.got()

        def body(k, carry):
            dst[pl.ds(pl.multiple_of(k * step, step), step), :] = scatter.total(k).astype(dst.dtype)
            return carry

        lax.fori_loop(0, scatter.chunks, body, 0)

    totals(mxs, grad_mix)
    weight_grads(0, (0,))
    hand_back(1)
    weight_grads(0, (1,))
    weight_grads(1)
    dws.fold(down_half)
    totals(dns, dense_out)
    ups.finish(mine_up)
    back_swap.arrive()
    grad_mix[...] += mm(place[...], got_back[...])
    for c in outs:
        c.wait()
    dws.x_sent()
    for task in [cot_swap, mxs, dns, *bks, ups, back_swap]:
        task.sent()


def middle(groups, lanes, local, cap, experts, slots, inputs, placed):
    rows, width = inputs[2].shape[0], inputs[0].shape[0]
    X = 1 << ((groups.bit_length() - 1) // 2)
    Y, Z = lanes // 2, groups // X
    everyone = rows * lanes
    shard = width // groups
    units = placed[2].shape[1]
    rows_e = lanes * groups * cap
    vmem, anywhere = pl.BlockSpec(memory_space=pltpu.VMEM), pl.BlockSpec(memory_space=pl.ANY)
    dma = pltpu.SemaphoreType.DMA
    of = jax.ShapeDtypeStruct
    low = lambda *shape: pltpu.VMEM(shape, bf16)
    wide = lambda *shape: pltpu.VMEM(shape, f32)
    expert_rows = (local, rows_e, width)
    outs = [
        (of((rows, width), f32), vmem),
        (of((rows, width), bf16), vmem),
        (of((SMALL, width), f32), vmem),
        (of((shard, units), bf16), vmem),
        (of((Z, shard, width), bf16), vmem),
        (of((lanes, groups, slots, width), bf16), anywhere),
        (of((local, width, units), bf16), anywhere),
        (of((local, units, width), bf16), anywhere),
    ]
    scratch = [low(everyone, width), low(everyone, width), low(width, units), low(units, width)]
    scratch += [low(everyone, units), low(everyone, units)]
    scratch += [low(lanes, groups, slots, width)] * 2
    scratch += [low(*expert_rows), low(*expert_rows), low(local, rows_e, units), low(local, rows_e, units)]
    scratch += [low(width, units), low(units, width)]
    scratch += [low(lanes, rows // 64, 64, width), low(Y, rows // 64, 64, width), low(Y - 1, rows // 64, 64, width)] * 2
    scratch += [low(2, Y, groups // 2, slots, width), low(2, Y - 1, groups // 2, slots, width)]
    scratch += [low(width, units), low(X - 1, Z, shard, units), low(Z - 1, shard, units)]
    scratch += [low(units, width), low(X - 1, Z, shard, width)]
    scratch += [low(groups * slots, width)] * 2 + [wide(everyone, SMALL)] * 2
    scratch += [dma((9,)), dma((4 * local + 1,)), dma((groups, Y)), dma((groups, Y)), dma((groups, lanes)), dma((groups, 1))]
    scratch += LaneSwap.sems(groups) + GroupScatter.sems(lanes, 1) * 2 + GroupScatter.sems(lanes, groups // 2) * 2
    scratch += LaneScatter.sems(groups, X) * 2 + LaneSwap.sems(groups)
    return pl.pallas_call(
        functools.partial(middle_kernel, groups, lanes, local, cap, experts),
        out_shape=[o for o, _ in outs],
        in_specs=[vmem] * len(inputs) + [anywhere] * len(placed),
        out_specs=[p for _, p in outs],
        scratch_shapes=scratch,
        compiler_params=pltpu.CompilerParams(collective_id=2, has_side_effects=True, vmem_limit_bytes=62 * 2**20),
        cost_estimate=pl.CostEstimate(flops=35 * 10**9, bytes_accessed=10**8, transcendentals=0),
        name="middle",
    )(*inputs, *placed)


def back_kernel(
    groups, lanes, experts,
    tokens, cot, small, attention_out, attn_mixed, place, meta_all, lse, grad_small, grad_mix_in, dense_out,
    mine_up, down_half, tok_part, qkv_in, output_in, attend_in, normed_in,
    layer_out, grad_tokens, small_out, all_attend, all_output, all_up, all_down,
    qkv, output_all, attend_all, normed, tk_h, tk_c, tk_y,
    go, go_c, go_y, gn, gn_c, gn_y, dw_z, ga, ga_x, ga_z, gl, gl_x, gl_z,
    sm, sm_x, sm_z, sm_mine, sm_all, ret_tok, got_tok, grad_mix, grad_mid, grad_attn, grad_mixed,
    grad_heads, grad_qkv, mask, dk, dv, valid_cols, mine_attend, mine_output, mine_down, stage_sem, *sems,
):
    s = Spot(groups, lanes)
    s.greet()
    rows, width = tokens.shape
    head_cols = width // lanes
    slots = place.shape[1] // groups
    shard = width // groups
    take = take_from(sems)
    step = 64

    def blocks(ref, n):
        return lambda i: ref.at[pl.ds(pl.multiple_of(i * n, n), n)]

    def cols(i):
        return pl.ds(pl.multiple_of(i * head_cols, head_cols), head_cols)

    loads = [
        pltpu.make_async_copy(src, dst, stage_sem.at[i])
        for i, (src, dst) in enumerate(
            [(output_in, output_all), (qkv_in, qkv), (attend_in, attend_all), (normed_in, normed)])
    ]
    tk = GroupScatter(s, lambda l: tok_part.at[l], tk_h, tk_c, tk_y, take(5), True)
    gos = GroupScatter(s, lambda l: go.at[l], None, go_c, go_y, take(5), False)
    gns = GroupScatter(s, lambda l: gn.at[l], None, gn_c, gn_y, take(5), False)
    dws = ZScatter(s, lambda d: down_half.at[d], dw_z, take(2))
    gas = [LaneScatter(s, blocks(ga.at[p], shard), None, ga_x.at[p], ga_z.at[p], take(5)) for p in range(3)]
    gls = LaneScatter(s, blocks(gl, shard), None, gl_x, gl_z, take(5))
    sms = LaneScatter(s, lambda w: sm.at[w], None, sm_x, sm_z, take(5))
    tok_swap = LaneSwap(s, blocks(ret_tok, slots), blocks(got_tok, slots), take(2))
    heads = GroupSwap(s, lambda l: grad_mixed.at[:, cols(l)], blocks(grad_heads, rows), take(2))
    f_attend = GroupGather(s, mine_attend, lambda l: all_attend.at[l], take(4))
    f_output = GroupGather(s, mine_output, lambda l: all_output.at[l], take(4))
    f_up = GroupGather(s, mine_up, lambda l: all_up.at[l], take(4))
    f_down = GroupGather(s, mine_down, lambda l: all_down.at[l], take(4))
    f_small = GroupGather(s, sm_mine, lambda l: sm_all.at[l], take(4))

    def pass_on(first, last):
        for p in range(first, last):
            tk.relay(p)

    def hand_back(first, last):
        for p in range(first, last):
            w = s.w_at(p)
            tk.got(p)
            ret_tok[pl.ds(pl.multiple_of(w * slots, slots), slots), :] = tk.total(p).astype(bf16)
            if p < groups - 1:
                tok_swap.copy(p + 1).start()
            else:
                tok_swap.own().start()

    def totals(scatter, dst):
        scatter.got()

        def body(k, carry):
            dst[pl.ds(pl.multiple_of(k * step, step), step), :] = scatter.total(k).astype(dst.dtype)
            return carry

        lax.fori_loop(0, scatter.chunks, body, 0)

    def over_rows(body, init):
        return lax.fori_loop(0, rows // step, lambda i, c: body(pl.ds(pl.multiple_of(i * step, step), step), c), init)

    for c in loads:
        c.start()
    dk[...] = jnp.zeros_like(dk)
    dv[...] = jnp.zeros_like(dv)
    gains = small[...].astype(f32).T
    mine = meta_all[s.l].T
    valid_cols[...] = jnp.broadcast_to(mine[:, 1:2], valid_cols.shape)

    def mid(at, gain_sum):
        normed_v, scale = norm_stats(tokens[at, :].astype(f32) + attention_out[at, :])
        grad = grad_mix_in[at, :]
        value = cot[at, :].astype(f32) * valid_cols[at, 0:1] + norm_back(normed_v, scale, gains[1:2, :], grad)
        grad_mid[at, :] = value
        grad_attn[at, :] = value.astype(bf16)
        return gain_sum + jnp.sum(grad * normed_v, axis=0, keepdims=True)

    mixer_gain_grad = over_rows(mid, jnp.zeros((1, width), f32))
    loads[0].wait()
    grad_mixed[...] = mm(grad_attn[...], output_all[...], 1, 1).astype(bf16)
    s.met()
    for l in range(lanes):
        heads.send(l)
    tk.start()
    dws.start()

    def out_grad(m, carry):
        value = mm(attn_mixed[:, cols(m)], grad_attn[...], 0, 0).astype(bf16)
        parts = head_cols // step
        for l in range(lanes):
            go[l, pl.ds(m * parts, parts)] = value[:, l * head_cols : (l + 1) * head_cols].reshape(parts, step, head_cols)
        return carry

    lax.fori_loop(0, lanes, out_grad, 0)
    gos.start()
    for c in loads[1:]:
        c.wait()
    heads.arrive()
    tk.ready()
    pass_on(0, groups)
    f_up.start()
    doc_cols = [meta_all[l].T[:, 0:1] for l in range(lanes)]
    for tile in range(lanes):
        attend_back_tile(tile, qkv, doc_cols, lse, grad_heads, grad_qkv, mask, dk, dv)
        if tile == 0:
            gos.ready()
            gos.relay()
        if tile == 2:
            hand_back(0, groups // 2)
    for pair in range(head_cols // PAIR):
        grad_qkv[:, head_cols + pair * PAIR : head_cols + (pair + 1) * PAIR] = dk[pair].astype(bf16)
        grad_qkv[:, 2 * head_cols + pair * PAIR : 2 * head_cols + (pair + 1) * PAIR] = dv[pair].astype(bf16)

    def attend_grad(p):
        def body(m, carry):
            value = mm(normed[:, cols(m)], grad_qkv[:, p * head_cols : (p + 1) * head_cols], 0, 0)
            ga[p, pl.ds(pl.multiple_of(m * head_cols, head_cols), head_cols), :] = value.astype(bf16)
            return carry

        lax.fori_loop(0, lanes, body, 0)
        gas[p].start()

    def rows_grad(l, carry):
        value = mm(grad_qkv[pl.ds(pl.multiple_of(l * rows, rows), rows), :], attend_all[...], 1, 1)
        gn[l] = value.astype(bf16).reshape(rows // step, step, width)
        return carry

    attend_grad(0)
    lax.fori_loop(0, lanes, rows_grad, 0)
    gns.start()
    attend_grad(1)
    attend_grad(2)
    gns.ready()
    gns.relay()
    hand_back(groups // 2, groups)
    gas[0].relay()
    totals(gos, gl)
    gls.start()
    gas[1].relay()
    gas[2].relay()
    f_up.forward()
    tok_swap.arrive()

    def layer(at, sums):
        attention = attention_out[at, :]
        residual = tokens[at, :].astype(f32) + attention
        normed_v, _ = norm_stats(residual)
        mix = (normed_v * gains[1:2, :]).astype(bf16)
        logits = mm(mix, small[...])
        blend, router = picked(logits, 2, 2), picked(logits, 4, experts)
        columns = lax.broadcasted_iota(jnp.int32, logits.shape, 1)
        route = valid_cols[at, 1:2].astype(jnp.int32)
        chosen = jnp.sum(jnp.where(columns == 4 + route, router, 0.0), axis=1, keepdims=True)
        ffn = blend[:, 2:3] * chosen * mm(place[at, :], got_tok[...]) + blend[:, 3:4] * dense_out[at, :].astype(f32)
        full = residual + ffn
        layer_out[at, :] = full.astype(bf16)
        valid = valid_cols[at, 0:1]
        got = [jnp.sum(valid * v * v, axis=(0, 1), keepdims=True) for v in (residual, full, attention, ffn)]
        got.append(jnp.sum(valid, axis=(0, 1), keepdims=True))
        return tuple(a + b for a, b in zip(sums, got))

    lane_of = lax.broadcasted_iota(jnp.int32, valid_cols.shape, 1)
    valid_cols[...] = jnp.where(lane_of == 1, mine[:, 2:3], mine[:, 1:2])
    sums = over_rows(layer, tuple(jnp.zeros((1, 1), f32) for _ in range(5)))
    totals(gns, grad_mix)

    def first(at, gain_sum):
        normed_v, scale = norm_stats(tokens[at, :].astype(f32))
        grad = grad_mix[at, :]
        grad_tokens[at, :] = (grad_mid[at, :] + norm_back(normed_v, scale, gains[0:1, :], grad)).astype(bf16)
        return gain_sum + jnp.sum(grad * normed_v, axis=0, keepdims=True)

    attend_gain_grad = over_rows(first, jnp.zeros((1, width), f32))
    used = sm_mine.shape[0]
    feature = lax.broadcasted_iota(jnp.int32, (used, shard), 0)
    place_of = lax.broadcasted_iota(jnp.int32, (used, shard), 1)
    tail = jnp.zeros((used, shard), f32)
    for i, v in enumerate(sums):
        tail = jnp.where(place_of == i, v, tail)
    for w in range(groups):
        here = slice(w * shard, (w + 1) * shard)
        value = jnp.where(feature == used - 1, tail, grad_small[0:used, here])
        value = jnp.where(feature == 0, attend_gain_grad[:, here], value)
        sm[w] = jnp.where(feature == 1, mixer_gain_grad[:, here], value)
    sms.start()
    gls.relay()
    dws.finish(mine_down)
    f_down.start()
    sms.relay()
    for p in range(3):
        gas[p].finish(mine_attend.at[:, pl.ds(p * head_cols, head_cols)])
    f_attend.start()
    gls.finish(mine_output)
    f_output.start()
    sms.finish(sm_mine)
    f_small.start()
    gathers = [f_up, f_down, f_attend, f_output, f_small]
    for task in gathers[1:]:
        task.forward()
    for task in gathers:
        task.arrive()
    small_out[...] = sum([sm_all[l] for l in range(1, lanes)], sm_all[0])
    for task in [tk, gos, gns, dws, *gas, gls, sms, tok_swap, heads] + gathers:
        task.sent()


def back(groups, lanes, experts, slots, inputs, placed):
    tokens = inputs[0]
    rows, width = tokens.shape
    X = 1 << ((groups.bit_length() - 1) // 2)
    Y, Z = lanes // 2, groups // X
    everyone = rows * lanes
    head_cols = width // lanes
    shard = width // groups
    hidden = inputs[-2].shape[1]
    vmem, anywhere = pl.BlockSpec(memory_space=pltpu.VMEM), pl.BlockSpec(memory_space=pl.ANY)
    dma = pltpu.SemaphoreType.DMA
    of = jax.ShapeDtypeStruct
    pairs = head_cols // PAIR
    low = lambda *shape: pltpu.VMEM(shape, bf16)
    wide = lambda *shape: pltpu.VMEM(shape, f32)

    def group_bufs(c, r, n, held=True):
        return ([low(Y, c, r, n)] if held else [low(lanes, c, r, n)]) + [low(Y, c, r, n), low(Y - 1, c, r, n)]

    def lane_bufs(n, held=True):
        return ([low(Z, shard, n)] if held else [low(width, n)]) + [low(X - 1, Z, shard, n), low(Z - 1, shard, n)]

    scratch = [low(everyone, 3 * head_cols), low(width, width), low(width, 3 * head_cols), low(everyone, width)]
    scratch += group_bufs(groups, slots, width)
    scratch += group_bufs(width // 64, 64, head_cols, False) + group_bufs(rows // 64, 64, width, False)
    scratch += [low(Z - 1, shard, width)] + [low(3, width, head_cols), low(3, X - 1, Z, shard, head_cols), low(3, Z - 1, shard, head_cols)] + lane_bufs(head_cols, False)
    used = -(-(5 + experts) // 8) * 8
    scratch += [wide(groups, used, shard), wide(X - 1, Z, used, shard), wide(Z - 1, used, shard)]
    scratch += [wide(used, shard), wide(lanes, used, shard)]
    scratch += [low(groups * slots, width)] * 2
    scratch += [wide(rows, width), wide(rows, width), low(rows, width), low(rows, width)]
    scratch += [low(everyone, head_cols), low(everyone, 3 * head_cols), wide(everyone, Q_TILE)]
    scratch += [wide(pairs, everyone, PAIR)] * 2 + [wide(rows, SMALL)]
    scratch += [low(shard, 3 * head_cols), low(shard, head_cols), low(shard, width)]
    scratch += [dma((4,))]
    scratch += GroupScatter.sems(lanes, groups) + GroupScatter.sems(lanes, 1) * 2
    scratch += [dma((Z,))] * 2 + LaneScatter.sems(groups, X) * 5
    scratch += LaneSwap.sems(groups) + GroupSwap.sems(lanes)
    scratch += GroupGather.sems(lanes) * 5
    outs = [
        (of((rows, width), bf16), vmem),
        (of((rows, width), bf16), vmem),
        (of((used, shard), f32), vmem),
        (of((lanes, shard, 3 * head_cols), bf16), anywhere),
        (of((lanes, shard, head_cols), bf16), anywhere),
        (of((lanes, shard, hidden), bf16), anywhere),
        (of((lanes, shard, width), bf16), anywhere),
    ]
    return pl.pallas_call(
        functools.partial(back_kernel, groups, lanes, experts),
        out_shape=[o for o, _ in outs],
        in_specs=[vmem] * len(inputs) + [anywhere] * len(placed),
        out_specs=[p for _, p in outs],
        scratch_shapes=scratch,
        compiler_params=pltpu.CompilerParams(collective_id=1, has_side_effects=True, vmem_limit_bytes=62 * 2**20),
        cost_estimate=pl.CostEstimate(flops=8 * 10**9, bytes_accessed=10**8, transcendentals=0),
        name="back",
    )(*inputs, *placed)


def lane_gather(part):
    return lax.all_gather(part, "wide", axis=0, tiled=True)


def lane_scatter(part):
    return lax.psum_scatter(part.astype(bf16), "wide", scatter_dimension=0, tiled=True)


def group_gather(part, axis=0):
    return lax.all_gather(part, "narrow", axis=axis, tiled=True)


def group_scatter(part, axis=0):
    return lax.psum_scatter(part.astype(bf16), "narrow", scatter_dimension=axis, tiled=True)


def lane_swap(part):
    return lax.all_to_all(part, "wide", split_axis=0, concat_axis=0, tiled=True)


def per_device(
    tokens, doc_ids, valid_mask, routes, cotangent, attend_gain, attend_weight, output_weight, mixer_gain,
    router_weight, blend_weight, up_weight, down_weight, expert_up, expert_down,
):
    rows, width = tokens.shape
    groups, lanes = lax.axis_size("wide"), lax.axis_size("narrow")
    group, lane = lax.axis_index("wide"), lax.axis_index("narrow")
    shard = attend_gain.shape[0]
    local = expert_up.shape[0]
    experts = local * groups
    hidden = up_weight.shape[1]
    fine = hidden // groups // lanes
    cap = max(2, (3 * rows + 2 * experts - 1) // (2 * experts))
    slots = -(-local * cap // 16) * 16
    all_rows = rows * lanes

    little = (
        doc_ids.reshape(1, rows), valid_mask.reshape(1, rows), routes.reshape(1, rows), attend_gain.reshape(1, shard),
        mixer_gain.reshape(1, shard), blend_weight.T, router_weight.T,
    )
    up_mine = up_weight
    if fine % 128:
        up_mine = lax.dynamic_index_in_dim(up_weight.reshape(shard, groups, lanes, fine), lane, 2, keepdims=False)
        up_mine = up_mine.reshape(shard, groups * fine)
    (
        lse, attn_mixed, attention_out, small, meta_all, place, packed_cot, normed_attend, qkv, attend_full, output_full, mix_all,
        got_mix, cot_mine, cot_all, up_full, down_full,
    ) = front(groups, lanes, local, cap, slots, tokens, cotangent, little, attend_weight, output_weight, up_mine, down_weight)
    doc_col = meta_all[:, 0].reshape(all_rows, 1)
    valid_all = meta_all[:, 1].reshape(all_rows, 1)
    attend_gain_row = small[:, 0].astype(f32)
    mixer_gain_row = small[:, 1].astype(f32)
    mix_cols = jnp.where((jnp.arange(SMALL) < 2)[None, :], 0, small)
    residual_mid = tokens.astype(f32) + attention_out
    mid_normed, mid_scale = norm_stats(residual_mid)
    normed_mix = (mid_normed * mixer_gain_row).astype(bf16)
    route = routes[:, 0]

    def give_back(partial):
        return mm(place, lane_swap(group_scatter(partial)))

    valid = valid_mask.astype(f32)[:, None]
    grad_layer = cotangent.astype(f32) * valid

    def widen(gathered, parts):
        full = gathered.reshape(lanes, shard, parts, -1)
        return full.transpose(1, 2, 0, 3).reshape(shard, -1).astype(f32)

    if all_rows * width <= 2**20 and shard % 128 == 0 and cap % 8 == 0 and slots == local * cap and local == 2 and fine == 128 and width == groups * fine and lanes * groups * cap <= all_rows:
        grad_mix, dense_out, grad_small, mine_up, down_half, tok_part, up_grads, down_grads = middle(
            groups, lanes, local, cap, experts, slots, (small, meta_all, place),
            (mix_all, cot_all, up_full, down_full, got_mix, cot_mine, packed_cot, expert_up, expert_down))
        layer_out, grad_tokens, small_out, out_attend, out_output, out_up, out_down = back(
            groups, lanes, experts, slots,
            (tokens, cotangent, small, attention_out, attn_mixed, place, meta_all, lse, grad_small, grad_mix,
             dense_out, mine_up, down_half),
            (tok_part, qkv, output_full, attend_full, normed_attend))
        (
            grad_expert_up, grad_expert_down, out_attend, out_output, out_up, out_down, layer_out, grad_tokens, gain_0, gain_1,
            out_blend, out_router, root,
        ) = finish(
            experts, up_grads, down_grads, out_attend, out_output, out_up, out_down, small_out, layer_out, grad_tokens)
        return (
            layer_out, grad_tokens, gain_0.reshape(shard), out_attend, out_output, gain_1.reshape(shard), out_router.T,
            out_blend.T, out_up, out_down, grad_expert_up, grad_expert_down, root.reshape(4),
        )

    got_cot = group_gather(lane_swap(packed_cot.reshape(groups, slots, width))[None])

    def coefficients(mix_rows):
        logits = mm(mix_rows, mix_cols)
        columns = jnp.arange(SMALL)[None, :]
        blend = soft_max(jnp.where((columns >= 2) & (columns < 4), logits, masked_score))
        router = soft_max(jnp.where((columns >= 4) & (columns < 4 + experts), logits, masked_score))
        return columns, blend, router

    columns, blend, _ = coefficients(mix_all)
    blend_0, blend_1 = blend[:, 2:3], blend[:, 3:4]
    grad_dense = (blend_1 * (cot_all.astype(f32) * valid_all.astype(f32))).astype(bf16)
    up_act, up_slope = gelu_both(mm(mix_all, up_full))
    up_act = up_act.astype(bf16)
    dense_part = mm(up_act, down_full)
    grad_up_act = mm(grad_dense, down_full, 1, 1)
    dense_dot = jnp.sum(up_act.astype(f32) * grad_up_act, axis=1, keepdims=True)
    grad_up_pre = (up_slope * grad_up_act).astype(bf16)
    dense_logits = (jnp.where(columns == 3, 1.0, 0.0) - jnp.where(columns == 2, 1.0, 0.0)) * (blend_0 * dense_dot)
    grad_mix_part = mm(grad_up_pre, up_full, 1, 1) + mm(dense_logits.astype(bf16), mix_cols, 1, 1)
    grad_small = mm(dense_logits.astype(bf16), mix_all, 0, 0)
    grad_up = mm(mix_all, grad_up_pre, 0, 0)
    grad_down = mm(up_act, grad_dense, 0, 0)

    def by_expert(received):
        split = received.reshape(lanes * groups, slots, width)[:, : local * cap]
        return split.reshape(lanes * groups, local, cap, width).transpose(1, 0, 2, 3).reshape(local, -1, width)

    def by_slot(values):
        split = values.reshape(local, lanes * groups, cap, width).transpose(1, 0, 2, 3)
        split = split.reshape(lanes * groups, local * cap, width)
        return jnp.pad(split, ((0, 0), (0, slots - local * cap), (0, 0))).reshape(-1, width)

    mix_e, cot_e = by_expert(got_mix), by_expert(got_cot)
    tok_parts, back_parts, up_grads, down_grads = [], [], [], []
    for e in range(local):
        _, blend, router = coefficients(mix_e[e])
        own = columns == 4 + group * local + e
        chosen = jnp.sum(jnp.where(own, router, 0.0), axis=1, keepdims=True)
        scale = blend[:, 2:3] * chosen
        grad_tok = (scale * cot_e[e].astype(f32)).astype(bf16)
        act, slope = gelu_both(mm(mix_e[e], expert_up[e]))
        act = act.astype(bf16)
        tok_parts.append((mm(act, expert_down[e])))
        grad_act = mm(grad_tok, expert_down[e], 1, 1)
        dot = jnp.sum(act.astype(f32) * grad_act, axis=1, keepdims=True)
        grad_hidden = (slope * grad_act).astype(bf16)
        logits = dot * (jnp.where(own, 1.0, 0.0) - router)
        logits += dot * blend[:, 3:4] * (jnp.where(columns == 2, 1.0, 0.0) - jnp.where(columns == 3, 1.0, 0.0))
        logits = logits.astype(bf16)
        back_parts.append(mm(grad_hidden, expert_up[e], 1, 1) + mm(logits, mix_cols, 1, 1))
        grad_small += mm(logits, mix_e[e], 0, 0)
        down_grads.append(mm(act, grad_tok, 0, 0))
        up_grads.append(mm(mix_e[e], grad_hidden, 0, 0))
    grad_expert_up, grad_expert_down = jnp.stack(up_grads), jnp.stack(down_grads)
    grad_small = grad_small.T
    expert_back = give_back(by_slot(jnp.stack(back_parts)))
    expert_tok = give_back(by_slot(jnp.stack(tok_parts)))

    dense_out = group_scatter(dense_part).astype(f32)
    _, blend, router = coefficients(normed_mix)
    own = columns == 4 + route[:, None]
    chosen = jnp.sum(jnp.where(own, router, 0.0), axis=1, keepdims=True)
    ffn_out = blend[:, 2:3] * chosen * expert_tok + blend[:, 3:4] * dense_out
    layer_full = residual_mid + ffn_out
    sums = jnp.stack(
        [jnp.sum(valid * v * v) for v in (residual_mid, layer_full, attention_out, ffn_out)] + [jnp.sum(valid)])

    grad_mix = group_scatter(grad_mix_part).astype(f32) + expert_back
    grad_mid = grad_layer + norm_back(mid_normed, mid_scale, mixer_gain_row, grad_mix)
    mixer_gain_grad = jnp.sum(grad_mix * mid_normed, axis=0)
    grad_attn = grad_mid.astype(bf16)
    grad_output = mm(attn_mixed, grad_attn, 0, 0)
    grad_mixed = mm(grad_attn, output_full, 1, 1).astype(bf16)
    grad_heads = lax.all_to_all(grad_mixed, "narrow", split_axis=1, concat_axis=0, tiled=True)
    grad_qkv = attend_back(qkv, doc_col, lse, grad_heads)
    grad_attend = mm(normed_attend, grad_qkv, 0, 0)
    grad_normed = group_scatter(mm(grad_qkv, attend_full, 1, 1)).astype(f32)
    in_normed, in_scale = norm_stats(tokens.astype(f32))
    grad_tokens = (grad_mid + norm_back(in_normed, in_scale, attend_gain_row, grad_normed)).astype(bf16)
    attend_gain_grad = jnp.sum(grad_normed * in_normed, axis=0)

    grad_small = jnp.where(columns == 0, attend_gain_grad[:, None], jnp.where(columns == 1, mixer_gain_grad[:, None], grad_small))
    small_out = lax.psum(lax.psum_scatter(grad_small, "wide", scatter_dimension=0, tiled=True), "narrow")
    sums = lax.psum(sums, ("wide", "narrow"))
    root_means = jnp.sqrt(sums[:4] / (jnp.maximum(sums[4], 1.0) * width))

    def share(part):
        return group_gather(part.astype(bf16)[None])

    out_attend = widen(share(lane_scatter(grad_attend)), 3)
    out_output = widen(share(lane_scatter(group_scatter(grad_output, axis=1))), 1)
    out_up = widen(share(lane_scatter(grad_up)), groups)
    out_down = group_gather(lane_scatter(grad_down).astype(bf16)).astype(f32)
    return (
        layer_full.astype(bf16), grad_tokens, small_out[:, 0], out_attend, out_output, small_out[:, 1],
        small_out[:, 4 : 4 + experts], small_out[:, 2:4], out_up, out_down, grad_expert_up, grad_expert_down, root_means,
    )


def solution(mesh):
    both = ("wide", "narrow")
    row, vec, mat = P(both, None), P("wide"), P("wide", None)
    up, down = P("wide", None, "narrow"), P("wide", "narrow", None)
    return jax.shard_map(
        per_device,
        mesh=mesh,
        in_specs=(row, P(both), P(both), row, row, vec, mat, mat, vec, mat, mat, mat, mat, up, down),
        out_specs=(row, row, vec, mat, mat, vec, mat, mat, mat, mat, up, down, P()),
        check_vma=False,
    )
```
